32 devices in a mesh: member: 4 (over z), lat: 4 (over y, core), lon: 2 (over x).
Axes of the slice: x: 2, y: 2, z: 4, core: 2. Of those that a mesh axis runs over, the one named last changes fastest.
Arguments:
- state: float32 [8, 5, 2, 128, 1024], P('member', None, None, 'lat', 'lon'), may hold values from -4 to 4
- kick: float32 [8, 5, 2, 128, 1024], P('member', None, None, 'lat', 'lon'), may hold values from -3 to 3
- forcing: float32 [5, 2, 128, 1024], P(None, None, 'lat', 'lon'), may hold values from -4 to 4
- coupling: float32 [2, 5, 5], replicated, may hold values from -3 to 3
- clone_src: int32 [8], replicated, may hold values from 0 to 7, as said below
Outputs:
- advanced: float32 [8, 5, 2, 128, 1024], P('member', None, None, 'lat', 'lon')
The draws below stay inside these ranges and needn't reach their ends.
Inputs may be any that keep to these rules, and one draw needn't show every extreme that they name: `clone_src`: entry m equals m for a member that is kept; a replaced member names a member that is kept.
All inputs are finite; a program needn't handle non-finite values.
Results may differ from the reference program's by a relative error of at most 0.00012.
Values sent between devices are 32-bit elements; how exact they have to be, the bound alone decides.
No kernel may reach another device: no remote copies, remote signals or barrier semaphores. Data moves between devices by JAX's collectives and lax.ppermute only.
A program may use at most 128 MiB of HBM per device.

```python
import jax
import jax.numpy as jnp
from jax import lax

VARS = 5
LEV = 2
STEPS = 4
MEM_DEV = 2
MEMBERS = 8
NLAT = 128
NLON = 1024


def draw_clone_src(key, part):
    keys = jax.random.split(key, 5)
    order = jax.random.permutation(keys[0], MEMBERS).astype(jnp.int32)
    cutoff = jax.random.randint(keys[1], (), 1, MEMBERS // 2 + 1).astype(jnp.int32)
    places = jnp.argsort(order, stable=True).astype(jnp.int32)
    replaced = places < cutoff
    first = jax.random.randint(keys[2], (MEMBERS,), 0, MEMBERS).astype(jnp.int32)
    second = jax.random.randint(keys[3], (MEMBERS,), 0, MEMBERS).astype(jnp.int32)
    ranks = jnp.minimum(first, second) % (MEMBERS - cutoff)
    source = jnp.take(order, cutoff + ranks)
    result = jnp.where(replaced, source, jnp.arange(MEMBERS, dtype=jnp.int32)).astype(jnp.int32)
    groups = MEMBERS // MEM_DEV
    anchor = jax.random.randint(keys[4], (), 0, groups).astype(jnp.int32)
    giver = (anchor * MEM_DEV).astype(jnp.int32)
    taker = ((anchor + 1) % groups * MEM_DEV + (MEM_DEV - 1)).astype(jnp.int32)
    result = jnp.where(result == taker, giver, result).astype(jnp.int32)
    result = result.at[giver].set(giver)
    result = result.at[taker].set(giver)
    return result.astype(jnp.int32)


def block_scale(key, shape, cuts, low, high):
    def one(axis_at, blocks):
        steps = jax.random.uniform(jax.random.fold_in(jax.random.fold_in(key, 6), axis_at), (blocks,), jnp.float32, low / len(cuts), high / len(cuts))
        return jnp.repeat(jnp.exp(steps), shape[axis_at] // blocks).reshape((-1,) + (1,) * (len(shape) - axis_at - 1))

    loudness = one(*cuts[0])
    for cut in cuts[1:]:
        loudness = loudness * one(*cut)
    return loudness


def bell_draw(own_key, extent, scale, most, cuts=(), kind=jnp.bfloat16):
    entries = scale * jax.random.normal(own_key, extent, jnp.float32)
    if cuts:
        entries = entries * block_scale(own_key, extent, cuts, -0.22, 0.18)
    return jnp.clip(entries, -most, most).astype(kind)


def setup_inputs(seed: int = 0) -> dict:
    seeds = jax.random.split(jax.random.key(seed), 6)
    state = bell_draw(seeds[0], (MEMBERS, VARS, LEV, NLAT, NLON), 1.0, 4.0, ((0, 4), (3, 4), (4, 2)), jnp.float32)
    kick = bell_draw(seeds[1], (MEMBERS, VARS, LEV, NLAT, NLON), 0.3, 3.0, ((0, 4), (3, 4), (4, 2)), jnp.float32)
    forcing = bell_draw(seeds[2], (VARS, LEV, NLAT, NLON), 1.0, 4.0, ((2, 4), (3, 2)), jnp.float32)
    coupling = bell_draw(seeds[3], (LEV, VARS, VARS), 0.3, 3.0, (), jnp.float32)
    clone_src = draw_clone_src(jax.random.fold_in(seeds[5], 71), 0)
    return {"state": state, "kick": kick, "forcing": forcing, "coupling": coupling, "clone_src": clone_src}


def advance(padded, forcing_c, coupling):
    h = padded.shape[3] - 4
    w = padded.shape[4] - 4

    def part(di, dj):
        return padded[:, :, :, 2 + di:2 + di + h, 2 + dj:2 + dj + w]

    centre = part(0, 0)
    along_x = (8.0 * (part(0, 1) - part(0, -1)) - (part(0, 2) - part(0, -2))) / 12.0
    along_y = (8.0 * (part(1, 0) - part(-1, 0)) - (part(2, 0) - part(-2, 0))) / 12.0
    near = part(0, 1) + part(0, -1) + part(1, 0) + part(-1, 0)
    far_sum = part(0, 2) + part(0, -2) + part(2, 0) + part(-2, 0)
    laplace = (16.0 * near - far_sum - 60.0 * centre) / 12.0
    wind_u = centre[:, 0:1]
    wind_v = centre[:, 1:2]
    mixed = jnp.einsum("kvw,mwkij->mvkij", coupling, centre, precision=lax.Precision.HIGHEST)
    return centre + (-0.05 * (wind_u * along_x + wind_v * along_y) + 0.05 * laplace + 0.25 * mixed + 0.1 * forcing_c)


def evolve(member, forcing, coupling):
    field = member[None]
    for step in range(STEPS):
        padded = jnp.pad(field, ((0, 0), (0, 0), (0, 0), (0, 0), (2, 2)), mode="wrap")
        padded = jnp.pad(padded, ((0, 0), (0, 0), (0, 0), (2, 2), (0, 0)))
        field = advance(padded, forcing, coupling)
    return field[0]


def reference(state, kick, forcing, coupling, clone_src):
    start = jnp.take(state, clone_src, axis=0) + kick
    return lax.map(lambda member: evolve(member, forcing, coupling), start)
```

```python
import functools

import jax
import jax.numpy as jnp
from jax import lax
from jax.experimental import pallas as pl
from jax.experimental.pallas import tpu as pltpu
from jax.sharding import PartitionSpec as P

STEPS = 4
REACH = 2
HALO = STEPS * REACH
LANES = 128
ROWS = 8
SPAN = LANES - 2 * HALO
K = 0.05 / 12.0
VMEM = 48 * 1024 * 1024


def lane_index(shape):
    return lax.broadcasted_iota(jnp.int32, shape, len(shape) - 1)


def turn(x, shift):
    shift = shift % LANES
    return x if shift == 0 else pltpu.roll(x, shift, x.ndim - 1)


def edge_kernel(field_ref, kick_ref, forcing_ref, start_ref, top_ref, bottom_ref, strip_ref):
    members, variables = field_ref.shape[0], field_ref.shape[1]
    height, width = field_ref.shape[3], field_ref.shape[4]
    lane = lane_index((height, LANES))

    def edges(slot, v, rows):
        top_ref[slot, v, 0] = rows[:HALO]
        bottom_ref[slot, v, 0] = rows[height - HALO :]
        both = jnp.where(lane < HALO, rows[:, :LANES], rows[:, width - LANES :])
        return turn(both, HALO + 2 * HALO * v)

    for slot in range(members + 1):
        strip = jnp.zeros((height, LANES), jnp.float32)
        for v in range(variables):
            if slot < members:
                rows = field_ref[slot, v, 0] + kick_ref[slot, v, 0]
                start_ref[slot, v, 0] = rows
            else:
                rows = forcing_ref[v, 0]
            packed = edges(slot, v, rows)
            strip = jnp.where(lane >= 2 * HALO * v, packed, strip)
        strip_ref[slot, 0] = strip


def edges_of(field, kick, forcing):
    members, variables, levels, height, width = field.shape
    full = (members, variables, 1, height, width)
    slots = members + 1
    shape = jax.ShapeDtypeStruct
    return pl.pallas_call(
        edge_kernel,
        grid=(levels,),
        in_specs=[
            pl.BlockSpec(full, lambda k: (0, 0, k, 0, 0)),
            pl.BlockSpec(full, lambda k: (0, 0, k, 0, 0)),
            pl.BlockSpec((variables, 1, height, width), lambda k: (0, k, 0, 0)),
        ],
        out_specs=[
            pl.BlockSpec(full, lambda k: (0, 0, k, 0, 0)),
            pl.BlockSpec((slots, variables, 1, HALO, width), lambda k: (0, 0, k, 0, 0)),
            pl.BlockSpec((slots, variables, 1, HALO, width), lambda k: (0, 0, k, 0, 0)),
            pl.BlockSpec((slots, 1, height, LANES), lambda k: (0, k, 0, 0)),
        ],
        out_shape=[
            shape(field.shape, jnp.float32),
            shape((slots, variables, levels, HALO, width), jnp.float32),
            shape((slots, variables, levels, HALO, width), jnp.float32),
            shape((slots, levels, height, LANES), jnp.float32),
        ],
        compiler_params=pltpu.CompilerParams(vmem_limit_bytes=VMEM),
    )(field, kick, forcing)


def exchange(top, bottom, strip):
    lats, lons = lax.axis_size("lat"), lax.axis_size("lon")
    assert lons == 2
    south = [(i, i + 1) for i in range(lats - 1)]
    north = [(i + 1, i) for i in range(lats - 1)]

    def crossed(pairs):
        return [(a * lons + j, b * lons + 1 - j) for a, b in pairs for j in range(lons)]

    above = lax.ppermute(bottom, "lat", south)
    below = lax.ppermute(top, "lat", north)
    side = lax.ppermute(strip, "lon", [(0, 1), (1, 0)])
    side_above = lax.ppermute(strip[:, :, -HALO:], ("lat", "lon"), crossed(south))
    side_below = lax.ppermute(strip[:, :, :HALO], ("lat", "lon"), crossed(north))
    return above, below, side, side_above, side_below


def cut(rows, strip, v):
    width = rows.shape[1]
    count = -(-width // SPAN)
    lane = lane_index((rows.shape[0], LANES))
    source = [rows[:, LANES * t : LANES * (t + 1)] for t in range(width // LANES)]
    tiles = []
    for c in range(count):
        first = SPAN * c - HALO
        if c == 0:
            tile = jnp.where(lane < HALO, turn(strip, -2 * HALO * v), turn(source[0], HALO))
        else:
            t, offset = first // LANES, first % LANES
            if t + 1 < len(source):
                later = turn(source[t + 1], -offset)
            else:
                later = turn(strip, LANES - offset - 2 * HALO * v - HALO)
            tile = jnp.where(lane < LANES - offset, turn(source[t], -offset), later)
        tiles.append(tile)
    return tiles


def step_kernel(
    start_ref, above_ref, below_ref, side_ref, side_above_ref, side_below_ref,
    forcing_ref, f_above_ref, f_below_ref, f_side_ref, f_side_above_ref, f_side_below_ref,
    coupling_ref, place_ref, out_ref, cells, source, result,
):
    level = pl.program_id(0)
    variables, height, width = start_ref.shape[1], start_ref.shape[3], start_ref.shape[4]
    count = -(-width // SPAN)
    blocks = (height + 2 * HALO) // ROWS
    base = ROWS

    def lay(rows, strip, v, target, at, scale):
        for c, tile in enumerate(cut(rows, strip, v)):
            target[c, v, at : at + rows.shape[0]] = tile if scale is None else tile * scale

    for v in range(variables):
        lay(above_ref[0, v, 0], side_above_ref[0, 0], v, cells.at[0], base, None)
        lay(start_ref[0, v, 0], side_ref[0, 0], v, cells.at[0], base + HALO, None)
        lay(below_ref[0, v, 0], side_below_ref[0, 0], v, cells.at[0], base + HALO + height, None)

    @pl.when(pl.program_id(1) == 0)
    def _():
        for v in range(variables):
            lay(f_above_ref[0, v, 0], f_side_above_ref[0, 0], v, source, 0, 0.1)
            lay(forcing_ref[v, 0], f_side_ref[0, 0], v, source, HALO, 0.1)
            lay(f_below_ref[0, v, 0], f_side_below_ref[0, 0], v, source, HALO + height, 0.1)

    weight = [
        [
            0.25 * coupling_ref[level * variables * variables + v * variables + w]
            + (1.0 - 60.0 * K if v == w else 0.0)
            for w in range(variables)
        ]
        for v in range(variables)
    ]
    at_top = place_ref[0] == 0
    at_bottom = place_ref[0] == place_ref[1] - 1

    @pl.loop(0, count)
    def _(c):
        for step in range(STEPS):
            now, later = cells.at[step % 2, c], cells.at[(step + 1) % 2, c]
            last = step == STEPS - 1
            for r in range(1, blocks - 1) if last else range(blocks):
                at = base + ROWS * r
                centre = [now[v, at : at + ROWS] for v in range(variables)]
                ku, kv = K * centre[0], K * centre[1]
                eu, ev = 8.0 * ku, 8.0 * kv
                east, west, far_east, far_west = 16.0 * K - eu, 16.0 * K + eu, ku - K, -K - ku
                south, north, far_south, far_north = 16.0 * K - ev, 16.0 * K + ev, kv - K, -K - kv
                for v in range(variables):
                    q = centre[v]
                    total = source[c, v, ROWS * r : ROWS * (r + 1)]
                    for w in range(variables):
                        total += weight[v][w] * centre[w]
                    along = east * turn(q, -1) + west * turn(q, 1)
                    along += far_east * turn(q, -2) + far_west * turn(q, 2)
                    across = south * now[v, at + 1 : at + 1 + ROWS] + north * now[v, at - 1 : at - 1 + ROWS]
                    across += far_south * now[v, at + 2 : at + 2 + ROWS] + far_north * now[v, at - 2 : at - 2 + ROWS]
                    total += along + across
                    if last:
                        result[c, v, ROWS * (r - 1) : ROWS * r] = total
                    else:
                        if r == 0:
                            total = jnp.where(at_top, 0.0, total)
                        if r == blocks - 1:
                            total = jnp.where(at_bottom, 0.0, total)
                        later[v, at : at + ROWS] = total

    lane = lane_index((height, LANES))
    for v in range(variables):
        for t in range(width // LANES):
            c, offset = LANES * t // SPAN, LANES * t % SPAN
            left = turn(result[c, v], -(offset + HALO))
            if c + 1 < count:
                right = turn(result[c + 1, v], SPAN - offset - HALO)
                left = jnp.where(lane < SPAN - offset, left, right)
            out_ref[0, v, 0, :, LANES * t : LANES * (t + 1)] = left


def advance(start, halo, forcing, coupling):
    members, variables, levels, height, width = start.shape
    above, below, side, side_above, side_below = halo
    slots = above.shape[0]
    count = -(-width // SPAN)
    tall = height + 2 * HALO
    place = jnp.stack([lax.axis_index("lat"), jnp.int32(lax.axis_size("lat"))])

    def field(rows):
        return (
            pl.BlockSpec((1, variables, 1, rows, width), lambda k, m: (m, 0, k, 0, 0)),
            pl.BlockSpec((1, variables, 1, rows, width), lambda k, m: (slots - 1, 0, k, 0, 0)),
        )

    def strips(rows):
        return (
            pl.BlockSpec((1, 1, rows, LANES), lambda k, m: (m, k, 0, 0)),
            pl.BlockSpec((1, 1, rows, LANES), lambda k, m: (slots - 1, k, 0, 0)),
        )

    main, _ = field(height)
    edge, f_edge = field(HALO)
    flank, f_flank = strips(height)
    corner, f_corner = strips(HALO)
    scalars = pl.BlockSpec(memory_space=pltpu.SMEM)
    return pl.pallas_call(
        step_kernel,
        grid=(levels, members),
        in_specs=[
            main, edge, edge, flank, corner, corner,
            pl.BlockSpec((variables, 1, height, width), lambda k, m: (0, k, 0, 0)),
            f_edge, f_edge, f_flank, f_corner, f_corner,
            scalars, scalars,
        ],
        out_specs=main,
        out_shape=jax.ShapeDtypeStruct(start.shape, jnp.float32),
        scratch_shapes=[
            pltpu.VMEM((2, count, variables, tall + 2 * ROWS, LANES), jnp.float32),
            pltpu.VMEM((count, variables, tall, LANES), jnp.float32),
            pltpu.VMEM((count, variables, height, LANES), jnp.float32),
        ],
        compiler_params=pltpu.CompilerParams(vmem_limit_bytes=VMEM),
    )(
        start, above, below, side, side_above, side_below,
        forcing, above, below, side, side_above, side_below,
        coupling.reshape(-1), place,
    )


def shards(state, kick, forcing, coupling, clone_src):
    per_dev = state.shape[0]
    group = lax.axis_index("member")
    sources = lax.dynamic_slice_in_dim(clone_src, group * per_dev, per_dev)
    piece = lax.all_gather(state, "member", axis=0, tiled=True)
    field = jnp.take(piece, sources, axis=0, mode="clip")
    start, top, bottom, strip = edges_of(field, kick, forcing)
    halo = exchange(top, bottom, strip)
    return advance(start, halo, forcing, coupling)


def solution(mesh):
    in_specs = (
        P("member", None, None, "lat", "lon"),
        P("member", None, None, "lat", "lon"),
        P(None, None, "lat", "lon"),
        P(),
        P(),
    )
    out_specs = P("member", None, None, "lat", "lon")
    return jax.shard_map(shards, mesh=mesh, in_specs=in_specs, out_specs=out_specs, check_vma=False)
```

```python
import functools

import functools

import jax
import jax.numpy as jnp
from jax import lax
from jax.experimental import pallas as pl
from jax.experimental.pallas import tpu as pltpu
from jax.sharding import PartitionSpec as P

STEPS = 4
REACH = 2
HALO = STEPS * REACH
LANES = 128
ROWS = 8
SPAN = LANES - 2 * HALO
K = 0.05 / 12.0
VMEM = 16 * 1024 * 1024


def lane_index(shape):
    return lax.broadcasted_iota(jnp.int32, shape, len(shape) - 1)


def turn(x, shift):
    shift = shift % LANES
    return x if shift == 0 else pltpu.roll(x, shift, x.ndim - 1)


def plan_kernel(groups, per_dev, most, clone_ref, group_ref, out_ref, ends):
    cases, sends, takes = 1, 1 + most, 1 + 3 * most
    me = group_ref[0]
    out_ref[0] = 1
    for t in range(most):
        out_ref[cases + t] = (1 << (2 * (groups - 2))) - 1
        out_ref[sends + 2 * t] = 0
        out_ref[sends + 2 * t + 1] = 0
    for j in range(per_dev):
        out_ref[takes + j] = -1 - clone_ref[me * per_dev + j] % per_dev

    for down in range(2):
        for t in range(most):
            ends[t] = 0
        for a in range(groups - 1):
            for b in range(a + 1, groups):
                source, target = (groups - 1 - a, groups - 1 - b) if down else (a, b)
                spans = sum(1 << (x - 1) for x in range(a + 1, b)) << (down * (groups - 2))
                for j in range(per_dev):
                    member = source * per_dev + j
                    wanted = [clone_ref[target * per_dev + i] == member for i in range(per_dev)]
                    need = wanted[0]
                    for other in wanted[1:]:
                        need = need | other

                    @pl.when(need)
                    def _():
                        t = jnp.int32(most - 1)
                        for earlier in reversed(range(most - 1)):
                            t = jnp.where(ends[earlier] <= a, earlier, t)
                        ends[t] = b
                        out_ref[0] = jnp.maximum(out_ref[0], t + 1)
                        out_ref[cases + t] = out_ref[cases + t] & ~spans

                        @pl.when(me == source)
                        def _():
                            out_ref[sends + 2 * t + down] = j

                        for i in range(per_dev):

                            @pl.when((me == target) & wanted[i])
                            def _():
                                out_ref[takes + i] = 2 * t + down


def plan_of(clone_src, groups, per_dev, most):
    group = lax.axis_index("member")[None]
    scalars = pl.BlockSpec(memory_space=pltpu.SMEM)
    plan = pl.pallas_call(
        functools.partial(plan_kernel, groups, per_dev, most),
        in_specs=[scalars, scalars],
        out_specs=scalars,
        out_shape=jax.ShapeDtypeStruct((1 + 3 * most + per_dev,), jnp.int32),
        scratch_shapes=[pltpu.SMEM((most,), jnp.int32)],
    )(clone_src, group)
    return plan[0], plan[1 : 1 + most], plan[1 + most : 1 + 3 * most], plan[1 + 3 * most :]


def send_round(case, groups, up, down):
    inner = groups - 2

    def chain(bits):
        stops = [0] + [x for x in range(1, groups - 1) if bits >> (x - 1) & 1] + [groups - 1]
        return list(zip(stops[:-1], stops[1:]))

    def branch(index):
        rising = chain(index & ((1 << inner) - 1))
        falling = [(groups - 1 - a, groups - 1 - b) for a, b in chain(index >> inner)]
        return lambda x, y: (lax.ppermute(x, "member", rising), lax.ppermute(y, "member", falling))

    return lax.switch(case, [branch(index) for index in range(1 << (2 * inner))], up, down)


def clones(state, clone_src):
    per_dev = state.shape[0]
    groups = lax.axis_size("member")
    if groups != 4:
        piece = lax.all_gather(state, "member", axis=0, tiled=True)
        sources = lax.dynamic_slice_in_dim(clone_src, lax.axis_index("member") * per_dev, per_dev)
        field = jnp.take(piece, sources, axis=0, mode="clip")
        return state, field, field[0], field[0], per_dev + jnp.arange(per_dev, dtype=jnp.int32)

    most = per_dev * (groups - 1)
    rounds, cases, sends, takes = plan_of(clone_src, groups, per_dev, most)

    def one(t):
        pick = lambda at: lax.dynamic_index_in_dim(state, sends[at], 0, keepdims=False)
        return send_round(cases[t], groups, pick(2 * t), pick(2 * t + 1))

    def earlier(t, held):
        up, down = one(t)
        arrives = (takes // 2 == t) & (takes >= 0)
        rows = []
        for j in range(per_dev):
            got = jnp.where(takes[j] % 2 == 1, down, up)
            rows.append(jnp.where(arrives[j], got, held[j]))
        return jnp.stack(rows)

    held = lax.fori_loop(0, rounds - 1, earlier, jnp.zeros_like(state))
    up, down = one(rounds - 1)
    place = jnp.where(
        takes < 0,
        -1 - takes,
        jnp.where(
            takes // 2 == rounds - 1,
            2 * per_dev + takes % 2,
            per_dev + jnp.arange(per_dev, dtype=jnp.int32),
        ),
    )
    return state, held, up, down, place


def edge_kernel(
    place_ref, state_ref, held_ref, up_ref, down_ref, kick_ref, forcing_ref,
    start_ref, top_ref, bottom_ref, strip_ref, field, done,
):
    members, variables, levels, height, width = field.shape
    lane = lane_index((height, LANES))
    options = [state_ref.at[j] for j in range(members)] + [held_ref.at[j] for j in range(members)]
    options += [up_ref, down_ref]
    for slot in range(members):
        for at, option in enumerate(options):

            @pl.when(place_ref[slot] == at)
            def _():
                pltpu.make_async_copy(option, field.at[slot], done.at[slot]).start()

    for slot in [members, *range(members)]:
        if slot < members:
            pltpu.make_async_copy(up_ref, field.at[slot], done.at[slot]).wait()
        for k in range(levels):
            strip = jnp.zeros((height, LANES), jnp.float32)
            for v in range(variables):
                if slot < members:
                    rows = field[slot, v, k] + kick_ref[slot, v, k]
                    start_ref[slot, v, k] = rows
                else:
                    rows = forcing_ref[v, k]
                top_ref[slot, v, k] = rows[:HALO]
                bottom_ref[slot, v, k] = rows[height - HALO :]
                both = jnp.where(lane < HALO, rows[:, :LANES], rows[:, width - LANES :])
                packed = turn(both, HALO + 2 * HALO * v)
                strip = jnp.where(lane >= 2 * HALO * v, packed, strip)
            strip_ref[slot, k] = strip


def edges_of(sources, kick, forcing):
    state, held, up, down, place = sources
    members, variables, levels, height, width = state.shape
    slots = members + 1
    shape = jax.ShapeDtypeStruct
    anywhere, here = pl.BlockSpec(memory_space=pl.ANY), pl.BlockSpec(memory_space=pltpu.VMEM)
    return pl.pallas_call(
        edge_kernel,
        in_specs=[pl.BlockSpec(memory_space=pltpu.SMEM)] + [anywhere] * 4 + [here] * 2,
        out_specs=[here] * 4,
        out_shape=[
            shape(state.shape, jnp.float32),
            shape((slots, variables, levels, HALO, width), jnp.float32),
            shape((slots, variables, levels, HALO, width), jnp.float32),
            shape((slots, levels, height, LANES), jnp.float32),
        ],
        scratch_shapes=[
            pltpu.VMEM(state.shape, jnp.float32),
            pltpu.SemaphoreType.DMA((members,)),
        ],
        compiler_params=pltpu.CompilerParams(vmem_limit_bytes=VMEM),
    )(place, state, held, up, down, kick, forcing)


def exchange(top, bottom, strip):
    lats, lons = lax.axis_size("lat"), lax.axis_size("lon")
    assert lons == 2
    south = [(i, i + 1) for i in range(lats - 1)]
    north = [(i + 1, i) for i in range(lats - 1)]

    def crossed(pairs):
        return [(a * lons + j, b * lons + 1 - j) for a, b in pairs for j in range(lons)]

    above = lax.ppermute(bottom, "lat", south)
    below = lax.ppermute(top, "lat", north)
    side = lax.ppermute(strip, "lon", [(0, 1), (1, 0)])
    side_above = lax.ppermute(strip[:, :, -HALO:], ("lat", "lon"), crossed(south))
    side_below = lax.ppermute(strip[:, :, :HALO], ("lat", "lon"), crossed(north))
    return above, below, side, side_above, side_below


def cut(rows, strip, v):
    width = rows.shape[1]
    count = -(-width // SPAN)
    lane = lane_index((rows.shape[0], LANES))
    source = [rows[:, LANES * t : LANES * (t + 1)] for t in range(width // LANES)]
    tiles = []
    for c in range(count):
        first = SPAN * c - HALO
        if c == 0:
            tile = jnp.where(lane < HALO, turn(strip, -2 * HALO * v), turn(source[0], HALO))
        else:
            t, offset = first // LANES, first % LANES
            if t + 1 < len(source):
                later = turn(source[t + 1], -offset)
            else:
                later = turn(strip, LANES - offset - 2 * HALO * v - HALO)
            tile = jnp.where(lane < LANES - offset, turn(source[t], -offset), later)
        tiles.append(tile)
    return tiles


def step_kernel(
    start_ref, above_ref, below_ref, side_ref, side_above_ref, side_below_ref,
    forcing_ref, f_above_ref, f_below_ref, f_side_ref, f_side_above_ref, f_side_below_ref,
    coupling_ref, place_ref, out_ref, cells, source, result,
):
    level = pl.program_id(0)
    variables, height, width = start_ref.shape[1], start_ref.shape[3], start_ref.shape[4]
    count = -(-width // SPAN)
    blocks = (height + 2 * HALO) // ROWS
    base = ROWS

    def lay(rows, strip, v, target, at, scale):
        for c, tile in enumerate(cut(rows, strip, v)):
            target[c, v, at : at + rows.shape[0]] = tile if scale is None else tile * scale

    for v in range(variables):
        lay(above_ref[0, v, 0], side_above_ref[0, 0], v, cells.at[0], base, None)
        lay(start_ref[0, v, 0], side_ref[0, 0], v, cells.at[0], base + HALO, None)
        lay(below_ref[0, v, 0], side_below_ref[0, 0], v, cells.at[0], base + HALO + height, None)

    @pl.when(pl.program_id(1) == 0)
    def _():
        for v in range(variables):
            lay(f_above_ref[0, v, 0], f_side_above_ref[0, 0], v, source, 0, 0.1)
            lay(forcing_ref[v, 0], f_side_ref[0, 0], v, source, HALO, 0.1)
            lay(f_below_ref[0, v, 0], f_side_below_ref[0, 0], v, source, HALO + height, 0.1)

    weight = [
        [
            0.25 * coupling_ref[level * variables * variables + v * variables + w]
            + (1.0 - 60.0 * K if v == w else 0.0)
            for w in range(variables)
        ]
        for v in range(variables)
    ]
    at_top = place_ref[0] == 0
    at_bottom = place_ref[0] == place_ref[1] - 1

    @pl.loop(0, count)
    def _(c):
        for step in range(STEPS):
            now, later = cells.at[step % 2, c], cells.at[(step + 1) % 2, c]
            last = step == STEPS - 1
            for r in range(1, blocks - 1) if last else range(blocks):
                at = base + ROWS * r
                centre = [now[v, at : at + ROWS] for v in range(variables)]
                ku, kv = K * centre[0], K * centre[1]
                eu, ev = 8.0 * ku, 8.0 * kv
                east, west, far_east, far_west = 16.0 * K - eu, 16.0 * K + eu, ku - K, -K - ku
                south, north, far_south, far_north = 16.0 * K - ev, 16.0 * K + ev, kv - K, -K - kv
                for v in range(variables):
                    q = centre[v]
                    total = source[c, v, ROWS * r : ROWS * (r + 1)]
                    for w in range(variables):
                        total += weight[v][w] * centre[w]
                    along = east * turn(q, -1) + west * turn(q, 1)
                    along += far_east * turn(q, -2) + far_west * turn(q, 2)
                    across = south * now[v, at + 1 : at + 1 + ROWS] + north * now[v, at - 1 : at - 1 + ROWS]
                    across += far_south * now[v, at + 2 : at + 2 + ROWS] + far_north * now[v, at - 2 : at - 2 + ROWS]
                    total += along + across
                    if last:
                        result[c, v, ROWS * (r - 1) : ROWS * r] = total
                    else:
                        if r == 0:
                            total = jnp.where(at_top, 0.0, total)
                        if r == blocks - 1:
                            total = jnp.where(at_bottom, 0.0, total)
                        later[v, at : at + ROWS] = total

    lane = lane_index((height, LANES))
    for v in range(variables):
        for t in range(width // LANES):
            c, offset = LANES * t // SPAN, LANES * t % SPAN
            left = turn(result[c, v], -(offset + HALO))
            if c + 1 < count:
                right = turn(result[c + 1, v], SPAN - offset - HALO)
                left = jnp.where(lane < SPAN - offset, left, right)
            out_ref[0, v, 0, :, LANES * t : LANES * (t + 1)] = left


def advance(start, halo, forcing, coupling):
    members, variables, levels, height, width = start.shape
    above, below, side, side_above, side_below = halo
    slots = above.shape[0]
    count = -(-width // SPAN)
    tall = height + 2 * HALO
    place = jnp.stack([lax.axis_index("lat"), jnp.int32(lax.axis_size("lat"))])

    def field(rows):
        return (
            pl.BlockSpec((1, variables, 1, rows, width), lambda k, m: (m, 0, k, 0, 0)),
            pl.BlockSpec((1, variables, 1, rows, width), lambda k, m: (slots - 1, 0, k, 0, 0)),
        )

    def strips(rows):
        return (
            pl.BlockSpec((1, 1, rows, LANES), lambda k, m: (m, k, 0, 0)),
            pl.BlockSpec((1, 1, rows, LANES), lambda k, m: (slots - 1, k, 0, 0)),
        )

    main, _ = field(height)
    edge, f_edge = field(HALO)
    flank, f_flank = strips(height)
    corner, f_corner = strips(HALO)
    scalars = pl.BlockSpec(memory_space=pltpu.SMEM)
    return pl.pallas_call(
        step_kernel,
        grid=(levels, members),
        in_specs=[
            main, edge, edge, flank, corner, corner,
            pl.BlockSpec((variables, 1, height, width), lambda k, m: (0, k, 0, 0)),
            f_edge, f_edge, f_flank, f_corner, f_corner,
            scalars, scalars,
        ],
        out_specs=main,
        out_shape=jax.ShapeDtypeStruct(start.shape, jnp.float32),
        scratch_shapes=[
            pltpu.VMEM((2, count, variables, tall + 2 * ROWS, LANES), jnp.float32),
            pltpu.VMEM((count, variables, tall, LANES), jnp.float32),
            pltpu.VMEM((count, variables, height, LANES), jnp.float32),
        ],
        compiler_params=pltpu.CompilerParams(vmem_limit_bytes=VMEM),
    )(
        start, above, below, side, side_above, side_below,
        forcing, above, below, side, side_above, side_below,
        coupling.reshape(-1), place,
    )


def shards(state, kick, forcing, coupling, clone_src):
    start, top, bottom, strip = edges_of(clones(state, clone_src), kick, forcing)
    halo = exchange(top, bottom, strip)
    return advance(start, halo, forcing, coupling)


def solution(mesh):
    in_specs = (
        P("member", None, None, "lat", "lon"),
        P("member", None, None, "lat", "lon"),
        P(None, None, "lat", "lon"),
        P(),
        P(),
    )
    out_specs = P("member", None, None, "lat", "lon")
    return jax.shard_map(shards, mesh=mesh, in_specs=in_specs, out_specs=out_specs, check_vma=False)
```

```python
import functools

import functools

import jax
import jax.numpy as jnp
from jax import lax
from jax.experimental import pallas as pl
from jax.experimental.pallas import tpu as pltpu
from jax.sharding import PartitionSpec as P

STEPS = 4
REACH = 2
HALO = STEPS * REACH
LANES = 128
ROWS = 8
SPAN = LANES - 2 * HALO
K = 0.05 / 12.0
VMEM = 16 * 1024 * 1024


def lane_index(shape):
    return lax.broadcasted_iota(jnp.int32, shape, len(shape) - 1)


def turn(x, shift):
    shift = shift % LANES
    return x if shift == 0 else pltpu.roll(x, shift, x.ndim - 1)


def chain(bits, groups):
    stops = [0] + [x for x in range(1, groups - 1) if bits >> (x - 1) & 1] + [groups - 1]
    return list(zip(stops[:-1], stops[1:]))


class Layout:
    def __init__(self, groups, per_dev):
        self.groups, self.per_dev = groups, per_dev
        self.most = per_dev * (groups - 1)
        self.patterns, self.sends = 1, 1 + 2 * self.most
        self.takes = self.sends + 2 * self.most
        self.place = self.takes + per_dev
        self.size = self.place + per_dev
        self.kinds = 1 + (1 << (groups - 2))


def plan_kernel(lay, clone_ref, group_ref, state_ref, plan_ref, index_ref, up_ref, down_ref, ends, done):
    groups, per_dev, most = lay.groups, lay.per_dev, lay.most
    me = group_ref[0]
    plan_ref[0] = 1
    for t in range(2 * most):
        plan_ref[lay.patterns + t] = 0
        plan_ref[lay.sends + t] = 0
    for i in range(per_dev):
        plan_ref[lay.takes + i] = -1 - clone_ref[me * per_dev + i] % per_dev

    for down in range(2):
        for t in range(most):
            ends[t] = 0
        for a in range(groups - 1):
            for b in range(a + 1, groups):
                source, target = (groups - 1 - a, groups - 1 - b) if down else (a, b)
                spans = sum(1 << (x - 1) for x in range(a + 1, b))
                for j in range(per_dev):
                    member = source * per_dev + j
                    wanted = [clone_ref[target * per_dev + i] == member for i in range(per_dev)]
                    need = functools.reduce(jnp.logical_or, wanted)

                    @pl.when(need)
                    def _():
                        t = jnp.int32(most - 1)
                        for earlier in reversed(range(most - 1)):
                            t = jnp.where(ends[earlier] <= a, earlier, t)
                        ends[t] = b
                        plan_ref[0] = jnp.maximum(plan_ref[0], t + 1)
                        at = 2 * t + down
                        before = plan_ref[lay.patterns + at]
                        bits = jnp.where(before == 0, lay.kinds - 2, before - 1)
                        plan_ref[lay.patterns + at] = 1 + (bits & ~spans)

                        @pl.when(me == source)
                        def _():
                            plan_ref[lay.sends + at] = j

                        for i in range(per_dev):

                            @pl.when((me == target) & wanted[i])
                            def _():
                                plan_ref[lay.takes + i] = at

    rounds = plan_ref[0]
    index = plan_ref[lay.patterns] * lay.kinds + plan_ref[lay.patterns + 1]
    index_ref[0] = jnp.where(rounds == 1, index, lay.kinds * lay.kinds)
    for i in range(per_dev):
        take = plan_ref[lay.takes + i]
        far = per_dev + jnp.where(rounds == 1, lax.rem(take, 2), i)
        plan_ref[lay.place + i] = jnp.where(take < 0, -1 - take, far)
    copies = [
        pltpu.make_async_copy(state_ref.at[plan_ref[lay.sends]], up_ref, done.at[0]),
        pltpu.make_async_copy(state_ref.at[plan_ref[lay.sends + 1]], down_ref, done.at[1]),
    ]
    for copy in copies:
        copy.start()
    for copy in copies:
        copy.wait()


def spec(space):
    return pl.BlockSpec(memory_space=space)


def plan_of(lay, clone_src, state):
    group = lax.axis_index("member")[None]
    shape = jax.ShapeDtypeStruct
    one = shape(state.shape[1:], state.dtype)
    return pl.pallas_call(
        functools.partial(plan_kernel, lay),
        in_specs=[spec(pltpu.SMEM), spec(pltpu.SMEM), spec(pl.ANY)],
        out_specs=[spec(pltpu.SMEM), spec(pltpu.SMEM), spec(pl.ANY), spec(pl.ANY)],
        out_shape=[shape((lay.size,), jnp.int32), shape((1,), jnp.int32), one, one],
        scratch_shapes=[pltpu.SMEM((lay.most,), jnp.int32), pltpu.SemaphoreType.DMA((2,))],
    )(clone_src, group, state)


def strips_kernel(lay, plan_ref, state_ref, kick_ref, forcing_ref, strips_ref, up_ref, down_ref):
    members, variables, levels, height, width = state_ref.shape
    lane = lane_index((height, LANES))
    for slot in range(2 * members + 1):
        for k in range(levels):
            strip = jnp.zeros((height, LANES), jnp.float32)
            for v in range(variables):
                if slot < members:
                    rows = state_ref.at[slot, v, k]
                elif slot < 2 * members:
                    rows = kick_ref.at[slot - members, v, k]
                else:
                    rows = forcing_ref.at[v, k]
                both = jnp.where(lane < HALO, rows[:, :LANES], rows[:, width - LANES :])
                strip = jnp.where(lane >= 2 * HALO * v, turn(both, HALO + 2 * HALO * v), strip)
            strips_ref[slot, k] = strip
    up_ref[...] = strips_ref[plan_ref[lay.sends]]
    down_ref[...] = strips_ref[plan_ref[lay.sends + 1]]


def strips_of(lay, plan, state, kick, forcing):
    members, variables, levels, height, width = state.shape
    shape = jax.ShapeDtypeStruct
    one = shape((levels, height, LANES), jnp.float32)
    here = spec(pltpu.VMEM)
    return pl.pallas_call(
        functools.partial(strips_kernel, lay),
        in_specs=[spec(pltpu.SMEM)] + [here] * 3,
        out_specs=[here] * 3,
        out_shape=[shape((2 * members + 1, levels, height, LANES), jnp.float32), one, one],
        compiler_params=pltpu.CompilerParams(vmem_limit_bytes=VMEM),
    )(plan, state, kick, forcing)


def lay_edges(rows_of, strip, top_ref, bottom_ref, at, variables, width):
    height = strip.shape[0]
    tiles = width // LANES
    for v in range(variables):
        rows = rows_of(v)
        for t in range(tiles):
            part = rows[:, LANES * t : LANES * (t + 1)]
            top_ref[(*at, v * tiles + t)] = part[:HALO]
            bottom_ref[(*at, v * tiles + t)] = part[height - HALO :]
    top_ref[(*at, variables * tiles)] = strip[:HALO]
    bottom_ref[(*at, variables * tiles)] = strip[height - HALO :]


def forcing_kernel(forcing_ref, sides_ref, top_ref, bottom_ref):
    variables, levels, height, width = forcing_ref.shape
    slots = sides_ref.shape[0]
    for k in range(levels):
        rows_of = lambda v: forcing_ref[v, k]
        lay_edges(rows_of, sides_ref[slots - 1, k], top_ref, bottom_ref, (0, k), variables, width)


def edge_shape(members, forcing):
    variables, levels, height, width = forcing.shape
    return jax.ShapeDtypeStruct((members, levels, variables * width // LANES + 1, HALO, LANES), jnp.float32)


def forcing_edges(forcing, sides):
    here = spec(pltpu.VMEM)
    return pl.pallas_call(
        forcing_kernel,
        in_specs=[here] * 2,
        out_specs=[here] * 2,
        out_shape=[edge_shape(1, forcing)] * 2,
        compiler_params=pltpu.CompilerParams(vmem_limit_bytes=VMEM),
    )(forcing, sides)


def pack_kernel(
    lay, plan_ref, state_ref, up_ref, down_ref, kick_ref, sides_ref, up_side_ref, down_side_ref,
    start_ref, side_ref, top_ref, bottom_ref, field, done,
):
    members, variables, levels, height, width = field.shape
    places = [plan_ref[lay.place + i] for i in range(members)]
    options = [state_ref.at[j] for j in range(members)] + [up_ref, down_ref]
    for i in range(members):
        for at, option in enumerate(options):

            @pl.when(places[i] == at)
            def _():
                pltpu.make_async_copy(option, field.at[i], done.at[i]).start()

    for i in range(members):
        pltpu.make_async_copy(up_ref, field.at[i], done.at[i]).wait()
        for k in range(levels):
            strip = down_side_ref[k]
            for at in reversed(range(members + 1)):
                other = up_side_ref[k] if at == members else sides_ref[at, k]
                strip = jnp.where(places[i] == at, other, strip)
            strip = strip + sides_ref[members + i, k]
            side_ref[i, k] = strip

            def rows_of(v):
                rows = field[i, v, k] + kick_ref[i, v, k]
                start_ref[i, v, k] = rows
                return rows

            lay_edges(rows_of, strip, top_ref, bottom_ref, (i, k), variables, width)


def pack(lay, plan, state, up, down, kick, sides, up_side, down_side):
    members, variables, levels, height, width = state.shape
    shape = jax.ShapeDtypeStruct
    here = spec(pltpu.VMEM)
    return pl.pallas_call(
        functools.partial(pack_kernel, lay),
        in_specs=[spec(pltpu.SMEM)] + [spec(pl.ANY)] * 3 + [here] * 4,
        out_specs=[here] * 4,
        out_shape=[
            shape(state.shape, jnp.float32),
            shape((members, levels, height, LANES), jnp.float32),
            edge_shape(members, kick[0]),
            edge_shape(members, kick[0]),
        ],
        scratch_shapes=[pltpu.VMEM(state.shape, jnp.float32), pltpu.SemaphoreType.DMA((members,))],
        compiler_params=pltpu.CompilerParams(vmem_limit_bytes=VMEM),
    )(plan, state, up, down, kick, sides, up_side, down_side)


def neighbours(top, bottom):
    lats = lax.axis_size("lat")
    above = lax.ppermute(bottom, "lat", [(i, i + 1) for i in range(lats - 1)])
    below = lax.ppermute(top, "lat", [(i + 1, i) for i in range(lats - 1)])
    return above, below


def beside(strips):
    assert lax.axis_size("lon") == 2
    return lax.ppermute(strips, "lon", [(0, 1), (1, 0)])


def send(lay, kinds, fields, sides):
    groups, lons = lay.groups, lax.axis_size("lon")
    fields, sides = list(fields), list(sides)
    for down, kind in enumerate(kinds):
        if kind:
            pairs = chain(kind - 1, groups)
            if down:
                pairs = [(groups - 1 - a, groups - 1 - b) for a, b in pairs]
            crossed = [(a * lons + j, b * lons + 1 - j) for a, b in pairs for j in range(lons)]
            fields[down] = lax.ppermute(fields[down], "member", pairs)
            sides[down] = lax.ppermute(sides[down], ("member", "lon"), crossed)
    return (*fields, *sides)


def pick_kernel(lay, step_ref, plan_ref, state_ref, strips_ref, index_ref, up_ref, down_ref, up_side_ref, down_side_ref, done):
    t = step_ref[0]
    index_ref[0] = plan_ref[lay.patterns + 2 * t] * lay.kinds + plan_ref[lay.patterns + 2 * t + 1]
    copies = []
    for way, (whole, part) in enumerate(((up_ref, up_side_ref), (down_ref, down_side_ref))):
        j = plan_ref[lay.sends + 2 * t + way]
        copies.append(pltpu.make_async_copy(state_ref.at[j], whole, done.at[2 * way]))
        copies.append(pltpu.make_async_copy(strips_ref.at[j], part, done.at[2 * way + 1]))
    for copy in copies:
        copy.start()
    for copy in copies:
        copy.wait()


def pick(lay, t, plan, state, strips):
    shape = jax.ShapeDtypeStruct
    whole, part = shape(state.shape[1:], jnp.float32), shape(strips.shape[1:], jnp.float32)
    return pl.pallas_call(
        functools.partial(pick_kernel, lay),
        in_specs=[spec(pltpu.SMEM)] * 2 + [spec(pl.ANY)] * 2,
        out_specs=[spec(pltpu.SMEM)] + [spec(pl.ANY)] * 4,
        out_shape=[shape((1,), jnp.int32), whole, whole, part, part],
        scratch_shapes=[pltpu.SemaphoreType.DMA((4,))],
    )(t[None], plan, state, strips)


def keep_kernel(lay, step_ref, plan_ref, up_ref, down_ref, up_side_ref, down_side_ref, *refs):
    held, done = refs[4:8], refs[8]
    t = step_ref[0]
    for wait in range(2):
        for i in range(lay.per_dev):
            for way, (whole, part) in enumerate(((up_ref, up_side_ref), (down_ref, down_side_ref))):

                @pl.when(plan_ref[lay.takes + i] == 2 * t + way)
                def _():
                    copies = [
                        pltpu.make_async_copy(whole, held[i], done.at[2 * i]),
                        pltpu.make_async_copy(part, held[lay.per_dev + i], done.at[2 * i + 1]),
                    ]
                    for copy in copies:
                        copy.wait() if wait else copy.start()


def keep(lay, t, plan, got, held):
    assert lay.per_dev == 2
    shape = jax.ShapeDtypeStruct
    return pl.pallas_call(
        functools.partial(keep_kernel, lay),
        in_specs=[spec(pltpu.SMEM)] * 2 + [spec(pl.ANY)] * 8,
        out_specs=[spec(pl.ANY)] * 4,
        out_shape=[shape(x.shape, x.dtype) for x in held],
        input_output_aliases={6 + i: i for i in range(4)},
        scratch_shapes=[pltpu.SemaphoreType.DMA((4,))],
    )(t[None], plan, *got, *held)


def prepared(state, kick, forcing, clone_src):
    per_dev, levels, height = state.shape[0], state.shape[2], state.shape[3]
    groups = lax.axis_size("member")
    lay = Layout(groups, per_dev)

    def rest(plan, fields, sides_far, strips):
        sides = beside(strips)
        f_above, f_below = neighbours(*forcing_edges(forcing, sides))
        start, side, top, bottom = pack(lay, plan, state, *fields, kick, sides, *sides_far)
        return start, side, top, bottom, f_above, f_below, sides[2 * per_dev :]

    if groups != 4:
        piece = lax.all_gather(state, "member", axis=0, tiled=True)
        sources = lax.dynamic_slice_in_dim(clone_src, lax.axis_index("member") * per_dev, per_dev)
        field = jnp.take(piece, sources, axis=0, mode="clip")
        plan = jnp.zeros((lay.size,), jnp.int32).at[lay.place :].set(jnp.arange(per_dev, dtype=jnp.int32))
        strips, a, b = strips_of(lay, plan, field, kick, forcing)
        state = field
        return rest(plan, (field[0], field[1]), (a, b), strips)

    plan, index, up, down = plan_of(lay, clone_src, state)

    def single(kinds):
        def run(plan, up, down):
            strips, up_side, down_side = strips_of(lay, plan, state, kick, forcing)
            got = send(lay, kinds, (up, down), (up_side, down_side))
            return rest(plan, got[:2], got[2:], strips)

        return run

    kinds = [(a, b) for a in range(lay.kinds) for b in range(lay.kinds)]

    def several(plan, up, down):
        strips, up_side, down_side = strips_of(lay, plan, state, kick, forcing)

        def one(t, held):
            at, *out = pick(lay, t, plan, state, strips)
            inner = [lambda a, b, c, d, kind=kind: send(lay, kind, (a, b), (c, d)) for kind in kinds]
            return tuple(keep(lay, t, plan, lax.switch(at[0], inner, *out), held))

        held = lax.fori_loop(0, plan[0], one, (up, down, up_side, down_side))
        return rest(plan, held[:2], held[2:], strips)

    return lax.switch(index[0], [single(kind) for kind in kinds] + [several], plan, up, down)


def cut(rows, strip, v):
    width = rows.shape[1]
    count = -(-width // SPAN)
    lane = lane_index((rows.shape[0], LANES))
    source = [rows[:, LANES * t : LANES * (t + 1)] for t in range(width // LANES)]
    tiles = []
    for c in range(count):
        first = SPAN * c - HALO
        if c == 0:
            tile = jnp.where(lane < HALO, turn(strip, -2 * HALO * v), turn(source[0], HALO))
        else:
            t, offset = first // LANES, first % LANES
            if t + 1 < len(source):
                later = turn(source[t + 1], -offset)
            else:
                later = turn(strip, LANES - offset - 2 * HALO * v - HALO)
            tile = jnp.where(lane < LANES - offset, turn(source[t], -offset), later)
        tiles.append(tile)
    return tiles


def step_kernel(
    start_ref, above_ref, below_ref, side_ref, forcing_ref, f_above_ref, f_below_ref, f_side_ref,
    coupling_ref, place_ref, out_ref, cells, source, result,
):
    level = pl.program_id(0)
    variables, height, width = start_ref.shape[1], start_ref.shape[3], start_ref.shape[4]
    count = -(-width // SPAN)
    blocks = (height + 2 * HALO) // ROWS
    base = ROWS

    def edge(ref, v):
        tiles = width // LANES
        rows = [ref[0, 0, v * tiles + t] for t in range(tiles)]
        return jnp.concatenate(rows, axis=1), ref[0, 0, variables * tiles]

    def lay(rows, strip, v, target, at, scale):
        for c, tile in enumerate(cut(rows, strip, v)):
            target[c, v, at : at + rows.shape[0]] = tile if scale is None else tile * scale

    for v in range(variables):
        lay(*edge(above_ref, v), v, cells.at[0], base, None)
        lay(start_ref[0, v, 0], side_ref[0, 0], v, cells.at[0], base + HALO, None)
        lay(*edge(below_ref, v), v, cells.at[0], base + HALO + height, None)

    @pl.when(pl.program_id(1) == 0)
    def _():
        for v in range(variables):
            lay(*edge(f_above_ref, v), v, source, 0, 0.1)
            lay(forcing_ref[v, 0], f_side_ref[0, 0], v, source, HALO, 0.1)
            lay(*edge(f_below_ref, v), v, source, HALO + height, 0.1)

    weight = [
        [
            0.25 * coupling_ref[level * variables * variables + v * variables + w]
            + (1.0 - 60.0 * K if v == w else 0.0)
            for w in range(variables)
        ]
        for v in range(variables)
    ]
    at_top = place_ref[0] == 0
    at_bottom = place_ref[0] == place_ref[1] - 1

    @pl.loop(0, count)
    def _(c):
        for step in range(STEPS):
            now, later = cells.at[step % 2, c], cells.at[(step + 1) % 2, c]
            last = step == STEPS - 1
            for r in range(1, blocks - 1) if last else range(blocks):
                at = base + ROWS * r
                centre = [now[v, at : at + ROWS] for v in range(variables)]
                ku, kv = K * centre[0], K * centre[1]
                eu, ev = 8.0 * ku, 8.0 * kv
                east, west, far_east, far_west = 16.0 * K - eu, 16.0 * K + eu, ku - K, -K - ku
                south, north, far_south, far_north = 16.0 * K - ev, 16.0 * K + ev, kv - K, -K - kv
                for v in range(variables):
                    q = centre[v]
                    total = source[c, v, ROWS * r : ROWS * (r + 1)]
                    for w in range(variables):
                        total += weight[v][w] * centre[w]
                    along = east * turn(q, -1) + west * turn(q, 1)
                    along += far_east * turn(q, -2) + far_west * turn(q, 2)
                    across = south * now[v, at + 1 : at + 1 + ROWS] + north * now[v, at - 1 : at - 1 + ROWS]
                    across += far_south * now[v, at + 2 : at + 2 + ROWS] + far_north * now[v, at - 2 : at - 2 + ROWS]
                    total += along + across
                    if last:
                        result[c, v, ROWS * (r - 1) : ROWS * r] = total
                    else:
                        if r == 0:
                            total = jnp.where(at_top, 0.0, total)
                        if r == blocks - 1:
                            total = jnp.where(at_bottom, 0.0, total)
                        later[v, at : at + ROWS] = total

    lane = lane_index((height, LANES))
    for v in range(variables):
        for t in range(width // LANES):
            c, offset = LANES * t // SPAN, LANES * t % SPAN
            left = turn(result[c, v], -(offset + HALO))
            if c + 1 < count:
                right = turn(result[c + 1, v], SPAN - offset - HALO)
                left = jnp.where(lane < SPAN - offset, left, right)
            out_ref[0, v, 0, :, LANES * t : LANES * (t + 1)] = left


def advance(start, halo, f_halo, forcing, coupling):
    members, variables, levels, height, width = start.shape
    above, below, side = halo
    f_above, f_below, f_side = f_halo
    tiles = above.shape[2]
    count = -(-width // SPAN)
    tall = height + 2 * HALO
    place = jnp.stack([lax.axis_index("lat"), jnp.int32(lax.axis_size("lat"))])
    main = pl.BlockSpec((1, variables, 1, height, width), lambda k, m: (m, 0, k, 0, 0))
    edge = pl.BlockSpec((1, 1, tiles, HALO, LANES), lambda k, m: (m, k, 0, 0, 0))
    f_edge = pl.BlockSpec((1, 1, tiles, HALO, LANES), lambda k, m: (0, k, 0, 0, 0))
    flank = pl.BlockSpec((1, 1, height, LANES), lambda k, m: (m, k, 0, 0))
    f_flank = pl.BlockSpec((1, 1, height, LANES), lambda k, m: (0, k, 0, 0))
    f_main = pl.BlockSpec((variables, 1, height, width), lambda k, m: (0, k, 0, 0))
    scalars = spec(pltpu.SMEM)
    return pl.pallas_call(
        step_kernel,
        grid=(levels, members),
        in_specs=[main, edge, edge, flank, f_main, f_edge, f_edge, f_flank, scalars, scalars],
        out_specs=main,
        out_shape=jax.ShapeDtypeStruct(start.shape, jnp.float32),
        scratch_shapes=[
            pltpu.VMEM((2, count, variables, tall + 2 * ROWS, LANES), jnp.float32),
            pltpu.VMEM((count, variables, tall, LANES), jnp.float32),
            pltpu.VMEM((count, variables, height, LANES), jnp.float32),
        ],
        compiler_params=pltpu.CompilerParams(vmem_limit_bytes=VMEM),
    )(start, above, below, side, forcing, f_above, f_below, f_side, coupling.reshape(-1), place)


def shards(state, kick, forcing, coupling, clone_src):
    start, side, top, bottom, *f_halo = prepared(state, kick, forcing, clone_src)
    halo = (*neighbours(top, bottom), side)
    return advance(start, halo, f_halo, forcing, coupling)


def solution(mesh):
    in_specs = (
        P("member", None, None, "lat", "lon"),
        P("member", None, None, "lat", "lon"),
        P(None, None, "lat", "lon"),
        P(),
        P(),
    )
    out_specs = P("member", None, None, "lat", "lon")
    return jax.shard_map(shards, mesh=mesh, in_specs=in_specs, out_specs=out_specs, check_vma=False)
```

```python
import functools

import functools

import jax
import jax.numpy as jnp
from jax import lax
from jax.experimental import pallas as pl
from jax.experimental.pallas import tpu as pltpu
from jax.sharding import PartitionSpec as P

STEPS = 4
REACH = 2
HALO = STEPS * REACH
LANES = 128
ROWS = 8
SPAN = LANES - 2 * HALO
K = 0.05 / 12.0
VMEM = 16 * 1024 * 1024


def lane_index(shape):
    return lax.broadcasted_iota(jnp.int32, shape, len(shape) - 1)


def turn(x, shift):
    shift = shift % LANES
    return x if shift == 0 else pltpu.roll(x, shift, x.ndim - 1)


def chain(bits, groups):
    stops = [0] + [x for x in range(1, groups - 1) if bits >> (x - 1) & 1] + [groups - 1]
    return list(zip(stops[:-1], stops[1:]))


class Layout:
    def __init__(self, groups, per_dev):
        self.groups, self.per_dev = groups, per_dev
        self.most = per_dev * (groups - 1)
        self.patterns, self.sends = 1, 1 + 2 * self.most
        self.takes = self.sends + 2 * self.most
        self.place = self.takes + per_dev
        self.size = self.place + per_dev
        self.kinds = 1 + (1 << (groups - 2))


def plan_lines(lay, clone_ref, group_ref, plan_ref, index_ref, ends):
    groups, per_dev, most = lay.groups, lay.per_dev, lay.most
    me = group_ref[0]
    plan_ref[0] = 1
    for t in range(2 * most):
        plan_ref[lay.patterns + t] = 0
        plan_ref[lay.sends + t] = 0
    for i in range(per_dev):
        plan_ref[lay.takes + i] = -1 - clone_ref[me * per_dev + i] % per_dev

    for down in range(2):
        for t in range(most):
            ends[t] = 0
        for a in range(groups - 1):
            for b in range(a + 1, groups):
                source, target = (groups - 1 - a, groups - 1 - b) if down else (a, b)
                spans = sum(1 << (x - 1) for x in range(a + 1, b))
                for j in range(per_dev):
                    member = source * per_dev + j
                    wanted = [clone_ref[target * per_dev + i] == member for i in range(per_dev)]
                    need = functools.reduce(jnp.logical_or, wanted)

                    @pl.when(need)
                    def _():
                        t = jnp.int32(most - 1)
                        for earlier in reversed(range(most - 1)):
                            t = jnp.where(ends[earlier] <= a, earlier, t)
                        ends[t] = b
                        plan_ref[0] = jnp.maximum(plan_ref[0], t + 1)
                        at = 2 * t + down
                        before = plan_ref[lay.patterns + at]
                        bits = jnp.where(before == 0, lay.kinds - 2, before - 1)
                        plan_ref[lay.patterns + at] = 1 + (bits & ~spans)

                        @pl.when(me == source)
                        def _():
                            plan_ref[lay.sends + at] = j

                        for i in range(per_dev):

                            @pl.when((me == target) & wanted[i])
                            def _():
                                plan_ref[lay.takes + i] = at

    index_ref[0] = plan_ref[lay.patterns] * lay.kinds + plan_ref[lay.patterns + 1]
    for i in range(per_dev):
        take = plan_ref[lay.takes + i]
        far = per_dev + jnp.where(take < 2, take, 2 + i)
        plan_ref[lay.place + i] = jnp.where(take < 0, -1 - take, far)


def first_kernel(
    lay, clone_ref, group_ref, state_ref, kick_ref, forcing_ref,
    plan_ref, index_ref, up_ref, down_ref, up_side_ref, down_side_ref, strips_ref, *refs,
):
    ends, state_ends, kick_ends, forcing_ends, done = refs[-5:]
    members, variables, levels, height, width = state_ref.shape
    parts = []
    for side, at in enumerate((0, width - LANES)):
        for ref, part in ((state_ref, state_ends), (kick_ref, kick_ends), (forcing_ref, forcing_ends)):
            piece = ref.at[(slice(None),) * (len(ref.shape) - 1) + (pl.ds(at, LANES),)]
            parts.append(pltpu.make_async_copy(piece, part.at[side], done.at[len(parts)]))
    for copy in parts:
        copy.start()
    plan_lines(lay, clone_ref, group_ref, plan_ref, index_ref, ends)
    sent = [plan_ref[lay.sends], plan_ref[lay.sends + 1]]
    whole = [
        pltpu.make_async_copy(state_ref.at[j], ref, done.at[len(parts) + way])
        for way, (j, ref) in enumerate(zip(sent, (up_ref, down_ref)))
    ]
    for copy in whole:
        copy.start()
    for copy in parts:
        copy.wait()
    lane = lane_index((height, LANES))

    @pl.loop(0, levels)
    def _(k):
        for slot in range(2 * members + 1):
            strip = jnp.zeros((height, LANES), jnp.float32)
            for v in range(variables):
                if slot < members:
                    low, high = (state_ends[side, slot, v, k] for side in range(2))
                elif slot < 2 * members:
                    low, high = (kick_ends[side, slot - members, v, k] for side in range(2))
                else:
                    low, high = (forcing_ends[side, v, k] for side in range(2))
                both = turn(jnp.where(lane < HALO, low, high), HALO + 2 * HALO * v)
                strip = jnp.where(lane >= 2 * HALO * v, both, strip)
            strips_ref[slot, k] = strip

    up_side_ref[...] = strips_ref[sent[0]]
    down_side_ref[...] = strips_ref[sent[1]]
    for copy in whole:
        copy.wait()


def spec(space):
    return pl.BlockSpec(memory_space=space)


def first(lay, group, clone_src, state, kick, forcing):
    members, variables, levels, height, width = state.shape
    shape = jax.ShapeDtypeStruct
    one = shape(state.shape[1:], jnp.float32)
    side = shape((levels, height, LANES), jnp.float32)
    strips = shape((2 * members + 1, levels, height, LANES), jnp.float32)
    ends = (2, members, variables, levels, height, LANES)
    scalar, here, anywhere = spec(pltpu.SMEM), spec(pltpu.VMEM), spec(pl.ANY)
    return pl.pallas_call(
        functools.partial(first_kernel, lay),
        in_specs=[scalar] * 2 + [anywhere] * 3,
        out_specs=[scalar] * 2 + [here] * 5 + [anywhere] * 4,
        out_shape=[shape((lay.size,), jnp.int32), shape((1,), jnp.int32), one, one, side, side, strips]
        + [one, one, side, side],
        scratch_shapes=[
            pltpu.SMEM((lay.most,), jnp.int32),
            pltpu.VMEM(ends, jnp.float32),
            pltpu.VMEM(ends, jnp.float32),
            pltpu.VMEM((2, *ends[2:]), jnp.float32),
            pltpu.SemaphoreType.DMA((8,)),
        ],
        compiler_params=pltpu.CompilerParams(vmem_limit_bytes=VMEM),
    )(clone_src, group[None], state, kick, forcing)


def lay_edges(rows_of, strip, top_ref, bottom_ref, at, variables, width):
    height = strip.shape[0]
    tiles = width // LANES
    for v in range(variables):
        rows = rows_of(v)
        for t in range(tiles):
            part = rows[:, LANES * t : LANES * (t + 1)]
            top_ref[(*at, v * tiles + t)] = part[:HALO]
            bottom_ref[(*at, v * tiles + t)] = part[height - HALO :]
    top_ref[(*at, variables * tiles)] = strip[:HALO]
    bottom_ref[(*at, variables * tiles)] = strip[height - HALO :]


def edge_shape(members, forcing):
    variables, levels, height, width = forcing.shape
    return jax.ShapeDtypeStruct((members, levels, variables * width // LANES + 1, HALO, LANES), jnp.float32)


def pack_kernel(
    lay, plan_ref, state_ref, up_ref, down_ref, kept_ref, also_ref, kick_ref, forcing_ref,
    sides_ref, up_side_ref, down_side_ref, kept_side_ref, also_side_ref,
    start_ref, side_ref, top_ref, bottom_ref, field, done,
):
    members, variables, levels, height, width = field.shape
    places = [plan_ref[lay.place + i] for i in range(members)]
    options = [state_ref.at[j] for j in range(members)] + [up_ref, down_ref, kept_ref, also_ref]
    others = [up_side_ref, down_side_ref, kept_side_ref, also_side_ref]
    for i in range(members):
        for at, option in enumerate(options):

            @pl.when(places[i] == at)
            def _():
                pltpu.make_async_copy(option, field.at[i], done.at[i]).start()

    @pl.loop(0, levels)
    def _(k):
        f_strip = sides_ref[2 * members, k]
        side_ref[members, k] = f_strip
        lay_edges(lambda v: forcing_ref[v, k], f_strip, top_ref, bottom_ref, (members, k), variables, width)

    for i in range(members):
        pltpu.make_async_copy(up_ref, field.at[i], done.at[i]).wait()

        @pl.loop(0, levels)
        def _(k):
            strip = others[-1][k]
            for at in reversed(range(len(options) - 1)):
                other = sides_ref[at, k] if at < members else others[at - members][k]
                strip = jnp.where(places[i] == at, other, strip)
            strip = strip + sides_ref[members + i, k]
            side_ref[i, k] = strip

            def rows_of(v):
                rows = field[i, v, k] + kick_ref[i, v, k]
                start_ref[i, v, k] = rows
                return rows

            lay_edges(rows_of, strip, top_ref, bottom_ref, (i, k), variables, width)


def pack(lay, plan, state, fields, kick, forcing, sides, far_sides):
    members, variables, levels, height, width = state.shape
    shape = jax.ShapeDtypeStruct
    here = spec(pltpu.VMEM)
    return pl.pallas_call(
        functools.partial(pack_kernel, lay),
        in_specs=[spec(pltpu.SMEM)] + [spec(pl.ANY)] * 5 + [here] * 7,
        out_specs=[here] * 4,
        out_shape=[
            shape(state.shape, jnp.float32),
            shape((members + 1, levels, height, LANES), jnp.float32),
            edge_shape(members + 1, forcing),
            edge_shape(members + 1, forcing),
        ],
        scratch_shapes=[pltpu.VMEM(state.shape, jnp.float32), pltpu.SemaphoreType.DMA((members,))],
        compiler_params=pltpu.CompilerParams(vmem_limit_bytes=VMEM),
    )(plan, state, *fields, kick, forcing, sides, *far_sides)


def neighbours(top, bottom):
    lats = lax.axis_size("lat")
    above = lax.ppermute(bottom, "lat", [(i, i + 1) for i in range(lats - 1)])
    below = lax.ppermute(top, "lat", [(i + 1, i) for i in range(lats - 1)])
    return above, below


def beside(strips):
    assert lax.axis_size("lon") == 2
    return lax.ppermute(strips, "lon", [(0, 1), (1, 0)])


def send(lay, kinds, fields, sides):
    groups, lons = lay.groups, lax.axis_size("lon")
    fields, sides = list(fields), list(sides)
    for down, kind in enumerate(kinds):
        if kind:
            pairs = chain(kind - 1, groups)
            if down:
                pairs = [(groups - 1 - a, groups - 1 - b) for a, b in pairs]
            crossed = [(a * lons + j, b * lons + 1 - j) for a, b in pairs for j in range(lons)]
            fields[down] = lax.ppermute(fields[down], "member", pairs)
            sides[down] = lax.ppermute(sides[down], ("member", "lon"), crossed)
    return (*fields, *sides)


def pick_kernel(lay, step_ref, plan_ref, state_ref, strips_ref, index_ref, up_ref, down_ref, up_side_ref, down_side_ref, done):
    t = step_ref[0]
    index_ref[0] = plan_ref[lay.patterns + 2 * t] * lay.kinds + plan_ref[lay.patterns + 2 * t + 1]
    copies = []
    for way, (whole, part) in enumerate(((up_ref, up_side_ref), (down_ref, down_side_ref))):
        j = plan_ref[lay.sends + 2 * t + way]
        copies.append(pltpu.make_async_copy(state_ref.at[j], whole, done.at[2 * way]))
        copies.append(pltpu.make_async_copy(strips_ref.at[j], part, done.at[2 * way + 1]))
    for copy in copies:
        copy.start()
    for copy in copies:
        copy.wait()


def pick(lay, t, plan, state, strips):
    shape = jax.ShapeDtypeStruct
    whole, part = shape(state.shape[1:], jnp.float32), shape(strips.shape[1:], jnp.float32)
    return pl.pallas_call(
        functools.partial(pick_kernel, lay),
        in_specs=[spec(pltpu.SMEM)] * 2 + [spec(pl.ANY)] * 2,
        out_specs=[spec(pltpu.SMEM)] + [spec(pltpu.VMEM)] * 4,
        out_shape=[shape((1,), jnp.int32), whole, whole, part, part],
        scratch_shapes=[pltpu.SemaphoreType.DMA((4,))],
        compiler_params=pltpu.CompilerParams(vmem_limit_bytes=VMEM),
    )(t[None], plan, state, strips)


def keep_kernel(lay, step_ref, plan_ref, up_ref, down_ref, up_side_ref, down_side_ref, *refs):
    held, done = refs[4:8], refs[8]
    t = step_ref[0]
    for wait in range(2):
        for i in range(lay.per_dev):
            for way, (whole, part) in enumerate(((up_ref, up_side_ref), (down_ref, down_side_ref))):

                @pl.when(plan_ref[lay.takes + i] == 2 * t + way)
                def _():
                    copies = [
                        pltpu.make_async_copy(whole, held[i], done.at[2 * i]),
                        pltpu.make_async_copy(part, held[lay.per_dev + i], done.at[2 * i + 1]),
                    ]
                    for copy in copies:
                        copy.wait() if wait else copy.start()


def keep(lay, t, plan, got, held):
    assert lay.per_dev == 2
    shape = jax.ShapeDtypeStruct
    return pl.pallas_call(
        functools.partial(keep_kernel, lay),
        in_specs=[spec(pltpu.SMEM)] * 2 + [spec(pltpu.VMEM)] * 4 + [spec(pl.ANY)] * 4,
        out_specs=[spec(pl.ANY)] * 4,
        out_shape=[shape(x.shape, x.dtype) for x in held],
        input_output_aliases={6 + i: i for i in range(4)},
        scratch_shapes=[pltpu.SemaphoreType.DMA((4,))],
        compiler_params=pltpu.CompilerParams(vmem_limit_bytes=VMEM),
    )(t[None], plan, *got, *held)


def prepared(state, kick, forcing, clone_src):
    per_dev, groups, group = state.shape[0], lax.axis_size("member"), lax.axis_index("member")
    lay = Layout(groups, per_dev)
    if groups != 4:
        piece = lax.all_gather(state, "member", axis=0, tiled=True)
        sources = lax.dynamic_slice_in_dim(clone_src, group * per_dev, per_dev)
        state = jnp.take(piece, sources, axis=0, mode="clip")
        lay = Layout(2, per_dev)
        still = jnp.arange(per_dev * 2, dtype=jnp.int32)
        plan, _, up, down, up_side, down_side, strips, *held = first(lay, jnp.int32(0), still, state, kick, forcing)
        plan = plan.at[lay.place :].set(still[:per_dev])
        got = (up, down, up_side, down_side)
    else:
        plan, index, *out, strips, a, b, c, d = first(lay, group, clone_src, state, kick, forcing)
        held = (a, b, c, d)
        kinds = [(a, b) for a in range(lay.kinds) for b in range(lay.kinds)]
        ways = [lambda a, b, c, d, kind=kind: send(lay, kind, (a, b), (c, d)) for kind in kinds]
        got = lax.switch(index[0], ways, *out)

        def later(t, held):
            at, *out = pick(lay, t, plan, state, strips)
            return tuple(keep(lay, t, plan, lax.switch(at[0], ways, *out), held))

        held = lax.fori_loop(1, plan[0], later, held)

    sides = beside(strips)
    fields = (*got[:2], *held[:2])
    return pack(lay, plan, state, fields, kick, forcing, sides, (*got[2:], *held[2:]))


def cut(rows, strip, v):
    width = rows.shape[1]
    count = -(-width // SPAN)
    lane = lane_index((rows.shape[0], LANES))
    source = [rows[:, LANES * t : LANES * (t + 1)] for t in range(width // LANES)]
    tiles = []
    for c in range(count):
        first = SPAN * c - HALO
        if c == 0:
            tile = jnp.where(lane < HALO, turn(strip, -2 * HALO * v), turn(source[0], HALO))
        else:
            t, offset = first // LANES, first % LANES
            if t + 1 < len(source):
                later = turn(source[t + 1], -offset)
            else:
                later = turn(strip, LANES - offset - 2 * HALO * v - HALO)
            tile = jnp.where(lane < LANES - offset, turn(source[t], -offset), later)
        tiles.append(tile)
    return tiles


def step_kernel(
    start_ref, above_ref, below_ref, side_ref, forcing_ref, f_above_ref, f_below_ref, f_side_ref,
    coupling_ref, place_ref, out_ref, cells, source, result,
):
    level = pl.program_id(0)
    variables, height, width = start_ref.shape[1], start_ref.shape[3], start_ref.shape[4]
    count = -(-width // SPAN)
    blocks = (height + 2 * HALO) // ROWS
    base = ROWS

    def edge(ref, v):
        tiles = width // LANES
        rows = [ref[0, 0, v * tiles + t] for t in range(tiles)]
        return jnp.concatenate(rows, axis=1), ref[0, 0, variables * tiles]

    def lay(rows, strip, v, target, at, scale):
        for c, tile in enumerate(cut(rows, strip, v)):
            target[c, v, at : at + rows.shape[0]] = tile if scale is None else tile * scale

    for v in range(variables):
        lay(*edge(above_ref, v), v, cells.at[0], base, None)
        lay(start_ref[0, v, 0], side_ref[0, 0], v, cells.at[0], base + HALO, None)
        lay(*edge(below_ref, v), v, cells.at[0], base + HALO + height, None)

    @pl.when(pl.program_id(1) == 0)
    def _():
        for v in range(variables):
            lay(*edge(f_above_ref, v), v, source, 0, 0.1)
            lay(forcing_ref[v, 0], f_side_ref[0, 0], v, source, HALO, 0.1)
            lay(*edge(f_below_ref, v), v, source, HALO + height, 0.1)

    weight = [
        [
            0.25 * coupling_ref[level * variables * variables + v * variables + w]
            + (1.0 - 60.0 * K if v == w else 0.0)
            for w in range(variables)
        ]
        for v in range(variables)
    ]
    at_top = place_ref[0] == 0
    at_bottom = place_ref[0] == place_ref[1] - 1

    @pl.loop(0, count)
    def _(c):
        for step in range(STEPS):
            now, later = cells.at[step % 2, c], cells.at[(step + 1) % 2, c]
            last = step == STEPS - 1
            for r in range(1, blocks - 1) if last else range(blocks):
                at = base + ROWS * r
                centre = [now[v, at : at + ROWS] for v in range(variables)]
                ku, kv = K * centre[0], K * centre[1]
                eu, ev = 8.0 * ku, 8.0 * kv
                east, west, far_east, far_west = 16.0 * K - eu, 16.0 * K + eu, ku - K, -K - ku
                south, north, far_south, far_north = 16.0 * K - ev, 16.0 * K + ev, kv - K, -K - kv
                for v in range(variables):
                    q = centre[v]
                    total = source[c, v, ROWS * r : ROWS * (r + 1)]
                    for w in range(variables):
                        total += weight[v][w] * centre[w]
                    along = east * turn(q, -1) + west * turn(q, 1)
                    along += far_east * turn(q, -2) + far_west * turn(q, 2)
                    across = south * now[v, at + 1 : at + 1 + ROWS] + north * now[v, at - 1 : at - 1 + ROWS]
                    across += far_south * now[v, at + 2 : at + 2 + ROWS] + far_north * now[v, at - 2 : at - 2 + ROWS]
                    total += along + across
                    if last:
                        result[c, v, ROWS * (r - 1) : ROWS * r] = total
                    else:
                        if r == 0:
                            total = jnp.where(at_top, 0.0, total)
                        if r == blocks - 1:
                            total = jnp.where(at_bottom, 0.0, total)
                        later[v, at : at + ROWS] = total

    lane = lane_index((height, LANES))
    for v in range(variables):
        for t in range(width // LANES):
            c, offset = LANES * t // SPAN, LANES * t % SPAN
            left = turn(result[c, v], -(offset + HALO))
            if c + 1 < count:
                right = turn(result[c + 1, v], SPAN - offset - HALO)
                left = jnp.where(lane < SPAN - offset, left, right)
            out_ref[0, v, 0, :, LANES * t : LANES * (t + 1)] = left


def advance(start, above, below, side, forcing, coupling):
    members, variables, levels, height, width = start.shape
    tiles = above.shape[2]
    count = -(-width // SPAN)
    tall = height + 2 * HALO
    place = jnp.stack([lax.axis_index("lat"), jnp.int32(lax.axis_size("lat"))])
    main = pl.BlockSpec((1, variables, 1, height, width), lambda k, m: (m, 0, k, 0, 0))
    edge = pl.BlockSpec((1, 1, tiles, HALO, LANES), lambda k, m: (m, k, 0, 0, 0))
    f_edge = pl.BlockSpec((1, 1, tiles, HALO, LANES), lambda k, m: (members, k, 0, 0, 0))
    flank = pl.BlockSpec((1, 1, height, LANES), lambda k, m: (m, k, 0, 0))
    f_flank = pl.BlockSpec((1, 1, height, LANES), lambda k, m: (members, k, 0, 0))
    f_main = pl.BlockSpec((variables, 1, height, width), lambda k, m: (0, k, 0, 0))
    scalars = spec(pltpu.SMEM)
    return pl.pallas_call(
        step_kernel,
        grid=(levels, members),
        in_specs=[main, edge, edge, flank, f_main, f_edge, f_edge, f_flank, scalars, scalars],
        out_specs=main,
        out_shape=jax.ShapeDtypeStruct(start.shape, jnp.float32),
        scratch_shapes=[
            pltpu.VMEM((2, count, variables, tall + 2 * ROWS, LANES), jnp.float32),
            pltpu.VMEM((count, variables, tall, LANES), jnp.float32),
            pltpu.VMEM((count, variables, height, LANES), jnp.float32),
        ],
        compiler_params=pltpu.CompilerParams(vmem_limit_bytes=VMEM),
    )(start, above, below, side, forcing, above, below, side, coupling.reshape(-1), place)


def shards(state, kick, forcing, coupling, clone_src):
    start, side, top, bottom = prepared(state, kick, forcing, clone_src)
    above, below = neighbours(top, bottom)
    return advance(start, above, below, side, forcing, coupling)


def solution(mesh):
    in_specs = (
        P("member", None, None, "lat", "lon"),
        P("member", None, None, "lat", "lon"),
        P(None, None, "lat", "lon"),
        P(),
        P(),
    )
    out_specs = P("member", None, None, "lat", "lon")
    return jax.shard_map(shards, mesh=mesh, in_specs=in_specs, out_specs=out_specs, check_vma=False)
```

```python
import functools

import functools

import jax
import jax.numpy as jnp
from jax import lax
from jax.experimental import pallas as pl
from jax.experimental.pallas import tpu as pltpu
from jax.sharding import PartitionSpec as P

STEPS = 4
REACH = 2
HALO = STEPS * REACH
LANES = 128
ROWS = 8
SPAN = LANES - 2 * HALO
K = 0.05 / 12.0
VMEM = 16 * 1024 * 1024


def lane_index(shape):
    return lax.broadcasted_iota(jnp.int32, shape, len(shape) - 1)


def turn(x, shift):
    shift = shift % LANES
    return x if shift == 0 else pltpu.roll(x, shift, x.ndim - 1)


def chain(bits, groups):
    stops = [0] + [x for x in range(1, groups - 1) if bits >> (x - 1) & 1] + [groups - 1]
    return list(zip(stops[:-1], stops[1:]))


class Layout:
    def __init__(self, groups, per_dev):
        self.groups, self.per_dev = groups, per_dev
        self.most = per_dev * (groups - 1)
        self.patterns, self.sends = 1, 1 + 2 * self.most
        self.takes = self.sends + 2 * self.most
        self.place = self.takes + per_dev
        self.size = self.place + per_dev
        self.kinds = 1 + (1 << (groups - 2))


def plan_lines(lay, clone_ref, group_ref, plan_ref, index_refs, ends):
    groups, per_dev, most = lay.groups, lay.per_dev, lay.most
    me = group_ref[0]
    plan_ref[0] = 1
    for t in range(2 * most):
        plan_ref[lay.patterns + t] = 0
        plan_ref[lay.sends + t] = 0
    for i in range(per_dev):
        plan_ref[lay.takes + i] = -1 - clone_ref[me * per_dev + i] % per_dev

    for down in range(2):
        for t in range(most):
            ends[t] = 0
        for a in range(groups - 1):
            for b in range(a + 1, groups):
                source, target = (groups - 1 - a, groups - 1 - b) if down else (a, b)
                spans = sum(1 << (x - 1) for x in range(a + 1, b))
                for j in range(per_dev):
                    member = source * per_dev + j
                    wanted = [clone_ref[target * per_dev + i] == member for i in range(per_dev)]
                    need = functools.reduce(jnp.logical_or, wanted)

                    @pl.when(need)
                    def _():
                        t = jnp.int32(most - 1)
                        for earlier in reversed(range(most - 1)):
                            t = jnp.where(ends[earlier] <= a, earlier, t)
                        ends[t] = b
                        plan_ref[0] = jnp.maximum(plan_ref[0], t + 1)
                        at = 2 * t + down
                        before = plan_ref[lay.patterns + at]
                        bits = jnp.where(before == 0, lay.kinds - 2, before - 1)
                        plan_ref[lay.patterns + at] = 1 + (bits & ~spans)

                        @pl.when(me == source)
                        def _():
                            plan_ref[lay.sends + at] = j

                        for i in range(per_dev):

                            @pl.when((me == target) & wanted[i])
                            def _():
                                plan_ref[lay.takes + i] = at

    for t in range(2):
        index_refs[t][0] = plan_ref[lay.patterns + 2 * t] * lay.kinds + plan_ref[lay.patterns + 2 * t + 1]
    index_refs[2][0] = jnp.where(plan_ref[0] > 2, 1, 0)
    for i in range(per_dev):
        take = plan_ref[lay.takes + i]
        far = per_dev + jnp.where(take < 4, take, 4 + i)
        plan_ref[lay.place + i] = jnp.where(take < 0, -1 - take, far)


def first_kernel(
    lay, clone_ref, group_ref, state_ref, kick_ref, forcing_ref, plan_ref, index_ref, second_ref, more_ref, *refs
):
    fields, sides, strips_ref = refs[:4], refs[4:8], refs[8]
    sources, ends, state_ends, kick_ends, forcing_ends, done = refs[-6:]
    members, variables, levels, height, width = state_ref.shape
    parts = [pltpu.make_async_copy(clone_ref, sources, done.at[0])]
    for side, at in enumerate((0, width - LANES)):
        for ref, part in ((state_ref, state_ends), (kick_ref, kick_ends), (forcing_ref, forcing_ends)):
            piece = ref.at[(slice(None),) * (len(ref.shape) - 1) + (pl.ds(at, LANES),)]
            parts.append(pltpu.make_async_copy(piece, part.at[side], done.at[len(parts)]))
    for copy in parts:
        copy.start()
    parts[0].wait()
    plan_lines(lay, sources, group_ref, plan_ref, (index_ref, second_ref, more_ref), ends)
    sent = [plan_ref[lay.sends + n] for n in range(4)]
    whole = [
        pltpu.make_async_copy(state_ref.at[j], ref, done.at[len(parts) + n])
        for n, (j, ref) in enumerate(zip(sent, fields))
    ]
    wanted = [plan_ref[lay.patterns + n] > 0 for n in range(4)]
    for copy, want in zip(whole, wanted):
        pl.when(want)(copy.start)
    for copy in parts[1:]:
        copy.wait()
    lane = lane_index((height, LANES))

    @pl.loop(0, levels)
    def _(k):
        for slot in range(2 * members + 1):
            strip = jnp.zeros((height, LANES), jnp.float32)
            for v in range(variables):
                if slot < members:
                    low, high = (state_ends[side, slot, v, k] for side in range(2))
                elif slot < 2 * members:
                    low, high = (kick_ends[side, slot - members, v, k] for side in range(2))
                else:
                    low, high = (forcing_ends[side, v, k] for side in range(2))
                both = turn(jnp.where(lane < HALO, low, high), HALO + 2 * HALO * v)
                strip = jnp.where(lane >= 2 * HALO * v, both, strip)
            strips_ref[slot, k] = strip

    for ref, j in zip(sides, sent):
        ref[...] = strips_ref[j]
    for copy, want in zip(whole, wanted):
        pl.when(want)(copy.wait)


def spec(space):
    return pl.BlockSpec(memory_space=space)


def first(lay, group, clone_src, state, kick, forcing):
    members, variables, levels, height, width = state.shape
    shape = jax.ShapeDtypeStruct
    one = shape(state.shape[1:], jnp.float32)
    side = shape((levels, height, LANES), jnp.float32)
    strips = shape((2 * members + 1, levels, height, LANES), jnp.float32)
    ends = (2, members, variables, levels, height, LANES)
    scalar, here, far = spec(pltpu.SMEM), spec(pltpu.VMEM), spec(pltpu.HBM)
    return pl.pallas_call(
        functools.partial(first_kernel, lay),
        in_specs=[far, scalar, far, far, far],
        out_specs=[scalar] * 4 + [here] * 9,
        out_shape=[shape((lay.size,), jnp.int32)] + [shape((1,), jnp.int32)] * 3 + [one] * 4 + [side] * 4 + [strips],
        scratch_shapes=[
            pltpu.SMEM(clone_src.shape, jnp.int32),
            pltpu.SMEM((lay.most,), jnp.int32),
            pltpu.VMEM(ends, jnp.float32),
            pltpu.VMEM(ends, jnp.float32),
            pltpu.VMEM((2, *ends[2:]), jnp.float32),
            pltpu.SemaphoreType.DMA((11,)),
        ],
        compiler_params=pltpu.CompilerParams(vmem_limit_bytes=VMEM),
    )(clone_src, group[None], state, kick, forcing)


def blank(*like):
    shapes = [jax.ShapeDtypeStruct(x.shape, x.dtype) for x in like]
    return pl.pallas_call(lambda *refs: None, out_specs=[spec(pl.ANY)] * len(like), out_shape=shapes)()


def edge_shape(members, forcing):
    variables, levels, height, width = forcing.shape
    return jax.ShapeDtypeStruct((members, levels, variables * width // LANES + 1, HALO, LANES), jnp.float32)


def pack_kernel(
    lay, plan_ref, state_ref, up_ref, down_ref, second_up_ref, second_down_ref, kept_ref, also_ref,
    kick_ref, forcing_ref, sides_ref, up_side_ref, down_side_ref, second_up_side_ref, second_down_side_ref,
    kept_side_ref, also_side_ref, start_ref, side_ref, top_ref, bottom_ref, field, done,
):
    members, variables, levels, height, width = state_ref.shape
    tiles = width // LANES

    def edges(slot, k, v, rows):
        for t in range(tiles):
            part = rows[:, LANES * t : LANES * (t + 1)]
            top_ref[slot, k, v * tiles + t] = part[:HALO]
            bottom_ref[slot, k, v * tiles + t] = part[height - HALO :]

    def flank(slot, k, strip):
        side_ref[slot, k] = strip
        top_ref[slot, k, variables * tiles] = strip[:HALO]
        bottom_ref[slot, k, variables * tiles] = strip[height - HALO :]

    @pl.loop(0, levels)
    def _(k):
        flank(members, k, sides_ref[2 * members, k])

        @pl.loop(0, variables)
        def _(v):
            edges(members, k, v, forcing_ref[v, k])

    whole = [state_ref.at[j] for j in range(members)] + [up_ref, down_ref, second_up_ref, second_down_ref]
    parts = [sides_ref.at[j] for j in range(members)]
    parts += [up_side_ref, down_side_ref, second_up_side_ref, second_down_side_ref]
    late = [(kept_ref, kept_side_ref), (also_ref, also_side_ref)]
    for i in range(members):
        place = plan_ref[lay.place + i]

        def fill(option, strip):
            @pl.loop(0, levels)
            def _(k):
                flank(i, k, strip[k] + sides_ref[members + i, k])

                @pl.loop(0, variables)
                def _(v):
                    rows = option[v, k] + kick_ref[i, v, k]
                    start_ref[i, v, k] = rows
                    edges(i, k, v, rows)

        for at, (option, strip) in enumerate(zip(whole, parts)):
            pl.when(place == at)(functools.partial(fill, option, strip))

        @pl.when(place >= len(whole))
        def _():
            copies = [
                pltpu.make_async_copy(late[i][0], field, done.at[0]),
                pltpu.make_async_copy(late[i][1], side_ref.at[i], done.at[1]),
            ]
            for copy in copies:
                copy.start()
            for copy in copies:
                copy.wait()
            fill(field, side_ref.at[i])


def pack(lay, plan, state, fields, kick, forcing, sides, far_sides):
    members, variables, levels, height, width = state.shape
    shape = jax.ShapeDtypeStruct
    here, anywhere = spec(pltpu.VMEM), spec(pl.ANY)
    return pl.pallas_call(
        functools.partial(pack_kernel, lay),
        in_specs=[spec(pltpu.SMEM)] + [here] * 5 + [anywhere] * 2 + [here] * 7 + [anywhere] * 2,
        out_specs=[here] * 4,
        out_shape=[
            shape(state.shape, jnp.float32),
            shape((members + 1, levels, height, LANES), jnp.float32),
            edge_shape(members + 1, forcing),
            edge_shape(members + 1, forcing),
        ],
        scratch_shapes=[pltpu.VMEM(state.shape[1:], jnp.float32), pltpu.SemaphoreType.DMA((2,))],
        compiler_params=pltpu.CompilerParams(vmem_limit_bytes=VMEM),
    )(plan, state, *fields, kick, forcing, sides, *far_sides)


def neighbours(top, bottom):
    lats = lax.axis_size("lat")
    above = lax.ppermute(bottom, "lat", [(i, i + 1) for i in range(lats - 1)])
    below = lax.ppermute(top, "lat", [(i + 1, i) for i in range(lats - 1)])
    return above, below


def beside(strips):
    assert lax.axis_size("lon") == 2
    return lax.ppermute(strips, "lon", [(0, 1), (1, 0)])


def send(lay, kinds, fields, sides):
    groups, lons = lay.groups, lax.axis_size("lon")
    fields, sides = list(fields), list(sides)
    for down, kind in enumerate(kinds):
        if kind:
            pairs = chain(kind - 1, groups)
            if down:
                pairs = [(groups - 1 - a, groups - 1 - b) for a, b in pairs]
            crossed = [(a * lons + j, b * lons + 1 - j) for a, b in pairs for j in range(lons)]
            fields[down] = lax.ppermute(fields[down], "member", pairs)
            sides[down] = lax.ppermute(sides[down], ("member", "lon"), crossed)
        else:
            fields[down], sides[down] = blank(fields[down], sides[down])
    return (*fields, *sides)


def pick_kernel(lay, step_ref, plan_ref, state_ref, strips_ref, index_ref, up_ref, down_ref, up_side_ref, down_side_ref, done):
    t = step_ref[0]
    index_ref[0] = plan_ref[lay.patterns + 2 * t] * lay.kinds + plan_ref[lay.patterns + 2 * t + 1]
    copies = []
    for way, (whole, part) in enumerate(((up_ref, up_side_ref), (down_ref, down_side_ref))):
        j = plan_ref[lay.sends + 2 * t + way]
        copies.append(pltpu.make_async_copy(state_ref.at[j], whole, done.at[2 * way]))
        copies.append(pltpu.make_async_copy(strips_ref.at[j], part, done.at[2 * way + 1]))
    for copy in copies:
        copy.start()
    for copy in copies:
        copy.wait()


def pick(lay, t, plan, state, strips):
    shape = jax.ShapeDtypeStruct
    whole, part = shape(state.shape[1:], jnp.float32), shape(strips.shape[1:], jnp.float32)
    return pl.pallas_call(
        functools.partial(pick_kernel, lay),
        in_specs=[spec(pltpu.SMEM)] * 2 + [spec(pl.ANY)] * 2,
        out_specs=[spec(pltpu.SMEM)] + [spec(pltpu.VMEM)] * 4,
        out_shape=[shape((1,), jnp.int32), whole, whole, part, part],
        scratch_shapes=[pltpu.SemaphoreType.DMA((4,))],
        compiler_params=pltpu.CompilerParams(vmem_limit_bytes=VMEM),
    )(t[None], plan, state, strips)


def keep_kernel(lay, step_ref, plan_ref, up_ref, down_ref, up_side_ref, down_side_ref, *refs):
    held, done = refs[4:8], refs[8]
    t = step_ref[0]
    for wait in range(2):
        for i in range(lay.per_dev):
            for way, (whole, part) in enumerate(((up_ref, up_side_ref), (down_ref, down_side_ref))):

                @pl.when(plan_ref[lay.takes + i] == 2 * t + way)
                def _():
                    copies = [
                        pltpu.make_async_copy(whole, held[i], done.at[2 * i]),
                        pltpu.make_async_copy(part, held[lay.per_dev + i], done.at[2 * i + 1]),
                    ]
                    for copy in copies:
                        copy.wait() if wait else copy.start()


def keep(lay, t, plan, got, held):
    assert lay.per_dev == 2
    shape = jax.ShapeDtypeStruct
    return pl.pallas_call(
        functools.partial(keep_kernel, lay),
        in_specs=[spec(pltpu.SMEM)] * 2 + [spec(pltpu.VMEM)] * 4 + [spec(pl.ANY)] * 4,
        out_specs=[spec(pl.ANY)] * 4,
        out_shape=[shape(x.shape, x.dtype) for x in held],
        input_output_aliases={6 + i: i for i in range(4)},
        scratch_shapes=[pltpu.SemaphoreType.DMA((4,))],
        compiler_params=pltpu.CompilerParams(vmem_limit_bytes=VMEM),
    )(t[None], plan, *got, *held)


def prepared(state, kick, forcing, clone_src):
    per_dev, groups, group = state.shape[0], lax.axis_size("member"), lax.axis_index("member")
    lay = Layout(groups, per_dev)
    if groups != 4:
        piece = lax.all_gather(state, "member", axis=0, tiled=True)
        sources = lax.dynamic_slice_in_dim(clone_src, group * per_dev, per_dev)
        state = jnp.take(piece, sources, axis=0, mode="clip")
        lay = Layout(3, per_dev)
        still = jnp.arange(per_dev * 3, dtype=jnp.int32)
        plan, _, _, _, *out, strips = first(lay, jnp.int32(0), still, state, kick, forcing)
        got, second = (*out[:2], *out[4:6]), (*out[2:4], *out[6:])
        held, sides = got, beside(strips)
    else:
        plan, index, following, more, *out, strips = first(lay, group, clone_src, state, kick, forcing)
        out, second = (*out[:2], *out[4:6]), (*out[2:4], *out[6:])
        kinds = [(a, b) for a in range(lay.kinds) for b in range(lay.kinds)]

        def opening(kind):
            return lambda a, b, c, d, strips: (*send(lay, kind, (a, b), (c, d)), beside(strips))

        ways = [lambda a, b, c, d, kind=kind: send(lay, kind, (a, b), (c, d)) for kind in kinds]
        *got, sides = lax.switch(index[0], [opening(kind) for kind in kinds], *out, strips)
        second = lax.switch(following[0], ways, *second)

        def later(t, held):
            at, *out = pick(lay, t, plan, state, strips)
            return tuple(keep(lay, t, plan, lax.switch(at[0], ways, *out), held))

        held = lax.switch(
            more[0],
            [lambda: tuple(blank(*got)), lambda: lax.fori_loop(2, plan[0], later, tuple(blank(*got)))],
        )

    fields = (*got[:2], *second[:2], *held[:2])
    far_sides = (*got[2:], *second[2:], *held[2:])
    return pack(lay, plan, state, fields, kick, forcing, sides, far_sides)


def cut(rows, strip, v):
    width = rows.shape[1]
    count = -(-width // SPAN)
    lane = lane_index((rows.shape[0], LANES))
    source = [rows[:, LANES * t : LANES * (t + 1)] for t in range(width // LANES)]
    tiles = []
    for c in range(count):
        first = SPAN * c - HALO
        if c == 0:
            tile = jnp.where(lane < HALO, turn(strip, -2 * HALO * v), turn(source[0], HALO))
        else:
            t, offset = first // LANES, first % LANES
            if t + 1 < len(source):
                later = turn(source[t + 1], -offset)
            else:
                later = turn(strip, LANES - offset - 2 * HALO * v - HALO)
            tile = jnp.where(lane < LANES - offset, turn(source[t], -offset), later)
        tiles.append(tile)
    return tiles


def step_kernel(
    start_ref, above_ref, below_ref, side_ref, forcing_ref, coupling_ref, place_ref, out_ref,
    cells, source, result, table, stage, done,
):
    members, variables, levels, height, width = start_ref.shape
    count = -(-width // SPAN)
    tall = height + 2 * HALO
    base = ROWS
    at_top = place_ref[0] == 0
    at_bottom = place_ref[0] == place_ref[1] - 1

    def edge(ref, slot, k, v):
        tiles = width // LANES
        rows = [ref[slot, k, v * tiles + t] for t in range(tiles)]
        return jnp.concatenate(rows, axis=1), ref[slot, k, variables * tiles]

    def lay(rows, strip, v, target, at, scale):
        for c, tile in enumerate(cut(rows, strip, v)):
            target[c, v, at : at + rows.shape[0]] = tile if scale is None else tile * scale

    def block(now, later, c, at, last):
        halves = range(2)
        first = [pl.ds(base + at + ROWS * h, ROWS) for h in halves]
        centre = [[now[v, first[h]] for v in range(variables)] for h in halves]
        ways = []
        for h in halves:
            ku, kv = K * centre[h][0], K * centre[h][1]
            eu, ev = 8.0 * ku, 8.0 * kv
            along = 16.0 * K - eu, 16.0 * K + eu, ku - K, -K - ku
            ways.append((along, (16.0 * K - ev, 16.0 * K + ev, kv - K, -K - kv)))
        for v in range(variables):
            weights = [table[v * variables + w] for w in range(variables)]
            for h in halves:
                q = centre[h][v]
                total = source[c, v, pl.ds(at + ROWS * h, ROWS)]
                for w in range(variables):
                    total += weights[w] * centre[h][w]
                along, across = ways[h]
                near = along[0] * turn(q, -1) + along[1] * turn(q, 1)
                far = along[2] * turn(q, -2) + along[3] * turn(q, 2)
                shifted = [now[v, pl.ds(base + at + ROWS * h + d, ROWS)] for d in (1, -1, 2, -2)]
                near += across[0] * shifted[0] + across[1] * shifted[1]
                far += across[2] * shifted[2] + across[3] * shifted[3]
                total += near + far
                if last:
                    result[c, v, pl.ds(at - HALO + ROWS * h, ROWS)] = total
                else:
                    later[v, first[h]] = total

    @pl.loop(0, levels * members)
    def _(job):
        k, m = job // members, job % members

        for v in range(variables):
            lay(*edge(above_ref, m, k, v), v, cells.at[0], base, None)
            lay(start_ref[m, v, k], side_ref[m, k], v, cells.at[0], base + HALO, None)
            lay(*edge(below_ref, m, k, v), v, cells.at[0], base + HALO + height, None)

        @pl.when(m == 0)
        def _():
            for v in range(variables):
                lay(*edge(above_ref, members, k, v), v, source, 0, 0.1)
                lay(forcing_ref[v, k], side_ref[members, k], v, source, HALO, 0.1)
                lay(*edge(below_ref, members, k, v), v, source, HALO + height, 0.1)
                for w in range(variables):
                    weight = 0.25 * coupling_ref[(k * variables + v) * variables + w]
                    weight = weight + (1.0 - 60.0 * K if v == w else 0.0)
                    table[v * variables + w] = jnp.full((ROWS, LANES), weight, jnp.float32)

        @pl.loop(0, count)
        def _(c):
            for step in range(STEPS):
                now, later = cells.at[step % 2, c], cells.at[(step + 1) % 2, c]
                last = step == STEPS - 1
                rows = (HALO, HALO + height) if last else (0, tall)

                @pl.loop(rows[0], rows[1], step=2 * ROWS)
                def _(at):
                    block(now, later, c, at, last)

                if not last:
                    for outside, at in ((at_top, base), (at_bottom, base + HALO + height)):

                        @pl.when(outside)
                        def _():
                            later[:, at : at + HALO] = jnp.zeros((variables, HALO, LANES), jnp.float32)

        slot = job % 2
        copy = pltpu.make_async_copy(stage.at[slot], out_ref.at[m, :, k], done.at[slot])
        pl.when(job >= 2)(copy.wait)
        lane = lane_index((height, LANES))
        for v in range(variables):
            for t in range(width // LANES):
                c, offset = LANES * t // SPAN, LANES * t % SPAN
                left = turn(result[c, v], -(offset + HALO))
                if c + 1 < count:
                    right = turn(result[c + 1, v], SPAN - offset - HALO)
                    left = jnp.where(lane < SPAN - offset, left, right)
                stage[slot, v, :, LANES * t : LANES * (t + 1)] = left
        copy.start()

    for slot in range(2):
        pltpu.make_async_copy(stage.at[slot], out_ref.at[0, :, 0], done.at[slot]).wait()


def advance(start, above, below, side, forcing, coupling):
    members, variables, levels, height, width = start.shape
    assert levels * members >= 2 and height % (2 * ROWS) == 0 and HALO == ROWS
    count = -(-width // SPAN)
    tall = height + 2 * HALO
    place = jnp.stack([lax.axis_index("lat"), jnp.int32(lax.axis_size("lat"))])
    here, scalars = spec(pltpu.VMEM), spec(pltpu.SMEM)
    return pl.pallas_call(
        step_kernel,
        in_specs=[here] * 5 + [scalars] * 2,
        out_specs=spec(pltpu.HBM),
        out_shape=jax.ShapeDtypeStruct(start.shape, jnp.float32),
        scratch_shapes=[
            pltpu.VMEM((2, count, variables, tall + 2 * ROWS, LANES), jnp.float32),
            pltpu.VMEM((count, variables, tall, LANES), jnp.float32),
            pltpu.VMEM((count, variables, height, LANES), jnp.float32),
            pltpu.VMEM((variables * variables, ROWS, LANES), jnp.float32),
            pltpu.VMEM((2, variables, height, width), jnp.float32),
            pltpu.SemaphoreType.DMA((2,)),
        ],
        compiler_params=pltpu.CompilerParams(vmem_limit_bytes=VMEM),
    )(start, above, below, side, forcing, coupling.reshape(-1), place)


def shards(state, kick, forcing, coupling, clone_src):
    start, side, top, bottom = prepared(state, kick, forcing, clone_src)
    above, below = neighbours(top, bottom)
    return advance(start, above, below, side, forcing, coupling)


def solution(mesh):
    in_specs = (
        P("member", None, None, "lat", "lon"),
        P("member", None, None, "lat", "lon"),
        P(None, None, "lat", "lon"),
        P(),
        P(),
    )
    out_specs = P("member", None, None, "lat", "lon")
    return jax.shard_map(shards, mesh=mesh, in_specs=in_specs, out_specs=out_specs, check_vma=False)
```

```python
import functools

import functools

import jax
import jax.numpy as jnp
from jax import lax
from jax.experimental import pallas as pl
from jax.experimental.pallas import tpu as pltpu
from jax.sharding import PartitionSpec as P

STEPS = 4
REACH = 2
HALO = STEPS * REACH
LANES = 128
ROWS = 8
SPAN = LANES - 2 * HALO
K = 0.05 / 12.0
VMEM = 12 * 1024 * 1024


def lane_index(shape):
    return lax.broadcasted_iota(jnp.int32, shape, len(shape) - 1)


def turn(x, shift):
    shift = shift % LANES
    return x if shift == 0 else pltpu.roll(x, shift, x.ndim - 1)


def chain(bits, groups):
    stops = [0] + [x for x in range(1, groups - 1) if bits >> (x - 1) & 1] + [groups - 1]
    return list(zip(stops[:-1], stops[1:]))


class Layout:
    def __init__(self, groups, per_dev):
        self.groups, self.per_dev = groups, per_dev
        self.most = per_dev * (groups - 1)
        self.patterns, self.sends = 1, 1 + 2 * self.most
        self.takes = self.sends + 2 * self.most
        self.place = self.takes + per_dev
        self.size = self.place + per_dev
        self.kinds = 1 + (1 << (groups - 2))


def plan_lines(lay, clone_ref, group_ref, plan_ref, index_refs, ends):
    groups, per_dev, most = lay.groups, lay.per_dev, lay.most
    me = group_ref[0]
    plan_ref[0] = 1
    for t in range(2 * most):
        plan_ref[lay.patterns + t] = 0
        plan_ref[lay.sends + t] = 0
    for i in range(per_dev):
        plan_ref[lay.takes + i] = -1 - clone_ref[me * per_dev + i] % per_dev

    for down in range(2):
        for t in range(most):
            ends[t] = 0
        for a in range(groups - 1):
            for b in range(a + 1, groups):
                source, target = (groups - 1 - a, groups - 1 - b) if down else (a, b)
                spans = sum(1 << (x - 1) for x in range(a + 1, b))
                for j in range(per_dev):
                    member = source * per_dev + j
                    wanted = [clone_ref[target * per_dev + i] == member for i in range(per_dev)]
                    need = functools.reduce(jnp.logical_or, wanted)

                    @pl.when(need)
                    def _():
                        t = jnp.int32(most - 1)
                        for earlier in reversed(range(most - 1)):
                            t = jnp.where(ends[earlier] <= a, earlier, t)
                        ends[t] = b
                        plan_ref[0] = jnp.maximum(plan_ref[0], t + 1)
                        at = 2 * t + down
                        before = plan_ref[lay.patterns + at]
                        bits = jnp.where(before == 0, lay.kinds - 2, before - 1)
                        plan_ref[lay.patterns + at] = 1 + (bits & ~spans)

                        @pl.when(me == source)
                        def _():
                            plan_ref[lay.sends + at] = j

                        for i in range(per_dev):

                            @pl.when((me == target) & wanted[i])
                            def _():
                                plan_ref[lay.takes + i] = at

    for t in range(2):
        index_refs[t][0] = plan_ref[lay.patterns + 2 * t] * lay.kinds + plan_ref[lay.patterns + 2 * t + 1]
    index_refs[1][0] = jnp.where(plan_ref[0] > 2, lay.kinds * lay.kinds, index_refs[1][0])
    for i in range(per_dev):
        take = plan_ref[lay.takes + i]
        near = jnp.where(plan_ref[0] > 2, 2, 4)
        far = per_dev + jnp.where(take < near, take, 4 + i)
        plan_ref[lay.place + i] = jnp.where(take < 0, -1 - take, far)


def first_kernel(
    lay, clone_ref, group_ref, state_ref, kick_ref, forcing_ref, plan_ref, index_ref, second_ref, *refs
):
    fields, sides, strips_ref = refs[:4], refs[4:8], refs[8]
    sources, ends, state_ends, kick_ends, forcing_ends, done = refs[-6:]
    members, variables, levels, height, width = state_ref.shape
    parts = [pltpu.make_async_copy(clone_ref, sources, done.at[0])]
    for side, at in enumerate((0, width - LANES)):
        for ref, part in ((state_ref, state_ends), (kick_ref, kick_ends), (forcing_ref, forcing_ends)):
            piece = ref.at[(slice(None),) * (len(ref.shape) - 1) + (pl.ds(at, LANES),)]
            parts.append(pltpu.make_async_copy(piece, part.at[side], done.at[len(parts)]))
    for copy in parts:
        copy.start()
    parts[0].wait()
    plan_lines(lay, sources, group_ref, plan_ref, (index_ref, second_ref), ends)
    sent = [plan_ref[lay.sends + n] for n in range(4)]
    whole = [
        pltpu.make_async_copy(state_ref.at[j], ref, done.at[len(parts) + n])
        for n, (j, ref) in enumerate(zip(sent, fields))
    ]
    wanted = [plan_ref[lay.patterns + n] > 0 for n in range(4)]
    for copy, want in zip(whole, wanted):
        pl.when(want)(copy.start)
    for copy in parts[1:]:
        copy.wait()
    lane = lane_index((height, LANES))

    @pl.loop(0, levels)
    def _(k):
        for slot in range(2 * members + 1):
            strip = jnp.zeros((height, LANES), jnp.float32)
            for v in range(variables):
                if slot < members:
                    low, high = (state_ends[side, slot, v, k] for side in range(2))
                elif slot < 2 * members:
                    low, high = (kick_ends[side, slot - members, v, k] for side in range(2))
                else:
                    low, high = (forcing_ends[side, v, k] for side in range(2))
                both = turn(jnp.where(lane < HALO, low, high), HALO + 2 * HALO * v)
                strip = jnp.where(lane >= 2 * HALO * v, both, strip)
            strips_ref[slot, k] = strip

    for ref, j in zip(sides, sent):
        ref[...] = strips_ref[j]
    for copy, want in zip(whole, wanted):
        pl.when(want)(copy.wait)


def spec(space):
    return pl.BlockSpec(memory_space=space)


def first(lay, group, clone_src, state, kick, forcing):
    members, variables, levels, height, width = state.shape
    shape = jax.ShapeDtypeStruct
    one = pltpu.VMEM(state.shape[1:], jnp.float32)
    side = pltpu.VMEM((levels, height, LANES), jnp.float32)
    strips = pltpu.VMEM((2 * members + 1, levels, height, LANES), jnp.float32)
    ends = (2, members, variables, levels, height, LANES)
    scalar, here, far = spec(pltpu.SMEM), spec(pltpu.VMEM), spec(pltpu.HBM)
    return pl.pallas_call(
        functools.partial(first_kernel, lay),
        in_specs=[far, scalar, far, far, far],
        out_specs=[scalar] * 3 + [here] * 9,
        out_shape=[shape((lay.size,), jnp.int32)] + [shape((1,), jnp.int32)] * 2 + [one] * 4 + [side] * 4 + [strips],
        scratch_shapes=[
            pltpu.SMEM(clone_src.shape, jnp.int32),
            pltpu.SMEM((lay.most,), jnp.int32),
            pltpu.VMEM(ends, jnp.float32),
            pltpu.VMEM(ends, jnp.float32),
            pltpu.VMEM((2, *ends[2:]), jnp.float32),
            pltpu.SemaphoreType.DMA((11,)),
        ],
        compiler_params=pltpu.CompilerParams(vmem_limit_bytes=VMEM),
    )(far_away(clone_src), group[None], far_away(state), far_away(kick), far_away(forcing))


def blank(*like):
    shapes = [pltpu.VMEM(x.shape, x.dtype) for x in like]
    return pl.pallas_call(lambda *refs: None, out_specs=[spec(pltpu.VMEM)] * len(like), out_shape=shapes)()


def far_away(x):
    return pltpu.with_memory_space_constraint(x, pltpu.HBM)


def nearby(x):
    return pltpu.with_memory_space_constraint(x, pltpu.VMEM)


def edge_shape(members, forcing):
    variables, levels, height, width = forcing.shape
    return pltpu.VMEM((members, levels, variables * width // LANES + 1, HALO, LANES), jnp.float32)


def pack_kernel(
    lay, plan_ref, state_ref, up_ref, down_ref, second_up_ref, second_down_ref, kept_ref, also_ref,
    kick_ref, forcing_ref, sides_ref, up_side_ref, down_side_ref, second_up_side_ref, second_down_side_ref,
    kept_side_ref, also_side_ref, start_ref, side_ref, top_ref, bottom_ref, field, done,
):
    members, variables, levels, height, width = state_ref.shape
    tiles = width // LANES

    def edges(slot, k, v, rows):
        for t in range(tiles):
            part = rows[:, LANES * t : LANES * (t + 1)]
            top_ref[slot, k, v * tiles + t] = part[:HALO]
            bottom_ref[slot, k, v * tiles + t] = part[height - HALO :]

    def flank(slot, k, strip):
        side_ref[slot, k] = strip
        top_ref[slot, k, variables * tiles] = strip[:HALO]
        bottom_ref[slot, k, variables * tiles] = strip[height - HALO :]

    @pl.loop(0, levels)
    def _(k):
        flank(members, k, sides_ref[2 * members, k])

        @pl.loop(0, variables)
        def _(v):
            edges(members, k, v, forcing_ref[v, k])

    whole = [state_ref.at[j] for j in range(members)] + [up_ref, down_ref, second_up_ref, second_down_ref]
    parts = [sides_ref.at[j] for j in range(members)]
    parts += [up_side_ref, down_side_ref, second_up_side_ref, second_down_side_ref]
    late = [(kept_ref, kept_side_ref), (also_ref, also_side_ref)]
    for i in range(members):
        place = plan_ref[lay.place + i]

        def fill(option, strip):
            @pl.loop(0, levels)
            def _(k):
                flank(i, k, strip[k] + sides_ref[members + i, k])

                @pl.loop(0, variables)
                def _(v):
                    rows = option[v, k] + kick_ref[i, v, k]
                    start_ref[i, v, k] = rows
                    edges(i, k, v, rows)

        for at, (option, strip) in enumerate(zip(whole, parts)):
            pl.when(place == at)(functools.partial(fill, option, strip))

        @pl.when(place >= len(whole))
        def _():
            copies = [
                pltpu.make_async_copy(late[i][0], field, done.at[0]),
                pltpu.make_async_copy(late[i][1], side_ref.at[i], done.at[1]),
            ]
            for copy in copies:
                copy.start()
            for copy in copies:
                copy.wait()
            fill(field, side_ref.at[i])


def pack(lay, plan, state, fields, kick, forcing, sides, far_sides):
    members, variables, levels, height, width = state.shape
    here, anywhere = spec(pltpu.VMEM), spec(pl.ANY)
    return pl.pallas_call(
        functools.partial(pack_kernel, lay),
        in_specs=[spec(pltpu.SMEM)] + [here] * 5 + [anywhere] * 2 + [here] * 7 + [anywhere] * 2,
        out_specs=[here] * 4,
        out_shape=[
            pltpu.VMEM(state.shape, jnp.float32),
            pltpu.VMEM((members + 1, levels, height, LANES), jnp.float32),
            edge_shape(members + 1, forcing),
            edge_shape(members + 1, forcing),
        ],
        scratch_shapes=[pltpu.VMEM(state.shape[1:], jnp.float32), pltpu.SemaphoreType.DMA((2,))],
        compiler_params=pltpu.CompilerParams(vmem_limit_bytes=VMEM),
    )(plan, *map(nearby, (state, *fields[:4])), *fields[4:], *map(nearby, (kick, forcing, sides, *far_sides[:4])), *far_sides[4:])


def neighbours(top, bottom):
    lats = lax.axis_size("lat")
    above = lax.ppermute(bottom, "lat", [(i, i + 1) for i in range(lats - 1)])
    below = lax.ppermute(top, "lat", [(i + 1, i) for i in range(lats - 1)])
    return above, below


def beside(strips):
    assert lax.axis_size("lon") == 2
    return lax.ppermute(strips, "lon", [(0, 1), (1, 0)])


def send(lay, kinds, fields, sides):
    groups, lons = lay.groups, lax.axis_size("lon")
    fields, sides = list(fields), list(sides)
    for down, kind in enumerate(kinds):
        if kind:
            pairs = chain(kind - 1, groups)
            if down:
                pairs = [(groups - 1 - a, groups - 1 - b) for a, b in pairs]
            crossed = [(a * lons + j, b * lons + 1 - j) for a, b in pairs for j in range(lons)]
            fields[down] = lax.ppermute(fields[down], "member", pairs)
            sides[down] = lax.ppermute(sides[down], ("member", "lon"), crossed)
        else:
            fields[down], sides[down] = blank(fields[down], sides[down])
    return (*fields, *sides)


def pick_kernel(lay, step_ref, plan_ref, state_ref, strips_ref, index_ref, up_ref, down_ref, up_side_ref, down_side_ref, done):
    t = step_ref[0]
    index_ref[0] = plan_ref[lay.patterns + 2 * t] * lay.kinds + plan_ref[lay.patterns + 2 * t + 1]
    copies = []
    for way, (whole, part) in enumerate(((up_ref, up_side_ref), (down_ref, down_side_ref))):
        j = plan_ref[lay.sends + 2 * t + way]
        copies.append(pltpu.make_async_copy(state_ref.at[j], whole, done.at[2 * way]))
        copies.append(pltpu.make_async_copy(strips_ref.at[j], part, done.at[2 * way + 1]))
    for copy in copies:
        copy.start()
    for copy in copies:
        copy.wait()


def pick(lay, t, plan, state, strips):
    shape = jax.ShapeDtypeStruct
    whole, part = shape(state.shape[1:], jnp.float32), shape(strips.shape[1:], jnp.float32)
    return pl.pallas_call(
        functools.partial(pick_kernel, lay),
        in_specs=[spec(pltpu.SMEM)] * 2 + [spec(pl.ANY)] * 2,
        out_specs=[spec(pltpu.SMEM)] + [spec(pltpu.VMEM)] * 4,
        out_shape=[shape((1,), jnp.int32), whole, whole, part, part],
        scratch_shapes=[pltpu.SemaphoreType.DMA((4,))],
        compiler_params=pltpu.CompilerParams(vmem_limit_bytes=VMEM),
    )(t[None], plan, state, strips)


def keep_kernel(lay, step_ref, plan_ref, up_ref, down_ref, up_side_ref, down_side_ref, *refs):
    held, done = refs[4:8], refs[8]
    t = step_ref[0]
    for wait in range(2):
        for i in range(lay.per_dev):
            for way, (whole, part) in enumerate(((up_ref, up_side_ref), (down_ref, down_side_ref))):

                @pl.when(plan_ref[lay.takes + i] == 2 * t + way)
                def _():
                    copies = [
                        pltpu.make_async_copy(whole, held[i], done.at[2 * i]),
                        pltpu.make_async_copy(part, held[lay.per_dev + i], done.at[2 * i + 1]),
                    ]
                    for copy in copies:
                        copy.wait() if wait else copy.start()


def keep(lay, t, plan, got, held):
    assert lay.per_dev == 2
    shape = jax.ShapeDtypeStruct
    return pl.pallas_call(
        functools.partial(keep_kernel, lay),
        in_specs=[spec(pltpu.SMEM)] * 2 + [spec(pltpu.VMEM)] * 4 + [spec(pl.ANY)] * 4,
        out_specs=[spec(pl.ANY)] * 4,
        out_shape=[shape(x.shape, x.dtype) for x in held],
        input_output_aliases={6 + i: i for i in range(4)},
        scratch_shapes=[pltpu.SemaphoreType.DMA((4,))],
        compiler_params=pltpu.CompilerParams(vmem_limit_bytes=VMEM),
    )(t[None], plan, *got, *held)


def prepared(state, kick, forcing, clone_src):
    per_dev, groups, group = state.shape[0], lax.axis_size("member"), lax.axis_index("member")
    lay = Layout(groups, per_dev)
    if groups != 4:
        piece = lax.all_gather(state, "member", axis=0, tiled=True)
        sources = lax.dynamic_slice_in_dim(clone_src, group * per_dev, per_dev)
        state = jnp.take(piece, sources, axis=0, mode="clip")
        lay = Layout(3, per_dev)
        still = jnp.arange(per_dev * 3, dtype=jnp.int32)
        plan, _, _, *out, strips = first(lay, jnp.int32(0), still, state, kick, forcing)
        got, second = (*out[:2], *out[4:6]), (*out[2:4], *out[6:])
        held, sides = got, beside(strips)
    else:
        plan, index, following, *out, strips = first(lay, group, clone_src, state, kick, forcing)
        out, second = (*out[:2], *out[4:6]), (*out[2:4], *out[6:])
        kinds = [(a, b) for a in range(lay.kinds) for b in range(lay.kinds)]

        def opening(kind):
            return lambda a, b, c, d, strips: (*send(lay, kind, (a, b), (c, d)), beside(strips))

        def middle(kind):
            return lambda a, b, c, d: (*send(lay, kind, (a, b), (c, d)), *blank(a, b, c, d))

        ways = [lambda a, b, c, d, kind=kind: send(lay, kind, (a, b), (c, d)) for kind in kinds]

        def later(t, held):
            at, *out = pick(lay, t, plan, state, strips)
            return tuple(keep(lay, t, plan, lax.switch(at[0], ways, *out), held))

        def several(a, b, c, d):
            return (a, b, c, d, *lax.fori_loop(1, plan[0], later, tuple(blank(a, b, c, d))))

        *got, sides = lax.switch(index[0], [opening(kind) for kind in kinds], *out, strips)
        *second, a, b, c, d = lax.switch(following[0], [middle(kind) for kind in kinds] + [several], *second)
        held = (a, b, c, d)

    fields = (*got[:2], *second[:2], *held[:2])
    far_sides = (*got[2:], *second[2:], *held[2:])
    return pack(lay, plan, state, fields, kick, forcing, sides, far_sides)


def cut(rows, strip, v):
    width = rows.shape[1]
    count = -(-width // SPAN)
    lane = lane_index((rows.shape[0], LANES))
    source = [rows[:, LANES * t : LANES * (t + 1)] for t in range(width // LANES)]
    tiles = []
    for c in range(count):
        first = SPAN * c - HALO
        if c == 0:
            tile = jnp.where(lane < HALO, turn(strip, -2 * HALO * v), turn(source[0], HALO))
        else:
            t, offset = first // LANES, first % LANES
            if t + 1 < len(source):
                later = turn(source[t + 1], -offset)
            else:
                later = turn(strip, LANES - offset - 2 * HALO * v - HALO)
            tile = jnp.where(lane < LANES - offset, turn(source[t], -offset), later)
        tiles.append(tile)
    return tiles


def step_kernel(
    start_ref, above_ref, below_ref, side_ref, forcing_ref, coupling_ref, place_ref, out_ref,
    cells, other, source, result, table, stage, done,
):
    members, variables, levels, height, width = start_ref.shape
    count = -(-width // SPAN)
    tall = height + 2 * HALO
    at_top = place_ref[0] == 0
    at_bottom = place_ref[0] == place_ref[1] - 1

    def edge(ref, slot, k, v):
        tiles = width // LANES
        rows = [ref[slot, k, v * tiles + t] for t in range(tiles)]
        return jnp.concatenate(rows, axis=1), ref[slot, k, variables * tiles]

    def lay(rows, strip, v, target, at, scale):
        for c, tile in enumerate(cut(rows, strip, v)):
            target[c, v, at : at + rows.shape[0]] = tile if scale is None else tile * scale

    blocks = tall // ROWS
    line = lax.broadcasted_iota(jnp.int32, (ROWS, LANES), 0)

    def advance_tile(now, later, c, last):
        tiles, turned = {}, {}

        def tile(v, r):
            if (v, r) not in tiles:
                tiles[v, r] = now[c, v, ROWS * r : ROWS * (r + 1)]
            return tiles[v, r]

        def rolled(v, r, d):
            if (v, r, d) not in turned:
                turned[v, r, d] = pltpu.roll(tile(v, r), -d % ROWS, 0)
            return turned[v, r, d]

        def shifted(v, r, d):
            own = rolled(v, r, d)
            if d > 0:
                return own if r + 1 == blocks else jnp.where(line < ROWS - d, own, rolled(v, r + 1, d))
            return own if r == 0 else jnp.where(line >= -d, own, rolled(v, r - 1, d))

        for r in range(1, blocks - 1) if last else range(blocks):
            centre = [tile(v, r) for v in range(variables)]
            ku, kv = K * centre[0], K * centre[1]
            eu, ev = 8.0 * ku, 8.0 * kv
            along = 16.0 * K - eu, 16.0 * K + eu, ku - K, -K - ku
            across = 16.0 * K - ev, 16.0 * K + ev, kv - K, -K - kv
            for v in range(variables):
                q = centre[v]
                total = source[c, v, ROWS * r : ROWS * (r + 1)]
                for w in range(variables):
                    total += table[v * variables + w] * centre[w]
                near = along[0] * turn(q, -1) + along[1] * turn(q, 1)
                far = along[2] * turn(q, -2) + along[3] * turn(q, 2)
                near += across[0] * shifted(v, r, 1) + across[1] * shifted(v, r, -1)
                far += across[2] * shifted(v, r, 2) + across[3] * shifted(v, r, -2)
                total += near + far
                if last:
                    result[c, v, ROWS * (r - 1) : ROWS * r] = total
                elif r in (0, blocks - 1):
                    later[c, v, ROWS * r : ROWS * (r + 1)] = jnp.where(at_top if r == 0 else at_bottom, 0.0, total)
                else:
                    later[c, v, ROWS * r : ROWS * (r + 1)] = total

    @pl.loop(0, levels * members)
    def _(job):
        k, m = job // members, job % members

        for v in range(variables):
            lay(*edge(above_ref, m, k, v), v, cells, 0, None)
            lay(start_ref[m, v, k], side_ref[m, k], v, cells, HALO, None)
            lay(*edge(below_ref, m, k, v), v, cells, HALO + height, None)

        @pl.when(m == 0)
        def _():
            for v in range(variables):
                lay(*edge(above_ref, members, k, v), v, source, 0, 0.1)
                lay(forcing_ref[v, k], side_ref[members, k], v, source, HALO, 0.1)
                lay(*edge(below_ref, members, k, v), v, source, HALO + height, 0.1)
                for w in range(variables):
                    weight = 0.25 * coupling_ref[(k * variables + v) * variables + w]
                    weight = weight + (1.0 - 60.0 * K if v == w else 0.0)
                    table[v * variables + w] = jnp.full((ROWS, LANES), weight, jnp.float32)

        @pl.loop(0, count)
        def _(c):
            for step in range(STEPS):
                now, later = (cells, other) if step % 2 == 0 else (other, cells)
                advance_tile(now, later, c, step == STEPS - 1)

        slot = job % 2
        copy = pltpu.make_async_copy(stage.at[slot], out_ref.at[m, :, k], done.at[slot])
        pl.when(job >= 2)(copy.wait)
        lane = lane_index((height, LANES))
        for v in range(variables):
            for t in range(width // LANES):
                c, offset = LANES * t // SPAN, LANES * t % SPAN
                left = turn(result[c, v], -(offset + HALO))
                if c + 1 < count:
                    right = turn(result[c + 1, v], SPAN - offset - HALO)
                    left = jnp.where(lane < SPAN - offset, left, right)
                stage[slot, v, :, LANES * t : LANES * (t + 1)] = left
        copy.start()

    for slot in range(2):
        pltpu.make_async_copy(stage.at[slot], out_ref.at[0, :, 0], done.at[slot]).wait()


def advance(start, above, below, side, forcing, coupling):
    members, variables, levels, height, width = start.shape
    assert levels * members >= 2 and height % ROWS == 0 and HALO == ROWS
    count = -(-width // SPAN)
    tall = height + 2 * HALO
    place = jnp.stack([lax.axis_index("lat"), jnp.int32(lax.axis_size("lat"))])
    here, scalars = spec(pltpu.VMEM), spec(pltpu.SMEM)
    return pl.pallas_call(
        step_kernel,
        in_specs=[here] * 5 + [scalars] * 2,
        out_specs=spec(pltpu.HBM),
        out_shape=jax.ShapeDtypeStruct(start.shape, jnp.float32),
        scratch_shapes=[
            pltpu.VMEM((count, variables, tall, LANES), jnp.float32),
            pltpu.VMEM((count, variables, tall, LANES), jnp.float32),
            pltpu.VMEM((count, variables, tall, LANES), jnp.float32),
            pltpu.VMEM((count, variables, height, LANES), jnp.float32),
            pltpu.VMEM((variables * variables, ROWS, LANES), jnp.float32),
            pltpu.VMEM((2, variables, height, width), jnp.float32),
            pltpu.SemaphoreType.DMA((2,)),
        ],
        compiler_params=pltpu.CompilerParams(vmem_limit_bytes=VMEM),
    )(start, above, below, side, forcing, coupling.reshape(-1), place)


def shards(state, kick, forcing, coupling, clone_src):
    start, side, top, bottom = prepared(state, kick, forcing, clone_src)
    above, below = neighbours(top, bottom)
    return advance(start, above, below, side, forcing, coupling)


def solution(mesh):
    in_specs = (
        P("member", None, None, "lat", "lon"),
        P("member", None, None, "lat", "lon"),
        P(None, None, "lat", "lon"),
        P(),
        P(),
    )
    out_specs = P("member", None, None, "lat", "lon")
    return jax.shard_map(shards, mesh=mesh, in_specs=in_specs, out_specs=out_specs, check_vma=False)
```

```python
import functools

import functools

import jax
import jax.numpy as jnp
from jax import lax
from jax.experimental import pallas as pl
from jax.experimental.pallas import tpu as pltpu
from jax.sharding import PartitionSpec as P

STEPS = 4
REACH = 2
HALO = STEPS * REACH
LANES = 128
ROWS = 8
SPAN = LANES - 2 * HALO
K = 0.05 / 12.0
VMEM = 10 * 1024 * 1024


def lane_index(shape):
    return lax.broadcasted_iota(jnp.int32, shape, len(shape) - 1)


def turn(x, shift):
    shift = shift % LANES
    return x if shift == 0 else pltpu.roll(x, shift, x.ndim - 1)


def chain(bits, groups):
    stops = [0] + [x for x in range(1, groups - 1) if bits >> (x - 1) & 1] + [groups - 1]
    return list(zip(stops[:-1], stops[1:]))


class Layout:
    def __init__(self, groups, per_dev):
        self.groups, self.per_dev = groups, per_dev
        self.most = per_dev * (groups - 1)
        self.patterns, self.sends = 1, 1 + 2 * self.most
        self.takes = self.sends + 2 * self.most
        self.place = self.takes + per_dev
        self.size = self.place + per_dev
        self.kinds = 1 + (1 << (groups - 2))


def plan_lines(lay, clone_ref, group_ref, plan_ref, index_refs, ends):
    groups, per_dev, most = lay.groups, lay.per_dev, lay.most
    me = group_ref[0]
    plan_ref[0] = 1
    for t in range(2 * most):
        plan_ref[lay.patterns + t] = 0
        plan_ref[lay.sends + t] = 0
    for i in range(per_dev):
        plan_ref[lay.takes + i] = -1 - clone_ref[me * per_dev + i] % per_dev

    for down in range(2):
        for t in range(most):
            ends[t] = 0
        for a in range(groups - 1):
            for b in range(a + 1, groups):
                source, target = (groups - 1 - a, groups - 1 - b) if down else (a, b)
                spans = sum(1 << (x - 1) for x in range(a + 1, b))
                for j in range(per_dev):
                    member = source * per_dev + j
                    wanted = [clone_ref[target * per_dev + i] == member for i in range(per_dev)]
                    need = functools.reduce(jnp.logical_or, wanted)

                    @pl.when(need)
                    def _():
                        t = jnp.int32(most - 1)
                        for earlier in reversed(range(most - 1)):
                            t = jnp.where(ends[earlier] <= a, earlier, t)
                        ends[t] = b
                        plan_ref[0] = jnp.maximum(plan_ref[0], t + 1)
                        at = 2 * t + down
                        before = plan_ref[lay.patterns + at]
                        bits = jnp.where(before == 0, lay.kinds - 2, before - 1)
                        plan_ref[lay.patterns + at] = 1 + (bits & ~spans)

                        @pl.when(me == source)
                        def _():
                            plan_ref[lay.sends + at] = j

                        for i in range(per_dev):

                            @pl.when((me == target) & wanted[i])
                            def _():
                                plan_ref[lay.takes + i] = at

    for t in range(2):
        index_refs[t][0] = plan_ref[lay.patterns + 2 * t] * lay.kinds + plan_ref[lay.patterns + 2 * t + 1]
    rounds = plan_ref[0]
    index_refs[1][0] = jnp.where(rounds > 2, 0, index_refs[1][0])
    index_refs[2][0] = jnp.where(rounds > 2, rounds, 1)
    for i in range(per_dev):
        take = plan_ref[lay.takes + i]
        far = per_dev + jnp.where((take < 2) | (rounds == 2), take, 2 + i)
        plan_ref[lay.place + i] = jnp.where(take < 0, -1 - take, far)


def first_kernel(
    lay, clone_ref, group_ref, state_ref, kick_ref, forcing_ref, plan_ref, index_ref, second_ref, stop_ref, *refs
):
    fields, sides, strips_ref = refs[:4], refs[4:8], refs[8]
    sources, ends, state_ends, kick_ends, forcing_ends, done = refs[-6:]
    members, variables, levels, height, width = state_ref.shape
    parts = [pltpu.make_async_copy(clone_ref, sources, done.at[0])]
    for side, at in enumerate((0, width - LANES)):
        for ref, part in ((state_ref, state_ends), (kick_ref, kick_ends), (forcing_ref, forcing_ends)):
            piece = ref.at[(slice(None),) * (len(ref.shape) - 1) + (pl.ds(at, LANES),)]
            parts.append(pltpu.make_async_copy(piece, part.at[side], done.at[len(parts)]))
    for copy in parts:
        copy.start()
    parts[0].wait()
    plan_lines(lay, sources, group_ref, plan_ref, (index_ref, second_ref, stop_ref), ends)
    sent = [plan_ref[lay.sends + n] for n in range(4)]
    whole = [
        pltpu.make_async_copy(state_ref.at[j], ref, done.at[len(parts) + n])
        for n, (j, ref) in enumerate(zip(sent, fields))
    ]
    wanted = [plan_ref[lay.patterns + n] > 0 for n in range(4)]
    for copy, want in zip(whole, wanted):
        pl.when(want)(copy.start)
    for copy in parts[1:]:
        copy.wait()
    lane = lane_index((height, LANES))

    @pl.loop(0, levels)
    def _(k):
        for slot in range(2 * members + 1):
            strip = jnp.zeros((height, LANES), jnp.float32)
            for v in range(variables):
                if slot < members:
                    low, high = (state_ends[side, slot, v, k] for side in range(2))
                elif slot < 2 * members:
                    low, high = (kick_ends[side, slot - members, v, k] for side in range(2))
                else:
                    low, high = (forcing_ends[side, v, k] for side in range(2))
                both = turn(jnp.where(lane < HALO, low, high), HALO + 2 * HALO * v)
                strip = jnp.where(lane >= 2 * HALO * v, both, strip)
            strips_ref[slot, k] = strip

    for ref, j in zip(sides, sent):
        ref[...] = strips_ref[j]
    for copy, want in zip(whole, wanted):
        pl.when(want)(copy.wait)


def spec(space):
    return pl.BlockSpec(memory_space=space)


def first(lay, group, clone_src, state, kick, forcing):
    members, variables, levels, height, width = state.shape
    shape = jax.ShapeDtypeStruct
    one = pltpu.VMEM(state.shape[1:], jnp.float32)
    side = pltpu.VMEM((levels, height, LANES), jnp.float32)
    strips = pltpu.VMEM((2 * members + 1, levels, height, LANES), jnp.float32)
    ends = (2, members, variables, levels, height, LANES)
    scalar, here, far = spec(pltpu.SMEM), spec(pltpu.VMEM), spec(pltpu.HBM)
    return pl.pallas_call(
        functools.partial(first_kernel, lay),
        in_specs=[far, scalar, far, far, far],
        out_specs=[scalar] * 4 + [here] * 9,
        out_shape=[shape((lay.size,), jnp.int32)] + [shape((1,), jnp.int32)] * 3 + [one] * 4 + [side] * 4 + [strips],
        scratch_shapes=[
            pltpu.SMEM(clone_src.shape, jnp.int32),
            pltpu.SMEM((lay.most,), jnp.int32),
            pltpu.VMEM(ends, jnp.float32),
            pltpu.VMEM(ends, jnp.float32),
            pltpu.VMEM((2, *ends[2:]), jnp.float32),
            pltpu.SemaphoreType.DMA((11,)),
        ],
        compiler_params=pltpu.CompilerParams(vmem_limit_bytes=VMEM),
    )(far_away(clone_src), group[None], far_away(state), far_away(kick), far_away(forcing))


def far_away(x):
    return pltpu.with_memory_space_constraint(x, pltpu.HBM)


def edge_shape(members, forcing):
    variables, levels, height, width = forcing.shape
    return pltpu.VMEM((members, levels, variables * width // LANES + 1, HALO, LANES), jnp.float32)


def pack_kernel(
    lay, plan_ref, state_ref, up_ref, down_ref, second_up_ref, second_down_ref, kick_ref, forcing_ref,
    sides_ref, up_side_ref, down_side_ref, second_up_side_ref, second_down_side_ref,
    start_ref, side_ref, top_ref, bottom_ref,
):
    members, variables, levels, height, width = state_ref.shape
    tiles = width // LANES

    def edges(slot, k, v, rows):
        for t in range(tiles):
            part = rows[:, LANES * t : LANES * (t + 1)]
            top_ref[slot, k, v * tiles + t] = part[:HALO]
            bottom_ref[slot, k, v * tiles + t] = part[height - HALO :]

    def flank(slot, k, strip):
        side_ref[slot, k] = strip
        top_ref[slot, k, variables * tiles] = strip[:HALO]
        bottom_ref[slot, k, variables * tiles] = strip[height - HALO :]

    @pl.loop(0, levels)
    def _(k):
        flank(members, k, sides_ref[2 * members, k])

        @pl.loop(0, variables)
        def _(v):
            edges(members, k, v, forcing_ref[v, k])

    whole = [state_ref.at[j] for j in range(members)] + [up_ref, down_ref, second_up_ref, second_down_ref]
    parts = [sides_ref.at[j] for j in range(members)]
    parts += [up_side_ref, down_side_ref, second_up_side_ref, second_down_side_ref]
    for i in range(members):

        def fill(option, strip):
            @pl.loop(0, levels)
            def _(k):
                flank(i, k, strip[k] + sides_ref[members + i, k])

                @pl.loop(0, variables)
                def _(v):
                    rows = option[v, k] + kick_ref[i, v, k]
                    start_ref[i, v, k] = rows
                    edges(i, k, v, rows)

        for at, (option, strip) in enumerate(zip(whole, parts)):
            pl.when(plan_ref[lay.place + i] == at)(functools.partial(fill, option, strip))


def pack(lay, plan, state, fields, kick, forcing, sides, far_sides):
    members, variables, levels, height, width = state.shape
    here = spec(pltpu.VMEM)
    return pl.pallas_call(
        functools.partial(pack_kernel, lay),
        in_specs=[spec(pltpu.SMEM)] + [here] * 12,
        out_specs=[here] * 4,
        out_shape=[
            pltpu.VMEM(state.shape, jnp.float32),
            pltpu.VMEM((members + 1, levels, height, LANES), jnp.float32),
            edge_shape(members + 1, forcing),
            edge_shape(members + 1, forcing),
        ],
        compiler_params=pltpu.CompilerParams(vmem_limit_bytes=VMEM),
    )(plan, state, *fields, kick, forcing, sides, *far_sides)


def neighbours(top, bottom):
    lats = lax.axis_size("lat")
    above = lax.ppermute(bottom, "lat", [(i, i + 1) for i in range(lats - 1)])
    below = lax.ppermute(top, "lat", [(i + 1, i) for i in range(lats - 1)])
    return above, below


def beside(strips):
    assert lax.axis_size("lon") == 2
    return lax.ppermute(strips, "lon", [(0, 1), (1, 0)])


def send(lay, kinds, fields, sides):
    groups, lons = lay.groups, lax.axis_size("lon")
    fields, sides = list(fields), list(sides)
    for down, kind in enumerate(kinds):
        if kind:
            pairs = chain(kind - 1, groups)
            if down:
                pairs = [(groups - 1 - a, groups - 1 - b) for a, b in pairs]
            crossed = [(a * lons + j, b * lons + 1 - j) for a, b in pairs for j in range(lons)]
            fields[down] = lax.ppermute(fields[down], "member", pairs)
            sides[down] = lax.ppermute(sides[down], ("member", "lon"), crossed)
    return (*fields, *sides)


def prepared(state, kick, forcing, clone_src):
    per_dev, groups, group = state.shape[0], lax.axis_size("member"), lax.axis_index("member")
    lay = Layout(groups, per_dev)
    if groups != 4:
        piece = lax.all_gather(state, "member", axis=0, tiled=True)
        sources = lax.dynamic_slice_in_dim(clone_src, group * per_dev, per_dev)
        state = jnp.take(piece, sources, axis=0, mode="clip")
        lay = Layout(3, per_dev)
        still = jnp.arange(per_dev * 3, dtype=jnp.int32)
        plan, _, _, _, *out, strips = first(lay, jnp.int32(0), still, state, kick, forcing)
        got, second = (*out[:2], *out[4:6]), (*out[2:4], *out[6:])
        sides = beside(strips)
    else:
        plan, index, following, stop, *out, strips = first(lay, group, clone_src, state, kick, forcing)
        out, second = (*out[:2], *out[4:6]), (*out[2:4], *out[6:])
        kinds = [(a, b) for a in range(lay.kinds) for b in range(lay.kinds)]

        def opening(kind):
            return lambda a, b, c, d, strips: (*send(lay, kind, (a, b), (c, d)), beside(strips))

        ways = [lambda a, b, c, d, kind=kind: send(lay, kind, (a, b), (c, d)) for kind in kinds]

        def later(t, held):
            takes = plan[lay.takes : lay.place]
            sent = [lax.dynamic_index_in_dim(plan, lay.sends + 2 * t + n, keepdims=False) for n in range(2)]
            wanted = [lax.dynamic_index_in_dim(plan, lay.patterns + 2 * t + n, keepdims=False) for n in range(2)]
            out = [lax.dynamic_index_in_dim(x, j, keepdims=False) for x in (state, strips) for j in sent]
            got = lax.switch(wanted[0] * lay.kinds + wanted[1], ways, *out)
            kept = []
            for x in range(2):
                for i in range(per_dev):
                    up, down = takes[i] == 2 * t, takes[i] == 2 * t + 1
                    new = jnp.where(up, got[2 * x], got[2 * x + 1])
                    kept.append(jnp.where(up | down, new, held[2 * x + i]))
            return tuple(kept)

        *got, sides = lax.switch(index[0], [opening(kind) for kind in kinds], *out, strips)
        second = lax.switch(following[0], ways, *second)
        second = lax.fori_loop(1, stop[0], later, second)

    assert per_dev == 2
    return pack(lay, plan, state, (*got[:2], *second[:2]), kick, forcing, sides, (*got[2:], *second[2:]))


def cut(rows, strip, v):
    width = rows.shape[1]
    count = -(-width // SPAN)
    lane = lane_index((rows.shape[0], LANES))
    source = [rows[:, LANES * t : LANES * (t + 1)] for t in range(width // LANES)]
    tiles = []
    for c in range(count):
        first = SPAN * c - HALO
        if c == 0:
            tile = jnp.where(lane < HALO, turn(strip, -2 * HALO * v), turn(source[0], HALO))
        else:
            t, offset = first // LANES, first % LANES
            if t + 1 < len(source):
                later = turn(source[t + 1], -offset)
            else:
                later = turn(strip, LANES - offset - 2 * HALO * v - HALO)
            tile = jnp.where(lane < LANES - offset, turn(source[t], -offset), later)
        tiles.append(tile)
    return tiles


def step_kernel(
    start_ref, above_ref, below_ref, side_ref, forcing_ref, coupling_ref, place_ref, out_ref,
    cells, other, source, result, table, stage, done,
):
    members, variables, levels, height, width = start_ref.shape
    count = -(-width // SPAN)
    tall = height + 2 * HALO
    at_top = place_ref[0] == 0
    at_bottom = place_ref[0] == place_ref[1] - 1

    def edge(ref, slot, k, v):
        tiles = width // LANES
        rows = [ref[slot, k, v * tiles + t] for t in range(tiles)]
        return jnp.concatenate(rows, axis=1), ref[slot, k, variables * tiles]

    def lay(rows, strip, v, target, at, scale):
        for c, tile in enumerate(cut(rows, strip, v)):
            target[c, v, at : at + rows.shape[0]] = tile if scale is None else tile * scale

    blocks = tall // ROWS
    line = lax.broadcasted_iota(jnp.int32, (ROWS, LANES), 0)

    def advance_tile(now, later, c, last):
        tiles, turned = {}, {}

        def tile(v, r):
            if (v, r) not in tiles:
                tiles[v, r] = now[c, v, ROWS * r : ROWS * (r + 1)]
            return tiles[v, r]

        def rolled(v, r, d):
            if (v, r, d) not in turned:
                turned[v, r, d] = pltpu.roll(tile(v, r), -d % ROWS, 0)
            return turned[v, r, d]

        def shifted(v, r, d):
            own = rolled(v, r, d)
            if d > 0:
                return own if r + 1 == blocks else jnp.where(line < ROWS - d, own, rolled(v, r + 1, d))
            return own if r == 0 else jnp.where(line >= -d, own, rolled(v, r - 1, d))

        for r in range(1, blocks - 1) if last else range(blocks):
            centre = [tile(v, r) for v in range(variables)]
            ku, kv = K * centre[0], K * centre[1]
            eu, ev = 8.0 * ku, 8.0 * kv
            along = 16.0 * K - eu, 16.0 * K + eu, ku - K, -K - ku
            across = 16.0 * K - ev, 16.0 * K + ev, kv - K, -K - kv
            for v in range(variables):
                q = centre[v]
                total = source[c, v, ROWS * r : ROWS * (r + 1)]
                for w in range(variables):
                    total += table[v * variables + w] * centre[w]
                near = along[0] * turn(q, -1) + along[1] * turn(q, 1)
                far = along[2] * turn(q, -2) + along[3] * turn(q, 2)
                near += across[0] * shifted(v, r, 1) + across[1] * shifted(v, r, -1)
                far += across[2] * shifted(v, r, 2) + across[3] * shifted(v, r, -2)
                total += near + far
                if last:
                    result[c, v, ROWS * (r - 1) : ROWS * r] = total
                elif r in (0, blocks - 1):
                    later[c, v, ROWS * r : ROWS * (r + 1)] = jnp.where(at_top if r == 0 else at_bottom, 0.0, total)
                else:
                    later[c, v, ROWS * r : ROWS * (r + 1)] = total

    @pl.loop(0, levels * members)
    def _(job):
        k, m = job // members, job % members

        for v in range(variables):
            lay(*edge(above_ref, m, k, v), v, cells, 0, None)
            lay(start_ref[m, v, k], side_ref[m, k], v, cells, HALO, None)
            lay(*edge(below_ref, m, k, v), v, cells, HALO + height, None)

        @pl.when(m == 0)
        def _():
            for v in range(variables):
                lay(*edge(above_ref, members, k, v), v, source, 0, 0.1)
                lay(forcing_ref[v, k], side_ref[members, k], v, source, HALO, 0.1)
                lay(*edge(below_ref, members, k, v), v, source, HALO + height, 0.1)
                for w in range(variables):
                    weight = 0.25 * coupling_ref[(k * variables + v) * variables + w]
                    weight = weight + (1.0 - 60.0 * K if v == w else 0.0)
                    table[v * variables + w] = jnp.full((ROWS, LANES), weight, jnp.float32)

        @pl.loop(0, count)
        def _(c):
            for step in range(STEPS):
                now, later = (cells, other) if step % 2 == 0 else (other, cells)
                advance_tile(now, later, c, step == STEPS - 1)

        slot = job % 2
        copy = pltpu.make_async_copy(stage.at[slot], out_ref.at[m, :, k], done.at[slot])
        pl.when(job >= 2)(copy.wait)
        lane = lane_index((height, LANES))
        for v in range(variables):
            for t in range(width // LANES):
                c, offset = LANES * t // SPAN, LANES * t % SPAN
                left = turn(result[c, v], -(offset + HALO))
                if c + 1 < count:
                    right = turn(result[c + 1, v], SPAN - offset - HALO)
                    left = jnp.where(lane < SPAN - offset, left, right)
                stage[slot, v, :, LANES * t : LANES * (t + 1)] = left
        copy.start()

    for slot in range(2):
        pltpu.make_async_copy(stage.at[slot], out_ref.at[0, :, 0], done.at[slot]).wait()


def advance(start, above, below, side, forcing, coupling):
    members, variables, levels, height, width = start.shape
    assert levels * members >= 2 and height % ROWS == 0 and HALO == ROWS
    count = -(-width // SPAN)
    tall = height + 2 * HALO
    place = jnp.stack([lax.axis_index("lat"), jnp.int32(lax.axis_size("lat"))])
    here, scalars = spec(pltpu.VMEM), spec(pltpu.SMEM)
    return pl.pallas_call(
        step_kernel,
        in_specs=[here] * 5 + [scalars] * 2,
        out_specs=spec(pltpu.HBM),
        out_shape=jax.ShapeDtypeStruct(start.shape, jnp.float32),
        scratch_shapes=[
            pltpu.VMEM((count, variables, tall, LANES), jnp.float32),
            pltpu.VMEM((count, variables, tall, LANES), jnp.float32),
            pltpu.VMEM((count, variables, tall, LANES), jnp.float32),
            pltpu.VMEM((count, variables, height, LANES), jnp.float32),
            pltpu.VMEM((variables * variables, ROWS, LANES), jnp.float32),
            pltpu.VMEM((2, variables, height, width), jnp.float32),
            pltpu.SemaphoreType.DMA((2,)),
        ],
        compiler_params=pltpu.CompilerParams(vmem_limit_bytes=VMEM),
    )(start, above, below, side, forcing, coupling.reshape(-1), place)


def shards(state, kick, forcing, coupling, clone_src):
    start, side, top, bottom = prepared(state, kick, forcing, clone_src)
    above, below = neighbours(top, bottom)
    return advance(start, above, below, side, forcing, coupling)


def solution(mesh):
    in_specs = (
        P("member", None, None, "lat", "lon"),
        P("member", None, None, "lat", "lon"),
        P(None, None, "lat", "lon"),
        P(),
        P(),
    )
    out_specs = P("member", None, None, "lat", "lon")
    return jax.shard_map(shards, mesh=mesh, in_specs=in_specs, out_specs=out_specs, check_vma=False)
```

```python
import functools

import functools

import jax
import jax.numpy as jnp
from jax import lax
from jax.experimental import pallas as pl
from jax.experimental.pallas import tpu as pltpu
from jax.sharding import PartitionSpec as P

STEPS = 4
REACH = 2
HALO = STEPS * REACH
LANES = 128
ROWS = 8
SPAN = LANES - 2 * HALO
K = 0.05 / 12.0
VMEM = 10 * 1024 * 1024


def lane_index(shape):
    return lax.broadcasted_iota(jnp.int32, shape, len(shape) - 1)


def turn(x, shift):
    shift = shift % LANES
    return x if shift == 0 else pltpu.roll(x, shift, x.ndim - 1)


def chain(bits, groups):
    stops = [0] + [x for x in range(1, groups - 1) if bits >> (x - 1) & 1] + [groups - 1]
    return list(zip(stops[:-1], stops[1:]))


class Layout:
    def __init__(self, groups, per_dev):
        self.groups, self.per_dev = groups, per_dev
        self.most = per_dev * (groups - 1)
        self.patterns, self.sends = 1, 1 + 2 * self.most
        self.takes = self.sends + 2 * self.most
        self.place = self.takes + per_dev
        self.size = self.place + per_dev
        self.kinds = 1 + (1 << (groups - 2))


def plan_lines(lay, clone_ref, group_ref, plan_ref, index_refs, ends):
    groups, per_dev, most = lay.groups, lay.per_dev, lay.most
    me = group_ref[0]
    plan_ref[0] = 1
    for t in range(2 * most):
        plan_ref[lay.patterns + t] = 0
        plan_ref[lay.sends + t] = 0
    for i in range(per_dev):
        plan_ref[lay.takes + i] = -1 - clone_ref[me * per_dev + i] % per_dev

    for down in range(2):
        for t in range(most):
            ends[t] = 0
        for a in range(groups - 1):
            for b in range(a + 1, groups):
                source, target = (groups - 1 - a, groups - 1 - b) if down else (a, b)
                spans = sum(1 << (x - 1) for x in range(a + 1, b))
                for j in range(per_dev):
                    member = source * per_dev + j
                    wanted = [clone_ref[target * per_dev + i] == member for i in range(per_dev)]
                    need = functools.reduce(jnp.logical_or, wanted)

                    @pl.when(need)
                    def _():
                        t = jnp.int32(most - 1)
                        for earlier in reversed(range(most - 1)):
                            t = jnp.where(ends[earlier] <= a, earlier, t)
                        ends[t] = b
                        plan_ref[0] = jnp.maximum(plan_ref[0], t + 1)
                        at = 2 * t + down
                        before = plan_ref[lay.patterns + at]
                        bits = jnp.where(before == 0, lay.kinds - 2, before - 1)
                        plan_ref[lay.patterns + at] = 1 + (bits & ~spans)

                        @pl.when(me == source)
                        def _():
                            plan_ref[lay.sends + at] = j

                        for i in range(per_dev):

                            @pl.when((me == target) & wanted[i])
                            def _():
                                plan_ref[lay.takes + i] = at

    for t in range(2):
        index_refs[t][0] = plan_ref[lay.patterns + 2 * t] * lay.kinds + plan_ref[lay.patterns + 2 * t + 1]
    rounds = plan_ref[0]
    index_refs[1][0] = jnp.where(rounds > 2, lay.kinds * lay.kinds, index_refs[1][0])
    for i in range(per_dev):
        take = plan_ref[lay.takes + i]
        far = per_dev + jnp.where((take < 2) | (rounds == 2), take, 2 + i)
        plan_ref[lay.place + i] = jnp.where(take < 0, -1 - take, far)


def first_kernel(
    lay, clone_ref, group_ref, state_ref, kick_ref, forcing_ref, plan_ref, index_ref, second_ref, *refs
):
    fields, sides, strips_ref = refs[:4], refs[4:8], refs[8]
    sources, ends, state_ends, kick_ends, forcing_ends, passing, done = refs[-7:]
    members, variables, levels, height, width = state_ref.shape
    parts = [pltpu.make_async_copy(clone_ref, sources, done.at[0])]
    for side, at in enumerate((0, width - LANES)):
        for ref, part in ((state_ref, state_ends), (kick_ref, kick_ends), (forcing_ref, forcing_ends)):
            piece = ref.at[(slice(None),) * (len(ref.shape) - 1) + (pl.ds(at, LANES),)]
            parts.append(pltpu.make_async_copy(piece, part.at[side], done.at[len(parts)]))
    for copy in parts:
        copy.start()
    parts[0].wait()
    plan_lines(lay, sources, group_ref, plan_ref, (index_ref, second_ref), ends)
    sent = [plan_ref[lay.sends + n] for n in range(4)]
    whole = [
        pltpu.make_async_copy(state_ref.at[j], ref, done.at[len(parts) + n])
        for n, (j, ref) in enumerate(zip(sent, (*fields[:2], passing.at[0], passing.at[1])))
    ]
    onward = [pltpu.make_async_copy(passing.at[n], fields[2 + n], done.at[len(parts) + 4 + n]) for n in range(2)]
    wanted = [plan_ref[lay.patterns + n] > 0 for n in range(4)]
    for copy, want in zip(whole, wanted):
        pl.when(want)(copy.start)
    for copy in parts[1:]:
        copy.wait()
    lane = lane_index((height, LANES))

    @pl.loop(0, levels)
    def _(k):
        for slot in range(2 * members + 1):
            strip = jnp.zeros((height, LANES), jnp.float32)
            for v in range(variables):
                if slot < members:
                    low, high = (state_ends[side, slot, v, k] for side in range(2))
                elif slot < 2 * members:
                    low, high = (kick_ends[side, slot - members, v, k] for side in range(2))
                else:
                    low, high = (forcing_ends[side, v, k] for side in range(2))
                both = turn(jnp.where(lane < HALO, low, high), HALO + 2 * HALO * v)
                strip = jnp.where(lane >= 2 * HALO * v, both, strip)
            strips_ref[slot, k] = strip

    for ref, j in zip(sides, sent):
        ref[...] = strips_ref[j]
    for copy, want in zip(whole, wanted):
        pl.when(want)(copy.wait)
    for copy, want in zip(onward, wanted[2:]):
        pl.when(want)(copy.start)
    for copy, want in zip(onward, wanted[2:]):
        pl.when(want)(copy.wait)


def spec(space):
    return pl.BlockSpec(memory_space=space)


def first(lay, group, clone_src, state, kick, forcing):
    members, variables, levels, height, width = state.shape
    shape = jax.ShapeDtypeStruct
    one = pltpu.VMEM(state.shape[1:], jnp.float32)
    side = pltpu.VMEM((levels, height, LANES), jnp.float32)
    strips = pltpu.VMEM((2 * members + 1, levels, height, LANES), jnp.float32)
    ends = (2, members, variables, levels, height, LANES)
    scalar, here, far = spec(pltpu.SMEM), spec(pltpu.VMEM), spec(pltpu.HBM)
    return pl.pallas_call(
        functools.partial(first_kernel, lay),
        in_specs=[far, scalar, far, far, far],
        out_specs=[scalar] * 3 + [here] * 2 + [spec(pl.ANY)] * 2 + [here] * 5,
        out_shape=[shape((lay.size,), jnp.int32)] + [shape((1,), jnp.int32)] * 2 + [one] * 2 + [pltpu.HBM(state.shape[1:], jnp.float32)] * 2 + [side] * 4 + [strips],
        scratch_shapes=[
            pltpu.SMEM(clone_src.shape, jnp.int32),
            pltpu.SMEM((lay.most,), jnp.int32),
            pltpu.VMEM(ends, jnp.float32),
            pltpu.VMEM(ends, jnp.float32),
            pltpu.VMEM((2, *ends[2:]), jnp.float32),
            pltpu.VMEM(state.shape, jnp.float32),
            pltpu.SemaphoreType.DMA((13,)),
        ],
        compiler_params=pltpu.CompilerParams(vmem_limit_bytes=VMEM),
    )(far_away(clone_src), group[None], far_away(state), far_away(kick), far_away(forcing))


def far_away(x):
    return pltpu.with_memory_space_constraint(x, pltpu.HBM)


def edge_shape(members, forcing):
    variables, levels, height, width = forcing.shape
    return jax.ShapeDtypeStruct((members, levels, variables * width // LANES + 1, HALO, LANES), jnp.float32)


def options_of(state_ref, refs):
    return [state_ref.at[j] for j in range(state_ref.shape[0])] + list(refs)


def pack_kernel(
    lay, plan_ref, state_ref, up_ref, down_ref, second_up_ref, second_down_ref, kick_ref, forcing_ref,
    sides_ref, up_side_ref, down_side_ref, second_up_side_ref, second_down_side_ref,
    side_ref, top_ref, bottom_ref, field_rows, kick_rows, forcing_rows, done,
):
    members, variables, levels, height, width = state_ref.shape
    tiles = width // LANES
    whole = options_of(state_ref, (up_ref, down_ref, second_up_ref, second_down_ref))
    parts = options_of(sides_ref.at[:members], (up_side_ref, down_side_ref, second_up_side_ref, second_down_side_ref))
    places = [plan_ref[lay.place + i] for i in range(members)]
    rows = [pl.ds(0, HALO), pl.ds(height - HALO, HALO)]
    f_copies = [pltpu.make_async_copy(forcing_ref.at[:, :, rows[n]], forcing_rows.at[n], done.at[0]) for n in range(2)]
    copies = []
    for i in range(members):
        for n in range(2):
            for at, option in enumerate(whole):

                @pl.when(places[i] == at)
                def _():
                    pltpu.make_async_copy(option.at[:, :, rows[n]], field_rows.at[i, n], done.at[1 + i]).start()

            copies.append(pltpu.make_async_copy(kick_ref.at[i, :, :, rows[n]], kick_rows.at[i, n], done.at[1 + i]))
    for copy in copies + f_copies:
        copy.start()

    def flank(slot, k, strip):
        side_ref[slot, k] = strip
        top_ref[slot, k, variables * tiles] = strip[:HALO]
        bottom_ref[slot, k, variables * tiles] = strip[height - HALO :]

    def edges(slot, rows_of):
        @pl.loop(0, levels)
        def _(k):
            for n, ref in enumerate((top_ref, bottom_ref)):
                for v in range(variables):
                    edge = rows_of(n, v, k)
                    for t in range(tiles):
                        ref[slot, k, v * tiles + t] = edge[:, LANES * t : LANES * (t + 1)]

    for k in range(levels):
        flank(members, k, sides_ref[2 * members, k])
        for i in range(members):
            strip = parts[-1][k]
            for at in reversed(range(len(parts) - 1)):
                strip = jnp.where(places[i] == at, parts[at][k], strip)
            flank(i, k, strip + sides_ref[members + i, k])
    for copy in f_copies:
        copy.wait()
    edges(members, lambda n, v, k: forcing_rows[n, v, k])
    for i in range(members):
        for n in range(2):
            pltpu.make_async_copy(kick_ref.at[i, :, :, rows[n]], field_rows.at[i, n], done.at[1 + i]).wait()
            copies[2 * i + n].wait()
        edges(i, lambda n, v, k: field_rows[i, n, v, k] + kick_rows[i, n, v, k])


def pack(lay, plan, state, fields, kick, forcing, sides, far_sides):
    members, variables, levels, height, width = state.shape
    here, anywhere = spec(pltpu.VMEM), spec(pl.ANY)
    rows = (members, 2, variables, levels, HALO, width)
    return pl.pallas_call(
        functools.partial(pack_kernel, lay),
        in_specs=[spec(pltpu.SMEM)] + [anywhere] * 7 + [here] * 5,
        out_specs=[here] * 3,
        out_shape=[
            jax.ShapeDtypeStruct((members + 1, levels, height, LANES), jnp.float32),
            edge_shape(members + 1, forcing),
            edge_shape(members + 1, forcing),
        ],
        scratch_shapes=[
            pltpu.VMEM(rows, jnp.float32),
            pltpu.VMEM(rows, jnp.float32),
            pltpu.VMEM(rows[1:], jnp.float32),
            pltpu.SemaphoreType.DMA((1 + members,)),
        ],
        compiler_params=pltpu.CompilerParams(vmem_limit_bytes=VMEM),
    )(plan, far_away(state), *fields, far_away(kick), far_away(forcing), sides, *far_sides)


def blank(*like):
    return pl.pallas_call(
        lambda *refs: None,
        out_specs=[spec(pl.ANY)] * len(like),
        out_shape=[jax.ShapeDtypeStruct(x.shape, x.dtype) for x in like],
        compiler_params=pltpu.CompilerParams(vmem_limit_bytes=1024 * 1024),
    )()


def neighbours(top, bottom):
    lats = lax.axis_size("lat")
    above = lax.ppermute(bottom, "lat", [(i, i + 1) for i in range(lats - 1)])
    below = lax.ppermute(top, "lat", [(i + 1, i) for i in range(lats - 1)])
    return above, below


def beside(strips):
    assert lax.axis_size("lon") == 2
    return lax.ppermute(strips, "lon", [(0, 1), (1, 0)])


def send(lay, kinds, fields, sides):
    groups, lons = lay.groups, lax.axis_size("lon")
    fields, sides = list(fields), list(sides)
    for down, kind in enumerate(kinds):
        if kind:
            pairs = chain(kind - 1, groups)
            if down:
                pairs = [(groups - 1 - a, groups - 1 - b) for a, b in pairs]
            crossed = [(a * lons + j, b * lons + 1 - j) for a, b in pairs for j in range(lons)]
            fields[down] = lax.ppermute(fields[down], "member", pairs)
            sides[down] = lax.ppermute(sides[down], ("member", "lon"), crossed)
        else:
            fields[down], sides[down] = blank(fields[down], sides[down])
    return (*fields, *sides)


def prepared(state, kick, forcing, clone_src):
    per_dev, groups, group = state.shape[0], lax.axis_size("member"), lax.axis_index("member")
    lay = Layout(groups, per_dev)
    if groups != 4:
        piece = lax.all_gather(state, "member", axis=0, tiled=True)
        sources = lax.dynamic_slice_in_dim(clone_src, group * per_dev, per_dev)
        state = jnp.take(piece, sources, axis=0, mode="clip")
        lay = Layout(3, per_dev)
        still = jnp.arange(per_dev * 3, dtype=jnp.int32)
        plan, _, _, *out, strips = first(lay, jnp.int32(0), still, state, kick, forcing)
        got, second = (*out[:2], *out[4:6]), (*out[2:4], *out[6:])
        sides = beside(strips)
    else:
        plan, index, following, *out, strips = first(lay, group, clone_src, state, kick, forcing)
        out, second = (*out[:2], *out[4:6]), (*out[2:4], *out[6:])
        kinds = [(a, b) for a in range(lay.kinds) for b in range(lay.kinds)]

        def opening(kind):
            return lambda a, b, c, d, strips: (*send(lay, kind, (a, b), (c, d)), beside(strips))

        ways = [lambda a, b, c, d, kind=kind: send(lay, kind, (a, b), (c, d)) for kind in kinds]

        def later(t, held):
            takes = plan[lay.takes : lay.place]
            sent = [lax.dynamic_index_in_dim(plan, lay.sends + 2 * t + n, keepdims=False) for n in range(2)]
            wanted = [lax.dynamic_index_in_dim(plan, lay.patterns + 2 * t + n, keepdims=False) for n in range(2)]
            out = [lax.dynamic_index_in_dim(x, j, keepdims=False) for x in (state, strips) for j in sent]
            got = lax.switch(wanted[0] * lay.kinds + wanted[1], ways, *out)
            kept = []
            for x in range(2):
                for i in range(per_dev):
                    up, down = takes[i] == 2 * t, takes[i] == 2 * t + 1
                    new = jnp.where(up, got[2 * x], got[2 * x + 1])
                    kept.append(jnp.where(up | down, new, held[2 * x + i]))
            return tuple(kept)

        *got, sides = lax.switch(index[0], [opening(kind) for kind in kinds], *out, strips)
        several = lambda *held: lax.fori_loop(1, plan[0], later, held)
        second = lax.switch(following[0], ways + [several], *second)

    assert per_dev == 2
    fields = (*got[:2], *second[:2])
    side, top, bottom = pack(lay, plan, state, fields, kick, forcing, sides, (*got[2:], *second[2:]))
    return plan[lay.place :], (state, *fields), side, top, bottom


def cut(rows, strip, v):
    width = rows.shape[1]
    count = -(-width // SPAN)
    lane = lane_index((rows.shape[0], LANES))
    source = [rows[:, LANES * t : LANES * (t + 1)] for t in range(width // LANES)]
    tiles = []
    for c in range(count):
        first = SPAN * c - HALO
        if c == 0:
            tile = jnp.where(lane < HALO, turn(strip, -2 * HALO * v), turn(source[0], HALO))
        else:
            t, offset = first // LANES, first % LANES
            if t + 1 < len(source):
                later = turn(source[t + 1], -offset)
            else:
                later = turn(strip, LANES - offset - 2 * HALO * v - HALO)
            tile = jnp.where(lane < LANES - offset, turn(source[t], -offset), later)
        tiles.append(tile)
    return tiles


def step_kernel(
    state_ref, up_ref, down_ref, second_up_ref, second_down_ref, kick_ref, forcing_ref, above_ref, below_ref, side_ref,
    coupling_ref, place_ref, lat_ref, out_ref, cells, other, source, result, table, stage, field, kicks, drive, done,
):
    members, variables, levels, height, width = state_ref.shape
    count = -(-width // SPAN)
    tall = height + 2 * HALO
    at_top = lat_ref[0] == 0
    at_bottom = lat_ref[0] == lat_ref[1] - 1
    options = options_of(state_ref, (up_ref, down_ref, second_up_ref, second_down_ref))

    def fetch(job, wait=False):
        k, m, slot = job // members, job % members, job % 2
        copies = [pltpu.make_async_copy(kick_ref.at[m, :, k], kicks.at[slot], done.at[2, slot])]
        if wait:
            copies.append(pltpu.make_async_copy(kick_ref.at[m, :, k], field.at[slot], done.at[1, slot]))
        else:
            for at, option in enumerate(options):

                @pl.when(place_ref[m] == at)
                def _():
                    pltpu.make_async_copy(option.at[:, k], field.at[slot], done.at[1, slot]).start()

        for copy in copies:
            copy.wait() if wait else copy.start()

        @pl.when(m == 0)
        def _():
            copy = pltpu.make_async_copy(forcing_ref.at[:, k], drive, done.at[3, 0])
            copy.wait() if wait else copy.start()

    def edge(ref, slot, k, v):
        tiles = width // LANES
        rows = [ref[slot, k, v * tiles + t] for t in range(tiles)]
        return jnp.concatenate(rows, axis=1), ref[slot, k, variables * tiles]

    def lay(rows, strip, v, target, at, scale):
        for c, tile in enumerate(cut(rows, strip, v)):
            target[c, v, at : at + rows.shape[0]] = tile if scale is None else tile * scale

    blocks = tall // ROWS
    line = lax.broadcasted_iota(jnp.int32, (ROWS, LANES), 0)

    def advance_tile(now, later, c, last):
        tiles, turned = {}, {}

        def tile(v, r):
            if (v, r) not in tiles:
                tiles[v, r] = now[c, v, ROWS * r : ROWS * (r + 1)]
            return tiles[v, r]

        def rolled(v, r, d):
            if (v, r, d) not in turned:
                turned[v, r, d] = pltpu.roll(tile(v, r), -d % ROWS, 0)
            return turned[v, r, d]

        def shifted(v, r, d):
            own = rolled(v, r, d)
            if d > 0:
                return own if r + 1 == blocks else jnp.where(line < ROWS - d, own, rolled(v, r + 1, d))
            return own if r == 0 else jnp.where(line >= -d, own, rolled(v, r - 1, d))

        for r in range(1, blocks - 1) if last else range(blocks):
            centre = [tile(v, r) for v in range(variables)]
            ku, kv = K * centre[0], K * centre[1]
            eu, ev = 8.0 * ku, 8.0 * kv
            along = 16.0 * K - eu, 16.0 * K + eu, ku - K, -K - ku
            across = 16.0 * K - ev, 16.0 * K + ev, kv - K, -K - kv
            for v in range(variables):
                q = centre[v]
                total = source[c, v, ROWS * r : ROWS * (r + 1)]
                for w in range(variables):
                    total += table[v * variables + w] * centre[w]
                near = along[0] * turn(q, -1) + along[1] * turn(q, 1)
                far = along[2] * turn(q, -2) + along[3] * turn(q, 2)
                near += across[0] * shifted(v, r, 1) + across[1] * shifted(v, r, -1)
                far += across[2] * shifted(v, r, 2) + across[3] * shifted(v, r, -2)
                total += near + far
                if last:
                    result[c, v, ROWS * (r - 1) : ROWS * r] = total
                elif r in (0, blocks - 1):
                    later[c, v, ROWS * r : ROWS * (r + 1)] = jnp.where(at_top if r == 0 else at_bottom, 0.0, total)
                else:
                    later[c, v, ROWS * r : ROWS * (r + 1)] = total

    fetch(0)

    @pl.loop(0, levels * members)
    def _(job):
        k, m, slot = job // members, job % members, job % 2
        fetch(job, wait=True)

        for v in range(variables):
            lay(*edge(above_ref, m, k, v), v, cells, 0, None)
            lay(field[slot, v] + kicks[slot, v], side_ref[m, k], v, cells, HALO, None)
            lay(*edge(below_ref, m, k, v), v, cells, HALO + height, None)

        @pl.when(m == 0)
        def _():
            for v in range(variables):
                lay(*edge(above_ref, members, k, v), v, source, 0, 0.1)
                lay(drive[v], side_ref[members, k], v, source, HALO, 0.1)
                lay(*edge(below_ref, members, k, v), v, source, HALO + height, 0.1)
                for w in range(variables):
                    weight = 0.25 * coupling_ref[(k * variables + v) * variables + w]
                    weight = weight + (1.0 - 60.0 * K if v == w else 0.0)
                    table[v * variables + w] = jnp.full((ROWS, LANES), weight, jnp.float32)

        @pl.when(job + 1 < levels * members)
        def _():
            fetch(job + 1)

        @pl.loop(0, count)
        def _(c):
            for step in range(STEPS):
                now, later = (cells, other) if step % 2 == 0 else (other, cells)
                advance_tile(now, later, c, step == STEPS - 1)

        copy = pltpu.make_async_copy(stage.at[slot], out_ref.at[m, :, k], done.at[0, slot])
        pl.when(job >= 2)(copy.wait)
        lane = lane_index((height, LANES))
        for v in range(variables):
            for t in range(width // LANES):
                c, offset = LANES * t // SPAN, LANES * t % SPAN
                left = turn(result[c, v], -(offset + HALO))
                if c + 1 < count:
                    right = turn(result[c + 1, v], SPAN - offset - HALO)
                    left = jnp.where(lane < SPAN - offset, left, right)
                stage[slot, v, :, LANES * t : LANES * (t + 1)] = left
        copy.start()

    for slot in range(2):
        pltpu.make_async_copy(stage.at[slot], out_ref.at[0, :, 0], done.at[0, slot]).wait()


def advance(place, sources, kick, forcing, above, below, side, coupling):
    members, variables, levels, height, width = kick.shape
    assert levels * members >= 2 and height % ROWS == 0 and HALO == ROWS
    count = -(-width // SPAN)
    tall = height + 2 * HALO
    lat = jnp.stack([lax.axis_index("lat"), jnp.int32(lax.axis_size("lat"))])
    here, scalars, anywhere = spec(pltpu.VMEM), spec(pltpu.SMEM), spec(pl.ANY)
    block = (variables, height, width)
    state, *others = sources
    return pl.pallas_call(
        step_kernel,
        in_specs=[anywhere] * 7 + [here] * 3 + [scalars] * 3,
        out_specs=spec(pltpu.HBM),
        out_shape=jax.ShapeDtypeStruct(kick.shape, jnp.float32),
        scratch_shapes=[
            pltpu.VMEM((count, variables, tall, LANES), jnp.float32),
            pltpu.VMEM((count, variables, tall, LANES), jnp.float32),
            pltpu.VMEM((count, variables, tall, LANES), jnp.float32),
            pltpu.VMEM((count, variables, height, LANES), jnp.float32),
            pltpu.VMEM((variables * variables, ROWS, LANES), jnp.float32),
            pltpu.VMEM((2, *block), jnp.float32),
            pltpu.VMEM((2, *block), jnp.float32),
            pltpu.VMEM((2, *block), jnp.float32),
            pltpu.VMEM(block, jnp.float32),
            pltpu.SemaphoreType.DMA((4, 2)),
        ],
        compiler_params=pltpu.CompilerParams(vmem_limit_bytes=VMEM),
    )(
        far_away(state), *others, far_away(kick), far_away(forcing), above, below, side, coupling.reshape(-1), place, lat
    )


def shards(state, kick, forcing, coupling, clone_src):
    place, sources, side, top, bottom = prepared(state, kick, forcing, clone_src)
    above, below = neighbours(top, bottom)
    return advance(place, sources, kick, forcing, above, below, side, coupling)


def solution(mesh):
    in_specs = (
        P("member", None, None, "lat", "lon"),
        P("member", None, None, "lat", "lon"),
        P(None, None, "lat", "lon"),
        P(),
        P(),
    )
    out_specs = P("member", None, None, "lat", "lon")
    return jax.shard_map(shards, mesh=mesh, in_specs=in_specs, out_specs=out_specs, check_vma=False)
```

```python
import functools

import functools

import jax
import jax.numpy as jnp
from jax import lax
from jax.experimental import pallas as pl
from jax.experimental.pallas import tpu as pltpu
from jax.sharding import PartitionSpec as P

STEPS = 4
REACH = 2
HALO = STEPS * REACH
LANES = 128
ROWS = 8
SPAN = LANES - 2 * HALO
K = 0.05 / 12.0
VMEM = 10 * 1024 * 1024


def lane_index(shape):
    return lax.broadcasted_iota(jnp.int32, shape, len(shape) - 1)


def turn(x, shift):
    shift = shift % LANES
    return x if shift == 0 else pltpu.roll(x, shift, x.ndim - 1)


def chain(bits, groups):
    stops = [0] + [x for x in range(1, groups - 1) if bits >> (x - 1) & 1] + [groups - 1]
    return list(zip(stops[:-1], stops[1:]))


class Layout:
    def __init__(self, groups, per_dev):
        self.groups, self.per_dev = groups, per_dev
        self.most = per_dev * (groups - 1)
        self.patterns, self.sends = 1, 1 + 2 * self.most
        self.takes = self.sends + 2 * self.most
        self.place = self.takes + per_dev
        self.size = self.place + per_dev
        self.kinds = 1 + (1 << (groups - 2))


def plan_lines(lay, clone_ref, group_ref, plan_ref, index_refs, ends):
    groups, per_dev, most = lay.groups, lay.per_dev, lay.most
    me = group_ref[0]
    plan_ref[0] = 1
    for t in range(2 * most):
        plan_ref[lay.patterns + t] = 0
        plan_ref[lay.sends + t] = 0
    for i in range(per_dev):
        plan_ref[lay.takes + i] = -1 - clone_ref[me * per_dev + i] % per_dev

    for down in range(2):
        for t in range(most):
            ends[t] = 0
        for a in range(groups - 1):
            for b in range(a + 1, groups):
                source, target = (groups - 1 - a, groups - 1 - b) if down else (a, b)
                spans = sum(1 << (x - 1) for x in range(a + 1, b))
                for j in range(per_dev):
                    member = source * per_dev + j
                    wanted = [clone_ref[target * per_dev + i] == member for i in range(per_dev)]
                    need = functools.reduce(jnp.logical_or, wanted)

                    @pl.when(need)
                    def _():
                        t = jnp.int32(most - 1)
                        for earlier in reversed(range(most - 1)):
                            t = jnp.where(ends[earlier] <= a, earlier, t)
                        ends[t] = b
                        plan_ref[0] = jnp.maximum(plan_ref[0], t + 1)
                        at = 2 * t + down
                        before = plan_ref[lay.patterns + at]
                        bits = jnp.where(before == 0, lay.kinds - 2, before - 1)
                        plan_ref[lay.patterns + at] = 1 + (bits & ~spans)

                        @pl.when(me == source)
                        def _():
                            plan_ref[lay.sends + at] = j

                        for i in range(per_dev):

                            @pl.when((me == target) & wanted[i])
                            def _():
                                plan_ref[lay.takes + i] = at

    for t in range(2):
        index_refs[t][0] = plan_ref[lay.patterns + 2 * t] * lay.kinds + plan_ref[lay.patterns + 2 * t + 1]
    rounds = plan_ref[0]
    index_refs[1][0] = jnp.where(rounds > 2, lay.kinds * lay.kinds, index_refs[1][0])
    for i in range(per_dev):
        take = plan_ref[lay.takes + i]
        far = per_dev + jnp.where((take < 2) | (rounds == 2), take, 2 + i)
        plan_ref[lay.place + i] = jnp.where(take < 0, -1 - take, far)


def first_kernel(
    lay, clone_ref, group_ref, state_ref, kick_ref, forcing_ref, plan_ref, index_ref, second_ref, *refs
):
    fields, sides, strips_ref = refs[:4], refs[4:8], refs[8]
    sources, ends, held, kick_ends, forcing_ends, done = refs[-6:]
    members, variables, levels, height, width = state_ref.shape
    copies = [pltpu.make_async_copy(clone_ref, sources, done.at[0]), pltpu.make_async_copy(state_ref, held, done.at[1])]
    for side, at in enumerate((0, width - LANES)):
        for ref, part in ((kick_ref, kick_ends), (forcing_ref, forcing_ends)):
            piece = ref.at[(slice(None),) * (len(ref.shape) - 1) + (pl.ds(at, LANES),)]
            copies.append(pltpu.make_async_copy(piece, part.at[side], done.at[len(copies)]))
    for copy in copies:
        copy.start()
    copies[0].wait()
    plan_lines(lay, sources, group_ref, plan_ref, (index_ref, second_ref), ends)
    copies[1].wait()
    sent = [plan_ref[lay.sends + n] for n in range(4)]
    wanted = [plan_ref[lay.patterns + n] > 0 for n in range(4)]
    later = [pltpu.make_async_copy(held.at[sent[n]], fields[n], done.at[4 + n]) for n in (2, 3)]
    for n in range(2):
        pl.when(wanted[2 + n])(later[n].start)

        @pl.when(wanted[n])
        def _():
            @pl.loop(0, variables)
            def _(v):
                for k in range(levels):
                    fields[n][v, k] = held[sent[n], v, k]

    for copy in copies[2:]:
        copy.wait()
    lane = lane_index((height, LANES))

    @pl.loop(0, levels)
    def _(k):
        for slot in range(2 * members + 1):
            strip = jnp.zeros((height, LANES), jnp.float32)
            for v in range(variables):
                if slot < members:
                    low, high = (held[slot, v, k, :, at : at + LANES] for at in (0, width - LANES))
                elif slot < 2 * members:
                    low, high = (kick_ends[side, slot - members, v, k] for side in range(2))
                else:
                    low, high = (forcing_ends[side, v, k] for side in range(2))
                both = turn(jnp.where(lane < HALO, low, high), HALO + 2 * HALO * v)
                strip = jnp.where(lane >= 2 * HALO * v, both, strip)
            strips_ref[slot, k] = strip

    for ref, j in zip(sides, sent):
        ref[...] = strips_ref[j]
    for n in range(2):
        pl.when(wanted[2 + n])(later[n].wait)


def spec(space):
    return pl.BlockSpec(memory_space=space)


def first(lay, group, clone_src, state, kick, forcing):
    members, variables, levels, height, width = state.shape
    shape = jax.ShapeDtypeStruct
    one = pltpu.VMEM(state.shape[1:], jnp.float32)
    side = pltpu.VMEM((levels, height, LANES), jnp.float32)
    strips = pltpu.VMEM((2 * members + 1, levels, height, LANES), jnp.float32)
    ends = (2, members, variables, levels, height, LANES)
    scalar, here, far = spec(pltpu.SMEM), spec(pltpu.VMEM), spec(pltpu.HBM)
    return pl.pallas_call(
        functools.partial(first_kernel, lay),
        in_specs=[far, scalar, far, far, far],
        out_specs=[scalar] * 3 + [here] * 2 + [spec(pl.ANY)] * 2 + [here] * 5,
        out_shape=[shape((lay.size,), jnp.int32)] + [shape((1,), jnp.int32)] * 2 + [one] * 2 + [pltpu.HBM(state.shape[1:], jnp.float32)] * 2 + [side] * 4 + [strips],
        scratch_shapes=[
            pltpu.SMEM(clone_src.shape, jnp.int32),
            pltpu.SMEM((lay.most,), jnp.int32),
            pltpu.VMEM(state.shape, jnp.float32),
            pltpu.VMEM(ends, jnp.float32),
            pltpu.VMEM((2, *ends[2:]), jnp.float32),
            pltpu.SemaphoreType.DMA((8,)),
        ],
        compiler_params=pltpu.CompilerParams(vmem_limit_bytes=VMEM),
    )(far_away(clone_src), group[None], far_away(state), far_away(kick), far_away(forcing))


def far_away(x):
    return pltpu.with_memory_space_constraint(x, pltpu.HBM)


def edge_shape(members, forcing):
    variables, levels, height, width = forcing.shape
    return jax.ShapeDtypeStruct((members, levels, variables * width // LANES + 1, HALO, LANES), jnp.float32)


def options_of(state_ref, refs):
    return [state_ref.at[j] for j in range(state_ref.shape[0])] + list(refs)


def pack_kernel(
    lay, plan_ref, state_ref, up_ref, down_ref, second_up_ref, second_down_ref, kick_ref, forcing_ref,
    sides_ref, up_side_ref, down_side_ref, second_up_side_ref, second_down_side_ref,
    side_ref, out_top, out_bottom, top_ref, bottom_ref, field_rows, kick_rows, forcing_rows, done,
):
    members, variables, levels, height, width = state_ref.shape
    tiles = width // LANES
    leaving = []
    whole = options_of(state_ref, (up_ref, down_ref, second_up_ref, second_down_ref))
    parts = options_of(sides_ref.at[:members], (up_side_ref, down_side_ref, second_up_side_ref, second_down_side_ref))
    places = [plan_ref[lay.place + i] for i in range(members)]
    rows = [pl.ds(0, HALO), pl.ds(height - HALO, HALO)]
    f_copies = [pltpu.make_async_copy(forcing_ref.at[:, :, rows[n]], forcing_rows.at[n], done.at[0]) for n in range(2)]
    copies = []
    for i in range(members):
        for n in range(2):
            for at, option in enumerate(whole):

                @pl.when(places[i] == at)
                def _():
                    pltpu.make_async_copy(option.at[:, :, rows[n]], field_rows.at[i, n], done.at[1 + i]).start()

            copies.append(pltpu.make_async_copy(kick_ref.at[i, :, :, rows[n]], kick_rows.at[i, n], done.at[1 + i]))
    for copy in copies + f_copies:
        copy.start()

    def flank(slot, k, strip):
        side_ref[slot, k] = strip
        top_ref[slot, k, variables * tiles] = strip[:HALO]
        bottom_ref[slot, k, variables * tiles] = strip[height - HALO :]

    def edges(slot, rows_of):
        @pl.loop(0, levels)
        def _(k):
            for n, ref in enumerate((top_ref, bottom_ref)):
                for v in range(variables):
                    edge = rows_of(n, v, k)
                    for t in range(tiles):
                        ref[slot, k, v * tiles + t] = edge[:, LANES * t : LANES * (t + 1)]

        for ref, out in ((top_ref, out_top), (bottom_ref, out_bottom)):
            leaving.append(pltpu.make_async_copy(ref.at[slot], out.at[slot], done.at[1 + members + len(leaving)]))
            leaving[-1].start()

    for k in range(levels):
        flank(members, k, sides_ref[2 * members, k])
        for i in range(members):
            strip = parts[-1][k]
            for at in reversed(range(len(parts) - 1)):
                strip = jnp.where(places[i] == at, parts[at][k], strip)
            flank(i, k, strip + sides_ref[members + i, k])
    for copy in f_copies:
        copy.wait()
    edges(members, lambda n, v, k: forcing_rows[n, v, k])
    for i in range(members):
        for n in range(2):
            pltpu.make_async_copy(kick_ref.at[i, :, :, rows[n]], field_rows.at[i, n], done.at[1 + i]).wait()
            copies[2 * i + n].wait()
        edges(i, lambda n, v, k: field_rows[i, n, v, k] + kick_rows[i, n, v, k])
    for copy in leaving:
        copy.wait()


def pack(lay, plan, state, fields, kick, forcing, sides, far_sides):
    members, variables, levels, height, width = state.shape
    here, anywhere = spec(pltpu.VMEM), spec(pl.ANY)
    rows = (members, 2, variables, levels, HALO, width)
    return pl.pallas_call(
        functools.partial(pack_kernel, lay),
        in_specs=[spec(pltpu.SMEM)] + [anywhere] * 7 + [here] * 5,
        out_specs=[here] + [anywhere] * 2,
        out_shape=[
            jax.ShapeDtypeStruct((members + 1, levels, height, LANES), jnp.float32),
            edge_shape(members + 1, forcing),
            edge_shape(members + 1, forcing),
        ],
        scratch_shapes=[
            pltpu.VMEM(edge_shape(members + 1, forcing).shape, jnp.float32),
            pltpu.VMEM(edge_shape(members + 1, forcing).shape, jnp.float32),
            pltpu.VMEM(rows, jnp.float32),
            pltpu.VMEM(rows, jnp.float32),
            pltpu.VMEM(rows[1:], jnp.float32),
            pltpu.SemaphoreType.DMA((3 + 3 * members,)),
        ],
        compiler_params=pltpu.CompilerParams(vmem_limit_bytes=VMEM),
    )(plan, far_away(state), *fields, far_away(kick), far_away(forcing), sides, *far_sides)


def blank(*like):
    return pl.pallas_call(
        lambda *refs: None,
        out_specs=[spec(pl.ANY)] * len(like),
        out_shape=[jax.ShapeDtypeStruct(x.shape, x.dtype) for x in like],
        compiler_params=pltpu.CompilerParams(vmem_limit_bytes=1024 * 1024),
    )()


def neighbours(top, bottom):
    lats = lax.axis_size("lat")
    above = lax.ppermute(bottom, "lat", [(i, i + 1) for i in range(lats - 1)])
    below = lax.ppermute(top, "lat", [(i + 1, i) for i in range(lats - 1)])
    return above, below


def beside(strips):
    assert lax.axis_size("lon") == 2
    return lax.ppermute(strips, "lon", [(0, 1), (1, 0)])


def send(lay, kinds, fields, sides):
    groups, lons = lay.groups, lax.axis_size("lon")
    fields, sides = list(fields), list(sides)
    for down, kind in enumerate(kinds):
        if kind:
            pairs = chain(kind - 1, groups)
            if down:
                pairs = [(groups - 1 - a, groups - 1 - b) for a, b in pairs]
            crossed = [(a * lons + j, b * lons + 1 - j) for a, b in pairs for j in range(lons)]
            fields[down] = lax.ppermute(fields[down], "member", pairs)
            sides[down] = lax.ppermute(sides[down], ("member", "lon"), crossed)
        else:
            fields[down], sides[down] = blank(fields[down], sides[down])
    return (*fields, *sides)


def prepared(state, kick, forcing, clone_src):
    per_dev, groups, group = state.shape[0], lax.axis_size("member"), lax.axis_index("member")
    lay = Layout(groups, per_dev)
    if groups != 4:
        piece = lax.all_gather(state, "member", axis=0, tiled=True)
        sources = lax.dynamic_slice_in_dim(clone_src, group * per_dev, per_dev)
        state = jnp.take(piece, sources, axis=0, mode="clip")
        lay = Layout(3, per_dev)
        still = jnp.arange(per_dev * 3, dtype=jnp.int32)
        plan, _, _, *out, strips = first(lay, jnp.int32(0), still, state, kick, forcing)
        got, second = (*out[:2], *out[4:6]), (*out[2:4], *out[6:])
        sides = beside(strips)
    else:
        plan, index, following, *out, strips = first(lay, group, clone_src, state, kick, forcing)
        out, second = (*out[:2], *out[4:6]), (*out[2:4], *out[6:])
        kinds = [(a, b) for a in range(lay.kinds) for b in range(lay.kinds)]

        def opening(kind):
            return lambda a, b, c, d, strips: (*send(lay, kind, (a, b), (c, d)), beside(strips))

        ways = [lambda a, b, c, d, kind=kind: send(lay, kind, (a, b), (c, d)) for kind in kinds]

        def later(t, held):
            takes = plan[lay.takes : lay.place]
            sent = [lax.dynamic_index_in_dim(plan, lay.sends + 2 * t + n, keepdims=False) for n in range(2)]
            wanted = [lax.dynamic_index_in_dim(plan, lay.patterns + 2 * t + n, keepdims=False) for n in range(2)]
            out = [lax.dynamic_index_in_dim(x, j, keepdims=False) for x in (state, strips) for j in sent]
            got = lax.switch(wanted[0] * lay.kinds + wanted[1], ways, *out)
            kept = []
            for x in range(2):
                for i in range(per_dev):
                    up, down = takes[i] == 2 * t, takes[i] == 2 * t + 1
                    new = jnp.where(up, got[2 * x], got[2 * x + 1])
                    kept.append(jnp.where(up | down, new, held[2 * x + i]))
            return tuple(kept)

        *got, sides = lax.switch(index[0], [opening(kind) for kind in kinds], *out, strips)
        several = lambda *held: lax.fori_loop(1, plan[0], later, held)
        second = lax.switch(following[0], ways + [several], *second)

    assert per_dev == 2
    fields = (*got[:2], *second[:2])
    side, top, bottom = pack(lay, plan, state, fields, kick, forcing, sides, (*got[2:], *second[2:]))
    return plan[lay.place :], (state, *fields), side, top, bottom


def cut(rows, strip, v):
    width = rows.shape[1]
    count = -(-width // SPAN)
    lane = lane_index((rows.shape[0], LANES))
    source = [rows[:, LANES * t : LANES * (t + 1)] for t in range(width // LANES)]
    tiles = []
    for c in range(count):
        first = SPAN * c - HALO
        if c == 0:
            tile = jnp.where(lane < HALO, turn(strip, -2 * HALO * v), turn(source[0], HALO))
        else:
            t, offset = first // LANES, first % LANES
            if t + 1 < len(source):
                later = turn(source[t + 1], -offset)
            else:
                later = turn(strip, LANES - offset - 2 * HALO * v - HALO)
            tile = jnp.where(lane < LANES - offset, turn(source[t], -offset), later)
        tiles.append(tile)
    return tiles


def step_kernel(
    state_ref, up_ref, down_ref, second_up_ref, second_down_ref, kick_ref, forcing_ref, above_ref, below_ref, side_ref,
    coupling_ref, place_ref, lat_ref, out_ref, cells, other, source, result, table, stage, field, kicks, drive, done,
):
    members, variables, levels, height, width = state_ref.shape
    count = -(-width // SPAN)
    tall = height + 2 * HALO
    at_top = lat_ref[0] == 0
    at_bottom = lat_ref[0] == lat_ref[1] - 1
    options = options_of(state_ref, (up_ref, down_ref, second_up_ref, second_down_ref))

    def fetch(job, wait=False):
        k, m, slot = job // members, job % members, job % 2
        copies = [pltpu.make_async_copy(kick_ref.at[m, :, k], kicks.at[slot], done.at[2, slot])]
        if wait:
            copies.append(pltpu.make_async_copy(kick_ref.at[m, :, k], field.at[slot], done.at[1, slot]))
        else:
            for at, option in enumerate(options):

                @pl.when(place_ref[m] == at)
                def _():
                    pltpu.make_async_copy(option.at[:, k], field.at[slot], done.at[1, slot]).start()

        for copy in copies:
            copy.wait() if wait else copy.start()

        @pl.when(m == 0)
        def _():
            copy = pltpu.make_async_copy(forcing_ref.at[:, k], drive, done.at[3, 0])
            copy.wait() if wait else copy.start()

    def edge(ref, slot, k, v):
        tiles = width // LANES
        rows = [ref[slot, k, v * tiles + t] for t in range(tiles)]
        return jnp.concatenate(rows, axis=1), ref[slot, k, variables * tiles]

    def lay(rows, strip, v, target, at, scale):
        for c, tile in enumerate(cut(rows, strip, v)):
            target[c, v, at : at + rows.shape[0]] = tile if scale is None else tile * scale

    blocks = tall // ROWS
    pad = ROWS
    origin = lat_ref[2]

    def advance_tile(now, later, c, last):
        def tile(v, r):
            return now[c, v, pad + ROWS * r : pad + ROWS * (r + 1)]

        def shifted(v, r, d):
            return now[c, v, pl.ds(origin + pad + ROWS * r + d, ROWS)]

        for r in range(1, blocks - 1) if last else range(blocks):
            centre = [tile(v, r) for v in range(variables)]
            ku, kv = K * centre[0], K * centre[1]
            eu, ev = 8.0 * ku, 8.0 * kv
            along = 16.0 * K - eu, 16.0 * K + eu, ku - K, -K - ku
            across = 16.0 * K - ev, 16.0 * K + ev, kv - K, -K - kv
            for v in range(variables):
                q = centre[v]
                total = source[c, v, ROWS * r : ROWS * (r + 1)]
                for w in range(variables):
                    total += table[v * variables + w] * centre[w]
                near = along[0] * turn(q, -1) + along[1] * turn(q, 1)
                far = along[2] * turn(q, -2) + along[3] * turn(q, 2)
                near += across[0] * shifted(v, r, 1) + across[1] * shifted(v, r, -1)
                far += across[2] * shifted(v, r, 2) + across[3] * shifted(v, r, -2)
                total += near + far
                if last:
                    result[c, v, ROWS * (r - 1) : ROWS * r] = total
                elif r in (0, blocks - 1):
                    later[c, v, pad + ROWS * r : pad + ROWS * (r + 1)] = jnp.where(at_top if r == 0 else at_bottom, 0.0, total)
                else:
                    later[c, v, pad + ROWS * r : pad + ROWS * (r + 1)] = total

    fetch(0)

    @pl.loop(0, levels * members)
    def _(job):
        k, m, slot = job // members, job % members, job % 2
        for v in range(variables):
            lay(*edge(above_ref, m, k, v), v, cells, pad, None)
            lay(*edge(below_ref, m, k, v), v, cells, pad + HALO + height, None)
        fetch(job, wait=True)
        for v in range(variables):
            lay(field[slot, v] + kicks[slot, v], side_ref[m, k], v, cells, pad + HALO, None)

        @pl.when(m == 0)
        def _():
            for v in range(variables):
                lay(*edge(above_ref, members, k, v), v, source, 0, 0.1)
                lay(drive[v], side_ref[members, k], v, source, HALO, 0.1)
                lay(*edge(below_ref, members, k, v), v, source, HALO + height, 0.1)
                for w in range(variables):
                    weight = 0.25 * coupling_ref[(k * variables + v) * variables + w]
                    weight = weight + (1.0 - 60.0 * K if v == w else 0.0)
                    table[v * variables + w] = jnp.full((ROWS, LANES), weight, jnp.float32)

        @pl.when(job + 1 < levels * members)
        def _():
            fetch(job + 1)

        @pl.loop(0, count)
        def _(c):
            for step in range(STEPS):
                now, later = (cells, other) if step % 2 == 0 else (other, cells)
                advance_tile(now, later, c, step == STEPS - 1)

        copy = pltpu.make_async_copy(stage.at[slot], out_ref.at[m, :, k], done.at[0, slot])
        pl.when(job >= 2)(copy.wait)
        lane = lane_index((height, LANES))
        for v in range(variables):
            for t in range(width // LANES):
                c, offset = LANES * t // SPAN, LANES * t % SPAN
                left = turn(result[c, v], -(offset + HALO))
                if c + 1 < count:
                    right = turn(result[c + 1, v], SPAN - offset - HALO)
                    left = jnp.where(lane < SPAN - offset, left, right)
                stage[slot, v, :, LANES * t : LANES * (t + 1)] = left
        copy.start()

    for slot in range(2):
        pltpu.make_async_copy(stage.at[slot], out_ref.at[0, :, 0], done.at[0, slot]).wait()


def advance(place, sources, kick, forcing, above, below, side, coupling):
    members, variables, levels, height, width = kick.shape
    assert levels * members >= 2 and height % ROWS == 0 and HALO == ROWS
    count = -(-width // SPAN)
    tall = height + 2 * HALO
    lat = jnp.stack([lax.axis_index("lat"), jnp.int32(lax.axis_size("lat")), jnp.int32(0)])
    here, scalars, anywhere = spec(pltpu.VMEM), spec(pltpu.SMEM), spec(pl.ANY)
    block = (variables, height, width)
    state, *others = sources
    return pl.pallas_call(
        step_kernel,
        in_specs=[anywhere] * 7 + [here] * 3 + [scalars] * 3,
        out_specs=spec(pltpu.HBM),
        out_shape=jax.ShapeDtypeStruct(kick.shape, jnp.float32),
        scratch_shapes=[
            pltpu.VMEM((count, variables, tall + 2 * ROWS, LANES), jnp.float32),
            pltpu.VMEM((count, variables, tall + 2 * ROWS, LANES), jnp.float32),
            pltpu.VMEM((count, variables, tall, LANES), jnp.float32),
            pltpu.VMEM((count, variables, height, LANES), jnp.float32),
            pltpu.VMEM((variables * variables, ROWS, LANES), jnp.float32),
            pltpu.VMEM((2, *block), jnp.float32),
            pltpu.VMEM((2, *block), jnp.float32),
            pltpu.VMEM((2, *block), jnp.float32),
            pltpu.VMEM(block, jnp.float32),
            pltpu.SemaphoreType.DMA((4, 2)),
        ],
        compiler_params=pltpu.CompilerParams(vmem_limit_bytes=VMEM),
    )(
        far_away(state), *others, far_away(kick), far_away(forcing), above, below, side, coupling.reshape(-1), place, lat
    )


def shards(state, kick, forcing, coupling, clone_src):
    place, sources, side, top, bottom = prepared(state, kick, forcing, clone_src)
    above, below = neighbours(top, bottom)
    return advance(place, sources, kick, forcing, above, below, side, coupling)


def solution(mesh):
    in_specs = (
        P("member", None, None, "lat", "lon"),
        P("member", None, None, "lat", "lon"),
        P(None, None, "lat", "lon"),
        P(),
        P(),
    )
    out_specs = P("member", None, None, "lat", "lon")
    return jax.shard_map(shards, mesh=mesh, in_specs=in_specs, out_specs=out_specs, check_vma=False)
```

```python
import functools

import functools

import jax
import jax.numpy as jnp
import numpy as np
from jax import lax
from jax.experimental import pallas as pl
from jax.experimental.pallas import tpu as pltpu
from jax.sharding import PartitionSpec as P

STEPS = 4
REACH = 2
HALO = STEPS * REACH
LANES = 128
ROWS = 8
SPAN = LANES - 2 * HALO
K = 0.05 / 12.0
VMEM = 10 * 1024 * 1024
BY_MATMUL = (2, 3, 4)


def lane_index(shape):
    return lax.broadcasted_iota(jnp.int32, shape, len(shape) - 1)


def turn(x, shift):
    shift = shift % LANES
    return x if shift == 0 else pltpu.roll(x, shift, x.ndim - 1)


def chain(bits, groups):
    stops = [0] + [x for x in range(1, groups - 1) if bits >> (x - 1) & 1] + [groups - 1]
    return list(zip(stops[:-1], stops[1:]))


class Layout:
    def __init__(self, groups, per_dev):
        self.groups, self.per_dev = groups, per_dev
        self.most = per_dev * (groups - 1)
        self.patterns, self.sends = 1, 1 + 2 * self.most
        self.takes = self.sends + 2 * self.most
        self.place = self.takes + per_dev
        self.size = self.place + per_dev
        self.kinds = 1 + (1 << (groups - 2))


def plan_lines(lay, clone_ref, group_ref, plan_ref, index_refs, ends):
    groups, per_dev, most = lay.groups, lay.per_dev, lay.most
    me = group_ref[0]
    plan_ref[0] = 1
    for t in range(2 * most):
        plan_ref[lay.patterns + t] = 0
        plan_ref[lay.sends + t] = 0
    for i in range(per_dev):
        plan_ref[lay.takes + i] = -1 - clone_ref[me * per_dev + i] % per_dev

    for down in range(2):
        for t in range(most):
            ends[t] = 0
        for a in range(groups - 1):
            for b in range(a + 1, groups):
                source, target = (groups - 1 - a, groups - 1 - b) if down else (a, b)
                spans = sum(1 << (x - 1) for x in range(a + 1, b))
                for j in range(per_dev):
                    member = source * per_dev + j
                    wanted = [clone_ref[target * per_dev + i] == member for i in range(per_dev)]
                    need = functools.reduce(jnp.logical_or, wanted)

                    @pl.when(need)
                    def _():
                        t = jnp.int32(most - 1)
                        for earlier in reversed(range(most - 1)):
                            t = jnp.where(ends[earlier] <= a, earlier, t)
                        ends[t] = b
                        plan_ref[0] = jnp.maximum(plan_ref[0], t + 1)
                        at = 2 * t + down
                        before = plan_ref[lay.patterns + at]
                        bits = jnp.where(before == 0, lay.kinds - 2, before - 1)
                        plan_ref[lay.patterns + at] = 1 + (bits & ~spans)

                        @pl.when(me == source)
                        def _():
                            plan_ref[lay.sends + at] = j

                        for i in range(per_dev):

                            @pl.when((me == target) & wanted[i])
                            def _():
                                plan_ref[lay.takes + i] = at

    for t in range(2):
        index_refs[t][0] = plan_ref[lay.patterns + 2 * t] * lay.kinds + plan_ref[lay.patterns + 2 * t + 1]
    rounds = plan_ref[0]
    index_refs[1][0] = jnp.where(rounds > 2, lay.kinds * lay.kinds, index_refs[1][0])
    for i in range(per_dev):
        take = plan_ref[lay.takes + i]
        far = per_dev + jnp.where((take < 2) | (rounds == 2), take, 2 + i)
        plan_ref[lay.place + i] = jnp.where(take < 0, -1 - take, far)


def first_kernel(
    lay, clone_ref, group_ref, state_ref, kick_ref, forcing_ref, plan_ref, index_ref, second_ref, *refs
):
    fields, sides, strips_ref = refs[:4], refs[4:8], refs[8]
    sources, ends, held, kick_ends, forcing_ends, done = refs[-6:]
    members, variables, levels, height, width = state_ref.shape
    copies = [pltpu.make_async_copy(clone_ref, sources, done.at[0]), pltpu.make_async_copy(state_ref, held, done.at[1])]
    for side, at in enumerate((0, width - LANES)):
        for ref, part in ((kick_ref, kick_ends), (forcing_ref, forcing_ends)):
            piece = ref.at[(slice(None),) * (len(ref.shape) - 1) + (pl.ds(at, LANES),)]
            copies.append(pltpu.make_async_copy(piece, part.at[side], done.at[len(copies)]))
    for copy in copies:
        copy.start()
    copies[0].wait()
    plan_lines(lay, sources, group_ref, plan_ref, (index_ref, second_ref), ends)
    copies[1].wait()
    sent = [plan_ref[lay.sends + n] for n in range(4)]
    wanted = [plan_ref[lay.patterns + n] > 0 for n in range(4)]
    later = [pltpu.make_async_copy(held.at[sent[n]], fields[n], done.at[4 + n]) for n in (2, 3)]
    for n in range(2):
        pl.when(wanted[2 + n])(later[n].start)

        @pl.when(wanted[n])
        def _():
            @pl.loop(0, variables)
            def _(v):
                for k in range(levels):
                    fields[n][v, k] = held[sent[n], v, k]

    for copy in copies[2:]:
        copy.wait()
    lane = lane_index((height, LANES))

    @pl.loop(0, levels)
    def _(k):
        for slot in range(2 * members + 1):
            strip = jnp.zeros((height, LANES), jnp.float32)
            for v in range(variables):
                if slot < members:
                    low, high = (held[slot, v, k, :, at : at + LANES] for at in (0, width - LANES))
                elif slot < 2 * members:
                    low, high = (kick_ends[side, slot - members, v, k] for side in range(2))
                else:
                    low, high = (forcing_ends[side, v, k] for side in range(2))
                both = turn(jnp.where(lane < HALO, low, high), HALO + 2 * HALO * v)
                strip = jnp.where(lane >= 2 * HALO * v, both, strip)
            strips_ref[slot, k] = strip

    for ref, j in zip(sides, sent):
        ref[...] = strips_ref[j]
    for n in range(2):
        pl.when(wanted[2 + n])(later[n].wait)


def spec(space):
    return pl.BlockSpec(memory_space=space)


def first(lay, group, clone_src, state, kick, forcing):
    members, variables, levels, height, width = state.shape
    shape = jax.ShapeDtypeStruct
    one = pltpu.VMEM(state.shape[1:], jnp.float32)
    side = pltpu.VMEM((levels, height, LANES), jnp.float32)
    strips = pltpu.VMEM((2 * members + 1, levels, height, LANES), jnp.float32)
    ends = (2, members, variables, levels, height, LANES)
    scalar, here, far = spec(pltpu.SMEM), spec(pltpu.VMEM), spec(pltpu.HBM)
    return pl.pallas_call(
        functools.partial(first_kernel, lay),
        in_specs=[far, scalar, far, far, far],
        out_specs=[scalar] * 3 + [here] * 2 + [spec(pl.ANY)] * 2 + [here] * 5,
        out_shape=[shape((lay.size,), jnp.int32)] + [shape((1,), jnp.int32)] * 2 + [one] * 2 + [pltpu.HBM(state.shape[1:], jnp.float32)] * 2 + [side] * 4 + [strips],
        scratch_shapes=[
            pltpu.SMEM(clone_src.shape, jnp.int32),
            pltpu.SMEM((lay.most,), jnp.int32),
            pltpu.VMEM(state.shape, jnp.float32),
            pltpu.VMEM(ends, jnp.float32),
            pltpu.VMEM((2, *ends[2:]), jnp.float32),
            pltpu.SemaphoreType.DMA((8,)),
        ],
        compiler_params=pltpu.CompilerParams(vmem_limit_bytes=VMEM),
    )(far_away(clone_src), group[None], far_away(state), far_away(kick), far_away(forcing))


def far_away(x):
    return pltpu.with_memory_space_constraint(x, pltpu.HBM)


def edge_shape(members, forcing):
    variables, levels, height, width = forcing.shape
    return jax.ShapeDtypeStruct((members, levels, variables * width // LANES + 1, HALO, LANES), jnp.float32)


def options_of(state_ref, refs):
    return [state_ref.at[j] for j in range(state_ref.shape[0])] + list(refs)


def pack_kernel(
    lay, plan_ref, state_ref, up_ref, down_ref, second_up_ref, second_down_ref, kick_ref, forcing_ref,
    sides_ref, up_side_ref, down_side_ref, second_up_side_ref, second_down_side_ref,
    side_ref, top_ref, bottom_ref, field_rows, kick_rows, forcing_rows, done,
):
    members, variables, levels, height, width = state_ref.shape
    tiles = width // LANES
    whole = options_of(state_ref, (up_ref, down_ref, second_up_ref, second_down_ref))
    parts = options_of(sides_ref.at[:members], (up_side_ref, down_side_ref, second_up_side_ref, second_down_side_ref))
    places = [plan_ref[lay.place + i] for i in range(members)]
    rows = [pl.ds(0, HALO), pl.ds(height - HALO, HALO)]
    f_copies = [pltpu.make_async_copy(forcing_ref.at[:, :, rows[n]], forcing_rows.at[n], done.at[0]) for n in range(2)]
    copies = []
    for i in range(members):
        for n in range(2):
            for at, option in enumerate(whole):

                @pl.when(places[i] == at)
                def _():
                    pltpu.make_async_copy(option.at[:, :, rows[n]], field_rows.at[i, n], done.at[1 + i]).start()

            copies.append(pltpu.make_async_copy(kick_ref.at[i, :, :, rows[n]], kick_rows.at[i, n], done.at[1 + i]))
    for copy in copies + f_copies:
        copy.start()

    def flank(slot, k, strip):
        side_ref[slot, k] = strip
        top_ref[slot, k, variables * tiles] = strip[:HALO]
        bottom_ref[slot, k, variables * tiles] = strip[height - HALO :]

    def edges(slot, rows_of):
        @pl.loop(0, levels)
        def _(k):
            for n, ref in enumerate((top_ref, bottom_ref)):
                for v in range(variables):
                    edge = rows_of(n, v, k)
                    for t in range(tiles):
                        ref[slot, k, v * tiles + t] = edge[:, LANES * t : LANES * (t + 1)]

    for k in range(levels):
        flank(members, k, sides_ref[2 * members, k])
        for i in range(members):
            strip = parts[-1][k]
            for at in reversed(range(len(parts) - 1)):
                strip = jnp.where(places[i] == at, parts[at][k], strip)
            flank(i, k, strip + sides_ref[members + i, k])
    for copy in f_copies:
        copy.wait()
    edges(members, lambda n, v, k: forcing_rows[n, v, k])
    for i in range(members):
        for n in range(2):
            pltpu.make_async_copy(kick_ref.at[i, :, :, rows[n]], field_rows.at[i, n], done.at[1 + i]).wait()
            copies[2 * i + n].wait()
        edges(i, lambda n, v, k: field_rows[i, n, v, k] + kick_rows[i, n, v, k])


def pack(lay, plan, state, fields, kick, forcing, sides, far_sides):
    members, variables, levels, height, width = state.shape
    here, anywhere = spec(pltpu.VMEM), spec(pl.ANY)
    rows = (members, 2, variables, levels, HALO, width)
    return pl.pallas_call(
        functools.partial(pack_kernel, lay),
        in_specs=[spec(pltpu.SMEM)] + [anywhere] * 7 + [here] * 5,
        out_specs=[here] * 3,
        out_shape=[
            jax.ShapeDtypeStruct((members + 1, levels, height, LANES), jnp.float32),
            edge_shape(members + 1, forcing),
            edge_shape(members + 1, forcing),
        ],
        scratch_shapes=[
            pltpu.VMEM(rows, jnp.float32),
            pltpu.VMEM(rows, jnp.float32),
            pltpu.VMEM(rows[1:], jnp.float32),
            pltpu.SemaphoreType.DMA((1 + members,)),
        ],
        compiler_params=pltpu.CompilerParams(vmem_limit_bytes=VMEM),
    )(plan, far_away(state), *fields, far_away(kick), far_away(forcing), sides, *far_sides)


def blank(*like):
    return pl.pallas_call(
        lambda *refs: None,
        out_specs=[spec(pl.ANY)] * len(like),
        out_shape=[jax.ShapeDtypeStruct(x.shape, x.dtype) for x in like],
        compiler_params=pltpu.CompilerParams(vmem_limit_bytes=1024 * 1024),
    )()


def neighbours(top, bottom):
    lats = lax.axis_size("lat")
    above = lax.ppermute(bottom, "lat", [(i, i + 1) for i in range(lats - 1)])
    below = lax.ppermute(top, "lat", [(i + 1, i) for i in range(lats - 1)])
    return above, below


def beside(strips):
    assert lax.axis_size("lon") == 2
    return lax.ppermute(strips, "lon", [(0, 1), (1, 0)])


def send(lay, kinds, fields, sides):
    groups, lons = lay.groups, lax.axis_size("lon")
    fields, sides = list(fields), list(sides)
    for down, kind in enumerate(kinds):
        if kind:
            pairs = chain(kind - 1, groups)
            if down:
                pairs = [(groups - 1 - a, groups - 1 - b) for a, b in pairs]
            crossed = [(a * lons + j, b * lons + 1 - j) for a, b in pairs for j in range(lons)]
            fields[down] = lax.ppermute(fields[down], "member", pairs)
            sides[down] = lax.ppermute(sides[down], ("member", "lon"), crossed)
        else:
            fields[down], sides[down] = blank(fields[down], sides[down])
    return (*fields, *sides)


def prepared(state, kick, forcing, clone_src):
    per_dev, groups, group = state.shape[0], lax.axis_size("member"), lax.axis_index("member")
    lay = Layout(groups, per_dev)
    if groups != 4:
        piece = lax.all_gather(state, "member", axis=0, tiled=True)
        sources = lax.dynamic_slice_in_dim(clone_src, group * per_dev, per_dev)
        state = jnp.take(piece, sources, axis=0, mode="clip")
        lay = Layout(3, per_dev)
        still = jnp.arange(per_dev * 3, dtype=jnp.int32)
        plan, _, _, *out, strips = first(lay, jnp.int32(0), still, state, kick, forcing)
        got, second = (*out[:2], *out[4:6]), (*out[2:4], *out[6:])
        sides = beside(strips)
    else:
        plan, index, following, *out, strips = first(lay, group, clone_src, state, kick, forcing)
        out, second = (*out[:2], *out[4:6]), (*out[2:4], *out[6:])
        kinds = [(a, b) for a in range(lay.kinds) for b in range(lay.kinds)]

        def opening(kind):
            return lambda a, b, c, d, strips: (*send(lay, kind, (a, b), (c, d)), beside(strips))

        ways = [lambda a, b, c, d, kind=kind: send(lay, kind, (a, b), (c, d)) for kind in kinds]

        def later(t, held):
            takes = plan[lay.takes : lay.place]
            sent = [lax.dynamic_index_in_dim(plan, lay.sends + 2 * t + n, keepdims=False) for n in range(2)]
            wanted = [lax.dynamic_index_in_dim(plan, lay.patterns + 2 * t + n, keepdims=False) for n in range(2)]
            out = [lax.dynamic_index_in_dim(x, j, keepdims=False) for x in (state, strips) for j in sent]
            got = lax.switch(wanted[0] * lay.kinds + wanted[1], ways, *out)
            kept = []
            for x in range(2):
                for i in range(per_dev):
                    up, down = takes[i] == 2 * t, takes[i] == 2 * t + 1
                    new = jnp.where(up, got[2 * x], got[2 * x + 1])
                    kept.append(jnp.where(up | down, new, held[2 * x + i]))
            return tuple(kept)

        *got, sides = lax.switch(index[0], [opening(kind) for kind in kinds], *out, strips)
        several = lambda *held: lax.fori_loop(1, plan[0], later, held)
        second = lax.switch(following[0], ways + [several], *second)

    assert per_dev == 2
    fields = (*got[:2], *second[:2])
    side, top, bottom = pack(lay, plan, state, fields, kick, forcing, sides, (*got[2:], *second[2:]))
    return plan[lay.place :], (state, *fields), side, top, bottom


def cut(rows, strip, v):
    width = rows.shape[1]
    count = -(-width // SPAN)
    lane = lane_index((rows.shape[0], LANES))
    source = [rows[:, LANES * t : LANES * (t + 1)] for t in range(width // LANES)]
    tiles = []
    for c in range(count):
        first = SPAN * c - HALO
        if c == 0:
            tile = jnp.where(lane < HALO, turn(strip, -2 * HALO * v), turn(source[0], HALO))
        else:
            t, offset = first // LANES, first % LANES
            if t + 1 < len(source):
                later = turn(source[t + 1], -offset)
            else:
                later = turn(strip, LANES - offset - 2 * HALO * v - HALO)
            tile = jnp.where(lane < LANES - offset, turn(source[t], -offset), later)
        tiles.append(tile)
    return tiles


def band():
    half = np.zeros((LANES, 2 * LANES), np.float32)
    for j in range(LANES):
        for d, slope, bend in ((1, 8, 16), (-1, -8, 16), (2, -1, -1), (-2, 1, -1)):
            half[(j + d) % LANES, j] = slope
            half[(j + d) % LANES, LANES + j] = bend
    return np.concatenate([half, half])


def step_kernel(
    state_ref, up_ref, down_ref, second_up_ref, second_down_ref, kick_ref, forcing_ref, above_ref, below_ref, side_ref,
    band_ref, coupling_ref, place_ref, lat_ref, out_ref, cells, other, source, result, table, stage, field, kicks, drive, sums, done,
):
    members, variables, levels, height, width = state_ref.shape
    count = -(-width // SPAN)
    tall = height + 2 * HALO
    at_top = lat_ref[0] == 0
    at_bottom = lat_ref[0] == lat_ref[1] - 1
    options = options_of(state_ref, (up_ref, down_ref, second_up_ref, second_down_ref))

    def fetch(job, wait=False):
        k, m, slot = job // members, job % members, job % 2
        copies = [pltpu.make_async_copy(kick_ref.at[m, :, k], kicks.at[slot], done.at[2, slot])]
        if wait:
            copies.append(pltpu.make_async_copy(kick_ref.at[m, :, k], field.at[slot], done.at[1, slot]))
        else:
            for at, option in enumerate(options):

                @pl.when(place_ref[m] == at)
                def _():
                    pltpu.make_async_copy(option.at[:, k], field.at[slot], done.at[1, slot]).start()

        for copy in copies:
            copy.wait() if wait else copy.start()

        @pl.when(m == 0)
        def _():
            copy = pltpu.make_async_copy(forcing_ref.at[:, k], drive, done.at[3, 0])
            copy.wait() if wait else copy.start()

    def edge(ref, slot, k, v):
        tiles = width // LANES
        rows = [ref[slot, k, v * tiles + t] for t in range(tiles)]
        return jnp.concatenate(rows, axis=1), ref[slot, k, variables * tiles]

    def lay(rows, strip, v, target, at, scale):
        for c, tile in enumerate(cut(rows, strip, v)):
            target[c, v, at : at + rows.shape[0]] = tile if scale is None else tile * scale

    blocks = tall // ROWS
    pad = ROWS
    origin = lat_ref[2]

    def advance_tile(now, later, c, last):
        def tile(v, r):
            return now[c, v, pad + ROWS * r : pad + ROWS * (r + 1)]

        def shifted(v, r, d):
            return now[c, v, pl.ds(origin + pad + ROWS * r + d, ROWS)]

        first, span = (ROWS, height) if last else (0, tall)
        parts = []
        for v in BY_MATMUL:
            rows = now[c, v, pad + first : pad + first + span]
            high = rows.astype(jnp.bfloat16)
            rest = (rows - high.astype(jnp.float32)).astype(jnp.bfloat16)
            parts.append(jnp.concatenate([high, rest], axis=1))
        parts = jnp.concatenate(parts, axis=0)
        sums[: parts.shape[0]] = jnp.dot(parts, band_ref[...], preferred_element_type=jnp.float32)

        for r in range(1, blocks - 1) if last else range(blocks):
            centre = [tile(v, r) for v in range(variables)]
            ku, kv = K * centre[0], K * centre[1]
            eu, ev = 8.0 * ku, 8.0 * kv
            along = 16.0 * K - eu, 16.0 * K + eu, ku - K, -K - ku
            across = 16.0 * K - ev, 16.0 * K + ev, kv - K, -K - kv
            for v in range(variables):
                q = centre[v]
                total = source[c, v, ROWS * r : ROWS * (r + 1)]
                for w in range(variables):
                    total += table[v * variables + w] * centre[w]
                if v in BY_MATMUL:
                    at = BY_MATMUL.index(v) * span + ROWS * r - first
                    near = K * sums[at : at + ROWS, LANES:]
                    far = -ku * sums[at : at + ROWS, :LANES]
                else:
                    near = along[0] * turn(q, -1) + along[1] * turn(q, 1)
                    far = along[2] * turn(q, -2) + along[3] * turn(q, 2)
                near += across[0] * shifted(v, r, 1) + across[1] * shifted(v, r, -1)
                far += across[2] * shifted(v, r, 2) + across[3] * shifted(v, r, -2)
                total += near + far
                if last:
                    result[c, v, ROWS * (r - 1) : ROWS * r] = total
                elif r in (0, blocks - 1):
                    later[c, v, pad + ROWS * r : pad + ROWS * (r + 1)] = jnp.where(at_top if r == 0 else at_bottom, 0.0, total)
                else:
                    later[c, v, pad + ROWS * r : pad + ROWS * (r + 1)] = total

    fetch(0)

    @pl.loop(0, levels * members)
    def _(job):
        k, m, slot = job // members, job % members, job % 2
        for v in range(variables):
            lay(*edge(above_ref, m, k, v), v, cells, pad, None)
            lay(*edge(below_ref, m, k, v), v, cells, pad + HALO + height, None)
        fetch(job, wait=True)
        for v in range(variables):
            lay(field[slot, v] + kicks[slot, v], side_ref[m, k], v, cells, pad + HALO, None)

        @pl.when(m == 0)
        def _():
            for v in range(variables):
                lay(*edge(above_ref, members, k, v), v, source, 0, 0.1)
                lay(drive[v], side_ref[members, k], v, source, HALO, 0.1)
                lay(*edge(below_ref, members, k, v), v, source, HALO + height, 0.1)
                for w in range(variables):
                    weight = 0.25 * coupling_ref[(k * variables + v) * variables + w]
                    weight = weight + (1.0 - 60.0 * K if v == w else 0.0)
                    table[v * variables + w] = jnp.full((ROWS, LANES), weight, jnp.float32)

        @pl.when(job + 1 < levels * members)
        def _():
            fetch(job + 1)

        @pl.loop(0, count)
        def _(c):
            for step in range(STEPS):
                now, later = (cells, other) if step % 2 == 0 else (other, cells)
                advance_tile(now, later, c, step == STEPS - 1)

        copy = pltpu.make_async_copy(stage.at[slot], out_ref.at[m, :, k], done.at[0, slot])
        pl.when(job >= 2)(copy.wait)
        lane = lane_index((height, LANES))
        for v in range(variables):
            for t in range(width // LANES):
                c, offset = LANES * t // SPAN, LANES * t % SPAN
                left = turn(result[c, v], -(offset + HALO))
                if c + 1 < count:
                    right = turn(result[c + 1, v], SPAN - offset - HALO)
                    left = jnp.where(lane < SPAN - offset, left, right)
                stage[slot, v, :, LANES * t : LANES * (t + 1)] = left
        copy.start()

    for slot in range(2):
        pltpu.make_async_copy(stage.at[slot], out_ref.at[0, :, 0], done.at[0, slot]).wait()


def advance(place, sources, kick, forcing, above, below, side, coupling):
    members, variables, levels, height, width = kick.shape
    assert levels * members >= 2 and height % ROWS == 0 and HALO == ROWS
    count = -(-width // SPAN)
    tall = height + 2 * HALO
    lat = jnp.stack([lax.axis_index("lat"), jnp.int32(lax.axis_size("lat")), jnp.int32(0)])
    here, scalars, anywhere = spec(pltpu.VMEM), spec(pltpu.SMEM), spec(pl.ANY)
    block = (variables, height, width)
    state, *others = sources
    return pl.pallas_call(
        step_kernel,
        in_specs=[anywhere] * 7 + [here] * 4 + [scalars] * 3,
        out_specs=spec(pltpu.HBM),
        out_shape=jax.ShapeDtypeStruct(kick.shape, jnp.float32),
        scratch_shapes=[
            pltpu.VMEM((count, variables, tall + 2 * ROWS, LANES), jnp.float32),
            pltpu.VMEM((count, variables, tall + 2 * ROWS, LANES), jnp.float32),
            pltpu.VMEM((count, variables, tall, LANES), jnp.float32),
            pltpu.VMEM((count, variables, height, LANES), jnp.float32),
            pltpu.VMEM((variables * variables, ROWS, LANES), jnp.float32),
            pltpu.VMEM((2, *block), jnp.float32),
            pltpu.VMEM((2, *block), jnp.float32),
            pltpu.VMEM((2, *block), jnp.float32),
            pltpu.VMEM(block, jnp.float32),
            pltpu.VMEM((len(BY_MATMUL) * tall, 2 * LANES), jnp.float32),
            pltpu.SemaphoreType.DMA((4, 2)),
        ],
        compiler_params=pltpu.CompilerParams(vmem_limit_bytes=VMEM),
    )(
        far_away(state), *others, far_away(kick), far_away(forcing), above, below, side,
        jnp.asarray(band(), jnp.bfloat16), coupling.reshape(-1), place, lat,
    )


def shards(state, kick, forcing, coupling, clone_src):
    place, sources, side, top, bottom = prepared(state, kick, forcing, clone_src)
    above, below = neighbours(top, bottom)
    return advance(place, sources, kick, forcing, above, below, side, coupling)


def solution(mesh):
    in_specs = (
        P("member", None, None, "lat", "lon"),
        P("member", None, None, "lat", "lon"),
        P(None, None, "lat", "lon"),
        P(),
        P(),
    )
    out_specs = P("member", None, None, "lat", "lon")
    return jax.shard_map(shards, mesh=mesh, in_specs=in_specs, out_specs=out_specs, check_vma=False)
```

```python
import functools

import functools

import jax
import jax.numpy as jnp
from jax import lax
from jax.experimental import pallas as pl
from jax.experimental.pallas import tpu as pltpu
from jax.sharding import PartitionSpec as P

STEPS = 4
REACH = 2
HALO = STEPS * REACH
LANES = 128
ROWS = 8
SPAN = LANES - 2 * HALO
K = 0.05 / 12.0
VMEM = 10 * 1024 * 1024


def lane_index(shape):
    return lax.broadcasted_iota(jnp.int32, shape, len(shape) - 1)


def turn(x, shift):
    shift = shift % LANES
    return x if shift == 0 else pltpu.roll(x, shift, x.ndim - 1)


def chain(bits, groups):
    stops = [0] + [x for x in range(1, groups - 1) if bits >> (x - 1) & 1] + [groups - 1]
    return list(zip(stops[:-1], stops[1:]))


class Layout:
    def __init__(self, groups, per_dev):
        self.groups, self.per_dev = groups, per_dev
        self.most = per_dev * (groups - 1)
        self.patterns, self.sends = 1, 1 + 2 * self.most
        self.takes = self.sends + 2 * self.most
        self.place = self.takes + per_dev
        self.size = self.place + per_dev
        self.kinds = 1 + (1 << (groups - 2))


def plan_lines(lay, clone_ref, group_ref, plan_ref, index_refs, ends):
    groups, per_dev, most = lay.groups, lay.per_dev, lay.most
    me = group_ref[0]
    plan_ref[0] = 1
    for t in range(2 * most):
        plan_ref[lay.patterns + t] = 0
        plan_ref[lay.sends + t] = 0
    for i in range(per_dev):
        plan_ref[lay.takes + i] = -1 - clone_ref[me * per_dev + i] % per_dev

    for down in range(2):
        for t in range(most):
            ends[t] = 0
        for a in range(groups - 1):
            for b in range(a + 1, groups):
                source, target = (groups - 1 - a, groups - 1 - b) if down else (a, b)
                spans = sum(1 << (x - 1) for x in range(a + 1, b))
                for j in range(per_dev):
                    member = source * per_dev + j
                    wanted = [clone_ref[target * per_dev + i] == member for i in range(per_dev)]
                    need = functools.reduce(jnp.logical_or, wanted)

                    @pl.when(need)
                    def _():
                        t = jnp.int32(most - 1)
                        for earlier in reversed(range(most - 1)):
                            t = jnp.where(ends[earlier] <= a, earlier, t)
                        ends[t] = b
                        plan_ref[0] = jnp.maximum(plan_ref[0], t + 1)
                        at = 2 * t + down
                        before = plan_ref[lay.patterns + at]
                        bits = jnp.where(before == 0, lay.kinds - 2, before - 1)
                        plan_ref[lay.patterns + at] = 1 + (bits & ~spans)

                        @pl.when(me == source)
                        def _():
                            plan_ref[lay.sends + at] = j

                        for i in range(per_dev):

                            @pl.when((me == target) & wanted[i])
                            def _():
                                plan_ref[lay.takes + i] = at

    for t in range(2):
        index_refs[t][0] = plan_ref[lay.patterns + 2 * t] * lay.kinds + plan_ref[lay.patterns + 2 * t + 1]
    rounds = plan_ref[0]
    index_refs[1][0] = jnp.where(rounds > 2, lay.kinds * lay.kinds, index_refs[1][0])
    for i in range(per_dev):
        take = plan_ref[lay.takes + i]
        far = per_dev + jnp.where((take < 2) | (rounds == 2), take, 2 + i)
        plan_ref[lay.place + i] = jnp.where(take < 0, -1 - take, far)


def first_kernel(
    lay, clone_ref, group_ref, state_ref, kick_ref, forcing_ref, plan_ref, index_ref, second_ref, *refs
):
    fields, sides, strips_ref = refs[:4], refs[4:8], refs[8]
    sources, ends, held, kick_ends, forcing_ends, done = refs[-6:]
    members, variables, levels, height, width = state_ref.shape
    copies = [pltpu.make_async_copy(clone_ref, sources, done.at[0]), pltpu.make_async_copy(state_ref, held, done.at[1])]
    for side, at in enumerate((0, width - LANES)):
        for ref, part in ((kick_ref, kick_ends), (forcing_ref, forcing_ends)):
            piece = ref.at[(slice(None),) * (len(ref.shape) - 1) + (pl.ds(at, LANES),)]
            copies.append(pltpu.make_async_copy(piece, part.at[side], done.at[len(copies)]))
    for copy in copies:
        copy.start()
    copies[0].wait()
    plan_lines(lay, sources, group_ref, plan_ref, (index_ref, second_ref), ends)
    copies[1].wait()
    sent = [plan_ref[lay.sends + n] for n in range(4)]
    wanted = [plan_ref[lay.patterns + n] > 0 for n in range(4)]
    later = [pltpu.make_async_copy(held.at[sent[n]], fields[n], done.at[4 + n]) for n in (2, 3)]
    for n in range(2):
        pl.when(wanted[2 + n])(later[n].start)

        @pl.when(wanted[n])
        def _():
            @pl.loop(0, variables)
            def _(v):
                for k in range(levels):
                    fields[n][v, k] = held[sent[n], v, k]

    for copy in copies[2:]:
        copy.wait()
    lane = lane_index((height, LANES))

    @pl.loop(0, levels)
    def _(k):
        for slot in range(2 * members + 1):
            strip = jnp.zeros((height, LANES), jnp.float32)
            for v in range(variables):
                if slot < members:
                    low, high = (held[slot, v, k, :, at : at + LANES] for at in (0, width - LANES))
                elif slot < 2 * members:
                    low, high = (kick_ends[side, slot - members, v, k] for side in range(2))
                else:
                    low, high = (forcing_ends[side, v, k] for side in range(2))
                both = turn(jnp.where(lane < HALO, low, high), HALO + 2 * HALO * v)
                strip = jnp.where(lane >= 2 * HALO * v, both, strip)
            strips_ref[slot, k] = strip

    for ref, j in zip(sides, sent):
        ref[...] = strips_ref[j]
    for n in range(2):
        pl.when(wanted[2 + n])(later[n].wait)


def spec(space):
    return pl.BlockSpec(memory_space=space)


def first(lay, group, clone_src, state, kick, forcing):
    members, variables, levels, height, width = state.shape
    shape = jax.ShapeDtypeStruct
    one = pltpu.VMEM(state.shape[1:], jnp.float32)
    side = pltpu.VMEM((levels, height, LANES), jnp.float32)
    strips = pltpu.VMEM((2 * members + 1, levels, height, LANES), jnp.float32)
    ends = (2, members, variables, levels, height, LANES)
    scalar, here, far = spec(pltpu.SMEM), spec(pltpu.VMEM), spec(pltpu.HBM)
    return pl.pallas_call(
        functools.partial(first_kernel, lay),
        in_specs=[far, scalar, far, far, far],
        out_specs=[scalar] * 3 + [here] * 2 + [spec(pl.ANY)] * 2 + [here] * 5,
        out_shape=[shape((lay.size,), jnp.int32)] + [shape((1,), jnp.int32)] * 2 + [one] * 2 + [pltpu.HBM(state.shape[1:], jnp.float32)] * 2 + [side] * 4 + [strips],
        scratch_shapes=[
            pltpu.SMEM(clone_src.shape, jnp.int32),
            pltpu.SMEM((lay.most,), jnp.int32),
            pltpu.VMEM(state.shape, jnp.float32),
            pltpu.VMEM(ends, jnp.float32),
            pltpu.VMEM((2, *ends[2:]), jnp.float32),
            pltpu.SemaphoreType.DMA((8,)),
        ],
        compiler_params=pltpu.CompilerParams(vmem_limit_bytes=VMEM),
    )(far_away(clone_src), group[None], far_away(state), far_away(kick), far_away(forcing))


def far_away(x):
    return pltpu.with_memory_space_constraint(x, pltpu.HBM)


def edge_shape(members, forcing):
    variables, levels, height, width = forcing.shape
    return jax.ShapeDtypeStruct((members, levels, variables * width // LANES + 1, HALO, LANES), jnp.float32)


def options_of(state_ref, refs):
    return [state_ref.at[j] for j in range(state_ref.shape[0])] + list(refs)


def pack_kernel(
    lay, plan_ref, state_ref, up_ref, down_ref, second_up_ref, second_down_ref, kick_ref, forcing_ref,
    sides_ref, up_side_ref, down_side_ref, second_up_side_ref, second_down_side_ref,
    side_ref, top_ref, bottom_ref, field_rows, kick_rows, forcing_rows, done,
):
    members, variables, levels, height, width = state_ref.shape
    tiles = width // LANES
    whole = options_of(state_ref, (up_ref, down_ref, second_up_ref, second_down_ref))
    parts = options_of(sides_ref.at[:members], (up_side_ref, down_side_ref, second_up_side_ref, second_down_side_ref))
    places = [plan_ref[lay.place + i] for i in range(members)]
    rows = [pl.ds(0, HALO), pl.ds(height - HALO, HALO)]
    f_copies = [pltpu.make_async_copy(forcing_ref.at[:, :, rows[n]], forcing_rows.at[n], done.at[0]) for n in range(2)]
    copies = []
    for i in range(members):
        for n in range(2):
            for at, option in enumerate(whole):

                @pl.when(places[i] == at)
                def _():
                    pltpu.make_async_copy(option.at[:, :, rows[n]], field_rows.at[i, n], done.at[1 + i]).start()

            copies.append(pltpu.make_async_copy(kick_ref.at[i, :, :, rows[n]], kick_rows.at[i, n], done.at[1 + i]))
    for copy in copies + f_copies:
        copy.start()

    def flank(slot, k, strip):
        side_ref[slot, k] = strip
        top_ref[slot, k, variables * tiles] = strip[:HALO]
        bottom_ref[slot, k, variables * tiles] = strip[height - HALO :]

    def edges(slot, rows_of):
        @pl.loop(0, levels)
        def _(k):
            for n, ref in enumerate((top_ref, bottom_ref)):
                for v in range(variables):
                    edge = rows_of(n, v, k)
                    for t in range(tiles):
                        ref[slot, k, v * tiles + t] = edge[:, LANES * t : LANES * (t + 1)]

    for k in range(levels):
        flank(members, k, sides_ref[2 * members, k])
        for i in range(members):
            strip = parts[-1][k]
            for at in reversed(range(len(parts) - 1)):
                strip = jnp.where(places[i] == at, parts[at][k], strip)
            flank(i, k, strip + sides_ref[members + i, k])
    for copy in f_copies:
        copy.wait()
    edges(members, lambda n, v, k: forcing_rows[n, v, k])
    for i in range(members):
        for n in range(2):
            pltpu.make_async_copy(kick_ref.at[i, :, :, rows[n]], field_rows.at[i, n], done.at[1 + i]).wait()
            copies[2 * i + n].wait()
        edges(i, lambda n, v, k: field_rows[i, n, v, k] + kick_rows[i, n, v, k])


def pack(lay, plan, state, fields, kick, forcing, sides, far_sides):
    members, variables, levels, height, width = state.shape
    here, anywhere = spec(pltpu.VMEM), spec(pl.ANY)
    rows = (members, 2, variables, levels, HALO, width)
    return pl.pallas_call(
        functools.partial(pack_kernel, lay),
        in_specs=[spec(pltpu.SMEM)] + [anywhere] * 7 + [here] * 5,
        out_specs=[here] * 3,
        out_shape=[
            jax.ShapeDtypeStruct((members + 1, levels, height, LANES), jnp.float32),
            edge_shape(members + 1, forcing),
            edge_shape(members + 1, forcing),
        ],
        scratch_shapes=[
            pltpu.VMEM(rows, jnp.float32),
            pltpu.VMEM(rows, jnp.float32),
            pltpu.VMEM(rows[1:], jnp.float32),
            pltpu.SemaphoreType.DMA((1 + members,)),
        ],
        compiler_params=pltpu.CompilerParams(vmem_limit_bytes=VMEM),
    )(plan, far_away(state), *fields, far_away(kick), far_away(forcing), sides, *far_sides)


def blank(*like):
    return pl.pallas_call(
        lambda *refs: None,
        out_specs=[spec(pl.ANY)] * len(like),
        out_shape=[jax.ShapeDtypeStruct(x.shape, x.dtype) for x in like],
        compiler_params=pltpu.CompilerParams(vmem_limit_bytes=1024 * 1024),
    )()


def neighbours(top, bottom):
    lats = lax.axis_size("lat")
    above = lax.ppermute(bottom, "lat", [(i, i + 1) for i in range(lats - 1)])
    below = lax.ppermute(top, "lat", [(i + 1, i) for i in range(lats - 1)])
    return above, below


def beside(strips):
    assert lax.axis_size("lon") == 2
    return lax.ppermute(strips, "lon", [(0, 1), (1, 0)])


def send(lay, kinds, fields, sides):
    groups, lons = lay.groups, lax.axis_size("lon")
    fields, sides = list(fields), list(sides)
    for down, kind in enumerate(kinds):
        if kind:
            pairs = chain(kind - 1, groups)
            if down:
                pairs = [(groups - 1 - a, groups - 1 - b) for a, b in pairs]
            crossed = [(a * lons + j, b * lons + 1 - j) for a, b in pairs for j in range(lons)]
            fields[down] = lax.ppermute(fields[down], "member", pairs)
            sides[down] = lax.ppermute(sides[down], ("member", "lon"), crossed)
        else:
            fields[down], sides[down] = blank(fields[down], sides[down])
    return (*fields, *sides)


def prepared(state, kick, forcing, clone_src):
    per_dev, groups, group = state.shape[0], lax.axis_size("member"), lax.axis_index("member")
    lay = Layout(groups, per_dev)
    if groups != 4:
        piece = lax.all_gather(state, "member", axis=0, tiled=True)
        sources = lax.dynamic_slice_in_dim(clone_src, group * per_dev, per_dev)
        state = jnp.take(piece, sources, axis=0, mode="clip")
        lay = Layout(3, per_dev)
        still = jnp.arange(per_dev * 3, dtype=jnp.int32)
        plan, _, _, *out, strips = first(lay, jnp.int32(0), still, state, kick, forcing)
        got, second = (*out[:2], *out[4:6]), (*out[2:4], *out[6:])
        sides = beside(strips)
    else:
        plan, index, following, *out, strips = first(lay, group, clone_src, state, kick, forcing)
        out, second = (*out[:2], *out[4:6]), (*out[2:4], *out[6:])
        kinds = [(a, b) for a in range(lay.kinds) for b in range(lay.kinds)]

        def opening(kind):
            return lambda a, b, c, d, strips: (*send(lay, kind, (a, b), (c, d)), beside(strips))

        ways = [lambda a, b, c, d, kind=kind: send(lay, kind, (a, b), (c, d)) for kind in kinds]

        def later(t, held):
            takes = plan[lay.takes : lay.place]
            sent = [lax.dynamic_index_in_dim(plan, lay.sends + 2 * t + n, keepdims=False) for n in range(2)]
            wanted = [lax.dynamic_index_in_dim(plan, lay.patterns + 2 * t + n, keepdims=False) for n in range(2)]
            out = [lax.dynamic_index_in_dim(x, j, keepdims=False) for x in (state, strips) for j in sent]
            got = lax.switch(wanted[0] * lay.kinds + wanted[1], ways, *out)
            kept = []
            for x in range(2):
                for i in range(per_dev):
                    up, down = takes[i] == 2 * t, takes[i] == 2 * t + 1
                    new = jnp.where(up, got[2 * x], got[2 * x + 1])
                    kept.append(jnp.where(up | down, new, held[2 * x + i]))
            return tuple(kept)

        *got, sides = lax.switch(index[0], [opening(kind) for kind in kinds], *out, strips)
        several = lambda *held: lax.fori_loop(1, plan[0], later, held)
        second = lax.switch(following[0], ways + [several], *second)

    assert per_dev == 2
    fields = (*got[:2], *second[:2])
    side, top, bottom = pack(lay, plan, state, fields, kick, forcing, sides, (*got[2:], *second[2:]))
    return plan[lay.place :], (state, *fields), side, top, bottom


def cut(rows, strip, v):
    strip = pltpu.roll(strip, lax.rem(LANES - 2 * HALO * v, LANES), 1)
    width = rows.shape[1]
    count = -(-width // SPAN)
    lane = lane_index((rows.shape[0], LANES))
    source = [rows[:, LANES * t : LANES * (t + 1)] for t in range(width // LANES)]
    tiles = []
    for c in range(count):
        first = SPAN * c - HALO
        if c == 0:
            tile = jnp.where(lane < HALO, strip, turn(source[0], HALO))
        else:
            t, offset = first // LANES, first % LANES
            if t + 1 < len(source):
                later = turn(source[t + 1], -offset)
            else:
                later = turn(strip, LANES - offset - HALO)
            tile = jnp.where(lane < LANES - offset, turn(source[t], -offset), later)
        tiles.append(tile)
    return tiles


def step_kernel(
    state_ref, up_ref, down_ref, second_up_ref, second_down_ref, kick_ref, forcing_ref, above_ref, below_ref, side_ref,
    coupling_ref, place_ref, lat_ref, out_ref, cells, other, source, result, table, stage, field, kicks, drive, done,
):
    members, variables, levels, height, width = state_ref.shape
    count = -(-width // SPAN)
    tall = height + 2 * HALO
    at_top = lat_ref[0] == 0
    at_bottom = lat_ref[0] == lat_ref[1] - 1
    options = options_of(state_ref, (up_ref, down_ref, second_up_ref, second_down_ref))

    def fetch(job, wait=False):
        k, m, slot = job // members, job % members, job % 2
        copies = [pltpu.make_async_copy(kick_ref.at[m, :, k], kicks.at[slot], done.at[2, slot])]
        if wait:
            copies.append(pltpu.make_async_copy(kick_ref.at[m, :, k], field.at[slot], done.at[1, slot]))
        else:
            for at, option in enumerate(options):

                @pl.when(place_ref[m] == at)
                def _():
                    pltpu.make_async_copy(option.at[:, k], field.at[slot], done.at[1, slot]).start()

        for copy in copies:
            copy.wait() if wait else copy.start()

        @pl.when(m == 0)
        def _():
            copy = pltpu.make_async_copy(forcing_ref.at[:, k], drive, done.at[3, 0])
            copy.wait() if wait else copy.start()

    def edge(ref, slot, k, v):
        tiles = width // LANES
        rows = [ref[slot, k, v * tiles + t] for t in range(tiles)]
        return jnp.concatenate(rows, axis=1), ref[slot, k, variables * tiles]

    def lay(rows, strip, v, target, at, scale):
        for c, tile in enumerate(cut(rows, strip, v)):
            target[c, v, at : at + rows.shape[0]] = tile if scale is None else tile * scale

    blocks = tall // ROWS
    pad = ROWS
    origin = lat_ref[2]

    def advance_tile(now, later, c, last):
        def tile(v, r):
            return now[c, v, pad + ROWS * r : pad + ROWS * (r + 1)]

        def shifted(v, r, d):
            return now[c, v, pl.ds(origin + pad + ROWS * r + d, ROWS)]

        for r in range(1, blocks - 1) if last else range(blocks):
            centre = [tile(v, r) for v in range(variables)]
            ku, kv = K * centre[0], K * centre[1]
            eu, ev = 8.0 * ku, 8.0 * kv
            along = 16.0 * K - eu, 16.0 * K + eu, ku - K, -K - ku
            across = 16.0 * K - ev, 16.0 * K + ev, kv - K, -K - kv
            for v in range(variables):
                q = centre[v]
                total = source[c, v, ROWS * r : ROWS * (r + 1)]
                for w in range(variables):
                    total += table[v * variables + w] * centre[w]
                near = along[0] * turn(q, -1) + along[1] * turn(q, 1)
                far = along[2] * turn(q, -2) + along[3] * turn(q, 2)
                near += across[0] * shifted(v, r, 1) + across[1] * shifted(v, r, -1)
                far += across[2] * shifted(v, r, 2) + across[3] * shifted(v, r, -2)
                total += near + far
                if last:
                    result[c, v, ROWS * (r - 1) : ROWS * r] = total
                elif r in (0, blocks - 1):
                    later[c, v, pad + ROWS * r : pad + ROWS * (r + 1)] = jnp.where(at_top if r == 0 else at_bottom, 0.0, total)
                else:
                    later[c, v, pad + ROWS * r : pad + ROWS * (r + 1)] = total

    fetch(0)

    @pl.loop(0, levels * members)
    def _(job):
        k, m, slot = job // members, job % members, job % 2
        @pl.loop(0, variables)
        def _(v):
            lay(*edge(above_ref, m, k, v), v, cells, pad, None)
            lay(*edge(below_ref, m, k, v), v, cells, pad + HALO + height, None)

        fetch(job, wait=True)

        @pl.loop(0, variables)
        def _(v):
            lay(field[slot, v] + kicks[slot, v], side_ref[m, k], v, cells, pad + HALO, None)

        @pl.when(m == 0)
        def _():
            @pl.loop(0, variables)
            def _(v):
                lay(*edge(above_ref, members, k, v), v, source, 0, 0.1)
                lay(drive[v], side_ref[members, k], v, source, HALO, 0.1)
                lay(*edge(below_ref, members, k, v), v, source, HALO + height, 0.1)
                for w in range(variables):
                    weight = 0.25 * coupling_ref[(k * variables + v) * variables + w]
                    weight = weight + jnp.where(v == w, 1.0 - 60.0 * K, 0.0)
                    table[v * variables + w] = jnp.full((ROWS, LANES), weight, jnp.float32)

        @pl.when(job + 1 < levels * members)
        def _():
            fetch(job + 1)

        for step in range(STEPS):
            now, later = (cells, other) if step % 2 == 0 else (other, cells)

            @pl.loop(0, count)
            def _(c):
                advance_tile(now, later, c, step == STEPS - 1)

        copy = pltpu.make_async_copy(stage.at[slot], out_ref.at[m, :, k], done.at[0, slot])
        pl.when(job >= 2)(copy.wait)
        lane = lane_index((height, LANES))

        @pl.loop(0, variables)
        def _(v):
            for t in range(width // LANES):
                c, offset = LANES * t // SPAN, LANES * t % SPAN
                left = turn(result[c, v], -(offset + HALO))
                if c + 1 < count:
                    right = turn(result[c + 1, v], SPAN - offset - HALO)
                    left = jnp.where(lane < SPAN - offset, left, right)
                stage[slot, v, :, LANES * t : LANES * (t + 1)] = left

        copy.start()

    for slot in range(2):
        pltpu.make_async_copy(stage.at[slot], out_ref.at[0, :, 0], done.at[0, slot]).wait()


def advance(place, sources, kick, forcing, above, below, side, coupling):
    members, variables, levels, height, width = kick.shape
    assert levels * members >= 2 and height % ROWS == 0 and HALO == ROWS
    count = -(-width // SPAN)
    tall = height + 2 * HALO
    lat = jnp.stack([lax.axis_index("lat"), jnp.int32(lax.axis_size("lat")), jnp.int32(0)])
    here, scalars, anywhere = spec(pltpu.VMEM), spec(pltpu.SMEM), spec(pl.ANY)
    block = (variables, height, width)
    state, *others = sources
    return pl.pallas_call(
        step_kernel,
        in_specs=[anywhere] * 7 + [here] * 3 + [scalars] * 3,
        out_specs=spec(pltpu.HBM),
        out_shape=jax.ShapeDtypeStruct(kick.shape, jnp.float32),
        scratch_shapes=[
            pltpu.VMEM((count, variables, tall + 2 * ROWS, LANES), jnp.float32),
            pltpu.VMEM((count, variables, tall + 2 * ROWS, LANES), jnp.float32),
            pltpu.VMEM((count, variables, tall, LANES), jnp.float32),
            pltpu.VMEM((count, variables, height, LANES), jnp.float32),
            pltpu.VMEM((variables * variables, ROWS, LANES), jnp.float32),
            pltpu.VMEM((2, *block), jnp.float32),
            pltpu.VMEM((2, *block), jnp.float32),
            pltpu.VMEM((2, *block), jnp.float32),
            pltpu.VMEM(block, jnp.float32),
            pltpu.SemaphoreType.DMA((4, 2)),
        ],
        compiler_params=pltpu.CompilerParams(vmem_limit_bytes=VMEM),
    )(
        far_away(state), *others, far_away(kick), far_away(forcing), above, below, side, coupling.reshape(-1), place, lat
    )


def shards(state, kick, forcing, coupling, clone_src):
    place, sources, side, top, bottom = prepared(state, kick, forcing, clone_src)
    above, below = neighbours(top, bottom)
    return advance(place, sources, kick, forcing, above, below, side, coupling)


def solution(mesh):
    in_specs = (
        P("member", None, None, "lat", "lon"),
        P("member", None, None, "lat", "lon"),
        P(None, None, "lat", "lon"),
        P(),
        P(),
    )
    out_specs = P("member", None, None, "lat", "lon")
    return jax.shard_map(shards, mesh=mesh, in_specs=in_specs, out_specs=out_specs, check_vma=False)
```

```python
import functools

import functools

import jax
import jax.numpy as jnp
import numpy as np
from jax import lax
from jax.experimental import pallas as pl
from jax.experimental.pallas import tpu as pltpu
from jax.sharding import PartitionSpec as P

STEPS = 4
REACH = 2
HALO = STEPS * REACH
LANES = 128
ROWS = 8
SPAN = LANES - 2 * HALO
K = 0.05 / 12.0
VMEM = 10 * 1024 * 1024
BY_MATMUL = (2, 3, 4)


def lane_index(shape):
    return lax.broadcasted_iota(jnp.int32, shape, len(shape) - 1)


def turn(x, shift):
    shift = shift % LANES
    return x if shift == 0 else pltpu.roll(x, shift, x.ndim - 1)


def chain(bits, groups):
    stops = [0] + [x for x in range(1, groups - 1) if bits >> (x - 1) & 1] + [groups - 1]
    return list(zip(stops[:-1], stops[1:]))


class Layout:
    def __init__(self, groups, per_dev):
        self.groups, self.per_dev = groups, per_dev
        self.most = per_dev * (groups - 1)
        self.patterns, self.sends = 1, 1 + 2 * self.most
        self.takes = self.sends + 2 * self.most
        self.place = self.takes + per_dev
        self.size = self.place + per_dev
        self.kinds = 1 + (1 << (groups - 2))


def plan_lines(lay, clone_ref, group_ref, plan_ref, index_refs, ends):
    groups, per_dev, most = lay.groups, lay.per_dev, lay.most
    me = group_ref[0]
    plan_ref[0] = 1
    for t in range(2 * most):
        plan_ref[lay.patterns + t] = 0
        plan_ref[lay.sends + t] = 0
    for i in range(per_dev):
        plan_ref[lay.takes + i] = -1 - clone_ref[me * per_dev + i] % per_dev

    for down in range(2):
        for t in range(most):
            ends[t] = 0
        for a in range(groups - 1):
            for b in range(a + 1, groups):
                source, target = (groups - 1 - a, groups - 1 - b) if down else (a, b)
                spans = sum(1 << (x - 1) for x in range(a + 1, b))
                for j in range(per_dev):
                    member = source * per_dev + j
                    wanted = [clone_ref[target * per_dev + i] == member for i in range(per_dev)]
                    need = functools.reduce(jnp.logical_or, wanted)

                    @pl.when(need)
                    def _():
                        t = jnp.int32(most - 1)
                        for earlier in reversed(range(most - 1)):
                            t = jnp.where(ends[earlier] <= a, earlier, t)
                        ends[t] = b
                        plan_ref[0] = jnp.maximum(plan_ref[0], t + 1)
                        at = 2 * t + down
                        before = plan_ref[lay.patterns + at]
                        bits = jnp.where(before == 0, lay.kinds - 2, before - 1)
                        plan_ref[lay.patterns + at] = 1 + (bits & ~spans)

                        @pl.when(me == source)
                        def _():
                            plan_ref[lay.sends + at] = j

                        for i in range(per_dev):

                            @pl.when((me == target) & wanted[i])
                            def _():
                                plan_ref[lay.takes + i] = at

    for t in range(2):
        index_refs[t][0] = plan_ref[lay.patterns + 2 * t] * lay.kinds + plan_ref[lay.patterns + 2 * t + 1]
    rounds = plan_ref[0]
    index_refs[1][0] = jnp.where(rounds > 2, lay.kinds * lay.kinds, index_refs[1][0])
    for i in range(per_dev):
        take = plan_ref[lay.takes + i]
        far = per_dev + jnp.where((take < 2) | (rounds == 2), take, 2 + i)
        plan_ref[lay.place + i] = jnp.where(take < 0, -1 - take, far)


def first_kernel(
    lay, clone_ref, group_ref, state_ref, kick_ref, forcing_ref, plan_ref, index_ref, second_ref, *refs
):
    fields, sides, strips_ref = refs[:4], refs[4:8], refs[8]
    sources, ends, held, kick_ends, forcing_ends, done = refs[-6:]
    members, variables, levels, height, width = state_ref.shape
    copies = [pltpu.make_async_copy(clone_ref, sources, done.at[0]), pltpu.make_async_copy(state_ref, held, done.at[1])]
    for side, at in enumerate((0, width - LANES)):
        for ref, part in ((kick_ref, kick_ends), (forcing_ref, forcing_ends)):
            piece = ref.at[(slice(None),) * (len(ref.shape) - 1) + (pl.ds(at, LANES),)]
            copies.append(pltpu.make_async_copy(piece, part.at[side], done.at[len(copies)]))
    for copy in copies:
        copy.start()
    copies[0].wait()
    plan_lines(lay, sources, group_ref, plan_ref, (index_ref, second_ref), ends)
    copies[1].wait()
    sent = [plan_ref[lay.sends + n] for n in range(4)]
    wanted = [plan_ref[lay.patterns + n] > 0 for n in range(4)]
    later = [pltpu.make_async_copy(held.at[sent[n]], fields[n], done.at[4 + n]) for n in (2, 3)]
    for n in range(2):
        pl.when(wanted[2 + n])(later[n].start)

        @pl.when(wanted[n])
        def _():
            @pl.loop(0, variables)
            def _(v):
                for k in range(levels):
                    fields[n][v, k] = held[sent[n], v, k]

    for copy in copies[2:]:
        copy.wait()
    lane = lane_index((height, LANES))

    @pl.loop(0, levels)
    def _(k):
        for slot in range(2 * members + 1):
            strip = jnp.zeros((height, LANES), jnp.float32)
            for v in range(variables):
                if slot < members:
                    low, high = (held[slot, v, k, :, at : at + LANES] for at in (0, width - LANES))
                elif slot < 2 * members:
                    low, high = (kick_ends[side, slot - members, v, k] for side in range(2))
                else:
                    low, high = (forcing_ends[side, v, k] for side in range(2))
                both = turn(jnp.where(lane < HALO, low, high), HALO + 2 * HALO * v)
                strip = jnp.where(lane >= 2 * HALO * v, both, strip)
            strips_ref[slot, k] = strip

    for ref, j in zip(sides, sent):
        ref[...] = strips_ref[j]
    for n in range(2):
        pl.when(wanted[2 + n])(later[n].wait)


def spec(space):
    return pl.BlockSpec(memory_space=space)


def first(lay, group, clone_src, state, kick, forcing):
    members, variables, levels, height, width = state.shape
    shape = jax.ShapeDtypeStruct
    one = pltpu.VMEM(state.shape[1:], jnp.float32)
    side = pltpu.VMEM((levels, height, LANES), jnp.float32)
    strips = pltpu.VMEM((2 * members + 1, levels, height, LANES), jnp.float32)
    ends = (2, members, variables, levels, height, LANES)
    scalar, here, far = spec(pltpu.SMEM), spec(pltpu.VMEM), spec(pltpu.HBM)
    return pl.pallas_call(
        functools.partial(first_kernel, lay),
        in_specs=[far, scalar, far, far, far],
        out_specs=[scalar] * 3 + [here] * 2 + [spec(pl.ANY)] * 2 + [here] * 5,
        out_shape=[shape((lay.size,), jnp.int32)] + [shape((1,), jnp.int32)] * 2 + [one] * 2 + [pltpu.HBM(state.shape[1:], jnp.float32)] * 2 + [side] * 4 + [strips],
        scratch_shapes=[
            pltpu.SMEM(clone_src.shape, jnp.int32),
            pltpu.SMEM((lay.most,), jnp.int32),
            pltpu.VMEM(state.shape, jnp.float32),
            pltpu.VMEM(ends, jnp.float32),
            pltpu.VMEM((2, *ends[2:]), jnp.float32),
            pltpu.SemaphoreType.DMA((8,)),
        ],
        compiler_params=pltpu.CompilerParams(vmem_limit_bytes=VMEM),
    )(far_away(clone_src), group[None], far_away(state), far_away(kick), far_away(forcing))


def far_away(x):
    return pltpu.with_memory_space_constraint(x, pltpu.HBM)


def edge_shape(members, forcing):
    variables, levels, height, width = forcing.shape
    return jax.ShapeDtypeStruct((members, levels, variables * width // LANES + 1, HALO, LANES), jnp.float32)


def options_of(state_ref, refs):
    return [state_ref.at[j] for j in range(state_ref.shape[0])] + list(refs)


def pack_kernel(
    lay, plan_ref, state_ref, up_ref, down_ref, second_up_ref, second_down_ref, kick_ref, forcing_ref,
    sides_ref, up_side_ref, down_side_ref, second_up_side_ref, second_down_side_ref,
    side_ref, top_ref, bottom_ref, field_rows, kick_rows, forcing_rows, done,
):
    members, variables, levels, height, width = state_ref.shape
    tiles = width // LANES
    whole = options_of(state_ref, (up_ref, down_ref, second_up_ref, second_down_ref))
    parts = options_of(sides_ref.at[:members], (up_side_ref, down_side_ref, second_up_side_ref, second_down_side_ref))
    places = [plan_ref[lay.place + i] for i in range(members)]
    rows = [pl.ds(0, HALO), pl.ds(height - HALO, HALO)]
    f_copies = [pltpu.make_async_copy(forcing_ref.at[:, :, rows[n]], forcing_rows.at[n], done.at[0]) for n in range(2)]
    copies = []
    for i in range(members):
        for n in range(2):
            for at, option in enumerate(whole):

                @pl.when(places[i] == at)
                def _():
                    pltpu.make_async_copy(option.at[:, :, rows[n]], field_rows.at[i, n], done.at[1 + i]).start()

            copies.append(pltpu.make_async_copy(kick_ref.at[i, :, :, rows[n]], kick_rows.at[i, n], done.at[1 + i]))
    for copy in copies + f_copies:
        copy.start()

    def flank(slot, k, strip):
        side_ref[slot, k] = strip
        top_ref[slot, k, variables * tiles] = strip[:HALO]
        bottom_ref[slot, k, variables * tiles] = strip[height - HALO :]

    def edges(slot, rows_of):
        @pl.loop(0, levels)
        def _(k):
            for n, ref in enumerate((top_ref, bottom_ref)):
                for v in range(variables):
                    edge = rows_of(n, v, k)
                    for t in range(tiles):
                        ref[slot, k, v * tiles + t] = edge[:, LANES * t : LANES * (t + 1)]

    for k in range(levels):
        flank(members, k, sides_ref[2 * members, k])
        for i in range(members):
            strip = parts[-1][k]
            for at in reversed(range(len(parts) - 1)):
                strip = jnp.where(places[i] == at, parts[at][k], strip)
            flank(i, k, strip + sides_ref[members + i, k])
    for copy in f_copies:
        copy.wait()
    edges(members, lambda n, v, k: forcing_rows[n, v, k])
    for i in range(members):
        for n in range(2):
            pltpu.make_async_copy(kick_ref.at[i, :, :, rows[n]], field_rows.at[i, n], done.at[1 + i]).wait()
            copies[2 * i + n].wait()
        edges(i, lambda n, v, k: field_rows[i, n, v, k] + kick_rows[i, n, v, k])


def pack(lay, plan, state, fields, kick, forcing, sides, far_sides):
    members, variables, levels, height, width = state.shape
    here, anywhere = spec(pltpu.VMEM), spec(pl.ANY)
    rows = (members, 2, variables, levels, HALO, width)
    return pl.pallas_call(
        functools.partial(pack_kernel, lay),
        in_specs=[spec(pltpu.SMEM)] + [anywhere] * 7 + [here] * 5,
        out_specs=[here] * 3,
        out_shape=[
            jax.ShapeDtypeStruct((members + 1, levels, height, LANES), jnp.float32),
            edge_shape(members + 1, forcing),
            edge_shape(members + 1, forcing),
        ],
        scratch_shapes=[
            pltpu.VMEM(rows, jnp.float32),
            pltpu.VMEM(rows, jnp.float32),
            pltpu.VMEM(rows[1:], jnp.float32),
            pltpu.SemaphoreType.DMA((1 + members,)),
        ],
        compiler_params=pltpu.CompilerParams(vmem_limit_bytes=VMEM),
    )(plan, far_away(state), *fields, far_away(kick), far_away(forcing), sides, *far_sides)


def blank(*like):
    return pl.pallas_call(
        lambda *refs: None,
        out_specs=[spec(pl.ANY)] * len(like),
        out_shape=[jax.ShapeDtypeStruct(x.shape, x.dtype) for x in like],
        compiler_params=pltpu.CompilerParams(vmem_limit_bytes=1024 * 1024),
    )()


def neighbours(top, bottom):
    lats = lax.axis_size("lat")
    above = lax.ppermute(bottom, "lat", [(i, i + 1) for i in range(lats - 1)])
    below = lax.ppermute(top, "lat", [(i + 1, i) for i in range(lats - 1)])
    return above, below


def beside(strips):
    assert lax.axis_size("lon") == 2
    return lax.ppermute(strips, "lon", [(0, 1), (1, 0)])


def send(lay, kinds, fields, sides):
    groups, lons = lay.groups, lax.axis_size("lon")
    fields, sides = list(fields), list(sides)
    for down, kind in enumerate(kinds):
        if kind:
            pairs = chain(kind - 1, groups)
            if down:
                pairs = [(groups - 1 - a, groups - 1 - b) for a, b in pairs]
            crossed = [(a * lons + j, b * lons + 1 - j) for a, b in pairs for j in range(lons)]
            fields[down] = lax.ppermute(fields[down], "member", pairs)
            sides[down] = lax.ppermute(sides[down], ("member", "lon"), crossed)
        else:
            fields[down], sides[down] = blank(fields[down], sides[down])
    return (*fields, *sides)


def prepared(state, kick, forcing, clone_src):
    per_dev, groups, group = state.shape[0], lax.axis_size("member"), lax.axis_index("member")
    lay = Layout(groups, per_dev)
    if groups != 4:
        piece = lax.all_gather(state, "member", axis=0, tiled=True)
        sources = lax.dynamic_slice_in_dim(clone_src, group * per_dev, per_dev)
        state = jnp.take(piece, sources, axis=0, mode="clip")
        lay = Layout(3, per_dev)
        still = jnp.arange(per_dev * 3, dtype=jnp.int32)
        plan, _, _, *out, strips = first(lay, jnp.int32(0), still, state, kick, forcing)
        got, second = (*out[:2], *out[4:6]), (*out[2:4], *out[6:])
        sides = beside(strips)
    else:
        plan, index, following, *out, strips = first(lay, group, clone_src, state, kick, forcing)
        out, second = (*out[:2], *out[4:6]), (*out[2:4], *out[6:])
        kinds = [(a, b) for a in range(lay.kinds) for b in range(lay.kinds)]

        def opening(kind):
            return lambda a, b, c, d, strips: (*send(lay, kind, (a, b), (c, d)), beside(strips))

        ways = [lambda a, b, c, d, kind=kind: send(lay, kind, (a, b), (c, d)) for kind in kinds]

        def later(t, held):
            takes = plan[lay.takes : lay.place]
            sent = [lax.dynamic_index_in_dim(plan, lay.sends + 2 * t + n, keepdims=False) for n in range(2)]
            wanted = [lax.dynamic_index_in_dim(plan, lay.patterns + 2 * t + n, keepdims=False) for n in range(2)]
            out = [lax.dynamic_index_in_dim(x, j, keepdims=False) for x in (state, strips) for j in sent]
            got = lax.switch(wanted[0] * lay.kinds + wanted[1], ways, *out)
            kept = []
            for x in range(2):
                for i in range(per_dev):
                    up, down = takes[i] == 2 * t, takes[i] == 2 * t + 1
                    new = jnp.where(up, got[2 * x], got[2 * x + 1])
                    kept.append(jnp.where(up | down, new, held[2 * x + i]))
            return tuple(kept)

        *got, sides = lax.switch(index[0], [opening(kind) for kind in kinds], *out, strips)
        several = lambda *held: lax.fori_loop(1, plan[0], later, held)
        second = lax.switch(following[0], ways + [several], *second)

    assert per_dev == 2
    fields = (*got[:2], *second[:2])
    side, top, bottom = pack(lay, plan, state, fields, kick, forcing, sides, (*got[2:], *second[2:]))
    return plan[lay.place :], (state, *fields), side, top, bottom


def cut(rows, strip, v):
    width = rows.shape[1]
    count = -(-width // SPAN)
    lane = lane_index((rows.shape[0], LANES))
    source = [rows[:, LANES * t : LANES * (t + 1)] for t in range(width // LANES)]
    tiles = []
    for c in range(count):
        first = SPAN * c - HALO
        if c == 0:
            tile = jnp.where(lane < HALO, turn(strip, -2 * HALO * v), turn(source[0], HALO))
        else:
            t, offset = first // LANES, first % LANES
            if t + 1 < len(source):
                later = turn(source[t + 1], -offset)
            else:
                later = turn(strip, LANES - offset - 2 * HALO * v - HALO)
            tile = jnp.where(lane < LANES - offset, turn(source[t], -offset), later)
        tiles.append(tile)
    return tiles


def band():
    half = np.zeros((LANES, 2 * LANES), np.float32)
    for j in range(LANES):
        for d, slope, bend in ((1, 8, 16), (-1, -8, 16), (2, -1, -1), (-2, 1, -1)):
            half[(j + d) % LANES, j] = slope
            half[(j + d) % LANES, LANES + j] = bend
    return np.concatenate([half, half])


def step_kernel(
    state_ref, up_ref, down_ref, second_up_ref, second_down_ref, kick_ref, forcing_ref, above_ref, below_ref, side_ref,
    band_ref, coupling_ref, place_ref, lat_ref, out_ref, cells, other, source, result, table, stage, field, kicks, drive, sums, done,
):
    members, variables, levels, height, width = state_ref.shape
    count = -(-width // SPAN)
    tall = height + 2 * HALO
    at_top = lat_ref[0] == 0
    at_bottom = lat_ref[0] == lat_ref[1] - 1
    options = options_of(state_ref, (up_ref, down_ref, second_up_ref, second_down_ref))

    def fetch(job, wait=False):
        k, m, slot = job // members, job % members, job % 2
        copies = [pltpu.make_async_copy(kick_ref.at[m, :, k], kicks.at[slot], done.at[2, slot])]
        if wait:
            copies.append(pltpu.make_async_copy(kick_ref.at[m, :, k], field.at[slot], done.at[1, slot]))
        else:
            for at, option in enumerate(options):

                @pl.when(place_ref[m] == at)
                def _():
                    pltpu.make_async_copy(option.at[:, k], field.at[slot], done.at[1, slot]).start()

        for copy in copies:
            copy.wait() if wait else copy.start()

        @pl.when(m == 0)
        def _():
            copy = pltpu.make_async_copy(forcing_ref.at[:, k], drive, done.at[3, 0])
            copy.wait() if wait else copy.start()

    def edge(ref, slot, k, v):
        tiles = width // LANES
        rows = [ref[slot, k, v * tiles + t] for t in range(tiles)]
        return jnp.concatenate(rows, axis=1), ref[slot, k, variables * tiles]

    def lay(rows, strip, v, target, at, scale):
        for c, tile in enumerate(cut(rows, strip, v)):
            target[c, v, at : at + rows.shape[0]] = tile if scale is None else tile * scale

    blocks = tall // ROWS
    pad = ROWS
    origin = lat_ref[2]

    def advance_tile(now, later, c, last):
        def tile(v, r):
            return now[c, v, pad + ROWS * r : pad + ROWS * (r + 1)]

        def shifted(v, r, d):
            return now[c, v, pl.ds(origin + pad + ROWS * r + d, ROWS)]

        first, span = (ROWS, height) if last else (0, tall)
        parts = []
        for v in BY_MATMUL:
            rows = now[c, v, pad + first : pad + first + span]
            high = rows.astype(jnp.bfloat16)
            rest = (rows - high.astype(jnp.float32)).astype(jnp.bfloat16)
            parts.append(jnp.concatenate([high, rest], axis=1))
        parts = jnp.concatenate(parts, axis=0)
        sums[: parts.shape[0]] = jnp.dot(parts, band_ref[...], preferred_element_type=jnp.float32)

        rolled = [v for v in range(variables) if v not in BY_MATMUL]
        order = [(r, group) for group in (rolled, BY_MATMUL) for r in (range(1, blocks - 1) if last else range(blocks))]
        for r, group in order:
            centre = [tile(v, r) for v in range(variables)]
            ku, kv = K * centre[0], K * centre[1]
            ev = 8.0 * kv
            across = 16.0 * K - ev, 16.0 * K + ev, kv - K, -K - kv
            if group is rolled:
                eu = 8.0 * ku
                along = 16.0 * K - eu, 16.0 * K + eu, ku - K, -K - ku
            for v in group:
                q = centre[v]
                total = source[c, v, ROWS * r : ROWS * (r + 1)]
                for w in range(variables):
                    total += table[v * variables + w] * centre[w]
                if group is rolled:
                    near = along[0] * turn(q, -1) + along[1] * turn(q, 1)
                    far = along[2] * turn(q, -2) + along[3] * turn(q, 2)
                else:
                    at = BY_MATMUL.index(v) * span + ROWS * r - first
                    near = K * sums[at : at + ROWS, LANES:]
                    far = -ku * sums[at : at + ROWS, :LANES]
                near += across[0] * shifted(v, r, 1) + across[1] * shifted(v, r, -1)
                far += across[2] * shifted(v, r, 2) + across[3] * shifted(v, r, -2)
                total += near + far
                if last:
                    result[c, v, ROWS * (r - 1) : ROWS * r] = total
                elif r in (0, blocks - 1):
                    edge_rows = jnp.where(at_top if r == 0 else at_bottom, 0.0, total)
                    later[c, v, pad + ROWS * r : pad + ROWS * (r + 1)] = edge_rows
                else:
                    later[c, v, pad + ROWS * r : pad + ROWS * (r + 1)] = total

    fetch(0)

    @pl.loop(0, levels * members)
    def _(job):
        k, m, slot = job // members, job % members, job % 2
        for v in range(variables):
            lay(*edge(above_ref, m, k, v), v, cells, pad, None)
            lay(*edge(below_ref, m, k, v), v, cells, pad + HALO + height, None)
        fetch(job, wait=True)
        for v in range(variables):
            lay(field[slot, v] + kicks[slot, v], side_ref[m, k], v, cells, pad + HALO, None)

        @pl.when(m == 0)
        def _():
            for v in range(variables):
                lay(*edge(above_ref, members, k, v), v, source, 0, 0.1)
                lay(drive[v], side_ref[members, k], v, source, HALO, 0.1)
                lay(*edge(below_ref, members, k, v), v, source, HALO + height, 0.1)
                for w in range(variables):
                    weight = 0.25 * coupling_ref[(k * variables + v) * variables + w]
                    weight = weight + (1.0 - 60.0 * K if v == w else 0.0)
                    table[v * variables + w] = jnp.full((ROWS, LANES), weight, jnp.float32)

        @pl.when(job + 1 < levels * members)
        def _():
            fetch(job + 1)

        @pl.loop(0, count)
        def _(c):
            for step in range(STEPS):
                now, later = (cells, other) if step % 2 == 0 else (other, cells)
                advance_tile(now, later, c, step == STEPS - 1)

        copy = pltpu.make_async_copy(stage.at[slot], out_ref.at[m, :, k], done.at[0, slot])
        pl.when(job >= 2)(copy.wait)
        lane = lane_index((height, LANES))
        for v in range(variables):
            for t in range(width // LANES):
                c, offset = LANES * t // SPAN, LANES * t % SPAN
                left = turn(result[c, v], -(offset + HALO))
                if c + 1 < count:
                    right = turn(result[c + 1, v], SPAN - offset - HALO)
                    left = jnp.where(lane < SPAN - offset, left, right)
                stage[slot, v, :, LANES * t : LANES * (t + 1)] = left
        copy.start()

    for slot in range(2):
        pltpu.make_async_copy(stage.at[slot], out_ref.at[0, :, 0], done.at[0, slot]).wait()


def advance(place, sources, kick, forcing, above, below, side, coupling):
    members, variables, levels, height, width = kick.shape
    assert levels * members >= 2 and height % ROWS == 0 and HALO == ROWS
    count = -(-width // SPAN)
    tall = height + 2 * HALO
    lat = jnp.stack([lax.axis_index("lat"), jnp.int32(lax.axis_size("lat")), jnp.int32(0)])
    here, scalars, anywhere = spec(pltpu.VMEM), spec(pltpu.SMEM), spec(pl.ANY)
    block = (variables, height, width)
    state, *others = sources
    return pl.pallas_call(
        step_kernel,
        in_specs=[anywhere] * 7 + [here] * 4 + [scalars] * 3,
        out_specs=spec(pltpu.HBM),
        out_shape=jax.ShapeDtypeStruct(kick.shape, jnp.float32),
        scratch_shapes=[
            pltpu.VMEM((count, variables, tall + 2 * ROWS, LANES), jnp.float32),
            pltpu.VMEM((count, variables, tall + 2 * ROWS, LANES), jnp.float32),
            pltpu.VMEM((count, variables, tall, LANES), jnp.float32),
            pltpu.VMEM((count, variables, height, LANES), jnp.float32),
            pltpu.VMEM((variables * variables, ROWS, LANES), jnp.float32),
            pltpu.VMEM((2, *block), jnp.float32),
            pltpu.VMEM((2, *block), jnp.float32),
            pltpu.VMEM((2, *block), jnp.float32),
            pltpu.VMEM(block, jnp.float32),
            pltpu.VMEM((len(BY_MATMUL) * tall, 2 * LANES), jnp.float32),
            pltpu.SemaphoreType.DMA((4, 2)),
        ],
        compiler_params=pltpu.CompilerParams(vmem_limit_bytes=VMEM),
    )(
        far_away(state), *others, far_away(kick), far_away(forcing), above, below, side,
        jnp.asarray(band(), jnp.bfloat16), coupling.reshape(-1), place, lat,
    )


def shards(state, kick, forcing, coupling, clone_src):
    place, sources, side, top, bottom = prepared(state, kick, forcing, clone_src)
    above, below = neighbours(top, bottom)
    return advance(place, sources, kick, forcing, above, below, side, coupling)


def solution(mesh):
    in_specs = (
        P("member", None, None, "lat", "lon"),
        P("member", None, None, "lat", "lon"),
        P(None, None, "lat", "lon"),
        P(),
        P(),
    )
    out_specs = P("member", None, None, "lat", "lon")
    return jax.shard_map(shards, mesh=mesh, in_specs=in_specs, out_specs=out_specs, check_vma=False)
```

```python
import functools

import functools

import jax
import jax.numpy as jnp
from jax import lax
from jax.experimental import pallas as pl
from jax.experimental.pallas import tpu as pltpu
from jax.sharding import PartitionSpec as P

STEPS = 4
REACH = 2
HALO = STEPS * REACH
LANES = 128
ROWS = 8
SPAN = LANES - 2 * HALO
K = 0.05 / 12.0
VMEM = 14 * 1024 * 1024


def lane_index(shape):
    return lax.broadcasted_iota(jnp.int32, shape, len(shape) - 1)


def turn(x, shift):
    shift = shift % LANES
    return x if shift == 0 else pltpu.roll(x, shift, x.ndim - 1)


def chain(bits, groups):
    stops = [0] + [x for x in range(1, groups - 1) if bits >> (x - 1) & 1] + [groups - 1]
    return list(zip(stops[:-1], stops[1:]))


class Layout:
    def __init__(self, groups, per_dev):
        self.groups, self.per_dev = groups, per_dev
        self.most = per_dev * (groups - 1)
        self.patterns, self.sends = 1, 1 + 2 * self.most
        self.takes = self.sends + 2 * self.most
        self.place = self.takes + per_dev
        self.size = self.place + per_dev
        self.kinds = 1 + (1 << (groups - 2))


def plan_lines(lay, clone_ref, group_ref, plan_ref, index_refs, ends):
    groups, per_dev, most = lay.groups, lay.per_dev, lay.most
    me = group_ref[0]
    plan_ref[0] = 1
    for t in range(2 * most):
        plan_ref[lay.patterns + t] = 0
        plan_ref[lay.sends + t] = 0
    for i in range(per_dev):
        plan_ref[lay.takes + i] = -1 - clone_ref[me * per_dev + i] % per_dev

    for down in range(2):
        for t in range(most):
            ends[t] = 0
        for a in range(groups - 1):
            for b in range(a + 1, groups):
                source, target = (groups - 1 - a, groups - 1 - b) if down else (a, b)
                spans = sum(1 << (x - 1) for x in range(a + 1, b))
                for j in range(per_dev):
                    member = source * per_dev + j
                    wanted = [clone_ref[target * per_dev + i] == member for i in range(per_dev)]
                    need = functools.reduce(jnp.logical_or, wanted)

                    @pl.when(need)
                    def _():
                        t = jnp.int32(most - 1)
                        for earlier in reversed(range(most - 1)):
                            t = jnp.where(ends[earlier] <= a, earlier, t)
                        ends[t] = b
                        plan_ref[0] = jnp.maximum(plan_ref[0], t + 1)
                        at = 2 * t + down
                        before = plan_ref[lay.patterns + at]
                        bits = jnp.where(before == 0, lay.kinds - 2, before - 1)
                        plan_ref[lay.patterns + at] = 1 + (bits & ~spans)

                        @pl.when(me == source)
                        def _():
                            plan_ref[lay.sends + at] = j

                        for i in range(per_dev):

                            @pl.when((me == target) & wanted[i])
                            def _():
                                plan_ref[lay.takes + i] = at

    for t in range(2):
        index_refs[t][0] = plan_ref[lay.patterns + 2 * t] * lay.kinds + plan_ref[lay.patterns + 2 * t + 1]
    rounds = plan_ref[0]
    index_refs[1][0] = jnp.where(rounds > 2, lay.kinds * lay.kinds, index_refs[1][0])
    for i in range(per_dev):
        take = plan_ref[lay.takes + i]
        far = per_dev + jnp.where((take < 2) | (rounds == 2), take, 2 + i)
        plan_ref[lay.place + i] = jnp.where(take < 0, -1 - take, far)


def first_kernel(
    lay, clone_ref, group_ref, state_ref, kick_ref, forcing_ref, plan_ref, index_ref, second_ref, *refs
):
    fields, sides, strips_ref = refs[:4], refs[4:8], refs[8]
    sources, ends, held, kick_ends, forcing_ends, done = refs[-6:]
    members, variables, levels, height, width = state_ref.shape
    copies = [pltpu.make_async_copy(clone_ref, sources, done.at[0]), pltpu.make_async_copy(state_ref, held, done.at[1])]
    for side, at in enumerate((0, width - LANES)):
        for ref, part in ((kick_ref, kick_ends), (forcing_ref, forcing_ends)):
            piece = ref.at[(slice(None),) * (len(ref.shape) - 1) + (pl.ds(at, LANES),)]
            copies.append(pltpu.make_async_copy(piece, part.at[side], done.at[len(copies)]))
    for copy in copies:
        copy.start()
    copies[0].wait()
    plan_lines(lay, sources, group_ref, plan_ref, (index_ref, second_ref), ends)
    copies[1].wait()
    sent = [plan_ref[lay.sends + n] for n in range(4)]
    wanted = [plan_ref[lay.patterns + n] > 0 for n in range(4)]
    later = [pltpu.make_async_copy(held.at[sent[n]], fields[n], done.at[4 + n]) for n in (2, 3)]
    for n in range(2):
        pl.when(wanted[2 + n])(later[n].start)

        @pl.when(wanted[n])
        def _():
            @pl.loop(0, variables)
            def _(v):
                for k in range(levels):
                    fields[n][v, k] = held[sent[n], v, k]

    for copy in copies[2:]:
        copy.wait()
    lane = lane_index((height, LANES))

    @pl.loop(0, levels)
    def _(k):
        for slot in range(2 * members + 1):
            strip = jnp.zeros((height, LANES), jnp.float32)
            for v in range(variables):
                if slot < members:
                    low, high = (held[slot, v, k, :, at : at + LANES] for at in (0, width - LANES))
                elif slot < 2 * members:
                    low, high = (kick_ends[side, slot - members, v, k] for side in range(2))
                else:
                    low, high = (forcing_ends[side, v, k] for side in range(2))
                both = turn(jnp.where(lane < HALO, low, high), HALO + 2 * HALO * v)
                strip = jnp.where(lane >= 2 * HALO * v, both, strip)
            strips_ref[slot, k] = strip

    for ref, j in zip(sides, sent):
        ref[...] = strips_ref[j]
    for n in range(2):
        pl.when(wanted[2 + n])(later[n].wait)


def spec(space):
    return pl.BlockSpec(memory_space=space)


def first(lay, group, clone_src, state, kick, forcing):
    members, variables, levels, height, width = state.shape
    shape = jax.ShapeDtypeStruct
    one = pltpu.VMEM(state.shape[1:], jnp.float32)
    side = pltpu.VMEM((levels, height, LANES), jnp.float32)
    strips = pltpu.VMEM((2 * members + 1, levels, height, LANES), jnp.float32)
    ends = (2, members, variables, levels, height, LANES)
    scalar, here, far = spec(pltpu.SMEM), spec(pltpu.VMEM), spec(pltpu.HBM)
    return pl.pallas_call(
        functools.partial(first_kernel, lay),
        in_specs=[far, scalar, far, far, far],
        out_specs=[scalar] * 3 + [here] * 2 + [spec(pl.ANY)] * 2 + [here] * 5,
        out_shape=[shape((lay.size,), jnp.int32)] + [shape((1,), jnp.int32)] * 2 + [one] * 2 + [pltpu.HBM(state.shape[1:], jnp.float32)] * 2 + [side] * 4 + [strips],
        scratch_shapes=[
            pltpu.SMEM(clone_src.shape, jnp.int32),
            pltpu.SMEM((lay.most,), jnp.int32),
            pltpu.VMEM(state.shape, jnp.float32),
            pltpu.VMEM(ends, jnp.float32),
            pltpu.VMEM((2, *ends[2:]), jnp.float32),
            pltpu.SemaphoreType.DMA((8,)),
        ],
        compiler_params=pltpu.CompilerParams(vmem_limit_bytes=VMEM),
    )(far_away(clone_src), group[None], far_away(state), far_away(kick), far_away(forcing))


def far_away(x):
    return pltpu.with_memory_space_constraint(x, pltpu.HBM)


def edge_shape(members, forcing):
    variables, levels, height, width = forcing.shape
    return jax.ShapeDtypeStruct((members, levels, variables * width // LANES + 1, HALO, LANES), jnp.float32)


def options_of(state_ref, refs):
    return [state_ref.at[j] for j in range(state_ref.shape[0])] + list(refs)


def pack_kernel(
    lay, plan_ref, state_ref, up_ref, down_ref, second_up_ref, second_down_ref, kick_ref, forcing_ref,
    sides_ref, up_side_ref, down_side_ref, second_up_side_ref, second_down_side_ref,
    side_ref, top_ref, bottom_ref, field_rows, kick_rows, forcing_rows, done,
):
    members, variables, levels, height, width = state_ref.shape
    tiles = width // LANES
    whole = options_of(state_ref, (up_ref, down_ref, second_up_ref, second_down_ref))
    parts = options_of(sides_ref.at[:members], (up_side_ref, down_side_ref, second_up_side_ref, second_down_side_ref))
    places = [plan_ref[lay.place + i] for i in range(members)]
    rows = [pl.ds(0, HALO), pl.ds(height - HALO, HALO)]
    f_copies = [pltpu.make_async_copy(forcing_ref.at[:, :, rows[n]], forcing_rows.at[n], done.at[0]) for n in range(2)]
    copies = []
    for i in range(members):
        for n in range(2):
            for at, option in enumerate(whole):

                @pl.when(places[i] == at)
                def _():
                    pltpu.make_async_copy(option.at[:, :, rows[n]], field_rows.at[i, n], done.at[1 + i]).start()

            copies.append(pltpu.make_async_copy(kick_ref.at[i, :, :, rows[n]], kick_rows.at[i, n], done.at[1 + i]))
    for copy in copies + f_copies:
        copy.start()

    def flank(slot, k, strip):
        side_ref[slot, k] = strip
        top_ref[slot, k, variables * tiles] = strip[:HALO]
        bottom_ref[slot, k, variables * tiles] = strip[height - HALO :]

    def edges(slot, rows_of):
        @pl.loop(0, levels)
        def _(k):
            for n, ref in enumerate((top_ref, bottom_ref)):
                for v in range(variables):
                    edge = rows_of(n, v, k)
                    for t in range(tiles):
                        ref[slot, k, v * tiles + t] = edge[:, LANES * t : LANES * (t + 1)]

    for k in range(levels):
        flank(members, k, sides_ref[2 * members, k])
        for i in range(members):
            strip = parts[-1][k]
            for at in reversed(range(len(parts) - 1)):
                strip = jnp.where(places[i] == at, parts[at][k], strip)
            flank(i, k, strip + sides_ref[members + i, k])
    for copy in f_copies:
        copy.wait()
    edges(members, lambda n, v, k: forcing_rows[n, v, k])
    for i in range(members):
        for n in range(2):
            pltpu.make_async_copy(kick_ref.at[i, :, :, rows[n]], field_rows.at[i, n], done.at[1 + i]).wait()
            copies[2 * i + n].wait()
        edges(i, lambda n, v, k: field_rows[i, n, v, k] + kick_rows[i, n, v, k])


def pack(lay, plan, state, fields, kick, forcing, sides, far_sides):
    members, variables, levels, height, width = state.shape
    here, anywhere = spec(pltpu.VMEM), spec(pl.ANY)
    rows = (members, 2, variables, levels, HALO, width)
    return pl.pallas_call(
        functools.partial(pack_kernel, lay),
        in_specs=[spec(pltpu.SMEM)] + [anywhere] * 7 + [here] * 5,
        out_specs=[here] * 3,
        out_shape=[
            jax.ShapeDtypeStruct((members + 1, levels, height, LANES), jnp.float32),
            edge_shape(members + 1, forcing),
            edge_shape(members + 1, forcing),
        ],
        scratch_shapes=[
            pltpu.VMEM(rows, jnp.float32),
            pltpu.VMEM(rows, jnp.float32),
            pltpu.VMEM(rows[1:], jnp.float32),
            pltpu.SemaphoreType.DMA((1 + members,)),
        ],
        compiler_params=pltpu.CompilerParams(vmem_limit_bytes=VMEM),
    )(plan, far_away(state), *fields, far_away(kick), far_away(forcing), sides, *far_sides)


def blank(*like):
    return pl.pallas_call(
        lambda *refs: None,
        out_specs=[spec(pl.ANY)] * len(like),
        out_shape=[jax.ShapeDtypeStruct(x.shape, x.dtype) for x in like],
        compiler_params=pltpu.CompilerParams(vmem_limit_bytes=1024 * 1024),
    )()


def neighbours(top, bottom):
    lats = lax.axis_size("lat")
    above = lax.ppermute(bottom, "lat", [(i, i + 1) for i in range(lats - 1)])
    below = lax.ppermute(top, "lat", [(i + 1, i) for i in range(lats - 1)])
    return above, below


def beside(strips):
    assert lax.axis_size("lon") == 2
    return lax.ppermute(strips, "lon", [(0, 1), (1, 0)])


def send(lay, kinds, fields, sides):
    groups, lons = lay.groups, lax.axis_size("lon")
    fields, sides = list(fields), list(sides)
    for down, kind in enumerate(kinds):
        if kind:
            pairs = chain(kind - 1, groups)
            if down:
                pairs = [(groups - 1 - a, groups - 1 - b) for a, b in pairs]
            crossed = [(a * lons + j, b * lons + 1 - j) for a, b in pairs for j in range(lons)]
            fields[down] = lax.ppermute(fields[down], "member", pairs)
            sides[down] = lax.ppermute(sides[down], ("member", "lon"), crossed)
        else:
            fields[down], sides[down] = blank(fields[down], sides[down])
    return (*fields, *sides)


def prepared(state, kick, forcing, clone_src):
    per_dev, groups, group = state.shape[0], lax.axis_size("member"), lax.axis_index("member")
    lay = Layout(groups, per_dev)
    if groups != 4:
        piece = lax.all_gather(state, "member", axis=0, tiled=True)
        sources = lax.dynamic_slice_in_dim(clone_src, group * per_dev, per_dev)
        state = jnp.take(piece, sources, axis=0, mode="clip")
        lay = Layout(3, per_dev)
        still = jnp.arange(per_dev * 3, dtype=jnp.int32)
        plan, _, _, *out, strips = first(lay, jnp.int32(0), still, state, kick, forcing)
        got, second = (*out[:2], *out[4:6]), (*out[2:4], *out[6:])
        sides = beside(strips)
    else:
        plan, index, following, *out, strips = first(lay, group, clone_src, state, kick, forcing)
        out, second = (*out[:2], *out[4:6]), (*out[2:4], *out[6:])
        kinds = [(a, b) for a in range(lay.kinds) for b in range(lay.kinds)]

        def opening(kind):
            return lambda a, b, c, d, strips: (*send(lay, kind, (a, b), (c, d)), beside(strips))

        ways = [lambda a, b, c, d, kind=kind: send(lay, kind, (a, b), (c, d)) for kind in kinds]

        def later(t, held):
            takes = plan[lay.takes : lay.place]
            sent = [lax.dynamic_index_in_dim(plan, lay.sends + 2 * t + n, keepdims=False) for n in range(2)]
            wanted = [lax.dynamic_index_in_dim(plan, lay.patterns + 2 * t + n, keepdims=False) for n in range(2)]
            out = [lax.dynamic_index_in_dim(x, j, keepdims=False) for x in (state, strips) for j in sent]
            got = lax.switch(wanted[0] * lay.kinds + wanted[1], ways, *out)
            kept = []
            for x in range(2):
                for i in range(per_dev):
                    up, down = takes[i] == 2 * t, takes[i] == 2 * t + 1
                    new = jnp.where(up, got[2 * x], got[2 * x + 1])
                    kept.append(jnp.where(up | down, new, held[2 * x + i]))
            return tuple(kept)

        *got, sides = lax.switch(index[0], [opening(kind) for kind in kinds], *out, strips)
        several = lambda *held: lax.fori_loop(1, plan[0], later, held)
        second = lax.switch(following[0], ways + [several], *second)

    assert per_dev == 2
    fields = (*got[:2], *second[:2])
    side, top, bottom = pack(lay, plan, state, fields, kick, forcing, sides, (*got[2:], *second[2:]))
    return plan[lay.place :], (state, *fields), side, top, bottom


def cut(rows, strip, v):
    width = rows.shape[1]
    count = -(-width // SPAN)
    lane = lane_index((rows.shape[0], LANES))
    source = [rows[:, LANES * t : LANES * (t + 1)] for t in range(width // LANES)]
    tiles = []
    for c in range(count):
        first = SPAN * c - HALO
        if c == 0:
            tile = jnp.where(lane < HALO, turn(strip, -2 * HALO * v), turn(source[0], HALO))
        else:
            t, offset = first // LANES, first % LANES
            if t + 1 < len(source):
                later = turn(source[t + 1], -offset)
            else:
                later = turn(strip, LANES - offset - 2 * HALO * v - HALO)
            tile = jnp.where(lane < LANES - offset, turn(source[t], -offset), later)
        tiles.append(tile)
    return tiles


def step_kernel(
    state_ref, up_ref, down_ref, second_up_ref, second_down_ref, kick_ref, forcing_ref, above_ref, below_ref, side_ref,
    coupling_ref, place_ref, lat_ref, out_ref, cells, other, source, result, table, stage, field, kicks, drive, done,
):
    members, variables, levels, height, width = state_ref.shape
    count = -(-width // SPAN)
    tall = height + 2 * HALO
    at_top = lat_ref[0] == 0
    at_bottom = lat_ref[0] == lat_ref[1] - 1
    options = options_of(state_ref, (up_ref, down_ref, second_up_ref, second_down_ref))

    def fetch(k, wait=()):
        slot = k % 2
        for m in wait or range(members):
            kick = pltpu.make_async_copy(kick_ref.at[m, :, k], kicks.at[slot, m], done.at[2, m])
            if wait:
                pltpu.make_async_copy(kick_ref.at[m, :, k], field.at[slot, m], done.at[1, m]).wait()
                kick.wait()
            else:
                for at, option in enumerate(options):

                    @pl.when(place_ref[m] == at)
                    def _():
                        pltpu.make_async_copy(option.at[:, k], field.at[slot, m], done.at[1, m]).start()

                kick.start()

    def driven(k):
        return pltpu.make_async_copy(forcing_ref.at[:, k], drive, done.at[3, 0])

    def edge(ref, slot, k, v):
        tiles = width // LANES
        rows = [ref[slot, k, v * tiles + t] for t in range(tiles)]
        return jnp.concatenate(rows, axis=1), ref[slot, k, variables * tiles]

    def lay(rows, strip, v, target, at, scale):
        for c, tile in enumerate(cut(rows, strip, v)):
            target[c, v, at : at + rows.shape[0]] = tile if scale is None else tile * scale

    blocks = tall // ROWS
    pad = ROWS
    origin = lat_ref[2]

    def advance_tile(now, later, c, last):
        for r in range(1, blocks - 1) if last else range(blocks):
            at = pad + ROWS * r
            centre, along, across = [], [], []
            for m in range(members):
                centre.append([now[m, c, v, at : at + ROWS] for v in range(variables)])
                ku, kv = K * centre[m][0], K * centre[m][1]
                eu, ev = 8.0 * ku, 8.0 * kv
                along.append((16.0 * K - eu, 16.0 * K + eu, ku - K, -K - ku))
                across.append((16.0 * K - ev, 16.0 * K + ev, kv - K, -K - kv))
            for v in range(variables):
                driving = source[c, v, ROWS * r : ROWS * (r + 1)]
                weights = [table[v * variables + w] for w in range(variables)]
                for m in range(members):
                    q = centre[m][v]
                    shifted = {d: now[m, c, v, pl.ds(origin + at + d, ROWS)] for d in (1, -1, 2, -2)}
                    total = driving
                    for w in range(variables):
                        total += weights[w] * centre[m][w]
                    near = along[m][0] * turn(q, -1) + along[m][1] * turn(q, 1)
                    far = along[m][2] * turn(q, -2) + along[m][3] * turn(q, 2)
                    near += across[m][0] * shifted[1] + across[m][1] * shifted[-1]
                    far += across[m][2] * shifted[2] + across[m][3] * shifted[-2]
                    total += near + far
                    if last:
                        result[m, c, v, ROWS * (r - 1) : ROWS * r] = total
                    elif r in (0, blocks - 1):
                        later[m, c, v, at : at + ROWS] = jnp.where(at_top if r == 0 else at_bottom, 0.0, total)
                    else:
                        later[m, c, v, at : at + ROWS] = total

    fetch(0)
    driven(0).start()

    @pl.loop(0, levels)
    def _(k):
        slot = k % 2
        for m in range(members):
            for v in range(variables):
                lay(*edge(above_ref, m, k, v), v, cells.at[m], pad, None)
                lay(*edge(below_ref, m, k, v), v, cells.at[m], pad + HALO + height, None)
        for v in range(variables):
            lay(*edge(above_ref, members, k, v), v, source, 0, 0.1)
            lay(*edge(below_ref, members, k, v), v, source, HALO + height, 0.1)
            for w in range(variables):
                weight = 0.25 * coupling_ref[(k * variables + v) * variables + w]
                weight = weight + (1.0 - 60.0 * K if v == w else 0.0)
                table[v * variables + w] = jnp.full((ROWS, LANES), weight, jnp.float32)
        for m in range(members):
            fetch(k, wait=(m,))
            for v in range(variables):
                lay(field[slot, m, v] + kicks[slot, m, v], side_ref[m, k], v, cells.at[m], pad + HALO, None)
        driven(k).wait()
        for v in range(variables):
            lay(drive[v], side_ref[members, k], v, source, HALO, 0.1)

        @pl.when(k + 1 < levels)
        def _():
            fetch(k + 1)
            driven(k + 1).start()

        @pl.loop(0, count)
        def _(c):
            for step in range(STEPS):
                now, later = (cells, other) if step % 2 == 0 else (other, cells)
                advance_tile(now, later, c, step == STEPS - 1)

        lane = lane_index((height, LANES))
        for m in range(members):
            copy = pltpu.make_async_copy(stage.at[m], out_ref.at[m, :, k], done.at[0, m])
            pl.when(k > 0)(copy.wait)
            for v in range(variables):
                for t in range(width // LANES):
                    c, offset = LANES * t // SPAN, LANES * t % SPAN
                    left = turn(result[m, c, v], -(offset + HALO))
                    if c + 1 < count:
                        right = turn(result[m, c + 1, v], SPAN - offset - HALO)
                        left = jnp.where(lane < SPAN - offset, left, right)
                    stage[m, v, :, LANES * t : LANES * (t + 1)] = left
            copy.start()

    for m in range(members):
        pltpu.make_async_copy(stage.at[m], out_ref.at[m, :, 0], done.at[0, m]).wait()


def advance(place, sources, kick, forcing, above, below, side, coupling):
    members, variables, levels, height, width = kick.shape
    assert height % ROWS == 0 and HALO == ROWS
    count = -(-width // SPAN)
    tall = height + 2 * HALO
    lat = jnp.stack([lax.axis_index("lat"), jnp.int32(lax.axis_size("lat")), jnp.int32(0)])
    here, scalars, anywhere = spec(pltpu.VMEM), spec(pltpu.SMEM), spec(pl.ANY)
    block = (variables, height, width)
    state, *others = sources
    return pl.pallas_call(
        step_kernel,
        in_specs=[anywhere] * 7 + [here] * 3 + [scalars] * 3,
        out_specs=spec(pltpu.HBM),
        out_shape=jax.ShapeDtypeStruct(kick.shape, jnp.float32),
        scratch_shapes=[
            pltpu.VMEM((members, count, variables, tall + 2 * ROWS, LANES), jnp.float32),
            pltpu.VMEM((members, count, variables, tall + 2 * ROWS, LANES), jnp.float32),
            pltpu.VMEM((count, variables, tall, LANES), jnp.float32),
            pltpu.VMEM((members, count, variables, height, LANES), jnp.float32),
            pltpu.VMEM((variables * variables, ROWS, LANES), jnp.float32),
            pltpu.VMEM((members, *block), jnp.float32),
            pltpu.VMEM((2, members, *block), jnp.float32),
            pltpu.VMEM((2, members, *block), jnp.float32),
            pltpu.VMEM(block, jnp.float32),
            pltpu.SemaphoreType.DMA((4, members)),
        ],
        compiler_params=pltpu.CompilerParams(vmem_limit_bytes=VMEM),
    )(
        far_away(state), *others, far_away(kick), far_away(forcing), above, below, side, coupling.reshape(-1), place, lat
    )


def shards(state, kick, forcing, coupling, clone_src):
    place, sources, side, top, bottom = prepared(state, kick, forcing, clone_src)
    above, below = neighbours(top, bottom)
    return advance(place, sources, kick, forcing, above, below, side, coupling)


def solution(mesh):
    in_specs = (
        P("member", None, None, "lat", "lon"),
        P("member", None, None, "lat", "lon"),
        P(None, None, "lat", "lon"),
        P(),
        P(),
    )
    out_specs = P("member", None, None, "lat", "lon")
    return jax.shard_map(shards, mesh=mesh, in_specs=in_specs, out_specs=out_specs, check_vma=False)
```

```python
import functools

import functools

import jax
import jax.numpy as jnp
from jax import lax
from jax.experimental import pallas as pl
from jax.experimental.pallas import tpu as pltpu
from jax.sharding import PartitionSpec as P

STEPS = 4
REACH = 2
HALO = STEPS * REACH
LANES = 128
ROWS = 8
SPAN = LANES - 2 * HALO
K = 0.05 / 12.0
VMEM = 14 * 1024 * 1024


def lane_index(shape):
    return lax.broadcasted_iota(jnp.int32, shape, len(shape) - 1)


def turn(x, shift):
    shift = shift % LANES
    return x if shift == 0 else pltpu.roll(x, shift, x.ndim - 1)


def chain(bits, groups):
    stops = [0] + [x for x in range(1, groups - 1) if bits >> (x - 1) & 1] + [groups - 1]
    return list(zip(stops[:-1], stops[1:]))


class Layout:
    def __init__(self, groups, per_dev):
        self.groups, self.per_dev = groups, per_dev
        self.most = per_dev * (groups - 1)
        self.patterns, self.sends = 1, 1 + 2 * self.most
        self.takes = self.sends + 2 * self.most
        self.place = self.takes + per_dev
        self.size = self.place + per_dev
        self.kinds = 1 + (1 << (groups - 2))


def plan_lines(lay, clone_ref, group_ref, plan_ref, index_refs, ends):
    groups, per_dev, most = lay.groups, lay.per_dev, lay.most
    me = group_ref[0]
    plan_ref[0] = 1
    for t in range(2 * most):
        plan_ref[lay.patterns + t] = 0
        plan_ref[lay.sends + t] = 0
    for i in range(per_dev):
        plan_ref[lay.takes + i] = -1 - clone_ref[me * per_dev + i] % per_dev

    for down in range(2):
        for t in range(most):
            ends[t] = 0
        for a in range(groups - 1):
            for b in range(a + 1, groups):
                source, target = (groups - 1 - a, groups - 1 - b) if down else (a, b)
                spans = sum(1 << (x - 1) for x in range(a + 1, b))
                for j in range(per_dev):
                    member = source * per_dev + j
                    wanted = [clone_ref[target * per_dev + i] == member for i in range(per_dev)]
                    need = functools.reduce(jnp.logical_or, wanted)

                    @pl.when(need)
                    def _():
                        t = jnp.int32(most - 1)
                        for earlier in reversed(range(most - 1)):
                            t = jnp.where(ends[earlier] <= a, earlier, t)
                        ends[t] = b
                        plan_ref[0] = jnp.maximum(plan_ref[0], t + 1)
                        at = 2 * t + down
                        before = plan_ref[lay.patterns + at]
                        bits = jnp.where(before == 0, lay.kinds - 2, before - 1)
                        plan_ref[lay.patterns + at] = 1 + (bits & ~spans)

                        @pl.when(me == source)
                        def _():
                            plan_ref[lay.sends + at] = j

                        for i in range(per_dev):

                            @pl.when((me == target) & wanted[i])
                            def _():
                                plan_ref[lay.takes + i] = at

    for t in range(2):
        index_refs[t][0] = plan_ref[lay.patterns + 2 * t] * lay.kinds + plan_ref[lay.patterns + 2 * t + 1]
    rounds = plan_ref[0]
    index_refs[1][0] = jnp.where(rounds > 2, lay.kinds * lay.kinds, index_refs[1][0])
    for i in range(per_dev):
        take = plan_ref[lay.takes + i]
        far = per_dev + jnp.where((take < 2) | (rounds == 2), take, 2 + i)
        plan_ref[lay.place + i] = jnp.where(take < 0, -1 - take, far)


def first_kernel(
    lay, clone_ref, group_ref, state_ref, kick_ref, forcing_ref, plan_ref, index_ref, second_ref, *refs
):
    fields, sides, strips_ref = refs[:4], refs[4:8], refs[8]
    sources, ends, held, kick_ends, forcing_ends, done = refs[-6:]
    members, variables, levels, height, width = state_ref.shape
    copies = [pltpu.make_async_copy(clone_ref, sources, done.at[0]), pltpu.make_async_copy(state_ref, held, done.at[1])]
    for side, at in enumerate((0, width - LANES)):
        for ref, part in ((kick_ref, kick_ends), (forcing_ref, forcing_ends)):
            piece = ref.at[(slice(None),) * (len(ref.shape) - 1) + (pl.ds(at, LANES),)]
            copies.append(pltpu.make_async_copy(piece, part.at[side], done.at[len(copies)]))
    for copy in copies:
        copy.start()
    copies[0].wait()
    plan_lines(lay, sources, group_ref, plan_ref, (index_ref, second_ref), ends)
    copies[1].wait()
    sent = [plan_ref[lay.sends + n] for n in range(4)]
    wanted = [plan_ref[lay.patterns + n] > 0 for n in range(4)]
    later = [pltpu.make_async_copy(held.at[sent[n]], fields[n], done.at[4 + n]) for n in (2, 3)]
    for n in range(2):
        pl.when(wanted[2 + n])(later[n].start)

        @pl.when(wanted[n])
        def _():
            @pl.loop(0, variables)
            def _(v):
                for k in range(levels):
                    fields[n][v, k] = held[sent[n], v, k]

    for copy in copies[2:]:
        copy.wait()
    lane = lane_index((height, LANES))

    @pl.loop(0, levels)
    def _(k):
        for slot in range(2 * members + 1):
            strip = jnp.zeros((height, LANES), jnp.float32)
            for v in range(variables):
                if slot < members:
                    low, high = (held[slot, v, k, :, at : at + LANES] for at in (0, width - LANES))
                elif slot < 2 * members:
                    low, high = (kick_ends[side, slot - members, v, k] for side in range(2))
                else:
                    low, high = (forcing_ends[side, v, k] for side in range(2))
                both = turn(jnp.where(lane < HALO, low, high), HALO + 2 * HALO * v)
                strip = jnp.where(lane >= 2 * HALO * v, both, strip)
            strips_ref[slot, k] = strip

    for ref, j in zip(sides, sent):
        ref[...] = strips_ref[j]
    for n in range(2):
        pl.when(wanted[2 + n])(later[n].wait)


def spec(space):
    return pl.BlockSpec(memory_space=space)


def first(lay, group, clone_src, state, kick, forcing):
    members, variables, levels, height, width = state.shape
    shape = jax.ShapeDtypeStruct
    one = pltpu.VMEM(state.shape[1:], jnp.float32)
    side = pltpu.VMEM((levels, height, LANES), jnp.float32)
    strips = pltpu.VMEM((2 * members + 1, levels, height, LANES), jnp.float32)
    ends = (2, members, variables, levels, height, LANES)
    scalar, here, far = spec(pltpu.SMEM), spec(pltpu.VMEM), spec(pltpu.HBM)
    return pl.pallas_call(
        functools.partial(first_kernel, lay),
        in_specs=[far, scalar, far, far, far],
        out_specs=[scalar] * 3 + [here] * 2 + [spec(pl.ANY)] * 2 + [here] * 5,
        out_shape=[shape((lay.size,), jnp.int32)] + [shape((1,), jnp.int32)] * 2 + [one] * 2 + [pltpu.HBM(state.shape[1:], jnp.float32)] * 2 + [side] * 4 + [strips],
        scratch_shapes=[
            pltpu.SMEM(clone_src.shape, jnp.int32),
            pltpu.SMEM((lay.most,), jnp.int32),
            pltpu.VMEM(state.shape, jnp.float32),
            pltpu.VMEM(ends, jnp.float32),
            pltpu.VMEM((2, *ends[2:]), jnp.float32),
            pltpu.SemaphoreType.DMA((8,)),
        ],
        compiler_params=pltpu.CompilerParams(vmem_limit_bytes=VMEM),
    )(far_away(clone_src), group[None], far_away(state), far_away(kick), far_away(forcing))


def far_away(x):
    return pltpu.with_memory_space_constraint(x, pltpu.HBM)


def edge_shape(members, forcing):
    variables, levels, height, width = forcing.shape
    return jax.ShapeDtypeStruct((members, levels, variables * width // LANES + 1, HALO, LANES), jnp.float32)


def options_of(state_ref, refs):
    return [state_ref.at[j] for j in range(state_ref.shape[0])] + list(refs)


def pack_kernel(
    lay, plan_ref, state_ref, up_ref, down_ref, second_up_ref, second_down_ref, kick_ref, forcing_ref,
    sides_ref, up_side_ref, down_side_ref, second_up_side_ref, second_down_side_ref,
    side_ref, top_ref, bottom_ref, field_rows, kick_rows, forcing_rows, strips, picked, done,
):
    members, variables, levels, height, width = state_ref.shape
    tiles = width // LANES
    whole = options_of(state_ref, (up_ref, down_ref, second_up_ref, second_down_ref))
    parts = [sides_ref.at[j] for j in range(members)]
    parts += [up_side_ref, down_side_ref, second_up_side_ref, second_down_side_ref]
    places = [plan_ref[lay.place + i] for i in range(members)]
    rows = [pl.ds(0, HALO), pl.ds(height - HALO, HALO)]
    f_copies = [pltpu.make_async_copy(forcing_ref.at[:, :, rows[n]], forcing_rows.at[n], done.at[0]) for n in range(2)]
    copies = []
    for i in range(members):
        for n in range(2):
            for at, option in enumerate(whole):

                @pl.when(places[i] == at)
                def _():
                    pltpu.make_async_copy(option.at[:, :, rows[n]], field_rows.at[i, n], done.at[1 + i]).start()

            copies.append(pltpu.make_async_copy(kick_ref.at[i, :, :, rows[n]], kick_rows.at[i, n], done.at[1 + i]))
    strip_copies = [pltpu.make_async_copy(sides_ref, strips, done.at[1 + members])]
    for i in range(members):
        for at, part in enumerate(parts):

            @pl.when(places[i] == at)
            def _():
                pltpu.make_async_copy(part, picked.at[i], done.at[2 + members + i]).start()

        strip_copies.append(pltpu.make_async_copy(up_side_ref, picked.at[i], done.at[2 + members + i]))
    for copy in [strip_copies[0]] + f_copies + copies:
        copy.start()

    def flank(slot, k, strip):
        side_ref[slot, k] = strip
        top_ref[slot, k, variables * tiles] = strip[:HALO]
        bottom_ref[slot, k, variables * tiles] = strip[height - HALO :]

    def edges(slot, rows_of):
        @pl.loop(0, levels)
        def _(k):
            for n, ref in enumerate((top_ref, bottom_ref)):
                for v in range(variables):
                    edge = rows_of(n, v, k)
                    for t in range(tiles):
                        ref[slot, k, v * tiles + t] = edge[:, LANES * t : LANES * (t + 1)]

    for copy in strip_copies:
        copy.wait()
    for k in range(levels):
        flank(members, k, strips[2 * members, k])
        for i in range(members):
            flank(i, k, picked[i, k] + strips[members + i, k])
    for copy in f_copies:
        copy.wait()
    edges(members, lambda n, v, k: forcing_rows[n, v, k])
    for i in range(members):
        for n in range(2):
            pltpu.make_async_copy(kick_ref.at[i, :, :, rows[n]], field_rows.at[i, n], done.at[1 + i]).wait()
            copies[2 * i + n].wait()
        edges(i, lambda n, v, k: field_rows[i, n, v, k] + kick_rows[i, n, v, k])


def pack(lay, plan, state, fields, kick, forcing, sides, far_sides):
    members, variables, levels, height, width = state.shape
    here, anywhere = spec(pltpu.VMEM), spec(pl.ANY)
    rows = (members, 2, variables, levels, HALO, width)
    return pl.pallas_call(
        functools.partial(pack_kernel, lay),
        in_specs=[spec(pltpu.SMEM)] + [anywhere] * 12,
        out_specs=[here] * 3,
        out_shape=[
            jax.ShapeDtypeStruct((members + 1, levels, height, LANES), jnp.float32),
            edge_shape(members + 1, forcing),
            edge_shape(members + 1, forcing),
        ],
        scratch_shapes=[
            pltpu.VMEM(rows, jnp.float32),
            pltpu.VMEM(rows, jnp.float32),
            pltpu.VMEM(rows[1:], jnp.float32),
            pltpu.VMEM(sides.shape, jnp.float32),
            pltpu.VMEM((members, levels, height, LANES), jnp.float32),
            pltpu.SemaphoreType.DMA((2 + 2 * members,)),
        ],
        compiler_params=pltpu.CompilerParams(vmem_limit_bytes=VMEM),
    )(plan, far_away(state), *fields, far_away(kick), far_away(forcing), sides, *far_sides)


def blank(*like):
    return pl.pallas_call(
        lambda *refs: None,
        out_specs=[spec(pl.ANY)] * len(like),
        out_shape=[jax.ShapeDtypeStruct(x.shape, x.dtype) for x in like],
        compiler_params=pltpu.CompilerParams(vmem_limit_bytes=1024 * 1024),
    )()


def neighbours(top, bottom):
    lats = lax.axis_size("lat")
    above = lax.ppermute(bottom, "lat", [(i, i + 1) for i in range(lats - 1)])
    below = lax.ppermute(top, "lat", [(i + 1, i) for i in range(lats - 1)])
    return above, below


def beside(strips):
    assert lax.axis_size("lon") == 2
    return lax.ppermute(strips, "lon", [(0, 1), (1, 0)])


def send(lay, kinds, fields, sides):
    groups, lons = lay.groups, lax.axis_size("lon")
    fields, sides = list(fields), list(sides)
    for down, kind in enumerate(kinds):
        if kind:
            pairs = chain(kind - 1, groups)
            if down:
                pairs = [(groups - 1 - a, groups - 1 - b) for a, b in pairs]
            crossed = [(a * lons + j, b * lons + 1 - j) for a, b in pairs for j in range(lons)]
            fields[down] = lax.ppermute(fields[down], "member", pairs)
            sides[down] = lax.ppermute(sides[down], ("member", "lon"), crossed)
        else:
            fields[down], sides[down] = blank(fields[down], sides[down])
    return (*fields, *sides)


def prepared(state, kick, forcing, clone_src):
    per_dev, groups, group = state.shape[0], lax.axis_size("member"), lax.axis_index("member")
    lay = Layout(groups, per_dev)
    if groups != 4:
        piece = lax.all_gather(state, "member", axis=0, tiled=True)
        sources = lax.dynamic_slice_in_dim(clone_src, group * per_dev, per_dev)
        state = jnp.take(piece, sources, axis=0, mode="clip")
        lay = Layout(3, per_dev)
        still = jnp.arange(per_dev * 3, dtype=jnp.int32)
        plan, _, _, *out, strips = first(lay, jnp.int32(0), still, state, kick, forcing)
        got, second = (*out[:2], *out[4:6]), (*out[2:4], *out[6:])
        sides = beside(strips)
    else:
        plan, index, following, *out, strips = first(lay, group, clone_src, state, kick, forcing)
        out, second = (*out[:2], *out[4:6]), (*out[2:4], *out[6:])
        kinds = [(a, b) for a in range(lay.kinds) for b in range(lay.kinds)]

        def opening(kind):
            return lambda a, b, c, d, strips: (*send(lay, kind, (a, b), (c, d)), beside(strips))

        ways = [lambda a, b, c, d, kind=kind: send(lay, kind, (a, b), (c, d)) for kind in kinds]

        def later(t, held):
            takes = plan[lay.takes : lay.place]
            sent = [lax.dynamic_index_in_dim(plan, lay.sends + 2 * t + n, keepdims=False) for n in range(2)]
            wanted = [lax.dynamic_index_in_dim(plan, lay.patterns + 2 * t + n, keepdims=False) for n in range(2)]
            out = [lax.dynamic_index_in_dim(x, j, keepdims=False) for x in (state, strips) for j in sent]
            got = lax.switch(wanted[0] * lay.kinds + wanted[1], ways, *out)
            kept = []
            for x in range(2):
                for i in range(per_dev):
                    up, down = takes[i] == 2 * t, takes[i] == 2 * t + 1
                    new = jnp.where(up, got[2 * x], got[2 * x + 1])
                    kept.append(jnp.where(up | down, new, held[2 * x + i]))
            return tuple(kept)

        *got, sides = lax.switch(index[0], [opening(kind) for kind in kinds], *out, strips)
        several = lambda *held: lax.fori_loop(1, plan[0], later, held)
        second = lax.switch(following[0], ways + [several], *second)

    assert per_dev == 2
    fields = (*got[:2], *second[:2])
    side, top, bottom = pack(lay, plan, state, fields, kick, forcing, sides, (*got[2:], *second[2:]))
    return plan[lay.place :], (state, *fields), side, top, bottom


def cut(rows, strip, v):
    width = rows.shape[1]
    count = -(-width // SPAN)
    lane = lane_index((rows.shape[0], LANES))
    source = [rows[:, LANES * t : LANES * (t + 1)] for t in range(width // LANES)]
    tiles = []
    for c in range(count):
        first = SPAN * c - HALO
        if c == 0:
            tile = jnp.where(lane < HALO, turn(strip, -2 * HALO * v), turn(source[0], HALO))
        else:
            t, offset = first // LANES, first % LANES
            if t + 1 < len(source):
                later = turn(source[t + 1], -offset)
            else:
                later = turn(strip, LANES - offset - 2 * HALO * v - HALO)
            tile = jnp.where(lane < LANES - offset, turn(source[t], -offset), later)
        tiles.append(tile)
    return tiles


def step_kernel(
    state_ref, up_ref, down_ref, second_up_ref, second_down_ref, kick_ref, forcing_ref, above_ref, below_ref, side_ref,
    coupling_ref, place_ref, lat_ref, out_ref, cells, other, source, result, table, stage, field, kicks, drive, done,
):
    members, variables, levels, height, width = state_ref.shape
    count = -(-width // SPAN)
    tall = height + 2 * HALO
    at_top = lat_ref[0] == 0
    at_bottom = lat_ref[0] == lat_ref[1] - 1
    options = options_of(state_ref, (up_ref, down_ref, second_up_ref, second_down_ref))

    def fetch(k, wait=()):
        slot = k % 2
        for m in wait or range(members):
            kick = pltpu.make_async_copy(kick_ref.at[m, :, k], kicks.at[slot, m], done.at[2, m])
            if wait:
                pltpu.make_async_copy(kick_ref.at[m, :, k], field.at[slot, m], done.at[1, m]).wait()
                kick.wait()
            else:
                for at, option in enumerate(options):

                    @pl.when(place_ref[m] == at)
                    def _():
                        pltpu.make_async_copy(option.at[:, k], field.at[slot, m], done.at[1, m]).start()

                kick.start()

    def leave(k, m=None, v=None, wait=False):
        if wait:
            for m in range(members):
                pltpu.make_async_copy(stage.at[m], out_ref.at[m, :, k], done.at[0, m]).wait()
        else:
            pltpu.make_async_copy(stage.at[m, v], out_ref.at[m, v, k], done.at[0, m]).start()

    def driven(k):
        return pltpu.make_async_copy(forcing_ref.at[:, k], drive, done.at[3, 0])

    def edge(ref, slot, k, v):
        tiles = width // LANES
        rows = [ref[slot, k, v * tiles + t] for t in range(tiles)]
        return jnp.concatenate(rows, axis=1), ref[slot, k, variables * tiles]

    def lay(rows, strip, v, target, at, scale):
        for c, tile in enumerate(cut(rows, strip, v)):
            target[c, v, at : at + rows.shape[0]] = tile if scale is None else tile * scale

    blocks = tall // ROWS
    pad = ROWS
    origin = lat_ref[2]

    line = lax.broadcasted_iota(jnp.int32, (ROWS, LANES), 0)
    north, south = range(blocks)[0], range(blocks)[-1]

    def advance_tile(step, now, later, c):
        last = step == STEPS - 1
        shared = 0 < step < STEPS - 1
        assert HALO - REACH * 2 <= ROWS // 2

        def load(ref, m, v, r, d=0):
            at = pad + ROWS * r
            return ref[m, c, v, at : at + ROWS] if d == 0 else ref[m, c, v, pl.ds(origin + at + d, ROWS)]

        def view(get, r):
            return jnp.where(line < ROWS // 2, get(south), get(north)) if r is None else get(r)

        inner = list(range(1, blocks - 1))
        for r in inner if last else [None] + inner if shared else range(blocks):
            centre, along, across = [], [], []
            for m in range(members):
                centre.append([view(lambda r: load(now, m, v, r), r) for v in range(variables)])
                ku, kv = K * centre[m][0], K * centre[m][1]
                eu, ev = 8.0 * ku, 8.0 * kv
                along.append((16.0 * K - eu, 16.0 * K + eu, ku - K, -K - ku))
                across.append((16.0 * K - ev, 16.0 * K + ev, kv - K, -K - kv))
            for v in range(variables):
                driving = view(lambda r: source[c, v, ROWS * r : ROWS * (r + 1)], r)
                weights = [table[v * variables + w] for w in range(variables)]
                for m in range(members):
                    q = centre[m][v]
                    shifted = {d: view(lambda r: load(now, m, v, r, d), r) for d in (1, -1, 2, -2)}
                    total = driving
                    for w in range(variables):
                        total += weights[w] * centre[m][w]
                    near = along[m][0] * turn(q, -1) + along[m][1] * turn(q, 1)
                    far = along[m][2] * turn(q, -2) + along[m][3] * turn(q, 2)
                    near += across[m][0] * shifted[1] + across[m][1] * shifted[-1]
                    far += across[m][2] * shifted[2] + across[m][3] * shifted[-2]
                    total += near + far
                    if last:
                        result[m, c, v, ROWS * (r - 1) : ROWS * r] = total
                        continue
                    for to, outside in ((north, at_top), (south, at_bottom)):
                        if r is None or r == to:
                            at = pad + ROWS * to
                            later[m, c, v, at : at + ROWS] = jnp.where(outside, 0.0, total)
                    if r in inner:
                        later[m, c, v, pad + ROWS * r : pad + ROWS * (r + 1)] = total

    fetch(0)
    driven(0).start()

    @pl.loop(0, levels)
    def _(k):
        slot = k % 2
        for m in range(members):
            for v in range(variables):
                lay(*edge(above_ref, m, k, v), v, cells.at[m], pad, None)
                lay(*edge(below_ref, m, k, v), v, cells.at[m], pad + HALO + height, None)
        for v in range(variables):
            lay(*edge(above_ref, members, k, v), v, source, 0, 0.1)
            lay(*edge(below_ref, members, k, v), v, source, HALO + height, 0.1)
            for w in range(variables):
                weight = 0.25 * coupling_ref[(k * variables + v) * variables + w]
                weight = weight + (1.0 - 60.0 * K if v == w else 0.0)
                table[v * variables + w] = jnp.full((ROWS, LANES), weight, jnp.float32)
        for m in range(members):
            fetch(k, wait=(m,))
            for v in range(variables):
                lay(field[slot, m, v] + kicks[slot, m, v], side_ref[m, k], v, cells.at[m], pad + HALO, None)
        driven(k).wait()
        for v in range(variables):
            lay(drive[v], side_ref[members, k], v, source, HALO, 0.1)

        @pl.when(k + 1 < levels)
        def _():
            fetch(k + 1)
            driven(k + 1).start()

        @pl.loop(0, count)
        def _(c):
            for step in range(STEPS):
                now, later = (cells, other) if step % 2 == 0 else (other, cells)
                advance_tile(step, now, later, c)

        lane = lane_index((height, LANES))

        @pl.when(k > 0)
        def _():
            leave(k, wait=True)

        for m in range(members):
            for v in range(variables):
                for t in range(width // LANES):
                    c, offset = LANES * t // SPAN, LANES * t % SPAN
                    left = turn(result[m, c, v], -(offset + HALO))
                    if c + 1 < count:
                        right = turn(result[m, c + 1, v], SPAN - offset - HALO)
                        left = jnp.where(lane < SPAN - offset, left, right)
                    stage[m, v, :, LANES * t : LANES * (t + 1)] = left
                leave(k, m, v)

    leave(0, wait=True)


def advance(place, sources, kick, forcing, above, below, side, coupling):
    members, variables, levels, height, width = kick.shape
    assert height % ROWS == 0 and HALO == ROWS
    count = -(-width // SPAN)
    tall = height + 2 * HALO
    lat = jnp.stack([lax.axis_index("lat"), jnp.int32(lax.axis_size("lat")), jnp.int32(0)])
    here, scalars, anywhere = spec(pltpu.VMEM), spec(pltpu.SMEM), spec(pl.ANY)
    block = (variables, height, width)
    state, *others = sources
    return pl.pallas_call(
        step_kernel,
        in_specs=[anywhere] * 7 + [here] * 3 + [scalars] * 3,
        out_specs=spec(pltpu.HBM),
        out_shape=jax.ShapeDtypeStruct(kick.shape, jnp.float32),
        scratch_shapes=[
            pltpu.VMEM((members, count, variables, tall + 2 * ROWS, LANES), jnp.float32),
            pltpu.VMEM((members, count, variables, tall + 2 * ROWS, LANES), jnp.float32),
            pltpu.VMEM((count, variables, tall, LANES), jnp.float32),
            pltpu.VMEM((members, count, variables, height, LANES), jnp.float32),
            pltpu.VMEM((variables * variables, ROWS, LANES), jnp.float32),
            pltpu.VMEM((members, *block), jnp.float32),
            pltpu.VMEM((2, members, *block), jnp.float32),
            pltpu.VMEM((2, members, *block), jnp.float32),
            pltpu.VMEM(block, jnp.float32),
            pltpu.SemaphoreType.DMA((4, members)),
        ],
        compiler_params=pltpu.CompilerParams(vmem_limit_bytes=VMEM),
    )(
        far_away(state), *others, far_away(kick), far_away(forcing), above, below, side, coupling.reshape(-1), place, lat
    )


def shards(state, kick, forcing, coupling, clone_src):
    place, sources, side, top, bottom = prepared(state, kick, forcing, clone_src)
    above, below = neighbours(top, bottom)
    return advance(place, sources, kick, forcing, above, below, side, coupling)


def solution(mesh):
    in_specs = (
        P("member", None, None, "lat", "lon"),
        P("member", None, None, "lat", "lon"),
        P(None, None, "lat", "lon"),
        P(),
        P(),
    )
    out_specs = P("member", None, None, "lat", "lon")
    return jax.shard_map(shards, mesh=mesh, in_specs=in_specs, out_specs=out_specs, check_vma=False)
```

```python
import functools
import itertools

import functools

import jax
import jax.numpy as jnp
import numpy as np
from jax import lax
from jax.experimental import pallas as pl
from jax.experimental.pallas import tpu as pltpu
from jax.sharding import PartitionSpec as P

STEPS = 4
REACH = 2
HALO = STEPS * REACH
LANES = 128
ROWS = 8
SPAN = LANES - 2 * HALO
K = 0.05 / 12.0
VMEM = 14 * 1024 * 1024


def lane_index(shape):
    return lax.broadcasted_iota(jnp.int32, shape, len(shape) - 1)


def turn(x, shift):
    shift = shift % LANES
    return x if shift == 0 else pltpu.roll(x, shift, x.ndim - 1)


def chain(bits, groups):
    stops = [0] + [x for x in range(1, groups - 1) if bits >> (x - 1) & 1] + [groups - 1]
    return list(zip(stops[:-1], stops[1:]))


def pairings(groups):
    found = []
    for sources in itertools.product(range(groups + 1), repeat=groups):
        pairs = [(a - 1, b) for b, a in enumerate(sources) if a]
        loads = [(e, a < b) for a, b in pairs for e in range(min(a, b), max(a, b))]
        if pairs and len({a for a, _ in pairs}) == len(pairs) and len(set(loads)) == len(loads) and all(a != b for a, b in pairs):
            found.append((sum(a * (groups + 1) ** b for b, a in enumerate(sources)), pairs))
    return found


class Layout:
    def __init__(self, groups, per_dev):
        self.groups, self.per_dev = groups, per_dev
        self.most = per_dev * (groups - 1)
        self.patterns, self.sends = 1, 1 + 2 * self.most
        self.takes = self.sends + 2 * self.most
        self.place = self.takes + per_dev
        self.size = self.place + per_dev
        self.kinds = 1 + (1 << (groups - 2))
        self.pairings = pairings(groups)
        self.branches = self.kinds * self.kinds + len(self.pairings)

    def table(self):
        table = np.zeros(((self.groups + 1) ** self.groups,), np.int32)
        for n, (code, _) in enumerate(self.pairings):
            table[code] = self.kinds * self.kinds + n
        return table


def plan_lines(lay, clone_ref, group_ref, plan_ref, index_refs, ends, owner, used, twice, falls, lookup):
    groups, per_dev, most = lay.groups, lay.per_dev, lay.most
    me = group_ref[0]
    plan_ref[0] = 1
    for t in range(2 * most):
        plan_ref[lay.patterns + t] = 0
        plan_ref[lay.sends + t] = 0
    for t in range(most):
        twice[t] = 0
        falls[t] = 0
        for g in range(groups):
            owner[t * groups + g] = 0
            used[t * groups + g] = 0
    for i in range(per_dev):
        plan_ref[lay.takes + i] = -1 - clone_ref[me * per_dev + i] % per_dev

    for down in range(2):
        for t in range(most):
            ends[t] = 0
        for a in range(groups - 1):
            for b in range(a + 1, groups):
                source, target = (groups - 1 - a, groups - 1 - b) if down else (a, b)
                spans = sum(1 << (x - 1) for x in range(a + 1, b))
                for j in range(per_dev):
                    member = source * per_dev + j
                    wanted = [clone_ref[target * per_dev + i] == member for i in range(per_dev)]
                    need = functools.reduce(jnp.logical_or, wanted)

                    @pl.when(need)
                    def _():
                        t = jnp.int32(most - 1)
                        for earlier in reversed(range(most - 1)):
                            t = jnp.where(ends[earlier] <= a, earlier, t)
                        ends[t] = b
                        plan_ref[0] = jnp.maximum(plan_ref[0], t + 1)
                        at = 2 * t + down
                        before = plan_ref[lay.patterns + at]
                        bits = jnp.where(before == 0, lay.kinds - 2, before - 1)
                        plan_ref[lay.patterns + at] = 1 + (bits & ~spans)
                        giver, taker = t * groups + source, t * groups + target
                        twice[t] = twice[t] | used[giver] | owner[taker]
                        used[giver] = 1
                        owner[taker] = source + 1

                        @pl.when(me == source)
                        def _():
                            plan_ref[lay.sends + at] = j
                            falls[t] = down

                        for i in range(per_dev):

                            @pl.when((me == target) & wanted[i])
                            def _():
                                plan_ref[lay.takes + i] = at

    lookup[1].wait()
    rounds = plan_ref[0]
    single = []
    for t in range(2):
        code = jnp.int32(0)
        for g in reversed(range(groups)):
            code = code * (groups + 1) + owner[t * groups + g]
        alone = (twice[t] == 0) if t == 0 else (twice[t] == 0) & (rounds <= 2)
        single.append(alone)
        up, down = lay.patterns + 2 * t, lay.patterns + 2 * t + 1
        chains = plan_ref[up] * lay.kinds + plan_ref[down]
        index = jnp.where(alone, lookup[0][code], chains)
        index_refs[t][0] = index if t == 0 else jnp.where(rounds > 2, lay.branches, index)

        @pl.when(alone & (falls[t] == 1))
        def _():
            plan_ref[lay.sends + 2 * t] = plan_ref[lay.sends + 2 * t + 1]

    for i in range(per_dev):
        take = plan_ref[lay.takes + i]
        slot = jnp.where((take // 2 == 0) & single[0], 0, jnp.where((take // 2 == 1) & single[1], 2, take))
        far = per_dev + jnp.where((take < 2) | (rounds == 2), slot, 2 + i)
        plan_ref[lay.place + i] = jnp.where(take < 0, -1 - take, far)


def first_kernel(
    lay, clone_ref, table_ref, group_ref, state_ref, kick_ref, forcing_ref, plan_ref, index_ref, second_ref, *refs
):
    fields, sides, strips_ref = refs[:4], refs[4:8], refs[8]
    sources, table, ends, owner, used, twice, falls, held, kick_ends, forcing_ends, done = refs[-11:]
    members, variables, levels, height, width = state_ref.shape
    copies = [pltpu.make_async_copy(clone_ref, sources, done.at[0]), pltpu.make_async_copy(state_ref, held, done.at[1])]
    for side, at in enumerate((0, width - LANES)):
        for ref, part in ((kick_ref, kick_ends), (forcing_ref, forcing_ends)):
            piece = ref.at[(slice(None),) * (len(ref.shape) - 1) + (pl.ds(at, LANES),)]
            copies.append(pltpu.make_async_copy(piece, part.at[side], done.at[len(copies)]))
    listed = pltpu.make_async_copy(table_ref, table, done.at[8])
    for copy in [copies[0], listed, *copies[1:]]:
        copy.start()
    copies[0].wait()
    indices = index_ref, second_ref
    plan_lines(lay, sources, group_ref, plan_ref, indices, ends, owner, used, twice, falls, (table, listed))
    copies[1].wait()
    sent = [plan_ref[lay.sends + n] for n in range(4)]
    given = [plan_ref[lay.patterns + n] for n in range(4)]
    wanted = [given[0] + given[1] > 0, given[1] > 0, given[2] + given[3] > 0, given[3] > 0]
    later = [pltpu.make_async_copy(held.at[sent[n]], fields[n], done.at[4 + n]) for n in (2, 3)]
    for n in range(2):
        pl.when(wanted[2 + n])(later[n].start)

        @pl.when(wanted[n])
        def _():
            @pl.loop(0, variables)
            def _(v):
                for k in range(levels):
                    fields[n][v, k] = held[sent[n], v, k]

    for copy in copies[2:]:
        copy.wait()
    lane = lane_index((height, LANES))

    @pl.loop(0, levels)
    def _(k):
        for slot in range(2 * members + 1):
            strip = jnp.zeros((height, LANES), jnp.float32)
            for v in range(variables):
                if slot < members:
                    low, high = (held[slot, v, k, :, at : at + LANES] for at in (0, width - LANES))
                elif slot < 2 * members:
                    low, high = (kick_ends[side, slot - members, v, k] for side in range(2))
                else:
                    low, high = (forcing_ends[side, v, k] for side in range(2))
                both = turn(jnp.where(lane < HALO, low, high), HALO + 2 * HALO * v)
                strip = jnp.where(lane >= 2 * HALO * v, both, strip)
            strips_ref[slot, k] = strip

    for ref, j in zip(sides, sent):
        ref[...] = strips_ref[j]
    for n in range(2):
        pl.when(wanted[2 + n])(later[n].wait)


def spec(space):
    return pl.BlockSpec(memory_space=space)


def first(lay, group, clone_src, state, kick, forcing):
    members, variables, levels, height, width = state.shape
    shape = jax.ShapeDtypeStruct
    one = pltpu.VMEM(state.shape[1:], jnp.float32)
    side = pltpu.VMEM((levels, height, LANES), jnp.float32)
    strips = pltpu.VMEM((2 * members + 1, levels, height, LANES), jnp.float32)
    ends = (2, members, variables, levels, height, LANES)
    scalar, here, far = spec(pltpu.SMEM), spec(pltpu.VMEM), spec(pltpu.HBM)
    return pl.pallas_call(
        functools.partial(first_kernel, lay),
        in_specs=[far, far, scalar, far, far, far],
        out_specs=[scalar] * 3 + [here] * 2 + [spec(pl.ANY)] * 2 + [here] * 5,
        out_shape=[shape((lay.size,), jnp.int32)] + [shape((1,), jnp.int32)] * 2 + [one] * 2 + [pltpu.HBM(state.shape[1:], jnp.float32)] * 2 + [side] * 4 + [strips],
        scratch_shapes=[
            pltpu.SMEM(clone_src.shape, jnp.int32),
            pltpu.SMEM(lay.table().shape, jnp.int32),
            pltpu.SMEM((lay.most,), jnp.int32),
            pltpu.SMEM((lay.most * lay.groups,), jnp.int32),
            pltpu.SMEM((lay.most * lay.groups,), jnp.int32),
            pltpu.SMEM((lay.most,), jnp.int32),
            pltpu.SMEM((lay.most,), jnp.int32),
            pltpu.VMEM(state.shape, jnp.float32),
            pltpu.VMEM(ends, jnp.float32),
            pltpu.VMEM((2, *ends[2:]), jnp.float32),
            pltpu.SemaphoreType.DMA((9,)),
        ],
        compiler_params=pltpu.CompilerParams(vmem_limit_bytes=VMEM),
    )(far_away(clone_src), jnp.asarray(lay.table()), group[None], far_away(state), far_away(kick), far_away(forcing))


def far_away(x):
    return pltpu.with_memory_space_constraint(x, pltpu.HBM)


def edge_shape(members, forcing):
    variables, levels, height, width = forcing.shape
    return jax.ShapeDtypeStruct((members, levels, variables * width // LANES + 1, HALO, LANES), jnp.float32)


def options_of(state_ref, refs):
    return [state_ref.at[j] for j in range(state_ref.shape[0])] + list(refs)


def pack_kernel(
    lay, plan_ref, state_ref, up_ref, down_ref, second_up_ref, second_down_ref, kick_ref, forcing_ref,
    sides_ref, up_side_ref, down_side_ref, second_up_side_ref, second_down_side_ref,
    side_ref, top_ref, bottom_ref, field_rows, kick_rows, forcing_rows, strips, picked, done,
):
    members, variables, levels, height, width = state_ref.shape
    tiles = width // LANES
    whole = options_of(state_ref, (up_ref, down_ref, second_up_ref, second_down_ref))
    parts = [sides_ref.at[j] for j in range(members)]
    parts += [up_side_ref, down_side_ref, second_up_side_ref, second_down_side_ref]
    places = [plan_ref[lay.place + i] for i in range(members)]
    rows = [pl.ds(0, HALO), pl.ds(height - HALO, HALO)]
    f_copies = [pltpu.make_async_copy(forcing_ref.at[:, :, rows[n]], forcing_rows.at[n], done.at[0]) for n in range(2)]
    copies = []
    for i in range(members):
        for n in range(2):
            for at, option in enumerate(whole):

                @pl.when(places[i] == at)
                def _():
                    pltpu.make_async_copy(option.at[:, :, rows[n]], field_rows.at[i, n], done.at[1 + i]).start()

            copies.append(pltpu.make_async_copy(kick_ref.at[i, :, :, rows[n]], kick_rows.at[i, n], done.at[1 + i]))
    strip_copies = [pltpu.make_async_copy(sides_ref, strips, done.at[1 + members])]
    for i in range(members):
        for at, part in enumerate(parts):

            @pl.when(places[i] == at)
            def _():
                pltpu.make_async_copy(part, picked.at[i], done.at[2 + members + i]).start()

        strip_copies.append(pltpu.make_async_copy(up_side_ref, picked.at[i], done.at[2 + members + i]))
    for copy in [strip_copies[0]] + f_copies + copies:
        copy.start()

    def flank(slot, k, strip):
        side_ref[slot, k] = strip
        top_ref[slot, k, variables * tiles] = strip[:HALO]
        bottom_ref[slot, k, variables * tiles] = strip[height - HALO :]

    def edges(slot, rows_of):
        @pl.loop(0, levels)
        def _(k):
            for n, ref in enumerate((top_ref, bottom_ref)):
                for v in range(variables):
                    edge = rows_of(n, v, k)
                    for t in range(tiles):
                        ref[slot, k, v * tiles + t] = edge[:, LANES * t : LANES * (t + 1)]

    for copy in strip_copies:
        copy.wait()
    for k in range(levels):
        flank(members, k, strips[2 * members, k])
        for i in range(members):
            flank(i, k, picked[i, k] + strips[members + i, k])
    for copy in f_copies:
        copy.wait()
    edges(members, lambda n, v, k: forcing_rows[n, v, k])
    for i in range(members):
        for n in range(2):
            pltpu.make_async_copy(kick_ref.at[i, :, :, rows[n]], field_rows.at[i, n], done.at[1 + i]).wait()
            copies[2 * i + n].wait()
        edges(i, lambda n, v, k: field_rows[i, n, v, k] + kick_rows[i, n, v, k])


def pack(lay, plan, state, fields, kick, forcing, sides, far_sides):
    members, variables, levels, height, width = state.shape
    here, anywhere = spec(pltpu.VMEM), spec(pl.ANY)
    rows = (members, 2, variables, levels, HALO, width)
    return pl.pallas_call(
        functools.partial(pack_kernel, lay),
        in_specs=[spec(pltpu.SMEM)] + [anywhere] * 12,
        out_specs=[here] * 3,
        out_shape=[
            jax.ShapeDtypeStruct((members + 1, levels, height, LANES), jnp.float32),
            edge_shape(members + 1, forcing),
            edge_shape(members + 1, forcing),
        ],
        scratch_shapes=[
            pltpu.VMEM(rows, jnp.float32),
            pltpu.VMEM(rows, jnp.float32),
            pltpu.VMEM(rows[1:], jnp.float32),
            pltpu.VMEM(sides.shape, jnp.float32),
            pltpu.VMEM((members, levels, height, LANES), jnp.float32),
            pltpu.SemaphoreType.DMA((2 + 2 * members,)),
        ],
        compiler_params=pltpu.CompilerParams(vmem_limit_bytes=VMEM),
    )(plan, far_away(state), *fields, far_away(kick), far_away(forcing), sides, *far_sides)


def blank(*like):
    return pl.pallas_call(
        lambda *refs: None,
        out_specs=[spec(pl.ANY)] * len(like),
        out_shape=[jax.ShapeDtypeStruct(x.shape, x.dtype) for x in like],
        compiler_params=pltpu.CompilerParams(vmem_limit_bytes=1024 * 1024),
    )()


def neighbours(top, bottom):
    lats = lax.axis_size("lat")
    above = lax.ppermute(bottom, "lat", [(i, i + 1) for i in range(lats - 1)])
    below = lax.ppermute(top, "lat", [(i + 1, i) for i in range(lats - 1)])
    return above, below


def beside(strips):
    assert lax.axis_size("lon") == 2
    return lax.ppermute(strips, "lon", [(0, 1), (1, 0)])


def send(lay, ways, fields, sides):
    lons = lax.axis_size("lon")
    fields, sides = list(fields), list(sides)
    for n, pairs in enumerate(ways):
        if pairs:
            crossed = [(a * lons + j, b * lons + 1 - j) for a, b in pairs for j in range(lons)]
            fields[n] = lax.ppermute(fields[n], "member", pairs)
            sides[n] = lax.ppermute(sides[n], ("member", "lon"), crossed)
        else:
            fields[n], sides[n] = blank(fields[n], sides[n])
    return (*fields, *sides)


def routes(lay):
    top = lay.groups - 1

    def both(up, down):
        rising = chain(up - 1, lay.groups) if up else []
        falling = [(top - a, top - b) for a, b in chain(down - 1, lay.groups)] if down else []
        return rising, falling

    chains = [both(up, down) for up in range(lay.kinds) for down in range(lay.kinds)]
    return chains, [(pairs, []) for _, pairs in lay.pairings]


def prepared(state, kick, forcing, clone_src):
    per_dev, groups, group = state.shape[0], lax.axis_size("member"), lax.axis_index("member")
    lay = Layout(4 if groups == 4 else 3, per_dev)
    if groups != 4:
        piece = lax.all_gather(state, "member", axis=0, tiled=True)
        sources = lax.dynamic_slice_in_dim(clone_src, group * per_dev, per_dev)
        state = jnp.take(piece, sources, axis=0, mode="clip")
        still = jnp.arange(per_dev * 3, dtype=jnp.int32)
        plan, _, _, *out, strips = first(lay, jnp.int32(0), still, state, kick, forcing)
        got, second = (*out[:2], *out[4:6]), (*out[2:4], *out[6:])
        sides = beside(strips)
    else:
        plan, index, following, *out, strips = first(lay, group, clone_src, state, kick, forcing)
        out, second = (*out[:2], *out[4:6]), (*out[2:4], *out[6:])
        chains, singles = routes(lay)

        def opening(way):
            return lambda a, b, c, d, strips: (*send(lay, way, (a, b), (c, d)), beside(strips))

        def plain(way):
            return lambda a, b, c, d: send(lay, way, (a, b), (c, d))

        def later(t, held):
            takes = plan[lay.takes : lay.place]
            sent = [lax.dynamic_index_in_dim(plan, lay.sends + 2 * t + n, keepdims=False) for n in range(2)]
            wanted = [lax.dynamic_index_in_dim(plan, lay.patterns + 2 * t + n, keepdims=False) for n in range(2)]
            out = [lax.dynamic_index_in_dim(x, j, keepdims=False) for x in (state, strips) for j in sent]
            got = lax.switch(wanted[0] * lay.kinds + wanted[1], [plain(way) for way in chains], *out)
            kept = []
            for x in range(2):
                for i in range(per_dev):
                    up, down = takes[i] == 2 * t, takes[i] == 2 * t + 1
                    new = jnp.where(up, got[2 * x], got[2 * x + 1])
                    kept.append(jnp.where(up | down, new, held[2 * x + i]))
            return tuple(kept)

        *got, sides = lax.switch(index[0], [opening(way) for way in chains + singles], *out, strips)
        several = lambda *held: lax.fori_loop(1, plan[0], later, held)
        second = lax.switch(following[0], [plain(way) for way in chains + singles] + [several], *second)

    assert per_dev == 2
    fields = (*got[:2], *second[:2])
    side, top, bottom = pack(lay, plan, state, fields, kick, forcing, sides, (*got[2:], *second[2:]))
    return plan[lay.place :], (state, *fields), side, top, bottom


def cut(rows, strip, v):
    width = rows.shape[1]
    count = -(-width // SPAN)
    lane = lane_index((rows.shape[0], LANES))
    source = [rows[:, LANES * t : LANES * (t + 1)] for t in range(width // LANES)]
    tiles = []
    for c in range(count):
        first = SPAN * c - HALO
        if c == 0:
            tile = jnp.where(lane < HALO, turn(strip, -2 * HALO * v), turn(source[0], HALO))
        else:
            t, offset = first // LANES, first % LANES
            if t + 1 < len(source):
                later = turn(source[t + 1], -offset)
            else:
                later = turn(strip, LANES - offset - 2 * HALO * v - HALO)
            tile = jnp.where(lane < LANES - offset, turn(source[t], -offset), later)
        tiles.append(tile)
    return tiles


def step_kernel(
    state_ref, up_ref, down_ref, second_up_ref, second_down_ref, kick_ref, forcing_ref, above_ref, below_ref, side_ref,
    coupling_ref, place_ref, lat_ref, out_ref, cells, other, source, result, table, stage, field, kicks, drive, done,
):
    members, variables, levels, height, width = state_ref.shape
    count = -(-width // SPAN)
    tall = height + 2 * HALO
    at_top = lat_ref[0] == 0
    at_bottom = lat_ref[0] == lat_ref[1] - 1
    options = options_of(state_ref, (up_ref, down_ref, second_up_ref, second_down_ref))

    def fetch(k, wait=()):
        slot = k % 2
        for m in wait or range(members):
            kick = pltpu.make_async_copy(kick_ref.at[m, :, k], kicks.at[slot, m], done.at[2, m])
            if wait:
                pltpu.make_async_copy(kick_ref.at[m, :, k], field.at[slot, m], done.at[1, m]).wait()
                kick.wait()
            else:
                for at, option in enumerate(options):

                    @pl.when(place_ref[m] == at)
                    def _():
                        pltpu.make_async_copy(option.at[:, k], field.at[slot, m], done.at[1, m]).start()

                kick.start()

    def leave(k, m=None, v=None, wait=False):
        if wait:
            for m in range(members):
                pltpu.make_async_copy(stage.at[m], out_ref.at[m, :, k], done.at[0, m]).wait()
        else:
            pltpu.make_async_copy(stage.at[m, v], out_ref.at[m, v, k], done.at[0, m]).start()

    def driven(k):
        return pltpu.make_async_copy(forcing_ref.at[:, k], drive, done.at[3, 0])

    def edge(ref, slot, k, v):
        tiles = width // LANES
        rows = [ref[slot, k, v * tiles + t] for t in range(tiles)]
        return jnp.concatenate(rows, axis=1), ref[slot, k, variables * tiles]

    def lay(rows, strip, v, target, at, scale):
        for c, tile in enumerate(cut(rows, strip, v)):
            target[c, v, at : at + rows.shape[0]] = tile if scale is None else tile * scale

    blocks = tall // ROWS
    pad = ROWS
    origin = lat_ref[2]

    line = lax.broadcasted_iota(jnp.int32, (ROWS, LANES), 0)
    north, south = range(blocks)[0], range(blocks)[-1]

    def advance_tile(step, now, later, c):
        last = step == STEPS - 1
        shared = 0 < step < STEPS - 1
        assert HALO - REACH * 2 <= ROWS // 2

        def load(ref, m, v, r, d=0):
            at = pad + ROWS * r
            return ref[m, c, v, at : at + ROWS] if d == 0 else ref[m, c, v, pl.ds(origin + at + d, ROWS)]

        def view(get, r):
            return jnp.where(line < ROWS // 2, get(south), get(north)) if r is None else get(r)

        inner = list(range(1, blocks - 1))
        for r in inner if last else [None] + inner if shared else range(blocks):
            centre, along, across = [], [], []
            for m in range(members):
                centre.append([view(lambda r: load(now, m, v, r), r) for v in range(variables)])
                ku, kv = K * centre[m][0], K * centre[m][1]
                eu, ev = 8.0 * ku, 8.0 * kv
                along.append((16.0 * K - eu, 16.0 * K + eu, ku - K, -K - ku))
                across.append((16.0 * K - ev, 16.0 * K + ev, kv - K, -K - kv))
            for v in range(variables):
                driving = view(lambda r: source[c, v, ROWS * r : ROWS * (r + 1)], r)
                weights = [table[v * variables + w] for w in range(variables)]
                for m in range(members):
                    q = centre[m][v]
                    shifted = {d: view(lambda r: load(now, m, v, r, d), r) for d in (1, -1, 2, -2)}
                    total = driving
                    for w in range(variables):
                        total += weights[w] * centre[m][w]
                    near = along[m][0] * turn(q, -1) + along[m][1] * turn(q, 1)
                    far = along[m][2] * turn(q, -2) + along[m][3] * turn(q, 2)
                    near += across[m][0] * shifted[1] + across[m][1] * shifted[-1]
                    far += across[m][2] * shifted[2] + across[m][3] * shifted[-2]
                    total += near + far
                    if last:
                        result[m, c, v, ROWS * (r - 1) : ROWS * r] = total
                        continue
                    for to, outside in ((north, at_top), (south, at_bottom)):
                        if r is None or r == to:
                            at = pad + ROWS * to
                            later[m, c, v, at : at + ROWS] = jnp.where(outside, 0.0, total)
                    if r in inner:
                        later[m, c, v, pad + ROWS * r : pad + ROWS * (r + 1)] = total

    fetch(0)
    driven(0).start()

    @pl.loop(0, levels)
    def _(k):
        slot = k % 2
        for m in range(members):
            for v in range(variables):
                lay(*edge(above_ref, m, k, v), v, cells.at[m], pad, None)
                lay(*edge(below_ref, m, k, v), v, cells.at[m], pad + HALO + height, None)
        for v in range(variables):
            lay(*edge(above_ref, members, k, v), v, source, 0, 0.1)
            lay(*edge(below_ref, members, k, v), v, source, HALO + height, 0.1)
            for w in range(variables):
                weight = 0.25 * coupling_ref[(k * variables + v) * variables + w]
                weight = weight + (1.0 - 60.0 * K if v == w else 0.0)
                table[v * variables + w] = jnp.full((ROWS, LANES), weight, jnp.float32)
        for m in range(members):
            fetch(k, wait=(m,))
            for v in range(variables):
                lay(field[slot, m, v] + kicks[slot, m, v], side_ref[m, k], v, cells.at[m], pad + HALO, None)
        driven(k).wait()
        for v in range(variables):
            lay(drive[v], side_ref[members, k], v, source, HALO, 0.1)

        @pl.when(k + 1 < levels)
        def _():
            fetch(k + 1)
            driven(k + 1).start()

        @pl.loop(0, count)
        def _(c):
            for step in range(STEPS):
                now, later = (cells, other) if step % 2 == 0 else (other, cells)
                advance_tile(step, now, later, c)

        lane = lane_index((height, LANES))

        @pl.when(k > 0)
        def _():
            leave(k, wait=True)

        for m in range(members):
            for v in range(variables):
                for t in range(width // LANES):
                    c, offset = LANES * t // SPAN, LANES * t % SPAN
                    left = turn(result[m, c, v], -(offset + HALO))
                    if c + 1 < count:
                        right = turn(result[m, c + 1, v], SPAN - offset - HALO)
                        left = jnp.where(lane < SPAN - offset, left, right)
                    stage[m, v, :, LANES * t : LANES * (t + 1)] = left
                leave(k, m, v)

    leave(0, wait=True)


def advance(place, sources, kick, forcing, above, below, side, coupling):
    members, variables, levels, height, width = kick.shape
    assert height % ROWS == 0 and HALO == ROWS
    count = -(-width // SPAN)
    tall = height + 2 * HALO
    lat = jnp.stack([lax.axis_index("lat"), jnp.int32(lax.axis_size("lat")), jnp.int32(0)])
    here, scalars, anywhere = spec(pltpu.VMEM), spec(pltpu.SMEM), spec(pl.ANY)
    block = (variables, height, width)
    state, *others = sources
    return pl.pallas_call(
        step_kernel,
        in_specs=[anywhere] * 7 + [here] * 3 + [scalars] * 3,
        out_specs=spec(pltpu.HBM),
        out_shape=jax.ShapeDtypeStruct(kick.shape, jnp.float32),
        scratch_shapes=[
            pltpu.VMEM((members, count, variables, tall + 2 * ROWS, LANES), jnp.float32),
            pltpu.VMEM((members, count, variables, tall + 2 * ROWS, LANES), jnp.float32),
            pltpu.VMEM((count, variables, tall, LANES), jnp.float32),
            pltpu.VMEM((members, count, variables, height, LANES), jnp.float32),
            pltpu.VMEM((variables * variables, ROWS, LANES), jnp.float32),
            pltpu.VMEM((members, *block), jnp.float32),
            pltpu.VMEM((2, members, *block), jnp.float32),
            pltpu.VMEM((2, members, *block), jnp.float32),
            pltpu.VMEM(block, jnp.float32),
            pltpu.SemaphoreType.DMA((4, members)),
        ],
        compiler_params=pltpu.CompilerParams(vmem_limit_bytes=VMEM),
    )(
        far_away(state), *others, far_away(kick), far_away(forcing), above, below, side, coupling.reshape(-1), place, lat
    )


def shards(state, kick, forcing, coupling, clone_src):
    place, sources, side, top, bottom = prepared(state, kick, forcing, clone_src)
    above, below = neighbours(top, bottom)
    return advance(place, sources, kick, forcing, above, below, side, coupling)


def solution(mesh):
    in_specs = (
        P("member", None, None, "lat", "lon"),
        P("member", None, None, "lat", "lon"),
        P(None, None, "lat", "lon"),
        P(),
        P(),
    )
    out_specs = P("member", None, None, "lat", "lon")
    return jax.shard_map(shards, mesh=mesh, in_specs=in_specs, out_specs=out_specs, check_vma=False)
```

```python
import functools
import itertools

import functools

import jax
import jax.numpy as jnp
import numpy as np
from jax import lax
from jax.experimental import pallas as pl
from jax.experimental.pallas import tpu as pltpu
from jax.sharding import PartitionSpec as P

STEPS = 4
REACH = 2
HALO = STEPS * REACH
LANES = 128
ROWS = 8
SPAN = LANES - 2 * HALO
K = 0.05 / 12.0
VMEM = 14 * 1024 * 1024


def lane_index(shape):
    return lax.broadcasted_iota(jnp.int32, shape, len(shape) - 1)


def turn(x, shift):
    shift = shift % LANES
    return x if shift == 0 else pltpu.roll(x, shift, x.ndim - 1)


def chain(bits, groups):
    stops = [0] + [x for x in range(1, groups - 1) if bits >> (x - 1) & 1] + [groups - 1]
    return list(zip(stops[:-1], stops[1:]))


SINGLES = 9


def pairings(groups):
    found = []
    for sources in itertools.product(range(groups + 1), repeat=groups):
        pairs = [(a - 1, b) for b, a in enumerate(sources) if a]
        loads = [(e, a < b) for a, b in pairs for e in range(min(a, b), max(a, b))]
        if pairs and len({a for a, _ in pairs}) == len(pairs) and len(set(loads)) == len(loads) and all(a != b for a, b in pairs):
            found.append((sum(a * (groups + 1) ** b for b, a in enumerate(sources)), pairs))
    return found


class Layout:
    def __init__(self, groups, per_dev):
        self.groups, self.per_dev = groups, per_dev
        self.most = per_dev * (groups - 1)
        self.patterns, self.sends = 1, 1 + 2 * self.most
        self.takes = self.sends + 2 * self.most
        self.place = self.takes + per_dev
        self.size = self.place + per_dev
        self.kinds = 1 + (1 << (groups - 2))
        self.pairings = pairings(groups)
        largest = [p for _, p in self.pairings if not any(set(p) < set(q) for _, q in self.pairings)]
        self.singles = sorted(largest, key=lambda p: (-len(p), sum(abs(a - b) for a, b in p)))[:SINGLES]

    def table(self):
        table = np.zeros(((self.groups + 1) ** self.groups,), np.int32)
        for code, pairs in self.pairings:
            if len({a < b for a, b in pairs}) == 2:
                fits = [n for n, single in enumerate(self.singles) if set(pairs) <= set(single)]
                table[code] = self.kinds * self.kinds + fits[0] if fits else 0
        return table


def plan_lines(lay, clone_ref, group_ref, plan_ref, index_refs, ends, owner, used, twice, falls, lookup):
    groups, per_dev, most = lay.groups, lay.per_dev, lay.most
    me = group_ref[0]
    plan_ref[0] = 1
    for t in range(2 * most):
        plan_ref[lay.patterns + t] = 0
        plan_ref[lay.sends + t] = 0
    for t in range(most):
        twice[t] = 0
        falls[t] = 0
        for g in range(groups):
            owner[t * groups + g] = 0
            used[t * groups + g] = 0
    for i in range(per_dev):
        plan_ref[lay.takes + i] = -1 - clone_ref[me * per_dev + i] % per_dev

    for down in range(2):
        for t in range(most):
            ends[t] = 0
        for a in range(groups - 1):
            for b in range(a + 1, groups):
                source, target = (groups - 1 - a, groups - 1 - b) if down else (a, b)
                spans = sum(1 << (x - 1) for x in range(a + 1, b))
                for j in range(per_dev):
                    member = source * per_dev + j
                    wanted = [clone_ref[target * per_dev + i] == member for i in range(per_dev)]
                    need = functools.reduce(jnp.logical_or, wanted)

                    @pl.when(need)
                    def _():
                        t = jnp.int32(most - 1)
                        for earlier in reversed(range(most - 1)):
                            t = jnp.where(ends[earlier] <= a, earlier, t)
                        ends[t] = b
                        plan_ref[0] = jnp.maximum(plan_ref[0], t + 1)
                        at = 2 * t + down
                        before = plan_ref[lay.patterns + at]
                        bits = jnp.where(before == 0, lay.kinds - 2, before - 1)
                        plan_ref[lay.patterns + at] = 1 + (bits & ~spans)
                        giver, taker = t * groups + source, t * groups + target
                        twice[t] = twice[t] | used[giver] | owner[taker]
                        used[giver] = 1
                        owner[taker] = source + 1

                        @pl.when(me == source)
                        def _():
                            plan_ref[lay.sends + at] = j
                            falls[t] = down

                        for i in range(per_dev):

                            @pl.when((me == target) & wanted[i])
                            def _():
                                plan_ref[lay.takes + i] = at

    lookup[1].wait()
    rounds = plan_ref[0]
    code = jnp.int32(0)
    for g in reversed(range(groups)):
        code = code * (groups + 1) + owner[g]
    branch = lookup[0][code]
    single = (twice[0] == 0) & (branch > 0)
    chains = [plan_ref[lay.patterns + 2 * t] * lay.kinds + plan_ref[lay.patterns + 2 * t + 1] for t in range(2)]
    index_refs[0][0] = jnp.where(single, branch, chains[0])
    index_refs[1][0] = jnp.where(rounds > 2, lay.kinds * lay.kinds, chains[1])

    @pl.when(single & (falls[0] == 1))
    def _():
        plan_ref[lay.sends] = plan_ref[lay.sends + 1]

    for i in range(per_dev):
        take = plan_ref[lay.takes + i]
        slot = jnp.where(single & (take < 2), 0, take)
        far = per_dev + jnp.where((take < 2) | (rounds == 2), slot, 2 + i)
        plan_ref[lay.place + i] = jnp.where(take < 0, -1 - take, far)


def first_kernel(
    lay, clone_ref, table_ref, group_ref, state_ref, kick_ref, forcing_ref, plan_ref, index_ref, second_ref, *refs
):
    fields, sides, strips_ref = refs[:4], refs[4:8], refs[8]
    sources, table, ends, owner, used, twice, falls, held, kick_ends, forcing_ends, done = refs[-11:]
    members, variables, levels, height, width = state_ref.shape
    copies = [pltpu.make_async_copy(clone_ref, sources, done.at[0]), pltpu.make_async_copy(state_ref, held, done.at[1])]
    for side, at in enumerate((0, width - LANES)):
        for ref, part in ((kick_ref, kick_ends), (forcing_ref, forcing_ends)):
            piece = ref.at[(slice(None),) * (len(ref.shape) - 1) + (pl.ds(at, LANES),)]
            copies.append(pltpu.make_async_copy(piece, part.at[side], done.at[len(copies)]))
    listed = pltpu.make_async_copy(table_ref, table, done.at[8])
    for copy in [copies[0], listed, *copies[1:]]:
        copy.start()
    copies[0].wait()
    indices = index_ref, second_ref
    plan_lines(lay, sources, group_ref, plan_ref, indices, ends, owner, used, twice, falls, (table, listed))
    copies[1].wait()
    sent = [plan_ref[lay.sends + n] for n in range(4)]
    given = [plan_ref[lay.patterns + n] for n in range(4)]
    wanted = [given[0] + given[1] > 0, given[1] > 0, given[2] > 0, given[3] > 0]
    later = [pltpu.make_async_copy(held.at[sent[n]], fields[n], done.at[4 + n]) for n in (2, 3)]
    for n in range(2):
        pl.when(wanted[2 + n])(later[n].start)

        @pl.when(wanted[n])
        def _():
            @pl.loop(0, variables)
            def _(v):
                for k in range(levels):
                    fields[n][v, k] = held[sent[n], v, k]

    for copy in copies[2:]:
        copy.wait()
    lane = lane_index((height, LANES))

    @pl.loop(0, levels)
    def _(k):
        for slot in range(2 * members + 1):
            strip = jnp.zeros((height, LANES), jnp.float32)
            for v in range(variables):
                if slot < members:
                    low, high = (held[slot, v, k, :, at : at + LANES] for at in (0, width - LANES))
                elif slot < 2 * members:
                    low, high = (kick_ends[side, slot - members, v, k] for side in range(2))
                else:
                    low, high = (forcing_ends[side, v, k] for side in range(2))
                both = turn(jnp.where(lane < HALO, low, high), HALO + 2 * HALO * v)
                strip = jnp.where(lane >= 2 * HALO * v, both, strip)
            strips_ref[slot, k] = strip

    for ref, j in zip(sides, sent):
        ref[...] = strips_ref[j]
    for n in range(2):
        pl.when(wanted[2 + n])(later[n].wait)


def spec(space):
    return pl.BlockSpec(memory_space=space)


def first(lay, group, clone_src, state, kick, forcing):
    members, variables, levels, height, width = state.shape
    shape = jax.ShapeDtypeStruct
    one = pltpu.VMEM(state.shape[1:], jnp.float32)
    side = pltpu.VMEM((levels, height, LANES), jnp.float32)
    strips = pltpu.VMEM((2 * members + 1, levels, height, LANES), jnp.float32)
    ends = (2, members, variables, levels, height, LANES)
    scalar, here, far = spec(pltpu.SMEM), spec(pltpu.VMEM), spec(pltpu.HBM)
    return pl.pallas_call(
        functools.partial(first_kernel, lay),
        in_specs=[far, far, scalar, far, far, far],
        out_specs=[scalar] * 3 + [here] * 2 + [spec(pl.ANY)] * 2 + [here] * 5,
        out_shape=[shape((lay.size,), jnp.int32)] + [shape((1,), jnp.int32)] * 2 + [one] * 2 + [pltpu.HBM(state.shape[1:], jnp.float32)] * 2 + [side] * 4 + [strips],
        scratch_shapes=[
            pltpu.SMEM(clone_src.shape, jnp.int32),
            pltpu.SMEM(lay.table().shape, jnp.int32),
            pltpu.SMEM((lay.most,), jnp.int32),
            pltpu.SMEM((lay.most * lay.groups,), jnp.int32),
            pltpu.SMEM((lay.most * lay.groups,), jnp.int32),
            pltpu.SMEM((lay.most,), jnp.int32),
            pltpu.SMEM((lay.most,), jnp.int32),
            pltpu.VMEM(state.shape, jnp.float32),
            pltpu.VMEM(ends, jnp.float32),
            pltpu.VMEM((2, *ends[2:]), jnp.float32),
            pltpu.SemaphoreType.DMA((9,)),
        ],
        compiler_params=pltpu.CompilerParams(vmem_limit_bytes=VMEM),
    )(far_away(clone_src), jnp.asarray(lay.table()), group[None], far_away(state), far_away(kick), far_away(forcing))


def far_away(x):
    return pltpu.with_memory_space_constraint(x, pltpu.HBM)


def edge_shape(members, forcing):
    variables, levels, height, width = forcing.shape
    return jax.ShapeDtypeStruct((members, levels, variables * width // LANES + 1, HALO, LANES), jnp.float32)


def options_of(state_ref, refs):
    return [state_ref.at[j] for j in range(state_ref.shape[0])] + list(refs)


def pack_kernel(
    lay, plan_ref, state_ref, up_ref, down_ref, second_up_ref, second_down_ref, kick_ref, forcing_ref,
    sides_ref, up_side_ref, down_side_ref, second_up_side_ref, second_down_side_ref,
    side_ref, top_ref, bottom_ref, field_rows, kick_rows, forcing_rows, strips, picked, done,
):
    members, variables, levels, height, width = state_ref.shape
    tiles = width // LANES
    whole = options_of(state_ref, (up_ref, down_ref, second_up_ref, second_down_ref))
    parts = [sides_ref.at[j] for j in range(members)]
    parts += [up_side_ref, down_side_ref, second_up_side_ref, second_down_side_ref]
    places = [plan_ref[lay.place + i] for i in range(members)]
    rows = [pl.ds(0, HALO), pl.ds(height - HALO, HALO)]
    f_copies = [pltpu.make_async_copy(forcing_ref.at[:, :, rows[n]], forcing_rows.at[n], done.at[0]) for n in range(2)]
    copies = []
    for i in range(members):
        for n in range(2):
            for at, option in enumerate(whole):

                @pl.when(places[i] == at)
                def _():
                    pltpu.make_async_copy(option.at[:, :, rows[n]], field_rows.at[i, n], done.at[1 + i]).start()

            copies.append(pltpu.make_async_copy(kick_ref.at[i, :, :, rows[n]], kick_rows.at[i, n], done.at[1 + i]))
    strip_copies = [pltpu.make_async_copy(sides_ref, strips, done.at[1 + members])]
    for i in range(members):
        for at, part in enumerate(parts):

            @pl.when(places[i] == at)
            def _():
                pltpu.make_async_copy(part, picked.at[i], done.at[2 + members + i]).start()

        strip_copies.append(pltpu.make_async_copy(up_side_ref, picked.at[i], done.at[2 + members + i]))
    for copy in [strip_copies[0]] + f_copies + copies:
        copy.start()

    def flank(slot, k, strip):
        side_ref[slot, k] = strip
        top_ref[slot, k, variables * tiles] = strip[:HALO]
        bottom_ref[slot, k, variables * tiles] = strip[height - HALO :]

    def edges(slot, rows_of):
        @pl.loop(0, levels)
        def _(k):
            for n, ref in enumerate((top_ref, bottom_ref)):
                for v in range(variables):
                    edge = rows_of(n, v, k)
                    for t in range(tiles):
                        ref[slot, k, v * tiles + t] = edge[:, LANES * t : LANES * (t + 1)]

    for copy in strip_copies:
        copy.wait()
    for k in range(levels):
        flank(members, k, strips[2 * members, k])
        for i in range(members):
            flank(i, k, picked[i, k] + strips[members + i, k])
    for copy in f_copies:
        copy.wait()
    edges(members, lambda n, v, k: forcing_rows[n, v, k])
    for i in range(members):
        for n in range(2):
            pltpu.make_async_copy(kick_ref.at[i, :, :, rows[n]], field_rows.at[i, n], done.at[1 + i]).wait()
            copies[2 * i + n].wait()
        edges(i, lambda n, v, k: field_rows[i, n, v, k] + kick_rows[i, n, v, k])


def pack(lay, plan, state, fields, kick, forcing, sides, far_sides):
    members, variables, levels, height, width = state.shape
    here, anywhere = spec(pltpu.VMEM), spec(pl.ANY)
    rows = (members, 2, variables, levels, HALO, width)
    return pl.pallas_call(
        functools.partial(pack_kernel, lay),
        in_specs=[spec(pltpu.SMEM)] + [anywhere] * 12,
        out_specs=[here] * 3,
        out_shape=[
            jax.ShapeDtypeStruct((members + 1, levels, height, LANES), jnp.float32),
            edge_shape(members + 1, forcing),
            edge_shape(members + 1, forcing),
        ],
        scratch_shapes=[
            pltpu.VMEM(rows, jnp.float32),
            pltpu.VMEM(rows, jnp.float32),
            pltpu.VMEM(rows[1:], jnp.float32),
            pltpu.VMEM(sides.shape, jnp.float32),
            pltpu.VMEM((members, levels, height, LANES), jnp.float32),
            pltpu.SemaphoreType.DMA((2 + 2 * members,)),
        ],
        compiler_params=pltpu.CompilerParams(vmem_limit_bytes=VMEM),
    )(plan, far_away(state), *fields, far_away(kick), far_away(forcing), sides, *far_sides)


def blank(*like):
    return pl.pallas_call(
        lambda *refs: None,
        out_specs=[spec(pl.ANY)] * len(like),
        out_shape=[jax.ShapeDtypeStruct(x.shape, x.dtype) for x in like],
        compiler_params=pltpu.CompilerParams(vmem_limit_bytes=1024 * 1024),
    )()


def neighbours(top, bottom):
    lats = lax.axis_size("lat")
    above = lax.ppermute(bottom, "lat", [(i, i + 1) for i in range(lats - 1)])
    below = lax.ppermute(top, "lat", [(i + 1, i) for i in range(lats - 1)])
    return above, below


def beside(strips):
    assert lax.axis_size("lon") == 2
    return lax.ppermute(strips, "lon", [(0, 1), (1, 0)])


def send(lay, ways, fields, sides):
    lons = lax.axis_size("lon")
    fields, sides = list(fields), list(sides)
    for n, pairs in enumerate(ways):
        if pairs:
            crossed = [(a * lons + j, b * lons + 1 - j) for a, b in pairs for j in range(lons)]
            fields[n] = lax.ppermute(fields[n], "member", pairs)
            sides[n] = lax.ppermute(sides[n], ("member", "lon"), crossed)
        else:
            fields[n], sides[n] = blank(fields[n], sides[n])
    return (*fields, *sides)


def routes(lay):
    top = lay.groups - 1

    def both(up, down):
        rising = chain(up - 1, lay.groups) if up else []
        falling = [(top - a, top - b) for a, b in chain(down - 1, lay.groups)] if down else []
        return rising, falling

    chains = [both(up, down) for up in range(lay.kinds) for down in range(lay.kinds)]
    return chains, [(pairs, []) for pairs in lay.singles]


def prepared(state, kick, forcing, clone_src):
    per_dev, groups, group = state.shape[0], lax.axis_size("member"), lax.axis_index("member")
    lay = Layout(4 if groups == 4 else 3, per_dev)
    if groups != 4:
        piece = lax.all_gather(state, "member", axis=0, tiled=True)
        sources = lax.dynamic_slice_in_dim(clone_src, group * per_dev, per_dev)
        state = jnp.take(piece, sources, axis=0, mode="clip")
        still = jnp.arange(per_dev * 3, dtype=jnp.int32)
        plan, _, _, *out, strips = first(lay, jnp.int32(0), still, state, kick, forcing)
        got, second = (*out[:2], *out[4:6]), (*out[2:4], *out[6:])
        sides = beside(strips)
    else:
        plan, index, following, *out, strips = first(lay, group, clone_src, state, kick, forcing)
        out, second = (*out[:2], *out[4:6]), (*out[2:4], *out[6:])
        chains, singles = routes(lay)

        def opening(way):
            return lambda a, b, c, d, strips: (*send(lay, way, (a, b), (c, d)), beside(strips))

        def plain(way):
            return lambda a, b, c, d: send(lay, way, (a, b), (c, d))

        def later(t, held):
            takes = plan[lay.takes : lay.place]
            sent = [lax.dynamic_index_in_dim(plan, lay.sends + 2 * t + n, keepdims=False) for n in range(2)]
            wanted = [lax.dynamic_index_in_dim(plan, lay.patterns + 2 * t + n, keepdims=False) for n in range(2)]
            out = [lax.dynamic_index_in_dim(x, j, keepdims=False) for x in (state, strips) for j in sent]
            got = lax.switch(wanted[0] * lay.kinds + wanted[1], [plain(way) for way in chains], *out)
            kept = []
            for x in range(2):
                for i in range(per_dev):
                    up, down = takes[i] == 2 * t, takes[i] == 2 * t + 1
                    new = jnp.where(up, got[2 * x], got[2 * x + 1])
                    kept.append(jnp.where(up | down, new, held[2 * x + i]))
            return tuple(kept)

        *got, sides = lax.switch(index[0], [opening(way) for way in chains + singles], *out, strips)
        several = lambda *held: lax.fori_loop(1, plan[0], later, held)
        second = lax.switch(following[0], [plain(way) for way in chains] + [several], *second)

    assert per_dev == 2
    fields = (*got[:2], *second[:2])
    side, top, bottom = pack(lay, plan, state, fields, kick, forcing, sides, (*got[2:], *second[2:]))
    return plan[lay.place :], (state, *fields), side, top, bottom


def cut(rows, strip, v):
    width = rows.shape[1]
    count = -(-width // SPAN)
    lane = lane_index((rows.shape[0], LANES))
    source = [rows[:, LANES * t : LANES * (t + 1)] for t in range(width // LANES)]
    tiles = []
    for c in range(count):
        first = SPAN * c - HALO
        if c == 0:
            tile = jnp.where(lane < HALO, turn(strip, -2 * HALO * v), turn(source[0], HALO))
        else:
            t, offset = first // LANES, first % LANES
            if t + 1 < len(source):
                later = turn(source[t + 1], -offset)
            else:
                later = turn(strip, LANES - offset - 2 * HALO * v - HALO)
            tile = jnp.where(lane < LANES - offset, turn(source[t], -offset), later)
        tiles.append(tile)
    return tiles


def step_kernel(
    state_ref, up_ref, down_ref, second_up_ref, second_down_ref, kick_ref, forcing_ref, above_ref, below_ref, side_ref,
    coupling_ref, place_ref, lat_ref, out_ref, cells, other, source, result, table, stage, field, kicks, drive, done,
):
    members, variables, levels, height, width = state_ref.shape
    count = -(-width // SPAN)
    tall = height + 2 * HALO
    at_top = lat_ref[0] == 0
    at_bottom = lat_ref[0] == lat_ref[1] - 1
    options = options_of(state_ref, (up_ref, down_ref, second_up_ref, second_down_ref))

    def fetch(k, wait=()):
        slot = k % 2
        for m in wait or range(members):
            kick = pltpu.make_async_copy(kick_ref.at[m, :, k], kicks.at[slot, m], done.at[2, m])
            if wait:
                pltpu.make_async_copy(kick_ref.at[m, :, k], field.at[slot, m], done.at[1, m]).wait()
                kick.wait()
            else:
                for at, option in enumerate(options):

                    @pl.when(place_ref[m] == at)
                    def _():
                        pltpu.make_async_copy(option.at[:, k], field.at[slot, m], done.at[1, m]).start()

                kick.start()

    def leave(k, m=None, v=None, wait=False):
        if wait:
            for m in range(members):
                pltpu.make_async_copy(stage.at[m], out_ref.at[m, :, k], done.at[0, m]).wait()
        else:
            pltpu.make_async_copy(stage.at[m, v], out_ref.at[m, v, k], done.at[0, m]).start()

    def driven(k):
        return pltpu.make_async_copy(forcing_ref.at[:, k], drive, done.at[3, 0])

    def edge(ref, slot, k, v):
        tiles = width // LANES
        rows = [ref[slot, k, v * tiles + t] for t in range(tiles)]
        return jnp.concatenate(rows, axis=1), ref[slot, k, variables * tiles]

    def lay(rows, strip, v, target, at, scale):
        for c, tile in enumerate(cut(rows, strip, v)):
            target[c, v, at : at + rows.shape[0]] = tile if scale is None else tile * scale

    blocks = tall // ROWS
    pad = ROWS
    origin = lat_ref[2]

    line = lax.broadcasted_iota(jnp.int32, (ROWS, LANES), 0)
    north, south = range(blocks)[0], range(blocks)[-1]

    def advance_tile(step, now, later, c):
        last = step == STEPS - 1
        shared = 0 < step < STEPS - 1
        assert HALO - REACH * 2 <= ROWS // 2

        def load(ref, m, v, r, d=0):
            at = pad + ROWS * r
            return ref[m, c, v, at : at + ROWS] if d == 0 else ref[m, c, v, pl.ds(origin + at + d, ROWS)]

        def view(get, r):
            return jnp.where(line < ROWS // 2, get(south), get(north)) if r is None else get(r)

        inner = list(range(1, blocks - 1))
        for r in inner if last else [None] + inner if shared else range(blocks):
            centre, along, across = [], [], []
            for m in range(members):
                centre.append([view(lambda r: load(now, m, v, r), r) for v in range(variables)])
                ku, kv = K * centre[m][0], K * centre[m][1]
                eu, ev = 8.0 * ku, 8.0 * kv
                along.append((16.0 * K - eu, 16.0 * K + eu, ku - K, -K - ku))
                across.append((16.0 * K - ev, 16.0 * K + ev, kv - K, -K - kv))
            for v in range(variables):
                driving = view(lambda r: source[c, v, ROWS * r : ROWS * (r + 1)], r)
                weights = [table[v * variables + w] for w in range(variables)]
                for m in range(members):
                    q = centre[m][v]
                    shifted = {d: view(lambda r: load(now, m, v, r, d), r) for d in (1, -1, 2, -2)}
                    total = driving
                    for w in range(variables):
                        total += weights[w] * centre[m][w]
                    near = along[m][0] * turn(q, -1) + along[m][1] * turn(q, 1)
                    far = along[m][2] * turn(q, -2) + along[m][3] * turn(q, 2)
                    near += across[m][0] * shifted[1] + across[m][1] * shifted[-1]
                    far += across[m][2] * shifted[2] + across[m][3] * shifted[-2]
                    total += near + far
                    if last:
                        result[m, c, v, ROWS * (r - 1) : ROWS * r] = total
                        continue
                    for to, outside in ((north, at_top), (south, at_bottom)):
                        if r is None or r == to:
                            at = pad + ROWS * to
                            later[m, c, v, at : at + ROWS] = jnp.where(outside, 0.0, total)
                    if r in inner:
                        later[m, c, v, pad + ROWS * r : pad + ROWS * (r + 1)] = total

    fetch(0)
    driven(0).start()

    @pl.loop(0, levels)
    def _(k):
        slot = k % 2
        for m in range(members):
            for v in range(variables):
                lay(*edge(above_ref, m, k, v), v, cells.at[m], pad, None)
                lay(*edge(below_ref, m, k, v), v, cells.at[m], pad + HALO + height, None)
        for v in range(variables):
            lay(*edge(above_ref, members, k, v), v, source, 0, 0.1)
            lay(*edge(below_ref, members, k, v), v, source, HALO + height, 0.1)
            for w in range(variables):
                weight = 0.25 * coupling_ref[(k * variables + v) * variables + w]
                weight = weight + (1.0 - 60.0 * K if v == w else 0.0)
                table[v * variables + w] = jnp.full((ROWS, LANES), weight, jnp.float32)
        for m in range(members):
            fetch(k, wait=(m,))
            for v in range(variables):
                lay(field[slot, m, v] + kicks[slot, m, v], side_ref[m, k], v, cells.at[m], pad + HALO, None)
        driven(k).wait()
        for v in range(variables):
            lay(drive[v], side_ref[members, k], v, source, HALO, 0.1)

        @pl.when(k + 1 < levels)
        def _():
            fetch(k + 1)
            driven(k + 1).start()

        @pl.loop(0, count)
        def _(c):
            for step in range(STEPS):
                now, later = (cells, other) if step % 2 == 0 else (other, cells)
                advance_tile(step, now, later, c)

        lane = lane_index((height, LANES))

        @pl.when(k > 0)
        def _():
            leave(k, wait=True)

        for m in range(members):
            for v in range(variables):
                for t in range(width // LANES):
                    c, offset = LANES * t // SPAN, LANES * t % SPAN
                    left = turn(result[m, c, v], -(offset + HALO))
                    if c + 1 < count:
                        right = turn(result[m, c + 1, v], SPAN - offset - HALO)
                        left = jnp.where(lane < SPAN - offset, left, right)
                    stage[m, v, :, LANES * t : LANES * (t + 1)] = left
                leave(k, m, v)

    leave(0, wait=True)


def advance(place, sources, kick, forcing, above, below, side, coupling):
    members, variables, levels, height, width = kick.shape
    assert height % ROWS == 0 and HALO == ROWS
    count = -(-width // SPAN)
    tall = height + 2 * HALO
    lat = jnp.stack([lax.axis_index("lat"), jnp.int32(lax.axis_size("lat")), jnp.int32(0)])
    here, scalars, anywhere = spec(pltpu.VMEM), spec(pltpu.SMEM), spec(pl.ANY)
    block = (variables, height, width)
    state, *others = sources
    return pl.pallas_call(
        step_kernel,
        in_specs=[anywhere] * 7 + [here] * 3 + [scalars] * 3,
        out_specs=spec(pltpu.HBM),
        out_shape=jax.ShapeDtypeStruct(kick.shape, jnp.float32),
        scratch_shapes=[
            pltpu.VMEM((members, count, variables, tall + 2 * ROWS, LANES), jnp.float32),
            pltpu.VMEM((members, count, variables, tall + 2 * ROWS, LANES), jnp.float32),
            pltpu.VMEM((count, variables, tall, LANES), jnp.float32),
            pltpu.VMEM((members, count, variables, height, LANES), jnp.float32),
            pltpu.VMEM((variables * variables, ROWS, LANES), jnp.float32),
            pltpu.VMEM((members, *block), jnp.float32),
            pltpu.VMEM((2, members, *block), jnp.float32),
            pltpu.VMEM((2, members, *block), jnp.float32),
            pltpu.VMEM(block, jnp.float32),
            pltpu.SemaphoreType.DMA((4, members)),
        ],
        compiler_params=pltpu.CompilerParams(vmem_limit_bytes=VMEM),
    )(
        far_away(state), *others, far_away(kick), far_away(forcing), above, below, side, coupling.reshape(-1), place, lat
    )


def shards(state, kick, forcing, coupling, clone_src):
    place, sources, side, top, bottom = prepared(state, kick, forcing, clone_src)
    above, below = neighbours(top, bottom)
    return advance(place, sources, kick, forcing, above, below, side, coupling)


def solution(mesh):
    in_specs = (
        P("member", None, None, "lat", "lon"),
        P("member", None, None, "lat", "lon"),
        P(None, None, "lat", "lon"),
        P(),
        P(),
    )
    out_specs = P("member", None, None, "lat", "lon")
    return jax.shard_map(shards, mesh=mesh, in_specs=in_specs, out_specs=out_specs, check_vma=False)
```

```python
import functools
import itertools

import functools

import jax
import jax.numpy as jnp
import numpy as np
from jax import lax
from jax.experimental import pallas as pl
from jax.experimental.pallas import tpu as pltpu
from jax.sharding import PartitionSpec as P

STEPS = 4
REACH = 2
HALO = STEPS * REACH
LANES = 128
ROWS = 8
SPAN = LANES - 2 * HALO
K = 0.05 / 12.0
VMEM = 14 * 1024 * 1024


def lane_index(shape):
    return lax.broadcasted_iota(jnp.int32, shape, len(shape) - 1)


def turn(x, shift):
    shift = shift % LANES
    return x if shift == 0 else pltpu.roll(x, shift, x.ndim - 1)


def chain(bits, groups):
    stops = [0] + [x for x in range(1, groups - 1) if bits >> (x - 1) & 1] + [groups - 1]
    return list(zip(stops[:-1], stops[1:]))


SINGLES = 9


def pairings(groups):
    found = []
    for sources in itertools.product(range(groups + 1), repeat=groups):
        pairs = [(a - 1, b) for b, a in enumerate(sources) if a]
        loads = [(e, a < b) for a, b in pairs for e in range(min(a, b), max(a, b))]
        if pairs and len({a for a, _ in pairs}) == len(pairs) and len(set(loads)) == len(loads) and all(a != b for a, b in pairs):
            found.append((sum(a * (groups + 1) ** b for b, a in enumerate(sources)), pairs))
    return found


class Layout:
    def __init__(self, groups, per_dev):
        self.groups, self.per_dev = groups, per_dev
        self.most = per_dev * (groups - 1)
        self.patterns, self.sends = 1, 1 + 2 * self.most
        self.takes = self.sends + 2 * self.most
        self.place = self.takes + per_dev
        self.size = self.place + per_dev
        self.kinds = 1 + (1 << (groups - 2))
        self.pairings = pairings(groups)
        largest = [p for _, p in self.pairings if not any(set(p) < set(q) for _, q in self.pairings)]
        self.singles = sorted(largest, key=lambda p: (-len(p), sum(abs(a - b) for a, b in p)))[:SINGLES]

    def table(self):
        table = np.zeros(((self.groups + 1) ** self.groups,), np.int32)
        for code, pairs in self.pairings:
            if len({a < b for a, b in pairs}) == 2:
                fits = [n for n, single in enumerate(self.singles) if set(pairs) <= set(single)]
                table[code] = self.kinds * self.kinds + fits[0] if fits else 0
        return table


def plan_lines(lay, clone_ref, group_ref, plan_ref, index_refs, ends, owner, used, twice, falls, lookup):
    groups, per_dev, most = lay.groups, lay.per_dev, lay.most
    me = group_ref[0]
    plan_ref[0] = 1
    for t in range(2 * most):
        plan_ref[lay.patterns + t] = 0
        plan_ref[lay.sends + t] = 0
    for t in range(most):
        twice[t] = 0
        falls[t] = 0
        for g in range(groups):
            owner[t * groups + g] = 0
            used[t * groups + g] = 0
    for i in range(per_dev):
        plan_ref[lay.takes + i] = -1 - clone_ref[me * per_dev + i] % per_dev

    for down in range(2):
        for t in range(most):
            ends[t] = 0
        for a in range(groups - 1):
            for b in range(a + 1, groups):
                source, target = (groups - 1 - a, groups - 1 - b) if down else (a, b)
                spans = sum(1 << (x - 1) for x in range(a + 1, b))
                for j in range(per_dev):
                    member = source * per_dev + j
                    wanted = [clone_ref[target * per_dev + i] == member for i in range(per_dev)]
                    need = functools.reduce(jnp.logical_or, wanted)

                    @pl.when(need)
                    def _():
                        t = jnp.int32(most - 1)
                        for earlier in reversed(range(most - 1)):
                            t = jnp.where(ends[earlier] <= a, earlier, t)
                        ends[t] = b
                        plan_ref[0] = jnp.maximum(plan_ref[0], t + 1)
                        at = 2 * t + down
                        before = plan_ref[lay.patterns + at]
                        bits = jnp.where(before == 0, lay.kinds - 2, before - 1)
                        plan_ref[lay.patterns + at] = 1 + (bits & ~spans)
                        giver, taker = t * groups + source, t * groups + target
                        twice[t] = twice[t] | used[giver] | owner[taker]
                        used[giver] = 1
                        owner[taker] = source + 1

                        @pl.when(me == source)
                        def _():
                            plan_ref[lay.sends + at] = j
                            falls[t] = down

                        for i in range(per_dev):

                            @pl.when((me == target) & wanted[i])
                            def _():
                                plan_ref[lay.takes + i] = at

    lookup[1].wait()
    rounds = plan_ref[0]
    code = jnp.int32(0)
    for g in reversed(range(groups)):
        code = code * (groups + 1) + owner[g]
    branch = lookup[0][code]
    single = (twice[0] == 0) & (branch > 0)
    chains = [plan_ref[lay.patterns + 2 * t] * lay.kinds + plan_ref[lay.patterns + 2 * t + 1] for t in range(2)]
    index_refs[0][0] = jnp.where(single, branch, chains[0])
    index_refs[1][0] = jnp.where(rounds > 2, lay.kinds * lay.kinds, chains[1])

    @pl.when(single & (falls[0] == 1))
    def _():
        plan_ref[lay.sends] = plan_ref[lay.sends + 1]

    for i in range(per_dev):
        take = plan_ref[lay.takes + i]
        slot = jnp.where(single & (take < 2), 0, take)
        far = per_dev + jnp.where((take < 2) | (rounds == 2), slot, 2 + i)
        plan_ref[lay.place + i] = jnp.where(take < 0, -1 - take, far)


def first_kernel(
    lay, clone_ref, table_ref, group_ref, state_ref, kick_ref, forcing_ref, plan_ref, index_ref, second_ref, *refs
):
    fields, sides, strips_ref = refs[:4], refs[4:8], refs[8]
    sources, table, ends, owner, used, twice, falls, held, kick_ends, forcing_ends, done = refs[-11:]
    members, variables, levels, height, width = state_ref.shape
    copies = [pltpu.make_async_copy(clone_ref, sources, done.at[0]), pltpu.make_async_copy(state_ref, held, done.at[1])]
    for side, at in enumerate((0, width - LANES)):
        for ref, part in ((kick_ref, kick_ends), (forcing_ref, forcing_ends)):
            piece = ref.at[(slice(None),) * (len(ref.shape) - 1) + (pl.ds(at, LANES),)]
            copies.append(pltpu.make_async_copy(piece, part.at[side], done.at[len(copies)]))
    listed = pltpu.make_async_copy(table_ref, table, done.at[8])
    for copy in [copies[0], listed, *copies[1:]]:
        copy.start()
    copies[0].wait()
    indices = index_ref, second_ref
    plan_lines(lay, sources, group_ref, plan_ref, indices, ends, owner, used, twice, falls, (table, listed))
    copies[1].wait()
    sent = [plan_ref[lay.sends + n] for n in range(4)]
    given = [plan_ref[lay.patterns + n] for n in range(4)]
    wanted = [given[0] + given[1] > 0, given[1] > 0, given[2] > 0, given[3] > 0]
    later = [pltpu.make_async_copy(held.at[sent[n]], fields[n], done.at[4 + n]) for n in (2, 3)]
    for n in range(2):
        pl.when(wanted[2 + n])(later[n].start)

        @pl.when(wanted[n])
        def _():
            @pl.loop(0, variables)
            def _(v):
                for k in range(levels):
                    fields[n][v, k] = held[sent[n], v, k]

    for copy in copies[2:]:
        copy.wait()
    lane = lane_index((height, LANES))

    @pl.loop(0, levels)
    def _(k):
        for slot in range(2 * members + 1):
            strip = jnp.zeros((height, LANES), jnp.float32)
            for v in range(variables):
                if slot < members:
                    low, high = (held[slot, v, k, :, at : at + LANES] for at in (0, width - LANES))
                elif slot < 2 * members:
                    low, high = (kick_ends[side, slot - members, v, k] for side in range(2))
                else:
                    low, high = (forcing_ends[side, v, k] for side in range(2))
                both = turn(jnp.where(lane < HALO, low, high), HALO + 2 * HALO * v)
                strip = jnp.where(lane >= 2 * HALO * v, both, strip)
            strips_ref[slot, k] = strip

    for ref, j in zip(sides, sent):
        ref[...] = strips_ref[j]
    for n in range(2):
        pl.when(wanted[2 + n])(later[n].wait)


def spec(space):
    return pl.BlockSpec(memory_space=space)


def first(lay, group, clone_src, state, kick, forcing):
    members, variables, levels, height, width = state.shape
    shape = jax.ShapeDtypeStruct
    one = pltpu.VMEM(state.shape[1:], jnp.float32)
    side = pltpu.VMEM((levels, height, LANES), jnp.float32)
    strips = pltpu.VMEM((2 * members + 1, levels, height, LANES), jnp.float32)
    ends = (2, members, variables, levels, height, LANES)
    scalar, here, far = spec(pltpu.SMEM), spec(pltpu.VMEM), spec(pltpu.HBM)
    return pl.pallas_call(
        functools.partial(first_kernel, lay),
        in_specs=[far, far, scalar, far, far, far],
        out_specs=[scalar] * 3 + [here] * 2 + [spec(pl.ANY)] * 2 + [here] * 5,
        out_shape=[shape((lay.size,), jnp.int32)] + [shape((1,), jnp.int32)] * 2 + [one] * 2 + [pltpu.HBM(state.shape[1:], jnp.float32)] * 2 + [side] * 4 + [strips],
        scratch_shapes=[
            pltpu.SMEM(clone_src.shape, jnp.int32),
            pltpu.SMEM(lay.table().shape, jnp.int32),
            pltpu.SMEM((lay.most,), jnp.int32),
            pltpu.SMEM((lay.most * lay.groups,), jnp.int32),
            pltpu.SMEM((lay.most * lay.groups,), jnp.int32),
            pltpu.SMEM((lay.most,), jnp.int32),
            pltpu.SMEM((lay.most,), jnp.int32),
            pltpu.VMEM(state.shape, jnp.float32),
            pltpu.VMEM(ends, jnp.float32),
            pltpu.VMEM((2, *ends[2:]), jnp.float32),
            pltpu.SemaphoreType.DMA((9,)),
        ],
        compiler_params=pltpu.CompilerParams(vmem_limit_bytes=VMEM),
    )(far_away(clone_src), far_away(jnp.asarray(lay.table())), group[None], far_away(state), far_away(kick), far_away(forcing))


def far_away(x):
    return pltpu.with_memory_space_constraint(x, pltpu.HBM)


def edge_shape(members, forcing):
    variables, levels, height, width = forcing.shape
    return jax.ShapeDtypeStruct((members, levels, variables * width // LANES + 1, HALO, LANES), jnp.float32)


def options_of(state_ref, refs):
    return [state_ref.at[j] for j in range(state_ref.shape[0])] + list(refs)


def pack_kernel(
    lay, plan_ref, state_ref, up_ref, down_ref, second_up_ref, second_down_ref, kick_ref, forcing_ref,
    sides_ref, up_side_ref, down_side_ref, second_up_side_ref, second_down_side_ref,
    side_ref, top_ref, bottom_ref, field_rows, kick_rows, forcing_rows, strips, picked, done,
):
    members, variables, levels, height, width = state_ref.shape
    tiles = width // LANES
    whole = options_of(state_ref, (up_ref, down_ref, second_up_ref, second_down_ref))
    parts = [sides_ref.at[j] for j in range(members)]
    parts += [up_side_ref, down_side_ref, second_up_side_ref, second_down_side_ref]
    places = [plan_ref[lay.place + i] for i in range(members)]
    rows = [pl.ds(0, HALO), pl.ds(height - HALO, HALO)]
    f_copies = [pltpu.make_async_copy(forcing_ref.at[:, :, rows[n]], forcing_rows.at[n], done.at[0]) for n in range(2)]
    copies = []
    for i in range(members):
        for n in range(2):
            for at, option in enumerate(whole):

                @pl.when(places[i] == at)
                def _():
                    pltpu.make_async_copy(option.at[:, :, rows[n]], field_rows.at[i, n], done.at[1 + i]).start()

            copies.append(pltpu.make_async_copy(kick_ref.at[i, :, :, rows[n]], kick_rows.at[i, n], done.at[1 + i]))
    strip_copies = [pltpu.make_async_copy(sides_ref, strips, done.at[1 + members])]
    for i in range(members):
        for at, part in enumerate(parts):

            @pl.when(places[i] == at)
            def _():
                pltpu.make_async_copy(part, picked.at[i], done.at[2 + members + i]).start()

        strip_copies.append(pltpu.make_async_copy(up_side_ref, picked.at[i], done.at[2 + members + i]))
    for copy in [strip_copies[0]] + f_copies + copies:
        copy.start()

    def flank(slot, k, strip):
        side_ref[slot, k] = strip
        top_ref[slot, k, variables * tiles] = strip[:HALO]
        bottom_ref[slot, k, variables * tiles] = strip[height - HALO :]

    def edges(slot, rows_of):
        @pl.loop(0, levels)
        def _(k):
            for n, ref in enumerate((top_ref, bottom_ref)):
                for v in range(variables):
                    edge = rows_of(n, v, k)
                    for t in range(tiles):
                        ref[slot, k, v * tiles + t] = edge[:, LANES * t : LANES * (t + 1)]

    for copy in strip_copies:
        copy.wait()
    for k in range(levels):
        flank(members, k, strips[2 * members, k])
        for i in range(members):
            flank(i, k, picked[i, k] + strips[members + i, k])
    for copy in f_copies:
        copy.wait()
    edges(members, lambda n, v, k: forcing_rows[n, v, k])
    for i in range(members):
        for n in range(2):
            pltpu.make_async_copy(kick_ref.at[i, :, :, rows[n]], field_rows.at[i, n], done.at[1 + i]).wait()
            copies[2 * i + n].wait()
        edges(i, lambda n, v, k: field_rows[i, n, v, k] + kick_rows[i, n, v, k])


def pack(lay, plan, state, fields, kick, forcing, sides, far_sides):
    members, variables, levels, height, width = state.shape
    here, anywhere = spec(pltpu.VMEM), spec(pl.ANY)
    rows = (members, 2, variables, levels, HALO, width)
    return pl.pallas_call(
        functools.partial(pack_kernel, lay),
        in_specs=[spec(pltpu.SMEM)] + [anywhere] * 12,
        out_specs=[here] * 3,
        out_shape=[
            jax.ShapeDtypeStruct((members + 1, levels, height, LANES), jnp.float32),
            edge_shape(members + 1, forcing),
            edge_shape(members + 1, forcing),
        ],
        scratch_shapes=[
            pltpu.VMEM(rows, jnp.float32),
            pltpu.VMEM(rows, jnp.float32),
            pltpu.VMEM(rows[1:], jnp.float32),
            pltpu.VMEM(sides.shape, jnp.float32),
            pltpu.VMEM((members, levels, height, LANES), jnp.float32),
            pltpu.SemaphoreType.DMA((2 + 2 * members,)),
        ],
        compiler_params=pltpu.CompilerParams(vmem_limit_bytes=VMEM),
    )(plan, far_away(state), *fields, far_away(kick), far_away(forcing), sides, *far_sides)


def blank(*like):
    return pl.pallas_call(
        lambda *refs: None,
        out_specs=[spec(pl.ANY)] * len(like),
        out_shape=[jax.ShapeDtypeStruct(x.shape, x.dtype) for x in like],
        compiler_params=pltpu.CompilerParams(vmem_limit_bytes=1024 * 1024),
    )()


def neighbours(top, bottom):
    lats = lax.axis_size("lat")
    above = lax.ppermute(bottom, "lat", [(i, i + 1) for i in range(lats - 1)])
    below = lax.ppermute(top, "lat", [(i + 1, i) for i in range(lats - 1)])
    return above, below


def beside(strips):
    assert lax.axis_size("lon") == 2
    return lax.ppermute(strips, "lon", [(0, 1), (1, 0)])


def send(lay, ways, fields, sides):
    lons = lax.axis_size("lon")
    fields, sides = list(fields), list(sides)
    for n, pairs in enumerate(ways):
        if pairs:
            crossed = [(a * lons + j, b * lons + 1 - j) for a, b in pairs for j in range(lons)]
            fields[n] = lax.ppermute(fields[n], "member", pairs)
            sides[n] = lax.ppermute(sides[n], ("member", "lon"), crossed)
        else:
            fields[n], sides[n] = blank(fields[n], sides[n])
    return (*fields, *sides)


def routes(lay):
    top = lay.groups - 1

    def both(up, down):
        rising = chain(up - 1, lay.groups) if up else []
        falling = [(top - a, top - b) for a, b in chain(down - 1, lay.groups)] if down else []
        return rising, falling

    chains = [both(up, down) for up in range(lay.kinds) for down in range(lay.kinds)]
    return chains, [(pairs, []) for pairs in lay.singles]


def prepared(state, kick, forcing, clone_src):
    per_dev, groups, group = state.shape[0], lax.axis_size("member"), lax.axis_index("member")
    lay = Layout(4 if groups == 4 else 3, per_dev)
    if groups != 4:
        piece = lax.all_gather(state, "member", axis=0, tiled=True)
        sources = lax.dynamic_slice_in_dim(clone_src, group * per_dev, per_dev)
        state = jnp.take(piece, sources, axis=0, mode="clip")
        still = jnp.arange(per_dev * 3, dtype=jnp.int32)
        plan, _, _, *out, strips = first(lay, jnp.int32(0), still, state, kick, forcing)
        got, second = (*out[:2], *out[4:6]), (*out[2:4], *out[6:])
        sides = beside(strips)
    else:
        plan, index, following, *out, strips = first(lay, group, clone_src, state, kick, forcing)
        out, second = (*out[:2], *out[4:6]), (*out[2:4], *out[6:])
        chains, singles = routes(lay)

        def opening(way):
            return lambda a, b, c, d, strips: (*send(lay, way, (a, b), (c, d)), beside(strips))

        def plain(way):
            return lambda a, b, c, d: send(lay, way, (a, b), (c, d))

        def later(t, held):
            takes = plan[lay.takes : lay.place]
            sent = [lax.dynamic_index_in_dim(plan, lay.sends + 2 * t + n, keepdims=False) for n in range(2)]
            wanted = [lax.dynamic_index_in_dim(plan, lay.patterns + 2 * t + n, keepdims=False) for n in range(2)]
            out = [lax.dynamic_index_in_dim(x, j, keepdims=False) for x in (state, strips) for j in sent]
            got = lax.switch(wanted[0] * lay.kinds + wanted[1], [plain(way) for way in chains], *out)
            kept = []
            for x in range(2):
                for i in range(per_dev):
                    up, down = takes[i] == 2 * t, takes[i] == 2 * t + 1
                    new = jnp.where(up, got[2 * x], got[2 * x + 1])
                    kept.append(jnp.where(up | down, new, held[2 * x + i]))
            return tuple(kept)

        *got, sides = lax.switch(index[0], [opening(way) for way in chains + singles], *out, strips)
        several = lambda *held: lax.fori_loop(1, plan[0], later, held)
        second = lax.switch(following[0], [plain(way) for way in chains] + [several], *second)

    assert per_dev == 2
    fields = (*got[:2], *second[:2])
    side, top, bottom = pack(lay, plan, state, fields, kick, forcing, sides, (*got[2:], *second[2:]))
    return plan[lay.place :], (state, *fields), side, top, bottom


def cut(rows, strip, v):
    width = rows.shape[1]
    count = -(-width // SPAN)
    lane = lane_index((rows.shape[0], LANES))
    source = [rows[:, LANES * t : LANES * (t + 1)] for t in range(width // LANES)]
    tiles = []
    for c in range(count):
        first = SPAN * c - HALO
        if c == 0:
            tile = jnp.where(lane < HALO, turn(strip, -2 * HALO * v), turn(source[0], HALO))
        else:
            t, offset = first // LANES, first % LANES
            if t + 1 < len(source):
                later = turn(source[t + 1], -offset)
            else:
                later = turn(strip, LANES - offset - 2 * HALO * v - HALO)
            tile = jnp.where(lane < LANES - offset, turn(source[t], -offset), later)
        tiles.append(tile)
    return tiles


def step_kernel(
    state_ref, up_ref, down_ref, second_up_ref, second_down_ref, kick_ref, forcing_ref, above_ref, below_ref, side_ref,
    coupling_ref, place_ref, lat_ref, out_ref, cells, other, source, result, table, stage, field, kicks, drive, done,
):
    members, variables, levels, height, width = state_ref.shape
    count = -(-width // SPAN)
    tall = height + 2 * HALO
    at_top = lat_ref[0] == 0
    at_bottom = lat_ref[0] == lat_ref[1] - 1
    options = options_of(state_ref, (up_ref, down_ref, second_up_ref, second_down_ref))

    def fetch(k, wait=()):
        slot = k % 2
        for m in wait or range(members):
            kick = pltpu.make_async_copy(kick_ref.at[m, :, k], kicks.at[slot, m], done.at[2, m])
            if wait:
                pltpu.make_async_copy(kick_ref.at[m, :, k], field.at[slot, m], done.at[1, m]).wait()
                kick.wait()
            else:
                for at, option in enumerate(options):

                    @pl.when(place_ref[m] == at)
                    def _():
                        pltpu.make_async_copy(option.at[:, k], field.at[slot, m], done.at[1, m]).start()

                kick.start()

    def leave(k, m=None, v=None, wait=False):
        if wait:
            for m in range(members):
                pltpu.make_async_copy(stage.at[m], out_ref.at[m, :, k], done.at[0, m]).wait()
        else:
            pltpu.make_async_copy(stage.at[m, v], out_ref.at[m, v, k], done.at[0, m]).start()

    def driven(k):
        return pltpu.make_async_copy(forcing_ref.at[:, k], drive, done.at[3, 0])

    def edge(ref, slot, k, v):
        tiles = width // LANES
        rows = [ref[slot, k, v * tiles + t] for t in range(tiles)]
        return jnp.concatenate(rows, axis=1), ref[slot, k, variables * tiles]

    def lay(rows, strip, v, target, at, scale):
        for c, tile in enumerate(cut(rows, strip, v)):
            target[c, v, at : at + rows.shape[0]] = tile if scale is None else tile * scale

    blocks = tall // ROWS
    pad = ROWS
    origin = lat_ref[2]

    line = lax.broadcasted_iota(jnp.int32, (ROWS, LANES), 0)
    north, south = range(blocks)[0], range(blocks)[-1]

    def advance_tile(step, now, later, c):
        last = step == STEPS - 1
        shared = 0 < step < STEPS - 1
        assert HALO - REACH * 2 <= ROWS // 2

        def load(ref, m, v, r, d=0):
            at = pad + ROWS * r
            return ref[m, c, v, at : at + ROWS] if d == 0 else ref[m, c, v, pl.ds(origin + at + d, ROWS)]

        def view(get, r):
            return jnp.where(line < ROWS // 2, get(south), get(north)) if r is None else get(r)

        inner = list(range(1, blocks - 1))
        for r in inner if last else [None] + inner if shared else range(blocks):
            centre, along, across = [], [], []
            for m in range(members):
                centre.append([view(lambda r: load(now, m, v, r), r) for v in range(variables)])
                ku, kv = K * centre[m][0], K * centre[m][1]
                eu, ev = 8.0 * ku, 8.0 * kv
                along.append((16.0 * K - eu, 16.0 * K + eu, ku - K, -K - ku))
                across.append((16.0 * K - ev, 16.0 * K + ev, kv - K, -K - kv))
            for v in range(variables):
                driving = view(lambda r: source[c, v, ROWS * r : ROWS * (r + 1)], r)
                weights = [table[v * variables + w] for w in range(variables)]
                for m in range(members):
                    q = centre[m][v]
                    shifted = {d: view(lambda r: load(now, m, v, r, d), r) for d in (1, -1, 2, -2)}
                    total = driving
                    for w in range(variables):
                        total += weights[w] * centre[m][w]
                    near = along[m][0] * turn(q, -1) + along[m][1] * turn(q, 1)
                    far = along[m][2] * turn(q, -2) + along[m][3] * turn(q, 2)
                    near += across[m][0] * shifted[1] + across[m][1] * shifted[-1]
                    far += across[m][2] * shifted[2] + across[m][3] * shifted[-2]
                    total += near + far
                    if last:
                        result[m, c, v, ROWS * (r - 1) : ROWS * r] = total
                        continue
                    for to, outside in ((north, at_top), (south, at_bottom)):
                        if r is None or r == to:
                            at = pad + ROWS * to
                            later[m, c, v, at : at + ROWS] = jnp.where(outside, 0.0, total)
                    if r in inner:
                        later[m, c, v, pad + ROWS * r : pad + ROWS * (r + 1)] = total

    fetch(0)
    driven(0).start()

    @pl.loop(0, levels)
    def _(k):
        slot = k % 2
        for m in range(members):
            for v in range(variables):
                lay(*edge(above_ref, m, k, v), v, cells.at[m], pad, None)
                lay(*edge(below_ref, m, k, v), v, cells.at[m], pad + HALO + height, None)
        for v in range(variables):
            lay(*edge(above_ref, members, k, v), v, source, 0, 0.1)
            lay(*edge(below_ref, members, k, v), v, source, HALO + height, 0.1)
            for w in range(variables):
                weight = 0.25 * coupling_ref[(k * variables + v) * variables + w]
                weight = weight + (1.0 - 60.0 * K if v == w else 0.0)
                table[v * variables + w] = jnp.full((ROWS, LANES), weight, jnp.float32)
        for m in range(members):
            fetch(k, wait=(m,))
            for v in range(variables):
                lay(field[slot, m, v] + kicks[slot, m, v], side_ref[m, k], v, cells.at[m], pad + HALO, None)
        driven(k).wait()
        for v in range(variables):
            lay(drive[v], side_ref[members, k], v, source, HALO, 0.1)

        @pl.when(k + 1 < levels)
        def _():
            fetch(k + 1)
            driven(k + 1).start()

        @pl.loop(0, count)
        def _(c):
            for step in range(STEPS):
                now, later = (cells, other) if step % 2 == 0 else (other, cells)
                advance_tile(step, now, later, c)

        lane = lane_index((height, LANES))

        @pl.when(k > 0)
        def _():
            leave(k, wait=True)

        for m in range(members):
            for v in range(variables):
                for t in range(width // LANES):
                    c, offset = LANES * t // SPAN, LANES * t % SPAN
                    left = turn(result[m, c, v], -(offset + HALO))
                    if c + 1 < count:
                        right = turn(result[m, c + 1, v], SPAN - offset - HALO)
                        left = jnp.where(lane < SPAN - offset, left, right)
                    stage[m, v, :, LANES * t : LANES * (t + 1)] = left
                leave(k, m, v)

    leave(0, wait=True)


def advance(place, sources, kick, forcing, above, below, side, coupling):
    members, variables, levels, height, width = kick.shape
    assert height % ROWS == 0 and HALO == ROWS
    count = -(-width // SPAN)
    tall = height + 2 * HALO
    lat = jnp.stack([lax.axis_index("lat"), jnp.int32(lax.axis_size("lat")), jnp.int32(0)])
    here, scalars, anywhere = spec(pltpu.VMEM), spec(pltpu.SMEM), spec(pl.ANY)
    block = (variables, height, width)
    state, *others = sources
    return pl.pallas_call(
        step_kernel,
        in_specs=[anywhere] * 7 + [here] * 3 + [scalars] * 3,
        out_specs=spec(pltpu.HBM),
        out_shape=jax.ShapeDtypeStruct(kick.shape, jnp.float32),
        scratch_shapes=[
            pltpu.VMEM((members, count, variables, tall + 2 * ROWS, LANES), jnp.float32),
            pltpu.VMEM((members, count, variables, tall + 2 * ROWS, LANES), jnp.float32),
            pltpu.VMEM((count, variables, tall, LANES), jnp.float32),
            pltpu.VMEM((members, count, variables, height, LANES), jnp.float32),
            pltpu.VMEM((variables * variables, ROWS, LANES), jnp.float32),
            pltpu.VMEM((members, *block), jnp.float32),
            pltpu.VMEM((2, members, *block), jnp.float32),
            pltpu.VMEM((2, members, *block), jnp.float32),
            pltpu.VMEM(block, jnp.float32),
            pltpu.SemaphoreType.DMA((4, members)),
        ],
        compiler_params=pltpu.CompilerParams(vmem_limit_bytes=VMEM),
    )(
        far_away(state), *others, far_away(kick), far_away(forcing), above, below, side, coupling.reshape(-1), place, lat
    )


def shards(state, kick, forcing, coupling, clone_src):
    place, sources, side, top, bottom = prepared(state, kick, forcing, clone_src)
    above, below = neighbours(top, bottom)
    return advance(place, sources, kick, forcing, above, below, side, coupling)


def solution(mesh):
    in_specs = (
        P("member", None, None, "lat", "lon"),
        P("member", None, None, "lat", "lon"),
        P(None, None, "lat", "lon"),
        P(),
        P(),
    )
    out_specs = P("member", None, None, "lat", "lon")
    return jax.shard_map(shards, mesh=mesh, in_specs=in_specs, out_specs=out_specs, check_vma=False)
```

```python
import functools
import itertools

import functools

import jax
import jax.numpy as jnp
import numpy as np
from jax import lax
from jax.experimental import pallas as pl
from jax.experimental.pallas import tpu as pltpu
from jax.sharding import PartitionSpec as P

STEPS = 4
REACH = 2
HALO = STEPS * REACH
LANES = 128
ROWS = 8
SPAN = LANES - 2 * HALO
K = 0.05 / 12.0
VMEM = 14 * 1024 * 1024


def lane_index(shape):
    return lax.broadcasted_iota(jnp.int32, shape, len(shape) - 1)


def turn(x, shift):
    shift = shift % LANES
    return x if shift == 0 else pltpu.roll(x, shift, x.ndim - 1)


def chain(bits, groups):
    stops = [0] + [x for x in range(1, groups - 1) if bits >> (x - 1) & 1] + [groups - 1]
    return list(zip(stops[:-1], stops[1:]))


SINGLES = 9


def pairings(groups):
    found = []
    for sources in itertools.product(range(groups + 1), repeat=groups):
        pairs = [(a - 1, b) for b, a in enumerate(sources) if a]
        loads = [(e, a < b) for a, b in pairs for e in range(min(a, b), max(a, b))]
        if pairs and len({a for a, _ in pairs}) == len(pairs) and len(set(loads)) == len(loads) and all(a != b for a, b in pairs):
            found.append((sum(a * (groups + 1) ** b for b, a in enumerate(sources)), pairs))
    return found


class Layout:
    def __init__(self, groups, per_dev):
        self.groups, self.per_dev = groups, per_dev
        self.most = per_dev * (groups - 1)
        self.patterns, self.sends = 1, 1 + 2 * self.most
        self.takes = self.sends + 2 * self.most
        self.place = self.takes + per_dev
        self.size = self.place + per_dev
        self.kinds = 1 + (1 << (groups - 2))
        self.pairings = pairings(groups)
        largest = [p for _, p in self.pairings if not any(set(p) < set(q) for _, q in self.pairings)]
        self.singles = sorted(largest, key=lambda p: (-len(p), sum(abs(a - b) for a, b in p)))[:SINGLES]

    def table(self):
        table = np.zeros(((self.groups + 1) ** self.groups,), np.int32)
        for code, pairs in self.pairings:
            if len({a < b for a, b in pairs}) == 2:
                fits = [n for n, single in enumerate(self.singles) if set(pairs) <= set(single)]
                table[code] = self.kinds * self.kinds + fits[0] if fits else 0
        return table


def plan_lines(lay, clone_ref, group_ref, plan_ref, index_refs, ends, owner, used, twice, falls, lookup):
    groups, per_dev, most = lay.groups, lay.per_dev, lay.most
    me = group_ref[0]
    plan_ref[0] = 1
    for t in range(2 * most):
        plan_ref[lay.patterns + t] = 0
        plan_ref[lay.sends + t] = 0
    for t in range(most):
        twice[t] = 0
        falls[t] = 0
        for g in range(groups):
            owner[t * groups + g] = 0
            used[t * groups + g] = 0
    for i in range(per_dev):
        plan_ref[lay.takes + i] = -1 - clone_ref[me * per_dev + i] % per_dev

    for down in range(2):
        for t in range(most):
            ends[t] = 0
        for a in range(groups - 1):
            for b in range(a + 1, groups):
                source, target = (groups - 1 - a, groups - 1 - b) if down else (a, b)
                spans = sum(1 << (x - 1) for x in range(a + 1, b))
                for j in range(per_dev):
                    member = source * per_dev + j
                    wanted = [clone_ref[target * per_dev + i] == member for i in range(per_dev)]
                    need = functools.reduce(jnp.logical_or, wanted)

                    @pl.when(need)
                    def _():
                        t = jnp.int32(most - 1)
                        for earlier in reversed(range(most - 1)):
                            t = jnp.where(ends[earlier] <= a, earlier, t)
                        ends[t] = b
                        plan_ref[0] = jnp.maximum(plan_ref[0], t + 1)
                        at = 2 * t + down
                        before = plan_ref[lay.patterns + at]
                        bits = jnp.where(before == 0, lay.kinds - 2, before - 1)
                        plan_ref[lay.patterns + at] = 1 + (bits & ~spans)
                        giver, taker = t * groups + source, t * groups + target
                        twice[t] = twice[t] | used[giver] | owner[taker]
                        used[giver] = 1
                        owner[taker] = source + 1

                        @pl.when(me == source)
                        def _():
                            plan_ref[lay.sends + at] = j
                            falls[t] = down

                        for i in range(per_dev):

                            @pl.when((me == target) & wanted[i])
                            def _():
                                plan_ref[lay.takes + i] = at

    lookup[1].wait()
    rounds = plan_ref[0]
    code = jnp.int32(0)
    for g in reversed(range(groups)):
        code = code * (groups + 1) + owner[g]
    branch = lookup[0][code]
    single = (twice[0] == 0) & (branch > 0)
    chains = [plan_ref[lay.patterns + 2 * t] * lay.kinds + plan_ref[lay.patterns + 2 * t + 1] for t in range(3)]
    index_refs[0][0] = jnp.where(single, branch, chains[0])
    index_refs[1][0] = chains[1]
    index_refs[2][0] = jnp.where(rounds > 3, lay.kinds * lay.kinds, chains[2])

    @pl.when(single & (falls[0] == 1))
    def _():
        plan_ref[lay.sends] = plan_ref[lay.sends + 1]

    for i in range(per_dev):
        take = plan_ref[lay.takes + i]
        slot = jnp.where(single & (take < 2), 0, take)
        far = per_dev + jnp.where((take < 4) | (rounds == 3), slot, 4 + i)
        plan_ref[lay.place + i] = jnp.where(take < 0, -1 - take, far)


def first_kernel(
    lay, clone_ref, table_ref, group_ref, state_ref, kick_ref, forcing_ref, plan_ref, index_ref, second_ref, third_ref, *refs
):
    fields, sides, strips_ref = refs[:6], refs[6:12], refs[12]
    sources, table, ends, owner, used, twice, falls, held, kick_ends, forcing_ends, done = refs[-11:]
    members, variables, levels, height, width = state_ref.shape
    copies = [pltpu.make_async_copy(clone_ref, sources, done.at[0]), pltpu.make_async_copy(state_ref, held, done.at[1])]
    for side, at in enumerate((0, width - LANES)):
        for ref, part in ((kick_ref, kick_ends), (forcing_ref, forcing_ends)):
            piece = ref.at[(slice(None),) * (len(ref.shape) - 1) + (pl.ds(at, LANES),)]
            copies.append(pltpu.make_async_copy(piece, part.at[side], done.at[len(copies)]))
    listed = pltpu.make_async_copy(table_ref, table, done.at[10])
    for copy in [copies[0], listed, *copies[1:]]:
        copy.start()
    copies[0].wait()
    indices = index_ref, second_ref, third_ref
    plan_lines(lay, sources, group_ref, plan_ref, indices, ends, owner, used, twice, falls, (table, listed))
    copies[1].wait()
    sent = [plan_ref[lay.sends + n] for n in range(6)]
    given = [plan_ref[lay.patterns + n] for n in range(6)]
    wanted = [given[0] + given[1] > 0, *(given[n] > 0 for n in range(1, 6))]
    later = [pltpu.make_async_copy(held.at[sent[n]], fields[n], done.at[4 + n]) for n in range(2, 6)]
    for n in range(4):
        pl.when(wanted[2 + n])(later[n].start)
    for n in range(2):

        @pl.when(wanted[n])
        def _():
            @pl.loop(0, variables)
            def _(v):
                for k in range(levels):
                    fields[n][v, k] = held[sent[n], v, k]

    for copy in copies[2:]:
        copy.wait()
    lane = lane_index((height, LANES))

    @pl.loop(0, levels)
    def _(k):
        for slot in range(2 * members + 1):
            strip = jnp.zeros((height, LANES), jnp.float32)
            for v in range(variables):
                if slot < members:
                    low, high = (held[slot, v, k, :, at : at + LANES] for at in (0, width - LANES))
                elif slot < 2 * members:
                    low, high = (kick_ends[side, slot - members, v, k] for side in range(2))
                else:
                    low, high = (forcing_ends[side, v, k] for side in range(2))
                both = turn(jnp.where(lane < HALO, low, high), HALO + 2 * HALO * v)
                strip = jnp.where(lane >= 2 * HALO * v, both, strip)
            strips_ref[slot, k] = strip

    for ref, j in zip(sides, sent):
        ref[...] = strips_ref[j]
    for n in range(4):
        pl.when(wanted[2 + n])(later[n].wait)


def spec(space):
    return pl.BlockSpec(memory_space=space)


def first(lay, group, clone_src, state, kick, forcing):
    members, variables, levels, height, width = state.shape
    shape = jax.ShapeDtypeStruct
    one = pltpu.VMEM(state.shape[1:], jnp.float32)
    side = pltpu.VMEM((levels, height, LANES), jnp.float32)
    strips = pltpu.VMEM((2 * members + 1, levels, height, LANES), jnp.float32)
    ends = (2, members, variables, levels, height, LANES)
    scalar, here, far = spec(pltpu.SMEM), spec(pltpu.VMEM), spec(pltpu.HBM)
    return pl.pallas_call(
        functools.partial(first_kernel, lay),
        in_specs=[far, far, scalar, far, far, far],
        out_specs=[scalar] * 4 + [here] * 2 + [spec(pl.ANY)] * 4 + [here] * 7,
        out_shape=[shape((lay.size,), jnp.int32)] + [shape((1,), jnp.int32)] * 3 + [one] * 2 + [pltpu.HBM(state.shape[1:], jnp.float32)] * 4 + [side] * 6 + [strips],
        scratch_shapes=[
            pltpu.SMEM(clone_src.shape, jnp.int32),
            pltpu.SMEM(lay.table().shape, jnp.int32),
            pltpu.SMEM((lay.most,), jnp.int32),
            pltpu.SMEM((lay.most * lay.groups,), jnp.int32),
            pltpu.SMEM((lay.most * lay.groups,), jnp.int32),
            pltpu.SMEM((lay.most,), jnp.int32),
            pltpu.SMEM((lay.most,), jnp.int32),
            pltpu.VMEM(state.shape, jnp.float32),
            pltpu.VMEM(ends, jnp.float32),
            pltpu.VMEM((2, *ends[2:]), jnp.float32),
            pltpu.SemaphoreType.DMA((11,)),
        ],
        compiler_params=pltpu.CompilerParams(vmem_limit_bytes=VMEM),
    )(far_away(clone_src), far_away(jnp.asarray(lay.table())), group[None], far_away(state), far_away(kick), far_away(forcing))


def far_away(x):
    return pltpu.with_memory_space_constraint(x, pltpu.HBM)


def edge_shape(members, forcing):
    variables, levels, height, width = forcing.shape
    return jax.ShapeDtypeStruct((members, levels, variables * width // LANES + 1, HALO, LANES), jnp.float32)


def options_of(state_ref, refs):
    return [state_ref.at[j] for j in range(state_ref.shape[0])] + list(refs)


def pack_kernel(
    lay, plan_ref, state_ref, *refs
):
    others, (kick_ref, forcing_ref, sides_ref), others_sides = refs[:6], refs[6:9], refs[9:15]
    side_ref, top_ref, bottom_ref, field_rows, kick_rows, forcing_rows, strips, picked, done = refs[15:]
    up_ref, up_side_ref = others[0], others_sides[0]
    members, variables, levels, height, width = state_ref.shape
    tiles = width // LANES
    whole = options_of(state_ref, others)
    parts = [sides_ref.at[j] for j in range(members)]
    parts += others_sides
    places = [plan_ref[lay.place + i] for i in range(members)]
    rows = [pl.ds(0, HALO), pl.ds(height - HALO, HALO)]
    f_copies = [pltpu.make_async_copy(forcing_ref.at[:, :, rows[n]], forcing_rows.at[n], done.at[0]) for n in range(2)]
    copies = []
    for i in range(members):
        for n in range(2):
            for at, option in enumerate(whole):

                @pl.when(places[i] == at)
                def _():
                    pltpu.make_async_copy(option.at[:, :, rows[n]], field_rows.at[i, n], done.at[1 + i]).start()

            copies.append(pltpu.make_async_copy(kick_ref.at[i, :, :, rows[n]], kick_rows.at[i, n], done.at[1 + i]))
    strip_copies = [pltpu.make_async_copy(sides_ref, strips, done.at[1 + members])]
    for i in range(members):
        for at, part in enumerate(parts):

            @pl.when(places[i] == at)
            def _():
                pltpu.make_async_copy(part, picked.at[i], done.at[2 + members + i]).start()

        strip_copies.append(pltpu.make_async_copy(up_side_ref, picked.at[i], done.at[2 + members + i]))
    for copy in [strip_copies[0]] + f_copies + copies:
        copy.start()

    def flank(slot, k, strip):
        side_ref[slot, k] = strip
        top_ref[slot, k, variables * tiles] = strip[:HALO]
        bottom_ref[slot, k, variables * tiles] = strip[height - HALO :]

    def edges(slot, rows_of):
        @pl.loop(0, levels)
        def _(k):
            for n, ref in enumerate((top_ref, bottom_ref)):
                for v in range(variables):
                    edge = rows_of(n, v, k)
                    for t in range(tiles):
                        ref[slot, k, v * tiles + t] = edge[:, LANES * t : LANES * (t + 1)]

    for copy in strip_copies:
        copy.wait()
    for k in range(levels):
        flank(members, k, strips[2 * members, k])
        for i in range(members):
            flank(i, k, picked[i, k] + strips[members + i, k])
    for copy in f_copies:
        copy.wait()
    edges(members, lambda n, v, k: forcing_rows[n, v, k])
    for i in range(members):
        for n in range(2):
            pltpu.make_async_copy(kick_ref.at[i, :, :, rows[n]], field_rows.at[i, n], done.at[1 + i]).wait()
            copies[2 * i + n].wait()
        edges(i, lambda n, v, k: field_rows[i, n, v, k] + kick_rows[i, n, v, k])


def pack(lay, plan, state, fields, kick, forcing, sides, far_sides):
    members, variables, levels, height, width = state.shape
    here, anywhere = spec(pltpu.VMEM), spec(pl.ANY)
    rows = (members, 2, variables, levels, HALO, width)
    return pl.pallas_call(
        functools.partial(pack_kernel, lay),
        in_specs=[spec(pltpu.SMEM)] + [anywhere] * 16,
        out_specs=[here] * 3,
        out_shape=[
            jax.ShapeDtypeStruct((members + 1, levels, height, LANES), jnp.float32),
            edge_shape(members + 1, forcing),
            edge_shape(members + 1, forcing),
        ],
        scratch_shapes=[
            pltpu.VMEM(rows, jnp.float32),
            pltpu.VMEM(rows, jnp.float32),
            pltpu.VMEM(rows[1:], jnp.float32),
            pltpu.VMEM(sides.shape, jnp.float32),
            pltpu.VMEM((members, levels, height, LANES), jnp.float32),
            pltpu.SemaphoreType.DMA((2 + 2 * members,)),
        ],
        compiler_params=pltpu.CompilerParams(vmem_limit_bytes=VMEM),
    )(plan, far_away(state), *fields, far_away(kick), far_away(forcing), sides, *far_sides)


def blank(*like):
    return pl.pallas_call(
        lambda *refs: None,
        out_specs=[spec(pl.ANY)] * len(like),
        out_shape=[jax.ShapeDtypeStruct(x.shape, x.dtype) for x in like],
        compiler_params=pltpu.CompilerParams(vmem_limit_bytes=1024 * 1024),
    )()


def neighbours(top, bottom):
    lats = lax.axis_size("lat")
    above = lax.ppermute(bottom, "lat", [(i, i + 1) for i in range(lats - 1)])
    below = lax.ppermute(top, "lat", [(i + 1, i) for i in range(lats - 1)])
    return above, below


def beside(strips):
    assert lax.axis_size("lon") == 2
    return lax.ppermute(strips, "lon", [(0, 1), (1, 0)])


def send(lay, ways, fields, sides):
    lons = lax.axis_size("lon")
    fields, sides = list(fields), list(sides)
    for n, pairs in enumerate(ways):
        if pairs:
            crossed = [(a * lons + j, b * lons + 1 - j) for a, b in pairs for j in range(lons)]
            fields[n] = lax.ppermute(fields[n], "member", pairs)
            sides[n] = lax.ppermute(sides[n], ("member", "lon"), crossed)
        else:
            fields[n], sides[n] = blank(fields[n], sides[n])
    return (*fields, *sides)


def routes(lay):
    top = lay.groups - 1

    def both(up, down):
        rising = chain(up - 1, lay.groups) if up else []
        falling = [(top - a, top - b) for a, b in chain(down - 1, lay.groups)] if down else []
        return rising, falling

    chains = [both(up, down) for up in range(lay.kinds) for down in range(lay.kinds)]
    return chains, [(pairs, []) for pairs in lay.singles]


def prepared(state, kick, forcing, clone_src):
    per_dev, groups, group = state.shape[0], lax.axis_size("member"), lax.axis_index("member")
    lay = Layout(4 if groups == 4 else 3, per_dev)
    if groups != 4:
        piece = lax.all_gather(state, "member", axis=0, tiled=True)
        sources = lax.dynamic_slice_in_dim(clone_src, group * per_dev, per_dev)
        state = jnp.take(piece, sources, axis=0, mode="clip")
        still = jnp.arange(per_dev * 3, dtype=jnp.int32)
        plan, _, _, _, *out, strips = first(lay, jnp.int32(0), still, state, kick, forcing)
        fields, far_sides = out[:6], out[6:]
        sides = beside(strips)
    else:
        plan, index, following, final, *out, strips = first(lay, group, clone_src, state, kick, forcing)
        first_out, second, third = ((*out[2 * n : 2 * n + 2], *out[6 + 2 * n : 8 + 2 * n]) for n in range(3))
        chains, singles = routes(lay)

        def opening(way):
            return lambda a, b, c, d, strips: (*send(lay, way, (a, b), (c, d)), beside(strips))

        def plain(way):
            return lambda a, b, c, d: send(lay, way, (a, b), (c, d))

        def everything(*like):
            lons = lax.axis_size("lon")
            held = [jnp.zeros_like(x) for x in like]
            for d in range(1, groups):
                pairs = [(a, (a + d) % groups) for a in range(groups)]
                crossed = [(a * lons + j, b * lons + 1 - j) for a, b in pairs for j in range(lons)]
                fields = lax.ppermute(state, "member", pairs)
                sides = lax.ppermute(strips[:per_dev], ("member", "lon"), crossed)
                for i in range(per_dev):
                    source = lax.dynamic_index_in_dim(clone_src, group * per_dev + i, keepdims=False)
                    here = source // per_dev == (group - d) % groups
                    for n, got in ((i, fields), (per_dev + i, sides)):
                        chosen = lax.dynamic_index_in_dim(got, source % per_dev, keepdims=False)
                        held[n] = jnp.where(here, chosen, held[n])
            return tuple(held)

        *got, sides = lax.switch(index[0], [opening(way) for way in chains + singles], *first_out, strips)
        second = lax.switch(following[0], [plain(way) for way in chains], *second)
        third = lax.switch(final[0], [plain(way) for way in chains] + [everything], *third)
        fields = (*got[:2], *second[:2], *third[:2])
        far_sides = (*got[2:], *second[2:], *third[2:])

    assert per_dev == 2
    side, top, bottom = pack(lay, plan, state, fields, kick, forcing, sides, far_sides)
    return plan[lay.place :], (state, *fields), side, top, bottom


def cut(rows, strip, v):
    width = rows.shape[1]
    count = -(-width // SPAN)
    lane = lane_index((rows.shape[0], LANES))
    source = [rows[:, LANES * t : LANES * (t + 1)] for t in range(width // LANES)]
    tiles = []
    for c in range(count):
        first = SPAN * c - HALO
        if c == 0:
            tile = jnp.where(lane < HALO, turn(strip, -2 * HALO * v), turn(source[0], HALO))
        else:
            t, offset = first // LANES, first % LANES
            if t + 1 < len(source):
                later = turn(source[t + 1], -offset)
            else:
                later = turn(strip, LANES - offset - 2 * HALO * v - HALO)
            tile = jnp.where(lane < LANES - offset, turn(source[t], -offset), later)
        tiles.append(tile)
    return tiles


def step_kernel(
    state_ref, up_ref, down_ref, second_up_ref, second_down_ref, third_up_ref, third_down_ref, kick_ref, forcing_ref,
    above_ref, below_ref, side_ref, coupling_ref, place_ref, lat_ref, out_ref, cells, other, source, result, table, stage, field, kicks, drive, done,
):
    members, variables, levels, height, width = state_ref.shape
    count = -(-width // SPAN)
    tall = height + 2 * HALO
    at_top = lat_ref[0] == 0
    at_bottom = lat_ref[0] == lat_ref[1] - 1
    options = options_of(state_ref, (up_ref, down_ref, second_up_ref, second_down_ref, third_up_ref, third_down_ref))

    def fetch(k, wait=()):
        slot = k % 2
        for m in wait or range(members):
            kick = pltpu.make_async_copy(kick_ref.at[m, :, k], kicks.at[slot, m], done.at[2, m])
            if wait:
                pltpu.make_async_copy(kick_ref.at[m, :, k], field.at[slot, m], done.at[1, m]).wait()
                kick.wait()
            else:
                for at, option in enumerate(options):

                    @pl.when(place_ref[m] == at)
                    def _():
                        pltpu.make_async_copy(option.at[:, k], field.at[slot, m], done.at[1, m]).start()

                kick.start()

    def leave(k, m=None, v=None, wait=False):
        if wait:
            for m in range(members):
                pltpu.make_async_copy(stage.at[m], out_ref.at[m, :, k], done.at[0, m]).wait()
        else:
            pltpu.make_async_copy(stage.at[m, v], out_ref.at[m, v, k], done.at[0, m]).start()

    def driven(k):
        return pltpu.make_async_copy(forcing_ref.at[:, k], drive, done.at[3, 0])

    def edge(ref, slot, k, v):
        tiles = width // LANES
        rows = [ref[slot, k, v * tiles + t] for t in range(tiles)]
        return jnp.concatenate(rows, axis=1), ref[slot, k, variables * tiles]

    def lay(rows, strip, v, target, at, scale):
        for c, tile in enumerate(cut(rows, strip, v)):
            target[c, v, at : at + rows.shape[0]] = tile if scale is None else tile * scale

    blocks = tall // ROWS
    pad = ROWS
    origin = lat_ref[2]

    line = lax.broadcasted_iota(jnp.int32, (ROWS, LANES), 0)
    north, south = range(blocks)[0], range(blocks)[-1]

    def advance_tile(step, now, later, c):
        last = step == STEPS - 1
        shared = 0 < step < STEPS - 1
        assert HALO - REACH * 2 <= ROWS // 2

        def load(ref, m, v, r, d=0):
            at = pad + ROWS * r
            return ref[m, c, v, at : at + ROWS] if d == 0 else ref[m, c, v, pl.ds(origin + at + d, ROWS)]

        def view(get, r):
            return jnp.where(line < ROWS // 2, get(south), get(north)) if r is None else get(r)

        inner = list(range(1, blocks - 1))
        for r in inner if last else [None] + inner if shared else range(blocks):
            centre, along, across = [], [], []
            for m in range(members):
                centre.append([view(lambda r: load(now, m, v, r), r) for v in range(variables)])
                ku, kv = K * centre[m][0], K * centre[m][1]
                eu, ev = 8.0 * ku, 8.0 * kv
                along.append((16.0 * K - eu, 16.0 * K + eu, ku - K, -K - ku))
                across.append((16.0 * K - ev, 16.0 * K + ev, kv - K, -K - kv))
            for v in range(variables):
                driving = view(lambda r: source[c, v, ROWS * r : ROWS * (r + 1)], r)
                weights = [table[v * variables + w] for w in range(variables)]
                for m in range(members):
                    q = centre[m][v]
                    shifted = {d: view(lambda r: load(now, m, v, r, d), r) for d in (1, -1, 2, -2)}
                    total = driving
                    for w in range(variables):
                        total += weights[w] * centre[m][w]
                    near = along[m][0] * turn(q, -1) + along[m][1] * turn(q, 1)
                    far = along[m][2] * turn(q, -2) + along[m][3] * turn(q, 2)
                    near += across[m][0] * shifted[1] + across[m][1] * shifted[-1]
                    far += across[m][2] * shifted[2] + across[m][3] * shifted[-2]
                    total += near + far
                    if last:
                        result[m, c, v, ROWS * (r - 1) : ROWS * r] = total
                        continue
                    for to, outside in ((north, at_top), (south, at_bottom)):
                        if r is None or r == to:
                            at = pad + ROWS * to
                            later[m, c, v, at : at + ROWS] = jnp.where(outside, 0.0, total)
                    if r in inner:
                        later[m, c, v, pad + ROWS * r : pad + ROWS * (r + 1)] = total

    fetch(0)
    driven(0).start()

    @pl.loop(0, levels)
    def _(k):
        slot = k % 2
        for m in range(members):
            for v in range(variables):
                lay(*edge(above_ref, m, k, v), v, cells.at[m], pad, None)
                lay(*edge(below_ref, m, k, v), v, cells.at[m], pad + HALO + height, None)
        for v in range(variables):
            lay(*edge(above_ref, members, k, v), v, source, 0, 0.1)
            lay(*edge(below_ref, members, k, v), v, source, HALO + height, 0.1)
            for w in range(variables):
                weight = 0.25 * coupling_ref[(k * variables + v) * variables + w]
                weight = weight + (1.0 - 60.0 * K if v == w else 0.0)
                table[v * variables + w] = jnp.full((ROWS, LANES), weight, jnp.float32)
        for m in range(members):
            fetch(k, wait=(m,))
            for v in range(variables):
                lay(field[slot, m, v] + kicks[slot, m, v], side_ref[m, k], v, cells.at[m], pad + HALO, None)
        driven(k).wait()
        for v in range(variables):
            lay(drive[v], side_ref[members, k], v, source, HALO, 0.1)

        @pl.when(k + 1 < levels)
        def _():
            fetch(k + 1)
            driven(k + 1).start()

        @pl.loop(0, count)
        def _(c):
            for step in range(STEPS):
                now, later = (cells, other) if step % 2 == 0 else (other, cells)
                advance_tile(step, now, later, c)

        lane = lane_index((height, LANES))

        @pl.when(k > 0)
        def _():
            leave(k, wait=True)

        for m in range(members):
            for v in range(variables):
                for t in range(width // LANES):
                    c, offset = LANES * t // SPAN, LANES * t % SPAN
                    left = turn(result[m, c, v], -(offset + HALO))
                    if c + 1 < count:
                        right = turn(result[m, c + 1, v], SPAN - offset - HALO)
                        left = jnp.where(lane < SPAN - offset, left, right)
                    stage[m, v, :, LANES * t : LANES * (t + 1)] = left
                leave(k, m, v)

    leave(0, wait=True)


def advance(place, sources, kick, forcing, above, below, side, coupling):
    members, variables, levels, height, width = kick.shape
    assert height % ROWS == 0 and HALO == ROWS
    count = -(-width // SPAN)
    tall = height + 2 * HALO
    lat = jnp.stack([lax.axis_index("lat"), jnp.int32(lax.axis_size("lat")), jnp.int32(0)])
    here, scalars, anywhere = spec(pltpu.VMEM), spec(pltpu.SMEM), spec(pl.ANY)
    block = (variables, height, width)
    state, *others = sources
    return pl.pallas_call(
        step_kernel,
        in_specs=[anywhere] * 9 + [here] * 3 + [scalars] * 3,
        out_specs=spec(pltpu.HBM),
        out_shape=jax.ShapeDtypeStruct(kick.shape, jnp.float32),
        scratch_shapes=[
            pltpu.VMEM((members, count, variables, tall + 2 * ROWS, LANES), jnp.float32),
            pltpu.VMEM((members, count, variables, tall + 2 * ROWS, LANES), jnp.float32),
            pltpu.VMEM((count, variables, tall, LANES), jnp.float32),
            pltpu.VMEM((members, count, variables, height, LANES), jnp.float32),
            pltpu.VMEM((variables * variables, ROWS, LANES), jnp.float32),
            pltpu.VMEM((members, *block), jnp.float32),
            pltpu.VMEM((2, members, *block), jnp.float32),
            pltpu.VMEM((2, members, *block), jnp.float32),
            pltpu.VMEM(block, jnp.float32),
            pltpu.SemaphoreType.DMA((4, members)),
        ],
        compiler_params=pltpu.CompilerParams(vmem_limit_bytes=VMEM),
    )(
        far_away(state), *others, far_away(kick), far_away(forcing), above, below, side, coupling.reshape(-1), place, lat
    )


def shards(state, kick, forcing, coupling, clone_src):
    place, sources, side, top, bottom = prepared(state, kick, forcing, clone_src)
    above, below = neighbours(top, bottom)
    return advance(place, sources, kick, forcing, above, below, side, coupling)


def solution(mesh):
    in_specs = (
        P("member", None, None, "lat", "lon"),
        P("member", None, None, "lat", "lon"),
        P(None, None, "lat", "lon"),
        P(),
        P(),
    )
    out_specs = P("member", None, None, "lat", "lon")
    return jax.shard_map(shards, mesh=mesh, in_specs=in_specs, out_specs=out_specs, check_vma=False)
```

```python
import functools
import itertools

import functools

import jax
import jax.numpy as jnp
import numpy as np
from jax import lax
from jax.experimental import pallas as pl
from jax.experimental.pallas import tpu as pltpu
from jax.sharding import PartitionSpec as P

STEPS = 4
REACH = 2
HALO = STEPS * REACH
LANES = 128
ROWS = 8
SPAN = LANES - 2 * HALO
K = 0.05 / 12.0
VMEM = 14 * 1024 * 1024


def lane_index(shape):
    return lax.broadcasted_iota(jnp.int32, shape, len(shape) - 1)


def turn(x, shift):
    shift = shift % LANES
    return x if shift == 0 else pltpu.roll(x, shift, x.ndim - 1)


def chain(bits, groups):
    stops = [0] + [x for x in range(1, groups - 1) if bits >> (x - 1) & 1] + [groups - 1]
    return list(zip(stops[:-1], stops[1:]))


SINGLES = 9


def pairings(groups):
    found = []
    for sources in itertools.product(range(groups + 1), repeat=groups):
        pairs = [(a - 1, b) for b, a in enumerate(sources) if a]
        loads = [(e, a < b) for a, b in pairs for e in range(min(a, b), max(a, b))]
        if pairs and len({a for a, _ in pairs}) == len(pairs) and len(set(loads)) == len(loads) and all(a != b for a, b in pairs):
            found.append((sum(a * (groups + 1) ** b for b, a in enumerate(sources)), pairs))
    return found


class Layout:
    def __init__(self, groups, per_dev):
        self.groups, self.per_dev = groups, per_dev
        self.most = per_dev * (groups - 1)
        self.patterns, self.sends = 1, 1 + 2 * self.most
        self.takes = self.sends + 2 * self.most
        self.place = self.takes + per_dev
        self.size = self.place + per_dev
        self.kinds = 1 + (1 << (groups - 2))
        self.pairings = pairings(groups)
        largest = [p for _, p in self.pairings if not any(set(p) < set(q) for _, q in self.pairings)]
        self.singles = sorted(largest, key=lambda p: (-len(p), sum(abs(a - b) for a, b in p)))[:SINGLES]

    def table(self):
        table = np.zeros(((self.groups + 1) ** self.groups,), np.int32)
        for code, pairs in self.pairings:
            if len({a < b for a, b in pairs}) == 2:
                fits = [n for n, single in enumerate(self.singles) if set(pairs) <= set(single)]
                table[code] = self.kinds * self.kinds + fits[0] if fits else 0
        return table


def plan_lines(lay, clone_ref, group_ref, plan_ref, index_refs, ends, owner, used, twice, falls, lookup):
    groups, per_dev, most = lay.groups, lay.per_dev, lay.most
    me = group_ref[0]
    plan_ref[0] = 1
    for t in range(2 * most):
        plan_ref[lay.patterns + t] = 0
        plan_ref[lay.sends + t] = 0
    for t in range(most):
        twice[t] = 0
        falls[t] = 0
        for g in range(groups):
            owner[t * groups + g] = 0
            used[t * groups + g] = 0
    for i in range(per_dev):
        plan_ref[lay.takes + i] = -1 - clone_ref[me * per_dev + i] % per_dev

    for down in range(2):
        for t in range(most):
            ends[t] = 0
        for a in range(groups - 1):
            for b in range(a + 1, groups):
                source, target = (groups - 1 - a, groups - 1 - b) if down else (a, b)
                spans = sum(1 << (x - 1) for x in range(a + 1, b))
                for j in range(per_dev):
                    member = source * per_dev + j
                    wanted = [clone_ref[target * per_dev + i] == member for i in range(per_dev)]
                    need = functools.reduce(jnp.logical_or, wanted)

                    @pl.when(need)
                    def _():
                        t = jnp.int32(most - 1)
                        for earlier in reversed(range(most - 1)):
                            t = jnp.where(ends[earlier] <= a, earlier, t)
                        ends[t] = b
                        plan_ref[0] = jnp.maximum(plan_ref[0], t + 1)
                        at = 2 * t + down
                        before = plan_ref[lay.patterns + at]
                        bits = jnp.where(before == 0, lay.kinds - 2, before - 1)
                        plan_ref[lay.patterns + at] = 1 + (bits & ~spans)
                        giver, taker = t * groups + source, t * groups + target
                        twice[t] = twice[t] | used[giver] | owner[taker]
                        used[giver] = 1
                        owner[taker] = source + 1

                        @pl.when(me == source)
                        def _():
                            plan_ref[lay.sends + at] = j
                            falls[t] = down

                        for i in range(per_dev):

                            @pl.when((me == target) & wanted[i])
                            def _():
                                plan_ref[lay.takes + i] = at

    lookup[1].wait()
    rounds = plan_ref[0]
    code = jnp.int32(0)
    for g in reversed(range(groups)):
        code = code * (groups + 1) + owner[g]
    branch = lookup[0][code]
    single = (twice[0] == 0) & (branch > 0)
    chains = [plan_ref[lay.patterns + 2 * t] * lay.kinds + plan_ref[lay.patterns + 2 * t + 1] for t in range(3)]
    index_refs[0][0] = jnp.where(single, branch, chains[0])
    index_refs[1][0] = chains[1]
    index_refs[2][0] = jnp.where(rounds > 3, lay.kinds * lay.kinds, chains[2])

    @pl.when(single & (falls[0] == 1))
    def _():
        plan_ref[lay.sends] = plan_ref[lay.sends + 1]

    for i in range(per_dev):
        take = plan_ref[lay.takes + i]
        slot = jnp.where(single & (take < 2), 0, take)
        far = per_dev + jnp.where((take < 4) | (rounds == 3), slot, 4 + i)
        plan_ref[lay.place + i] = jnp.where(take < 0, -1 - take, far)


def first_kernel(
    lay, clone_ref, table_ref, group_ref, state_ref, kick_ref, forcing_ref, plan_ref, index_ref, second_ref, third_ref, *refs
):
    fields, sides, strips_ref = refs[:6], refs[6:12], refs[12]
    sources, table, ends, owner, used, twice, falls, held, kick_ends, forcing_ends, done = refs[-11:]
    members, variables, levels, height, width = state_ref.shape
    copies = [pltpu.make_async_copy(clone_ref, sources, done.at[0]), pltpu.make_async_copy(state_ref, held, done.at[1])]
    for side, at in enumerate((0, width - LANES)):
        for ref, part in ((kick_ref, kick_ends), (forcing_ref, forcing_ends)):
            piece = ref.at[(slice(None),) * (len(ref.shape) - 1) + (pl.ds(at, LANES),)]
            copies.append(pltpu.make_async_copy(piece, part.at[side], done.at[len(copies)]))
    listed = pltpu.make_async_copy(table_ref, table, done.at[10])
    for copy in [copies[0], listed, *copies[1:]]:
        copy.start()
    copies[0].wait()
    indices = index_ref, second_ref, third_ref
    plan_lines(lay, sources, group_ref, plan_ref, indices, ends, owner, used, twice, falls, (table, listed))
    copies[1].wait()
    sent = [plan_ref[lay.sends + n] for n in range(6)]
    given = [plan_ref[lay.patterns + n] for n in range(6)]
    wanted = [given[0] + given[1] > 0, *(given[n] > 0 for n in range(1, 6))]
    later = [pltpu.make_async_copy(held.at[sent[n]], fields[n], done.at[4 + n]) for n in range(2, 6)]
    for n in range(4):
        pl.when(wanted[2 + n])(later[n].start)
    for n in range(2):

        @pl.when(wanted[n])
        def _():
            @pl.loop(0, variables)
            def _(v):
                for k in range(levels):
                    fields[n][v, k] = held[sent[n], v, k]

    for copy in copies[2:]:
        copy.wait()
    lane = lane_index((height, LANES))

    @pl.loop(0, levels)
    def _(k):
        for slot in range(2 * members + 1):
            strip = jnp.zeros((height, LANES), jnp.float32)
            for v in range(variables):
                if slot < members:
                    low, high = (held[slot, v, k, :, at : at + LANES] for at in (0, width - LANES))
                elif slot < 2 * members:
                    low, high = (kick_ends[side, slot - members, v, k] for side in range(2))
                else:
                    low, high = (forcing_ends[side, v, k] for side in range(2))
                both = turn(jnp.where(lane < HALO, low, high), HALO + 2 * HALO * v)
                strip = jnp.where(lane >= 2 * HALO * v, both, strip)
            strips_ref[slot, k] = strip

    for ref, j in zip(sides, sent):
        ref[...] = strips_ref[j]
    for n in range(4):
        pl.when(wanted[2 + n])(later[n].wait)


def spec(space):
    return pl.BlockSpec(memory_space=space)


def first(lay, group, clone_src, state, kick, forcing):
    members, variables, levels, height, width = state.shape
    shape = jax.ShapeDtypeStruct
    one = pltpu.VMEM(state.shape[1:], jnp.float32)
    side = pltpu.VMEM((levels, height, LANES), jnp.float32)
    strips = pltpu.VMEM((2 * members + 1, levels, height, LANES), jnp.float32)
    ends = (2, members, variables, levels, height, LANES)
    scalar, here, far = spec(pltpu.SMEM), spec(pltpu.VMEM), spec(pltpu.HBM)
    return pl.pallas_call(
        functools.partial(first_kernel, lay),
        in_specs=[far, far, scalar, far, far, far],
        out_specs=[scalar] * 4 + [here] * 2 + [spec(pl.ANY)] * 4 + [here] * 7,
        out_shape=[shape((lay.size,), jnp.int32)] + [shape((1,), jnp.int32)] * 3 + [one] * 2 + [pltpu.HBM(state.shape[1:], jnp.float32)] * 4 + [side] * 6 + [strips],
        scratch_shapes=[
            pltpu.SMEM(clone_src.shape, jnp.int32),
            pltpu.SMEM(lay.table().shape, jnp.int32),
            pltpu.SMEM((lay.most,), jnp.int32),
            pltpu.SMEM((lay.most * lay.groups,), jnp.int32),
            pltpu.SMEM((lay.most * lay.groups,), jnp.int32),
            pltpu.SMEM((lay.most,), jnp.int32),
            pltpu.SMEM((lay.most,), jnp.int32),
            pltpu.VMEM(state.shape, jnp.float32),
            pltpu.VMEM(ends, jnp.float32),
            pltpu.VMEM((2, *ends[2:]), jnp.float32),
            pltpu.SemaphoreType.DMA((11,)),
        ],
        compiler_params=pltpu.CompilerParams(vmem_limit_bytes=VMEM),
    )(far_away(clone_src), far_away(jnp.asarray(lay.table())), group[None], far_away(state), far_away(kick), far_away(forcing))


def far_away(x):
    return pltpu.with_memory_space_constraint(x, pltpu.HBM)


def edge_shape(members, forcing):
    variables, levels, height, width = forcing.shape
    return jax.ShapeDtypeStruct((members, levels, variables * width // LANES + 1, HALO, LANES), jnp.float32)


def where_found(place, members, local, others, act):
    pl.when(place < members)(lambda: act(local(place)))

    @pl.when(place >= members)
    def _():
        for n, other in enumerate(others[:2]):
            pl.when(place == members + n)(functools.partial(act, other))

        @pl.when(place >= members + 2)
        def _():
            for n, other in enumerate(others[2:]):
                pl.when(place == members + 2 + n)(functools.partial(act, other))


def pack_kernel(
    lay, plan_ref, state_ref, *refs
):
    others, (kick_ref, forcing_ref, sides_ref), others_sides = refs[:6], refs[6:9], refs[9:15]
    side_ref, top_ref, bottom_ref, field_rows, kick_rows, forcing_rows, strips, picked, done = refs[15:]
    up_ref, up_side_ref = others[0], others_sides[0]
    members, variables, levels, height, width = state_ref.shape
    tiles = width // LANES
    places = [plan_ref[lay.place + i] for i in range(members)]
    rows = [pl.ds(0, HALO), pl.ds(height - HALO, HALO)]
    f_copies = [pltpu.make_async_copy(forcing_ref.at[:, :, rows[n]], forcing_rows.at[n], done.at[0]) for n in range(2)]
    copies = []
    for i in range(members):

        def bring(source):
            whole, part = source
            for n in range(2):
                pltpu.make_async_copy(whole.at[:, :, rows[n]], field_rows.at[i, n], done.at[1 + i]).start()
            pltpu.make_async_copy(part, picked.at[i], done.at[2 + members + i]).start()

        local = lambda j: (state_ref.at[j], sides_ref.at[j])
        where_found(places[i], members, local, list(zip(others, others_sides)), bring)
        for n in range(2):
            copies.append(pltpu.make_async_copy(kick_ref.at[i, :, :, rows[n]], kick_rows.at[i, n], done.at[1 + i]))
    strip_copies = [pltpu.make_async_copy(sides_ref, strips, done.at[1 + members])]
    for i in range(members):
        strip_copies.append(pltpu.make_async_copy(up_side_ref, picked.at[i], done.at[2 + members + i]))
    for copy in [strip_copies[0]] + f_copies + copies:
        copy.start()

    def flank(slot, k, strip):
        side_ref[slot, k] = strip
        top_ref[slot, k, variables * tiles] = strip[:HALO]
        bottom_ref[slot, k, variables * tiles] = strip[height - HALO :]

    def edges(slot, rows_of):
        @pl.loop(0, levels)
        def _(k):
            for n, ref in enumerate((top_ref, bottom_ref)):
                for v in range(variables):
                    edge = rows_of(n, v, k)
                    for t in range(tiles):
                        ref[slot, k, v * tiles + t] = edge[:, LANES * t : LANES * (t + 1)]

    for copy in strip_copies:
        copy.wait()
    for k in range(levels):
        flank(members, k, strips[2 * members, k])
        for i in range(members):
            flank(i, k, picked[i, k] + strips[members + i, k])
    for copy in f_copies:
        copy.wait()
    edges(members, lambda n, v, k: forcing_rows[n, v, k])
    for i in range(members):
        for n in range(2):
            pltpu.make_async_copy(kick_ref.at[i, :, :, rows[n]], field_rows.at[i, n], done.at[1 + i]).wait()
            copies[2 * i + n].wait()
        edges(i, lambda n, v, k: field_rows[i, n, v, k] + kick_rows[i, n, v, k])


def pack(lay, plan, state, fields, kick, forcing, sides, far_sides):
    members, variables, levels, height, width = state.shape
    here, anywhere = spec(pltpu.VMEM), spec(pl.ANY)
    rows = (members, 2, variables, levels, HALO, width)
    return pl.pallas_call(
        functools.partial(pack_kernel, lay),
        in_specs=[spec(pltpu.SMEM)] + [anywhere] * 16,
        out_specs=[here] * 3,
        out_shape=[
            jax.ShapeDtypeStruct((members + 1, levels, height, LANES), jnp.float32),
            edge_shape(members + 1, forcing),
            edge_shape(members + 1, forcing),
        ],
        scratch_shapes=[
            pltpu.VMEM(rows, jnp.float32),
            pltpu.VMEM(rows, jnp.float32),
            pltpu.VMEM(rows[1:], jnp.float32),
            pltpu.VMEM(sides.shape, jnp.float32),
            pltpu.VMEM((members, levels, height, LANES), jnp.float32),
            pltpu.SemaphoreType.DMA((2 + 2 * members,)),
        ],
        compiler_params=pltpu.CompilerParams(vmem_limit_bytes=VMEM),
    )(plan, far_away(state), *fields, far_away(kick), far_away(forcing), sides, *far_sides)


def blank(*like):
    return pl.pallas_call(
        lambda *refs: None,
        out_specs=[spec(pl.ANY)] * len(like),
        out_shape=[jax.ShapeDtypeStruct(x.shape, x.dtype) for x in like],
        compiler_params=pltpu.CompilerParams(vmem_limit_bytes=1024 * 1024),
    )()


def neighbours(top, bottom):
    lats = lax.axis_size("lat")
    above = lax.ppermute(bottom, "lat", [(i, i + 1) for i in range(lats - 1)])
    below = lax.ppermute(top, "lat", [(i + 1, i) for i in range(lats - 1)])
    return above, below


def beside(strips):
    assert lax.axis_size("lon") == 2
    return lax.ppermute(strips, "lon", [(0, 1), (1, 0)])


def send(lay, ways, fields, sides):
    lons = lax.axis_size("lon")
    fields, sides = list(fields), list(sides)
    for n, pairs in enumerate(ways):
        if pairs:
            crossed = [(a * lons + j, b * lons + 1 - j) for a, b in pairs for j in range(lons)]
            fields[n] = lax.ppermute(fields[n], "member", pairs)
            sides[n] = lax.ppermute(sides[n], ("member", "lon"), crossed)
        else:
            fields[n], sides[n] = blank(fields[n], sides[n])
    return (*fields, *sides)


def routes(lay):
    top = lay.groups - 1

    def both(up, down):
        rising = chain(up - 1, lay.groups) if up else []
        falling = [(top - a, top - b) for a, b in chain(down - 1, lay.groups)] if down else []
        return rising, falling

    chains = [both(up, down) for up in range(lay.kinds) for down in range(lay.kinds)]
    return chains, [(pairs, []) for pairs in lay.singles]


def prepared(state, kick, forcing, clone_src):
    per_dev, groups, group = state.shape[0], lax.axis_size("member"), lax.axis_index("member")
    lay = Layout(4 if groups == 4 else 3, per_dev)
    if groups != 4:
        piece = lax.all_gather(state, "member", axis=0, tiled=True)
        sources = lax.dynamic_slice_in_dim(clone_src, group * per_dev, per_dev)
        state = jnp.take(piece, sources, axis=0, mode="clip")
        still = jnp.arange(per_dev * 3, dtype=jnp.int32)
        plan, _, _, _, *out, strips = first(lay, jnp.int32(0), still, state, kick, forcing)
        fields, far_sides = out[:6], out[6:]
        sides = beside(strips)
    else:
        plan, index, following, final, *out, strips = first(lay, group, clone_src, state, kick, forcing)
        first_out, second, third = ((*out[2 * n : 2 * n + 2], *out[6 + 2 * n : 8 + 2 * n]) for n in range(3))
        chains, singles = routes(lay)

        def opening(way):
            return lambda a, b, c, d, strips: (*send(lay, way, (a, b), (c, d)), beside(strips))

        def plain(way):
            return lambda a, b, c, d: send(lay, way, (a, b), (c, d))

        def everything(*like):
            lons = lax.axis_size("lon")
            held = [jnp.zeros_like(x) for x in like]
            for d in range(1, groups):
                pairs = [(a, (a + d) % groups) for a in range(groups)]
                crossed = [(a * lons + j, b * lons + 1 - j) for a, b in pairs for j in range(lons)]
                fields = lax.ppermute(state, "member", pairs)
                sides = lax.ppermute(strips[:per_dev], ("member", "lon"), crossed)
                for i in range(per_dev):
                    source = lax.dynamic_index_in_dim(clone_src, group * per_dev + i, keepdims=False)
                    here = source // per_dev == (group - d) % groups
                    for n, got in ((i, fields), (per_dev + i, sides)):
                        chosen = lax.dynamic_index_in_dim(got, source % per_dev, keepdims=False)
                        held[n] = jnp.where(here, chosen, held[n])
            return tuple(held)

        *got, sides = lax.switch(index[0], [opening(way) for way in chains + singles], *first_out, strips)
        second = lax.switch(following[0], [plain(way) for way in chains], *second)
        third = lax.switch(final[0], [plain(way) for way in chains] + [everything], *third)
        fields = (*got[:2], *second[:2], *third[:2])
        far_sides = (*got[2:], *second[2:], *third[2:])

    assert per_dev == 2
    side, top, bottom = pack(lay, plan, state, fields, kick, forcing, sides, far_sides)
    return plan[lay.place :], (state, *fields), side, top, bottom


def cut(rows, strip, v):
    width = rows.shape[1]
    count = -(-width // SPAN)
    lane = lane_index((rows.shape[0], LANES))
    source = [rows[:, LANES * t : LANES * (t + 1)] for t in range(width // LANES)]
    tiles = []
    for c in range(count):
        first = SPAN * c - HALO
        if c == 0:
            tile = jnp.where(lane < HALO, turn(strip, -2 * HALO * v), turn(source[0], HALO))
        else:
            t, offset = first // LANES, first % LANES
            if t + 1 < len(source):
                later = turn(source[t + 1], -offset)
            else:
                later = turn(strip, LANES - offset - 2 * HALO * v - HALO)
            tile = jnp.where(lane < LANES - offset, turn(source[t], -offset), later)
        tiles.append(tile)
    return tiles


def step_kernel(
    state_ref, up_ref, down_ref, second_up_ref, second_down_ref, third_up_ref, third_down_ref, kick_ref, forcing_ref,
    above_ref, below_ref, side_ref, coupling_ref, place_ref, lat_ref, out_ref, cells, other, source, result, table, stage, field, kicks, drive, done,
):
    members, variables, levels, height, width = state_ref.shape
    count = -(-width // SPAN)
    tall = height + 2 * HALO
    at_top = lat_ref[0] == 0
    at_bottom = lat_ref[0] == lat_ref[1] - 1
    others = up_ref, down_ref, second_up_ref, second_down_ref, third_up_ref, third_down_ref

    def fetch(k, wait=()):
        slot = k % 2
        for m in wait or range(members):
            kick = pltpu.make_async_copy(kick_ref.at[m, :, k], kicks.at[slot, m], done.at[2, m])
            if wait:
                pltpu.make_async_copy(kick_ref.at[m, :, k], field.at[slot, m], done.at[1, m]).wait()
                kick.wait()
            else:

                def bring(whole):
                    pltpu.make_async_copy(whole.at[:, k], field.at[slot, m], done.at[1, m]).start()

                where_found(place_ref[m], members, lambda j: state_ref.at[j], others, bring)
                kick.start()

    def leave(k, m=None, v=None, wait=False):
        if wait:
            for m in range(members):
                pltpu.make_async_copy(stage.at[m], out_ref.at[m, :, k], done.at[0, m]).wait()
        else:
            pltpu.make_async_copy(stage.at[m, v], out_ref.at[m, v, k], done.at[0, m]).start()

    def driven(k):
        return pltpu.make_async_copy(forcing_ref.at[:, k], drive, done.at[3, 0])

    def edge(ref, slot, k, v):
        tiles = width // LANES
        rows = [ref[slot, k, v * tiles + t] for t in range(tiles)]
        return jnp.concatenate(rows, axis=1), ref[slot, k, variables * tiles]

    def lay(rows, strip, v, target, at, scale):
        for c, tile in enumerate(cut(rows, strip, v)):
            target[c, v, at : at + rows.shape[0]] = tile if scale is None else tile * scale

    blocks = tall // ROWS
    pad = ROWS
    origin = lat_ref[2]

    line = lax.broadcasted_iota(jnp.int32, (ROWS, LANES), 0)
    north, south = range(blocks)[0], range(blocks)[-1]

    def advance_tile(step, now, later, c):
        last = step == STEPS - 1
        shared = 0 < step < STEPS - 1
        assert HALO - REACH * 2 <= ROWS // 2

        def load(ref, m, v, r, d=0):
            at = pad + ROWS * r
            return ref[m, c, v, at : at + ROWS] if d == 0 else ref[m, c, v, pl.ds(origin + at + d, ROWS)]

        def view(get, r):
            return jnp.where(line < ROWS // 2, get(south), get(north)) if r is None else get(r)

        inner = list(range(1, blocks - 1))
        for r in inner if last else [None] + inner if shared else range(blocks):
            centre, along, across = [], [], []
            for m in range(members):
                centre.append([view(lambda r: load(now, m, v, r), r) for v in range(variables)])
                ku, kv = K * centre[m][0], K * centre[m][1]
                eu, ev = 8.0 * ku, 8.0 * kv
                along.append((16.0 * K - eu, 16.0 * K + eu, ku - K, -K - ku))
                across.append((16.0 * K - ev, 16.0 * K + ev, kv - K, -K - kv))
            for v in range(variables):
                driving = view(lambda r: source[c, v, ROWS * r : ROWS * (r + 1)], r)
                weights = [table[v * variables + w] for w in range(variables)]
                for m in range(members):
                    q = centre[m][v]
                    shifted = {d: view(lambda r: load(now, m, v, r, d), r) for d in (1, -1, 2, -2)}
                    total = driving
                    for w in range(variables):
                        total += weights[w] * centre[m][w]
                    near = along[m][0] * turn(q, -1) + along[m][1] * turn(q, 1)
                    far = along[m][2] * turn(q, -2) + along[m][3] * turn(q, 2)
                    near += across[m][0] * shifted[1] + across[m][1] * shifted[-1]
                    far += across[m][2] * shifted[2] + across[m][3] * shifted[-2]
                    total += near + far
                    if last:
                        result[m, c, v, ROWS * (r - 1) : ROWS * r] = total
                        continue
                    for to, outside in ((north, at_top), (south, at_bottom)):
                        if r is None or r == to:
                            at = pad + ROWS * to
                            later[m, c, v, at : at + ROWS] = jnp.where(outside, 0.0, total)
                    if r in inner:
                        later[m, c, v, pad + ROWS * r : pad + ROWS * (r + 1)] = total

    fetch(0)
    driven(0).start()

    @pl.loop(0, levels)
    def _(k):
        slot = k % 2
        for m in range(members):
            for v in range(variables):
                lay(*edge(above_ref, m, k, v), v, cells.at[m], pad, None)
                lay(*edge(below_ref, m, k, v), v, cells.at[m], pad + HALO + height, None)
        for v in range(variables):
            lay(*edge(above_ref, members, k, v), v, source, 0, 0.1)
            lay(*edge(below_ref, members, k, v), v, source, HALO + height, 0.1)
            for w in range(variables):
                weight = 0.25 * coupling_ref[(k * variables + v) * variables + w]
                weight = weight + (1.0 - 60.0 * K if v == w else 0.0)
                table[v * variables + w] = jnp.full((ROWS, LANES), weight, jnp.float32)
        for m in range(members):
            fetch(k, wait=(m,))
            for v in range(variables):
                lay(field[slot, m, v] + kicks[slot, m, v], side_ref[m, k], v, cells.at[m], pad + HALO, None)
        driven(k).wait()
        for v in range(variables):
            lay(drive[v], side_ref[members, k], v, source, HALO, 0.1)

        @pl.when(k + 1 < levels)
        def _():
            fetch(k + 1)
            driven(k + 1).start()

        @pl.loop(0, count)
        def _(c):
            for step in range(STEPS):
                now, later = (cells, other) if step % 2 == 0 else (other, cells)
                advance_tile(step, now, later, c)

        lane = lane_index((height, LANES))

        @pl.when(k > 0)
        def _():
            leave(k, wait=True)

        for m in range(members):
            for v in range(variables):
                for t in range(width // LANES):
                    c, offset = LANES * t // SPAN, LANES * t % SPAN
                    left = turn(result[m, c, v], -(offset + HALO))
                    if c + 1 < count:
                        right = turn(result[m, c + 1, v], SPAN - offset - HALO)
                        left = jnp.where(lane < SPAN - offset, left, right)
                    stage[m, v, :, LANES * t : LANES * (t + 1)] = left
                leave(k, m, v)

    leave(0, wait=True)


def advance(place, sources, kick, forcing, above, below, side, coupling):
    members, variables, levels, height, width = kick.shape
    assert height % ROWS == 0 and HALO == ROWS
    count = -(-width // SPAN)
    tall = height + 2 * HALO
    lat = jnp.stack([lax.axis_index("lat"), jnp.int32(lax.axis_size("lat")), jnp.int32(0)])
    here, scalars, anywhere = spec(pltpu.VMEM), spec(pltpu.SMEM), spec(pl.ANY)
    block = (variables, height, width)
    state, *others = sources
    return pl.pallas_call(
        step_kernel,
        in_specs=[anywhere] * 9 + [here] * 3 + [scalars] * 3,
        out_specs=spec(pltpu.HBM),
        out_shape=jax.ShapeDtypeStruct(kick.shape, jnp.float32),
        scratch_shapes=[
            pltpu.VMEM((members, count, variables, tall + 2 * ROWS, LANES), jnp.float32),
            pltpu.VMEM((members, count, variables, tall + 2 * ROWS, LANES), jnp.float32),
            pltpu.VMEM((count, variables, tall, LANES), jnp.float32),
            pltpu.VMEM((members, count, variables, height, LANES), jnp.float32),
            pltpu.VMEM((variables * variables, ROWS, LANES), jnp.float32),
            pltpu.VMEM((members, *block), jnp.float32),
            pltpu.VMEM((2, members, *block), jnp.float32),
            pltpu.VMEM((2, members, *block), jnp.float32),
            pltpu.VMEM(block, jnp.float32),
            pltpu.SemaphoreType.DMA((4, members)),
        ],
        compiler_params=pltpu.CompilerParams(vmem_limit_bytes=VMEM),
    )(
        far_away(state), *others, far_away(kick), far_away(forcing), above, below, side, coupling.reshape(-1), place, lat
    )


def shards(state, kick, forcing, coupling, clone_src):
    place, sources, side, top, bottom = prepared(state, kick, forcing, clone_src)
    above, below = neighbours(top, bottom)
    return advance(place, sources, kick, forcing, above, below, side, coupling)


def solution(mesh):
    in_specs = (
        P("member", None, None, "lat", "lon"),
        P("member", None, None, "lat", "lon"),
        P(None, None, "lat", "lon"),
        P(),
        P(),
    )
    out_specs = P("member", None, None, "lat", "lon")
    return jax.shard_map(shards, mesh=mesh, in_specs=in_specs, out_specs=out_specs, check_vma=False)
```

```python
import functools
import itertools

import functools

import jax
import jax.numpy as jnp
import numpy as np
from jax import lax
from jax.experimental import pallas as pl
from jax.experimental.pallas import tpu as pltpu
from jax.sharding import PartitionSpec as P

STEPS = 4
REACH = 2
HALO = STEPS * REACH
LANES = 128
ROWS = 8
SPAN = LANES - 2 * HALO
K = 0.05 / 12.0
VMEM = 14 * 1024 * 1024


def lane_index(shape):
    return lax.broadcasted_iota(jnp.int32, shape, len(shape) - 1)


def turn(x, shift):
    shift = shift % LANES
    return x if shift == 0 else pltpu.roll(x, shift, x.ndim - 1)


def chain(bits, groups):
    stops = [0] + [x for x in range(1, groups - 1) if bits >> (x - 1) & 1] + [groups - 1]
    return list(zip(stops[:-1], stops[1:]))


SINGLES = 9


def pairings(groups):
    found = []
    for sources in itertools.product(range(groups + 1), repeat=groups):
        pairs = [(a - 1, b) for b, a in enumerate(sources) if a]
        loads = [(e, a < b) for a, b in pairs for e in range(min(a, b), max(a, b))]
        if pairs and len({a for a, _ in pairs}) == len(pairs) and len(set(loads)) == len(loads) and all(a != b for a, b in pairs):
            found.append((sum(a * (groups + 1) ** b for b, a in enumerate(sources)), pairs))
    return found


class Layout:
    def __init__(self, groups, per_dev):
        self.groups, self.per_dev = groups, per_dev
        self.most = per_dev * (groups - 1)
        self.patterns, self.sends = 1, 1 + 2 * self.most
        self.takes = self.sends + 2 * self.most
        self.place = self.takes + per_dev
        self.size = self.place + per_dev
        self.kinds = 1 + (1 << (groups - 2))
        self.pairings = pairings(groups)
        largest = [p for _, p in self.pairings if not any(set(p) < set(q) for _, q in self.pairings)]
        self.singles = sorted(largest, key=lambda p: (-len(p), sum(abs(a - b) for a, b in p)))[:SINGLES]

    def table(self):
        table = np.zeros(((self.groups + 1) ** self.groups,), np.int32)
        for code, pairs in self.pairings:
            if len({a < b for a, b in pairs}) == 2:
                fits = [n for n, single in enumerate(self.singles) if set(pairs) <= set(single)]
                table[code] = self.kinds * self.kinds + fits[0] if fits else 0
        return table


def plan_lines(lay, clone_ref, group_ref, plan_ref, index_refs, ends, owner, used, twice, falls, lookup):
    groups, per_dev, most = lay.groups, lay.per_dev, lay.most
    me = group_ref[0]
    plan_ref[0] = 1
    for t in range(2 * most):
        plan_ref[lay.patterns + t] = 0
        plan_ref[lay.sends + t] = 0
    for t in range(most):
        twice[t] = 0
        falls[t] = 0
        for g in range(groups):
            owner[t * groups + g] = 0
            used[t * groups + g] = 0
    for i in range(per_dev):
        plan_ref[lay.takes + i] = -1 - clone_ref[me * per_dev + i] % per_dev

    for down in range(2):
        for t in range(most):
            ends[t] = 0
        for a in range(groups - 1):
            for b in range(a + 1, groups):
                source, target = (groups - 1 - a, groups - 1 - b) if down else (a, b)
                spans = sum(1 << (x - 1) for x in range(a + 1, b))
                for j in range(per_dev):
                    member = source * per_dev + j
                    wanted = [clone_ref[target * per_dev + i] == member for i in range(per_dev)]
                    need = functools.reduce(jnp.logical_or, wanted)

                    @pl.when(need)
                    def _():
                        t = jnp.int32(most - 1)
                        for earlier in reversed(range(most - 1)):
                            t = jnp.where(ends[earlier] <= a, earlier, t)
                        ends[t] = b
                        plan_ref[0] = jnp.maximum(plan_ref[0], t + 1)
                        at = 2 * t + down
                        before = plan_ref[lay.patterns + at]
                        bits = jnp.where(before == 0, lay.kinds - 2, before - 1)
                        plan_ref[lay.patterns + at] = 1 + (bits & ~spans)
                        giver, taker = t * groups + source, t * groups + target
                        twice[t] = twice[t] | used[giver] | owner[taker]
                        used[giver] = 1
                        owner[taker] = source + 1

                        @pl.when(me == source)
                        def _():
                            plan_ref[lay.sends + at] = j
                            falls[t] = down

                        for i in range(per_dev):

                            @pl.when((me == target) & wanted[i])
                            def _():
                                plan_ref[lay.takes + i] = at

    lookup[1].wait()
    rounds = plan_ref[0]
    code = jnp.int32(0)
    for g in reversed(range(groups)):
        code = code * (groups + 1) + owner[g]
    branch = lookup[0][code]
    single = (twice[0] == 0) & (branch > 0)
    chains = [plan_ref[lay.patterns + 2 * t] * lay.kinds + plan_ref[lay.patterns + 2 * t + 1] for t in range(3)]
    index_refs[0][0] = jnp.where(single, branch, chains[0])
    index_refs[1][0] = chains[1]
    index_refs[2][0] = jnp.where(rounds > 3, lay.kinds * lay.kinds, chains[2])

    @pl.when(single & (falls[0] == 1))
    def _():
        plan_ref[lay.sends] = plan_ref[lay.sends + 1]

    for i in range(per_dev):
        take = plan_ref[lay.takes + i]
        slot = jnp.where(single & (take < 2), 0, take)
        far = per_dev + jnp.where((take < 4) | (rounds == 3), slot, 4 + i)
        plan_ref[lay.place + i] = jnp.where(take < 0, -1 - take, far)


def first_kernel(
    lay, clone_ref, table_ref, group_ref, state_ref, kick_ref, forcing_ref, plan_ref, index_ref, second_ref, third_ref, *refs
):
    fields, sides, strips_ref = refs[:6], refs[6:12], refs[12]
    sources, table, ends, owner, used, twice, falls, held, kick_ends, forcing_ends, done = refs[-11:]
    members, variables, levels, height, width = state_ref.shape
    copies = [pltpu.make_async_copy(clone_ref, sources, done.at[0]), pltpu.make_async_copy(state_ref, held, done.at[1])]
    for side, at in enumerate((0, width - LANES)):
        for ref, part in ((kick_ref, kick_ends), (forcing_ref, forcing_ends)):
            piece = ref.at[(slice(None),) * (len(ref.shape) - 1) + (pl.ds(at, LANES),)]
            copies.append(pltpu.make_async_copy(piece, part.at[side], done.at[len(copies)]))
    listed = pltpu.make_async_copy(table_ref, table, done.at[10])
    for copy in [copies[0], listed, *copies[1:]]:
        copy.start()
    copies[0].wait()
    indices = index_ref, second_ref, third_ref
    plan_lines(lay, sources, group_ref, plan_ref, indices, ends, owner, used, twice, falls, (table, listed))
    copies[1].wait()
    sent = [plan_ref[lay.sends + n] for n in range(6)]
    given = [plan_ref[lay.patterns + n] for n in range(6)]
    wanted = [given[0] + given[1] > 0, *(given[n] > 0 for n in range(1, 6))]
    later = [pltpu.make_async_copy(held.at[sent[n]], fields[n], done.at[4 + n]) for n in range(2, 6)]
    for n in range(4):
        pl.when(wanted[2 + n])(later[n].start)
    for n in range(2):

        @pl.when(wanted[n])
        def _():
            @pl.loop(0, variables)
            def _(v):
                for k in range(levels):
                    fields[n][v, k] = held[sent[n], v, k]

    for copy in copies[2:]:
        copy.wait()
    lane = lane_index((height, LANES))

    @pl.loop(0, levels)
    def _(k):
        for slot in range(2 * members + 1):
            strip = jnp.zeros((height, LANES), jnp.float32)
            for v in range(variables):
                if slot < members:
                    low, high = (held[slot, v, k, :, at : at + LANES] for at in (0, width - LANES))
                elif slot < 2 * members:
                    low, high = (kick_ends[side, slot - members, v, k] for side in range(2))
                else:
                    low, high = (forcing_ends[side, v, k] for side in range(2))
                both = turn(jnp.where(lane < HALO, low, high), HALO + 2 * HALO * v)
                strip = jnp.where(lane >= 2 * HALO * v, both, strip)
            strips_ref[slot, k] = strip

    for ref, j in zip(sides, sent):
        ref[...] = strips_ref[j]
    for n in range(4):
        pl.when(wanted[2 + n])(later[n].wait)


def spec(space):
    return pl.BlockSpec(memory_space=space)


def first(lay, group, clone_src, state, kick, forcing):
    members, variables, levels, height, width = state.shape
    shape = jax.ShapeDtypeStruct
    one = pltpu.VMEM(state.shape[1:], jnp.float32)
    side = pltpu.VMEM((levels, height, LANES), jnp.float32)
    strips = pltpu.VMEM((2 * members + 1, levels, height, LANES), jnp.float32)
    ends = (2, members, variables, levels, height, LANES)
    scalar, here, far = spec(pltpu.SMEM), spec(pltpu.VMEM), spec(pltpu.HBM)
    return pl.pallas_call(
        functools.partial(first_kernel, lay),
        in_specs=[far, far, scalar, far, far, far],
        out_specs=[scalar] * 4 + [here] * 2 + [spec(pl.ANY)] * 4 + [here] * 7,
        out_shape=[shape((lay.size,), jnp.int32)] + [shape((1,), jnp.int32)] * 3 + [one] * 2 + [pltpu.HBM(state.shape[1:], jnp.float32)] * 4 + [side] * 6 + [strips],
        scratch_shapes=[
            pltpu.SMEM(clone_src.shape, jnp.int32),
            pltpu.SMEM(lay.table().shape, jnp.int32),
            pltpu.SMEM((lay.most,), jnp.int32),
            pltpu.SMEM((lay.most * lay.groups,), jnp.int32),
            pltpu.SMEM((lay.most * lay.groups,), jnp.int32),
            pltpu.SMEM((lay.most,), jnp.int32),
            pltpu.SMEM((lay.most,), jnp.int32),
            pltpu.VMEM(state.shape, jnp.float32),
            pltpu.VMEM(ends, jnp.float32),
            pltpu.VMEM((2, *ends[2:]), jnp.float32),
            pltpu.SemaphoreType.DMA((11,)),
        ],
        compiler_params=pltpu.CompilerParams(vmem_limit_bytes=VMEM),
    )(far_away(clone_src), far_away(jnp.asarray(lay.table())), group[None], far_away(state), far_away(kick), far_away(forcing))


def far_away(x):
    return pltpu.with_memory_space_constraint(x, pltpu.HBM)


def edge_shape(members, forcing):
    variables, levels, height, width = forcing.shape
    return jax.ShapeDtypeStruct((members, levels, variables * width // LANES + 1, HALO, LANES), jnp.float32)


def where_found(place, members, local, others, act):
    pl.when(place < members)(lambda: act(local(place)))

    @pl.when(place >= members)
    def _():
        for n, other in enumerate(others[:2]):
            pl.when(place == members + n)(functools.partial(act, other))

        @pl.when(place >= members + 2)
        def _():
            for n, other in enumerate(others[2:]):
                pl.when(place == members + 2 + n)(functools.partial(act, other))


def pack_kernel(
    lay, plan_ref, state_ref, *refs
):
    others, (kick_ref, forcing_ref, sides_ref), others_sides = refs[:6], refs[6:9], refs[9:15]
    side_ref, top_ref, bottom_ref, field_rows, kick_rows, forcing_rows, strips, picked, done = refs[15:]
    up_ref, up_side_ref = others[0], others_sides[0]
    members, variables, levels, height, width = state_ref.shape
    tiles = width // LANES
    places = [plan_ref[lay.place + i] for i in range(members)]
    rows = [pl.ds(0, HALO), pl.ds(height - HALO, HALO)]
    f_copies = [pltpu.make_async_copy(forcing_ref.at[:, :, rows[n]], forcing_rows.at[n], done.at[0]) for n in range(2)]
    copies = []
    for i in range(members):

        def bring(source):
            whole, part = source
            for n in range(2):
                pltpu.make_async_copy(whole.at[:, :, rows[n]], field_rows.at[i, n], done.at[1 + i]).start()
            pltpu.make_async_copy(part, picked.at[i], done.at[2 + members + i]).start()

        local = lambda j: (state_ref.at[j], sides_ref.at[j])
        where_found(places[i], members, local, list(zip(others, others_sides)), bring)
        for n in range(2):
            copies.append(pltpu.make_async_copy(kick_ref.at[i, :, :, rows[n]], kick_rows.at[i, n], done.at[1 + i]))
    strip_copies = [pltpu.make_async_copy(sides_ref, strips, done.at[1 + members])]
    for i in range(members):
        strip_copies.append(pltpu.make_async_copy(up_side_ref, picked.at[i], done.at[2 + members + i]))
    for copy in [strip_copies[0]] + f_copies + copies:
        copy.start()

    def flank(slot, k, strip):
        side_ref[slot, k] = strip
        top_ref[slot, k, variables * tiles] = strip[:HALO]
        bottom_ref[slot, k, variables * tiles] = strip[height - HALO :]

    def edges(slot, rows_of):
        @pl.loop(0, levels)
        def _(k):
            for n, ref in enumerate((top_ref, bottom_ref)):
                for v in range(variables):
                    edge = rows_of(n, v, k)
                    for t in range(tiles):
                        ref[slot, k, v * tiles + t] = edge[:, LANES * t : LANES * (t + 1)]

    for copy in strip_copies:
        copy.wait()
    for k in range(levels):
        flank(members, k, strips[2 * members, k])
        for i in range(members):
            flank(i, k, picked[i, k] + strips[members + i, k])
    for copy in f_copies:
        copy.wait()
    edges(members, lambda n, v, k: forcing_rows[n, v, k])
    for i in range(members):
        for n in range(2):
            pltpu.make_async_copy(kick_ref.at[i, :, :, rows[n]], field_rows.at[i, n], done.at[1 + i]).wait()
            copies[2 * i + n].wait()
        edges(i, lambda n, v, k: field_rows[i, n, v, k] + kick_rows[i, n, v, k])


def pack(lay, plan, state, fields, kick, forcing, sides, far_sides):
    members, variables, levels, height, width = state.shape
    here, anywhere = spec(pltpu.VMEM), spec(pl.ANY)
    rows = (members, 2, variables, levels, HALO, width)
    return pl.pallas_call(
        functools.partial(pack_kernel, lay),
        in_specs=[spec(pltpu.SMEM)] + [anywhere] * 16,
        out_specs=[here] * 3,
        out_shape=[
            jax.ShapeDtypeStruct((members + 1, levels, height, LANES), jnp.float32),
            edge_shape(members + 1, forcing),
            edge_shape(members + 1, forcing),
        ],
        scratch_shapes=[
            pltpu.VMEM(rows, jnp.float32),
            pltpu.VMEM(rows, jnp.float32),
            pltpu.VMEM(rows[1:], jnp.float32),
            pltpu.VMEM(sides.shape, jnp.float32),
            pltpu.VMEM((members, levels, height, LANES), jnp.float32),
            pltpu.SemaphoreType.DMA((2 + 2 * members,)),
        ],
        compiler_params=pltpu.CompilerParams(vmem_limit_bytes=VMEM),
    )(plan, far_away(state), *fields, far_away(kick), far_away(forcing), sides, *far_sides)


def blank(*like):
    return pl.pallas_call(
        lambda *refs: None,
        out_specs=[spec(pl.ANY)] * len(like),
        out_shape=[jax.ShapeDtypeStruct(x.shape, x.dtype) for x in like],
        compiler_params=pltpu.CompilerParams(vmem_limit_bytes=1024 * 1024),
    )()


def neighbours(top, bottom):
    lats = lax.axis_size("lat")
    above = lax.ppermute(bottom, "lat", [(i, i + 1) for i in range(lats - 1)])
    below = lax.ppermute(top, "lat", [(i + 1, i) for i in range(lats - 1)])
    return above, below


def beside(strips):
    assert lax.axis_size("lon") == 2
    return lax.ppermute(strips, "lon", [(0, 1), (1, 0)])


def send(lay, ways, fields, sides):
    lons = lax.axis_size("lon")
    fields, sides = list(fields), list(sides)
    for n, pairs in enumerate(ways):
        if pairs:
            crossed = [(a * lons + j, b * lons + 1 - j) for a, b in pairs for j in range(lons)]
            fields[n] = lax.ppermute(fields[n], "member", pairs)
            sides[n] = lax.ppermute(sides[n], ("member", "lon"), crossed)
        else:
            fields[n], sides[n] = blank(fields[n], sides[n])
    return (*fields, *sides)


def routes(lay):
    top = lay.groups - 1

    def both(up, down):
        rising = chain(up - 1, lay.groups) if up else []
        falling = [(top - a, top - b) for a, b in chain(down - 1, lay.groups)] if down else []
        return rising, falling

    chains = [both(up, down) for up in range(lay.kinds) for down in range(lay.kinds)]
    return chains, [(pairs, []) for pairs in lay.singles]


def prepared(state, kick, forcing, clone_src):
    per_dev, groups, group = state.shape[0], lax.axis_size("member"), lax.axis_index("member")
    lay = Layout(4 if groups == 4 else 3, per_dev)
    if groups != 4:
        piece = lax.all_gather(state, "member", axis=0, tiled=True)
        sources = lax.dynamic_slice_in_dim(clone_src, group * per_dev, per_dev)
        state = jnp.take(piece, sources, axis=0, mode="clip")
        still = jnp.arange(per_dev * 3, dtype=jnp.int32)
        plan, _, _, _, *out, strips = first(lay, jnp.int32(0), still, state, kick, forcing)
        fields, far_sides = out[:6], out[6:]
        sides = beside(strips)
    else:
        plan, index, following, final, *out, strips = first(lay, group, clone_src, state, kick, forcing)
        first_out, second, third = ((*out[2 * n : 2 * n + 2], *out[6 + 2 * n : 8 + 2 * n]) for n in range(3))
        chains, singles = routes(lay)

        def opening(way):
            return lambda a, b, c, d, strips: (*send(lay, way, (a, b), (c, d)), beside(strips))

        def plain(way):
            return lambda a, b, c, d: send(lay, way, (a, b), (c, d))

        def everything(*like):
            lons = lax.axis_size("lon")
            held = [jnp.zeros_like(x) for x in like]
            for d in range(1, groups):
                pairs = [(a, (a + d) % groups) for a in range(groups)]
                crossed = [(a * lons + j, b * lons + 1 - j) for a, b in pairs for j in range(lons)]
                fields = lax.ppermute(state, "member", pairs)
                sides = lax.ppermute(strips[:per_dev], ("member", "lon"), crossed)
                for i in range(per_dev):
                    source = lax.dynamic_index_in_dim(clone_src, group * per_dev + i, keepdims=False)
                    here = source // per_dev == (group - d) % groups
                    for n, got in ((i, fields), (per_dev + i, sides)):
                        chosen = lax.dynamic_index_in_dim(got, source % per_dev, keepdims=False)
                        held[n] = jnp.where(here, chosen, held[n])
            return tuple(held)

        *got, sides = lax.switch(index[0], [opening(way) for way in chains + singles], *first_out, strips)
        second = lax.switch(following[0], [plain(way) for way in chains], *second)
        third = lax.switch(final[0], [plain(way) for way in chains] + [everything], *third)
        fields = (*got[:2], *second[:2], *third[:2])
        far_sides = (*got[2:], *second[2:], *third[2:])

    assert per_dev == 2
    side, top, bottom = pack(lay, plan, state, fields, kick, forcing, sides, far_sides)
    return plan[lay.place :], (state, *fields), side, top, bottom


def cut(rows, strip, v):
    width = rows.shape[1]
    count = -(-width // SPAN)
    lane = lane_index((rows.shape[0], LANES))
    source = [rows[:, LANES * t : LANES * (t + 1)] for t in range(width // LANES)]
    tiles = []
    for c in range(count):
        first = SPAN * c - HALO
        if c == 0:
            tile = jnp.where(lane < HALO, turn(strip, -2 * HALO * v), turn(source[0], HALO))
        else:
            t, offset = first // LANES, first % LANES
            if t + 1 < len(source):
                later = turn(source[t + 1], -offset)
            else:
                later = turn(strip, LANES - offset - 2 * HALO * v - HALO)
            tile = jnp.where(lane < LANES - offset, turn(source[t], -offset), later)
        tiles.append(tile)
    return tiles


def step_kernel(
    state_ref, up_ref, down_ref, second_up_ref, second_down_ref, third_up_ref, third_down_ref, kick_ref, forcing_ref,
    above_ref, below_ref, side_ref, coupling_ref, place_ref, lat_ref, out_ref, cells, other, source, result, table, stage, field, kicks, drive, done,
):
    members, variables, levels, height, width = state_ref.shape
    count = -(-width // SPAN)
    tall = height + 2 * HALO
    at_top = lat_ref[0] == 0
    at_bottom = lat_ref[0] == lat_ref[1] - 1
    others = up_ref, down_ref, second_up_ref, second_down_ref, third_up_ref, third_down_ref

    def fetch():
        for m in range(members):

            def bring(whole):
                for k in range(levels):
                    pltpu.make_async_copy(whole.at[:, k], field.at[k, m], done.at[1 + k, m]).start()

            where_found(place_ref[m], members, lambda j: state_ref.at[j], others, bring)
            for k in range(levels):
                pltpu.make_async_copy(kick_ref.at[m, :, k], kicks.at[k, m], done.at[1 + levels + k, m]).start()

    def fetched(k, m):
        pltpu.make_async_copy(kick_ref.at[m, :, k], field.at[k, m], done.at[1 + k, m]).wait()
        pltpu.make_async_copy(kick_ref.at[m, :, k], kicks.at[k, m], done.at[1 + levels + k, m]).wait()

    def leave(k, m=None, v=None, wait=False):
        if wait:
            for m in range(members):
                pltpu.make_async_copy(stage.at[m], out_ref.at[m, :, k], done.at[0, m]).wait()
        else:
            pltpu.make_async_copy(stage.at[m, v], out_ref.at[m, v, k], done.at[0, m]).start()

    def driven(k):
        return pltpu.make_async_copy(forcing_ref.at[:, k], drive, done.at[1 + 2 * levels, 0])

    def edge(ref, slot, k, v):
        tiles = width // LANES
        rows = [ref[slot, k, v * tiles + t] for t in range(tiles)]
        return jnp.concatenate(rows, axis=1), ref[slot, k, variables * tiles]

    def lay(rows, strip, v, target, at, scale):
        for c, tile in enumerate(cut(rows, strip, v)):
            target[c, v, at : at + rows.shape[0]] = tile if scale is None else tile * scale

    blocks = tall // ROWS
    pad = ROWS
    origin = lat_ref[2]

    line = lax.broadcasted_iota(jnp.int32, (ROWS, LANES), 0)
    north, south = range(blocks)[0], range(blocks)[-1]

    def advance_tile(step, now, later, c):
        last = step == STEPS - 1
        shared = 0 < step < STEPS - 1
        assert HALO - REACH * 2 <= ROWS // 2

        def load(ref, m, v, r, d=0):
            at = pad + ROWS * r
            return ref[m, c, v, at : at + ROWS] if d == 0 else ref[m, c, v, pl.ds(origin + at + d, ROWS)]

        def view(get, r):
            return jnp.where(line < ROWS // 2, get(south), get(north)) if r is None else get(r)

        inner = list(range(1, blocks - 1))
        for r in inner if last else [None] + inner if shared else range(blocks):
            centre, along, across = [], [], []
            for m in range(members):
                centre.append([view(lambda r: load(now, m, v, r), r) for v in range(variables)])
                ku, kv = K * centre[m][0], K * centre[m][1]
                eu, ev = 8.0 * ku, 8.0 * kv
                along.append((16.0 * K - eu, 16.0 * K + eu, ku - K, -K - ku))
                across.append((16.0 * K - ev, 16.0 * K + ev, kv - K, -K - kv))
            for v in range(variables):
                driving = view(lambda r: source[c, v, ROWS * r : ROWS * (r + 1)], r)
                weights = [table[v * variables + w] for w in range(variables)]
                for m in range(members):
                    q = centre[m][v]
                    shifted = {d: view(lambda r: load(now, m, v, r, d), r) for d in (1, -1, 2, -2)}
                    total = driving
                    for w in range(variables):
                        total += weights[w] * centre[m][w]
                    near = along[m][0] * turn(q, -1) + along[m][1] * turn(q, 1)
                    far = along[m][2] * turn(q, -2) + along[m][3] * turn(q, 2)
                    near += across[m][0] * shifted[1] + across[m][1] * shifted[-1]
                    far += across[m][2] * shifted[2] + across[m][3] * shifted[-2]
                    total += near + far
                    if last:
                        result[m, c, v, ROWS * (r - 1) : ROWS * r] = total
                        continue
                    for to, outside in ((north, at_top), (south, at_bottom)):
                        if r is None or r == to:
                            at = pad + ROWS * to
                            later[m, c, v, at : at + ROWS] = jnp.where(outside, 0.0, total)
                    if r in inner:
                        later[m, c, v, pad + ROWS * r : pad + ROWS * (r + 1)] = total

    fetch()
    driven(0).start()

    @pl.loop(0, levels)
    def _(k):
        for m in range(members):
            for v in range(variables):
                lay(*edge(above_ref, m, k, v), v, cells.at[m], pad, None)
                lay(*edge(below_ref, m, k, v), v, cells.at[m], pad + HALO + height, None)
        for v in range(variables):
            lay(*edge(above_ref, members, k, v), v, source, 0, 0.1)
            lay(*edge(below_ref, members, k, v), v, source, HALO + height, 0.1)
            for w in range(variables):
                weight = 0.25 * coupling_ref[(k * variables + v) * variables + w]
                weight = weight + (1.0 - 60.0 * K if v == w else 0.0)
                table[v * variables + w] = jnp.full((ROWS, LANES), weight, jnp.float32)
        for m in range(members):
            fetched(k, m)
            for v in range(variables):
                lay(field[k, m, v] + kicks[k, m, v], side_ref[m, k], v, cells.at[m], pad + HALO, None)
        driven(k).wait()
        for v in range(variables):
            lay(drive[v], side_ref[members, k], v, source, HALO, 0.1)

        @pl.when(k + 1 < levels)
        def _():
            driven(k + 1).start()

        @pl.loop(0, count)
        def _(c):
            for step in range(STEPS):
                now, later = (cells, other) if step % 2 == 0 else (other, cells)
                advance_tile(step, now, later, c)

        lane = lane_index((height, LANES))

        @pl.when(k > 0)
        def _():
            leave(k, wait=True)

        for m in range(members):
            for v in range(variables):
                for t in range(width // LANES):
                    c, offset = LANES * t // SPAN, LANES * t % SPAN
                    left = turn(result[m, c, v], -(offset + HALO))
                    if c + 1 < count:
                        right = turn(result[m, c + 1, v], SPAN - offset - HALO)
                        left = jnp.where(lane < SPAN - offset, left, right)
                    stage[m, v, :, LANES * t : LANES * (t + 1)] = left
                leave(k, m, v)

    leave(0, wait=True)


def advance(place, sources, kick, forcing, above, below, side, coupling):
    members, variables, levels, height, width = kick.shape
    assert height % ROWS == 0 and HALO == ROWS
    count = -(-width // SPAN)
    tall = height + 2 * HALO
    lat = jnp.stack([lax.axis_index("lat"), jnp.int32(lax.axis_size("lat")), jnp.int32(0)])
    here, scalars, anywhere = spec(pltpu.VMEM), spec(pltpu.SMEM), spec(pl.ANY)
    block = (variables, height, width)
    state, *others = sources
    return pl.pallas_call(
        step_kernel,
        in_specs=[anywhere] * 9 + [here] * 3 + [scalars] * 3,
        out_specs=spec(pltpu.HBM),
        out_shape=jax.ShapeDtypeStruct(kick.shape, jnp.float32),
        scratch_shapes=[
            pltpu.VMEM((members, count, variables, tall + 2 * ROWS, LANES), jnp.float32),
            pltpu.VMEM((members, count, variables, tall + 2 * ROWS, LANES), jnp.float32),
            pltpu.VMEM((count, variables, tall, LANES), jnp.float32),
            pltpu.VMEM((members, count, variables, height, LANES), jnp.float32),
            pltpu.VMEM((variables * variables, ROWS, LANES), jnp.float32),
            pltpu.VMEM((members, *block), jnp.float32),
            pltpu.VMEM((levels, members, *block), jnp.float32),
            pltpu.VMEM((levels, members, *block), jnp.float32),
            pltpu.VMEM(block, jnp.float32),
            pltpu.SemaphoreType.DMA((2 + 2 * levels, members)),
        ],
        compiler_params=pltpu.CompilerParams(vmem_limit_bytes=VMEM),
    )(
        far_away(state), *others, far_away(kick), far_away(forcing), above, below, side, coupling.reshape(-1), place, lat
    )


def shards(state, kick, forcing, coupling, clone_src):
    place, sources, side, top, bottom = prepared(state, kick, forcing, clone_src)
    above, below = neighbours(top, bottom)
    return advance(place, sources, kick, forcing, above, below, side, coupling)


def solution(mesh):
    in_specs = (
        P("member", None, None, "lat", "lon"),
        P("member", None, None, "lat", "lon"),
        P(None, None, "lat", "lon"),
        P(),
        P(),
    )
    out_specs = P("member", None, None, "lat", "lon")
    return jax.shard_map(shards, mesh=mesh, in_specs=in_specs, out_specs=out_specs, check_vma=False)
```

```python
import functools
import itertools

import functools

import jax
import jax.numpy as jnp
import numpy as np
from jax import lax
from jax.experimental import pallas as pl
from jax.experimental.pallas import tpu as pltpu
from jax.sharding import PartitionSpec as P

STEPS = 4
REACH = 2
HALO = STEPS * REACH
LANES = 128
ROWS = 8
SPAN = LANES - 2 * HALO
K = 0.05 / 12.0
VMEM = 14 * 1024 * 1024


def lane_index(shape):
    return lax.broadcasted_iota(jnp.int32, shape, len(shape) - 1)


def turn(x, shift):
    shift = shift % LANES
    return x if shift == 0 else pltpu.roll(x, shift, x.ndim - 1)


def chain(bits, groups):
    stops = [0] + [x for x in range(1, groups - 1) if bits >> (x - 1) & 1] + [groups - 1]
    return list(zip(stops[:-1], stops[1:]))


SINGLES = 9


def pairings(groups):
    found = []
    for sources in itertools.product(range(groups + 1), repeat=groups):
        pairs = [(a - 1, b) for b, a in enumerate(sources) if a]
        loads = [(e, a < b) for a, b in pairs for e in range(min(a, b), max(a, b))]
        if pairs and len({a for a, _ in pairs}) == len(pairs) and len(set(loads)) == len(loads) and all(a != b for a, b in pairs):
            found.append((sum(a * (groups + 1) ** b for b, a in enumerate(sources)), pairs))
    return found


class Layout:
    def __init__(self, groups, per_dev):
        self.groups, self.per_dev = groups, per_dev
        self.most = per_dev * (groups - 1)
        self.patterns, self.sends = 1, 1 + 2 * self.most
        self.takes = self.sends + 2 * self.most
        self.place = self.takes + per_dev
        self.size = self.place + per_dev
        self.kinds = 1 + (1 << (groups - 2))
        self.pairings = pairings(groups)
        largest = [p for _, p in self.pairings if not any(set(p) < set(q) for _, q in self.pairings)]
        self.singles = sorted(largest, key=lambda p: (-len(p), sum(abs(a - b) for a, b in p)))[:SINGLES]

    def table(self):
        table = np.zeros(((self.groups + 1) ** self.groups,), np.int32)
        for code, pairs in self.pairings:
            if len({a < b for a, b in pairs}) == 2:
                fits = [n for n, single in enumerate(self.singles) if set(pairs) <= set(single)]
                table[code] = self.kinds * self.kinds + fits[0] if fits else 0
        return table


def plan_lines(lay, clone_ref, group_ref, plan_ref, index_refs, ends, owner, used, twice, falls, lookup):
    groups, per_dev, most = lay.groups, lay.per_dev, lay.most
    me = group_ref[0]
    plan_ref[0] = 1
    for t in range(2 * most):
        plan_ref[lay.patterns + t] = 0
        plan_ref[lay.sends + t] = 0
    for t in range(most):
        twice[t] = 0
        falls[t] = 0
        for g in range(groups):
            owner[t * groups + g] = 0
            used[t * groups + g] = 0
    for i in range(per_dev):
        plan_ref[lay.takes + i] = -1 - clone_ref[me * per_dev + i] % per_dev

    for down in range(2):
        for t in range(most):
            ends[t] = 0
        for a in range(groups - 1):
            for b in range(a + 1, groups):
                source, target = (groups - 1 - a, groups - 1 - b) if down else (a, b)
                spans = sum(1 << (x - 1) for x in range(a + 1, b))
                for j in range(per_dev):
                    member = source * per_dev + j
                    wanted = [clone_ref[target * per_dev + i] == member for i in range(per_dev)]
                    need = functools.reduce(jnp.logical_or, wanted)

                    @pl.when(need)
                    def _():
                        t = jnp.int32(most - 1)
                        for earlier in reversed(range(most - 1)):
                            t = jnp.where(ends[earlier] <= a, earlier, t)
                        ends[t] = b
                        plan_ref[0] = jnp.maximum(plan_ref[0], t + 1)
                        at = 2 * t + down
                        before = plan_ref[lay.patterns + at]
                        bits = jnp.where(before == 0, lay.kinds - 2, before - 1)
                        plan_ref[lay.patterns + at] = 1 + (bits & ~spans)
                        giver, taker = t * groups + source, t * groups + target
                        twice[t] = twice[t] | used[giver] | owner[taker]
                        used[giver] = 1
                        owner[taker] = source + 1

                        @pl.when(me == source)
                        def _():
                            plan_ref[lay.sends + at] = j
                            falls[t] = down

                        for i in range(per_dev):

                            @pl.when((me == target) & wanted[i])
                            def _():
                                plan_ref[lay.takes + i] = at

    lookup[1].wait()
    rounds = plan_ref[0]
    code = jnp.int32(0)
    for g in reversed(range(groups)):
        code = code * (groups + 1) + owner[g]
    branch = lookup[0][code]
    single = (twice[0] == 0) & (branch > 0)
    chains = [plan_ref[lay.patterns + 2 * t] * lay.kinds + plan_ref[lay.patterns + 2 * t + 1] for t in range(3)]
    index_refs[0][0] = jnp.where(single, branch, chains[0])
    index_refs[1][0] = chains[1]
    index_refs[2][0] = jnp.where(rounds > 3, lay.kinds * lay.kinds, chains[2])

    @pl.when(single & (falls[0] == 1))
    def _():
        plan_ref[lay.sends] = plan_ref[lay.sends + 1]

    for i in range(per_dev):
        take = plan_ref[lay.takes + i]
        slot = jnp.where(single & (take < 2), 0, take)
        far = per_dev + jnp.where((take < 4) | (rounds == 3), slot, 4 + i)
        plan_ref[lay.place + i] = jnp.where(take < 0, -1 - take, far)


def first_kernel(
    lay, clone_ref, table_ref, group_ref, state_ref, kick_ref, forcing_ref, plan_ref, index_ref, second_ref, third_ref, *refs
):
    fields, sides, strips_ref = refs[:6], refs[6:12], refs[12]
    sources, table, ends, owner, used, twice, falls, held, kick_ends, forcing_ends, done = refs[-11:]
    members, variables, levels, height, width = state_ref.shape
    copies = [pltpu.make_async_copy(clone_ref, sources, done.at[0]), pltpu.make_async_copy(state_ref, held, done.at[1])]
    for side, at in enumerate((0, width - LANES)):
        for ref, part in ((kick_ref, kick_ends), (forcing_ref, forcing_ends)):
            piece = ref.at[(slice(None),) * (len(ref.shape) - 1) + (pl.ds(at, LANES),)]
            copies.append(pltpu.make_async_copy(piece, part.at[side], done.at[len(copies)]))
    listed = pltpu.make_async_copy(table_ref, table, done.at[10])
    for copy in [copies[0], listed, *copies[1:]]:
        copy.start()
    copies[0].wait()
    indices = index_ref, second_ref, third_ref
    plan_lines(lay, sources, group_ref, plan_ref, indices, ends, owner, used, twice, falls, (table, listed))
    copies[1].wait()
    sent = [plan_ref[lay.sends + n] for n in range(6)]
    given = [plan_ref[lay.patterns + n] for n in range(6)]
    wanted = [given[0] + given[1] > 0, *(given[n] > 0 for n in range(1, 6))]
    later = [pltpu.make_async_copy(held.at[sent[n]], fields[n], done.at[4 + n]) for n in range(2, 6)]
    for n in range(4):
        pl.when(wanted[2 + n])(later[n].start)
    for n in range(2):

        @pl.when(wanted[n])
        def _():
            @pl.loop(0, variables)
            def _(v):
                for k in range(levels):
                    fields[n][v, k] = held[sent[n], v, k]

    for copy in copies[2:]:
        copy.wait()
    lane = lane_index((height, LANES))

    @pl.loop(0, levels)
    def _(k):
        for slot in range(2 * members + 1):
            strip = jnp.zeros((height, LANES), jnp.float32)
            for v in range(variables):
                if slot < members:
                    low, high = (held[slot, v, k, :, at : at + LANES] for at in (0, width - LANES))
                elif slot < 2 * members:
                    low, high = (kick_ends[side, slot - members, v, k] for side in range(2))
                else:
                    low, high = (forcing_ends[side, v, k] for side in range(2))
                both = turn(jnp.where(lane < HALO, low, high), HALO + 2 * HALO * v)
                strip = jnp.where(lane >= 2 * HALO * v, both, strip)
            strips_ref[slot, k] = strip

    for ref, j in zip(sides, sent):
        ref[...] = strips_ref[j]
    for n in range(4):
        pl.when(wanted[2 + n])(later[n].wait)


def spec(space):
    return pl.BlockSpec(memory_space=space)


def first(lay, group, clone_src, state, kick, forcing):
    members, variables, levels, height, width = state.shape
    shape = jax.ShapeDtypeStruct
    one = pltpu.VMEM(state.shape[1:], jnp.float32)
    side = pltpu.VMEM((levels, height, LANES), jnp.float32)
    strips = pltpu.VMEM((2 * members + 1, levels, height, LANES), jnp.float32)
    ends = (2, members, variables, levels, height, LANES)
    scalar, here, far = spec(pltpu.SMEM), spec(pltpu.VMEM), spec(pltpu.HBM)
    return pl.pallas_call(
        functools.partial(first_kernel, lay),
        in_specs=[far, far, scalar, far, far, far],
        out_specs=[scalar] * 4 + [here] * 2 + [spec(pl.ANY)] * 4 + [here] * 7,
        out_shape=[shape((lay.size,), jnp.int32)] + [shape((1,), jnp.int32)] * 3 + [one] * 2 + [pltpu.HBM(state.shape[1:], jnp.float32)] * 4 + [side] * 6 + [strips],
        scratch_shapes=[
            pltpu.SMEM(clone_src.shape, jnp.int32),
            pltpu.SMEM(lay.table().shape, jnp.int32),
            pltpu.SMEM((lay.most,), jnp.int32),
            pltpu.SMEM((lay.most * lay.groups,), jnp.int32),
            pltpu.SMEM((lay.most * lay.groups,), jnp.int32),
            pltpu.SMEM((lay.most,), jnp.int32),
            pltpu.SMEM((lay.most,), jnp.int32),
            pltpu.VMEM(state.shape, jnp.float32),
            pltpu.VMEM(ends, jnp.float32),
            pltpu.VMEM((2, *ends[2:]), jnp.float32),
            pltpu.SemaphoreType.DMA((11,)),
        ],
        compiler_params=pltpu.CompilerParams(vmem_limit_bytes=VMEM),
    )(far_away(clone_src), far_away(jnp.asarray(lay.table())), group[None], far_away(state), far_away(kick), far_away(forcing))


def far_away(x):
    return pltpu.with_memory_space_constraint(x, pltpu.HBM)


def edge_shape(members, forcing):
    variables, levels, height, width = forcing.shape
    return jax.ShapeDtypeStruct((members, levels, variables * width // LANES + 1, HALO, LANES), jnp.float32)


def where_found(place, members, local, others, act):
    pl.when(place < members)(lambda: act(local(place)))

    @pl.when(place >= members)
    def _():
        for n, other in enumerate(others[:2]):
            pl.when(place == members + n)(functools.partial(act, other))

        @pl.when(place >= members + 2)
        def _():
            for n, other in enumerate(others[2:]):
                pl.when(place == members + 2 + n)(functools.partial(act, other))


def pack_kernel(
    lay, plan_ref, state_ref, *refs
):
    others, (kick_ref, forcing_ref, sides_ref), others_sides = refs[:6], refs[6:9], refs[9:15]
    side_ref, top_ref, bottom_ref, field_rows, kick_rows, forcing_rows, strips, picked, done = refs[15:]
    up_ref, up_side_ref = others[0], others_sides[0]
    members, variables, levels, height, width = state_ref.shape
    tiles = width // LANES
    places = [plan_ref[lay.place + i] for i in range(members)]
    rows = [pl.ds(0, HALO), pl.ds(height - HALO, HALO)]
    f_copies = [pltpu.make_async_copy(forcing_ref.at[:, :, rows[n]], forcing_rows.at[n], done.at[0]) for n in range(2)]
    copies = []
    for i in range(members):

        def bring(source):
            whole, part = source
            for n in range(2):
                pltpu.make_async_copy(whole.at[:, :, rows[n]], field_rows.at[i, n], done.at[1 + i]).start()
            pltpu.make_async_copy(part, picked.at[i], done.at[2 + members + i]).start()

        local = lambda j: (state_ref.at[j], sides_ref.at[j])
        where_found(places[i], members, local, list(zip(others, others_sides)), bring)
        for n in range(2):
            copies.append(pltpu.make_async_copy(kick_ref.at[i, :, :, rows[n]], kick_rows.at[i, n], done.at[1 + i]))
    strip_copies = [pltpu.make_async_copy(sides_ref, strips, done.at[1 + members])]
    for i in range(members):
        strip_copies.append(pltpu.make_async_copy(up_side_ref, picked.at[i], done.at[2 + members + i]))
    for copy in [strip_copies[0]] + f_copies + copies:
        copy.start()

    def flank(slot, k, strip):
        side_ref[slot, k] = strip
        top_ref[slot, k, variables * tiles] = strip[:HALO]
        bottom_ref[slot, k, variables * tiles] = strip[height - HALO :]

    def edges(slot, rows_of):
        @pl.loop(0, levels)
        def _(k):
            for n, ref in enumerate((top_ref, bottom_ref)):
                for v in range(variables):
                    edge = rows_of(n, v, k)
                    for t in range(tiles):
                        ref[slot, k, v * tiles + t] = edge[:, LANES * t : LANES * (t + 1)]

    for copy in strip_copies:
        copy.wait()
    for k in range(levels):
        flank(members, k, strips[2 * members, k])
        for i in range(members):
            flank(i, k, picked[i, k] + strips[members + i, k])
    for copy in f_copies:
        copy.wait()
    edges(members, lambda n, v, k: forcing_rows[n, v, k])
    for i in range(members):
        for n in range(2):
            pltpu.make_async_copy(kick_ref.at[i, :, :, rows[n]], field_rows.at[i, n], done.at[1 + i]).wait()
            copies[2 * i + n].wait()
        edges(i, lambda n, v, k: field_rows[i, n, v, k] + kick_rows[i, n, v, k])


def pack(lay, plan, state, fields, kick, forcing, sides, far_sides):
    members, variables, levels, height, width = state.shape
    here, anywhere = spec(pltpu.VMEM), spec(pl.ANY)
    rows = (members, 2, variables, levels, HALO, width)
    return pl.pallas_call(
        functools.partial(pack_kernel, lay),
        in_specs=[spec(pltpu.SMEM)] + [anywhere] * 16,
        out_specs=[here] * 3,
        out_shape=[
            jax.ShapeDtypeStruct((members + 1, levels, height, LANES), jnp.float32),
            edge_shape(members + 1, forcing),
            edge_shape(members + 1, forcing),
        ],
        scratch_shapes=[
            pltpu.VMEM(rows, jnp.float32),
            pltpu.VMEM(rows, jnp.float32),
            pltpu.VMEM(rows[1:], jnp.float32),
            pltpu.VMEM(sides.shape, jnp.float32),
            pltpu.VMEM((members, levels, height, LANES), jnp.float32),
            pltpu.SemaphoreType.DMA((2 + 2 * members,)),
        ],
        compiler_params=pltpu.CompilerParams(vmem_limit_bytes=VMEM),
    )(plan, far_away(state), *fields, far_away(kick), far_away(forcing), sides, *far_sides)


def blank(*like):
    return pl.pallas_call(
        lambda *refs: None,
        out_specs=[spec(pl.ANY)] * len(like),
        out_shape=[jax.ShapeDtypeStruct(x.shape, x.dtype) for x in like],
        compiler_params=pltpu.CompilerParams(vmem_limit_bytes=1024 * 1024),
    )()


def neighbours(top, bottom):
    lats = lax.axis_size("lat")
    above = lax.ppermute(bottom, "lat", [(i, i + 1) for i in range(lats - 1)])
    below = lax.ppermute(top, "lat", [(i + 1, i) for i in range(lats - 1)])
    return above, below


def beside(strips):
    assert lax.axis_size("lon") == 2
    return lax.ppermute(strips, "lon", [(0, 1), (1, 0)])


def send(lay, ways, fields, sides):
    lons = lax.axis_size("lon")
    fields, sides = list(fields), list(sides)
    for n, pairs in enumerate(ways):
        if pairs:
            crossed = [(a * lons + j, b * lons + 1 - j) for a, b in pairs for j in range(lons)]
            fields[n] = lax.ppermute(fields[n], "member", pairs)
            sides[n] = lax.ppermute(sides[n], ("member", "lon"), crossed)
        else:
            fields[n], sides[n] = blank(fields[n], sides[n])
    return (*fields, *sides)


def routes(lay):
    top = lay.groups - 1

    def both(up, down):
        rising = chain(up - 1, lay.groups) if up else []
        falling = [(top - a, top - b) for a, b in chain(down - 1, lay.groups)] if down else []
        return rising, falling

    chains = [both(up, down) for up in range(lay.kinds) for down in range(lay.kinds)]
    return chains, [(pairs, []) for pairs in lay.singles]


def prepared(state, kick, forcing, clone_src):
    per_dev, groups, group = state.shape[0], lax.axis_size("member"), lax.axis_index("member")
    lay = Layout(4 if groups == 4 else 3, per_dev)
    if groups != 4:
        piece = lax.all_gather(state, "member", axis=0, tiled=True)
        sources = lax.dynamic_slice_in_dim(clone_src, group * per_dev, per_dev)
        state = jnp.take(piece, sources, axis=0, mode="clip")
        still = jnp.arange(per_dev * 3, dtype=jnp.int32)
        plan, _, _, _, *out, strips = first(lay, jnp.int32(0), still, state, kick, forcing)
        fields, far_sides = out[:6], out[6:]
        sides = beside(strips)
    else:
        plan, index, following, final, *out, strips = first(lay, group, clone_src, state, kick, forcing)
        first_out, second, third = ((*out[2 * n : 2 * n + 2], *out[6 + 2 * n : 8 + 2 * n]) for n in range(3))
        chains, singles = routes(lay)

        def opening(way):
            return lambda a, b, c, d, strips: (*send(lay, way, (a, b), (c, d)), beside(strips))

        def plain(way):
            return lambda a, b, c, d: send(lay, way, (a, b), (c, d))

        def everything(*like):
            lons = lax.axis_size("lon")
            held = [jnp.zeros_like(x) for x in like]
            for d in range(1, groups):
                pairs = [(a, (a + d) % groups) for a in range(groups)]
                crossed = [(a * lons + j, b * lons + 1 - j) for a, b in pairs for j in range(lons)]
                fields = lax.ppermute(state, "member", pairs)
                sides = lax.ppermute(strips[:per_dev], ("member", "lon"), crossed)
                for i in range(per_dev):
                    source = lax.dynamic_index_in_dim(clone_src, group * per_dev + i, keepdims=False)
                    here = source // per_dev == (group - d) % groups
                    for n, got in ((i, fields), (per_dev + i, sides)):
                        chosen = lax.dynamic_index_in_dim(got, source % per_dev, keepdims=False)
                        held[n] = jnp.where(here, chosen, held[n])
            return tuple(held)

        *got, sides = lax.switch(index[0], [opening(way) for way in chains + singles], *first_out, strips)
        second = lax.switch(following[0], [plain(way) for way in chains], *second)
        third = lax.switch(final[0], [plain(way) for way in chains] + [everything], *third)
        fields = (*got[:2], *second[:2], *third[:2])
        far_sides = (*got[2:], *second[2:], *third[2:])

    assert per_dev == 2
    side, top, bottom = pack(lay, plan, state, fields, kick, forcing, sides, far_sides)
    return plan[lay.place :], (state, *fields), side, top, bottom


def cut(rows, strip, v):
    width = rows.shape[1]
    count = -(-width // SPAN)
    lane = lane_index((rows.shape[0], LANES))
    source = [rows[:, LANES * t : LANES * (t + 1)] for t in range(width // LANES)]
    tiles = []
    for c in range(count):
        first = SPAN * c - HALO
        if c == 0:
            tile = jnp.where(lane < HALO, turn(strip, -2 * HALO * v), turn(source[0], HALO))
        else:
            t, offset = first // LANES, first % LANES
            if t + 1 < len(source):
                later = turn(source[t + 1], -offset)
            else:
                later = turn(strip, LANES - offset - 2 * HALO * v - HALO)
            tile = jnp.where(lane < LANES - offset, turn(source[t], -offset), later)
        tiles.append(tile)
    return tiles


def step_kernel(
    state_ref, up_ref, down_ref, second_up_ref, second_down_ref, third_up_ref, third_down_ref, kick_ref, forcing_ref,
    above_ref, below_ref, side_ref, coupling_ref, place_ref, lat_ref, out_ref, cells, other, source, result, table, stage, field, kicks, drive, done,
):
    members, variables, levels, height, width = state_ref.shape
    count = -(-width // SPAN)
    tall = height + 2 * HALO
    at_top = lat_ref[0] == 0
    at_bottom = lat_ref[0] == lat_ref[1] - 1
    others = up_ref, down_ref, second_up_ref, second_down_ref, third_up_ref, third_down_ref

    def fetch(k, wait=()):
        slot = k % 2
        for m in wait or range(members):
            kick = pltpu.make_async_copy(kick_ref.at[m, :, k], kicks.at[slot, m], done.at[2, m])
            if wait:
                pltpu.make_async_copy(kick_ref.at[m, :, k], field.at[slot, m], done.at[1, m]).wait()
                kick.wait()
            else:

                def bring(whole):
                    pltpu.make_async_copy(whole.at[:, k], field.at[slot, m], done.at[1, m]).start()

                where_found(place_ref[m], members, lambda j: state_ref.at[j], others, bring)
                kick.start()

    def leave(k, m=None, v=None, wait=False):
        if wait:
            for m in range(members):
                pltpu.make_async_copy(stage.at[m], out_ref.at[m, :, k], done.at[0, m]).wait()
        else:
            pltpu.make_async_copy(stage.at[m, v], out_ref.at[m, v, k], done.at[0, m]).start()

    def driven(k):
        return pltpu.make_async_copy(forcing_ref.at[:, k], drive, done.at[3, 0])

    def edge(ref, slot, k, v):
        tiles = width // LANES
        rows = [ref[slot, k, v * tiles + t] for t in range(tiles)]
        return jnp.concatenate(rows, axis=1), ref[slot, k, variables * tiles]

    def lay(rows, strip, v, target, at, scale):
        for c, tile in enumerate(cut(rows, strip, v)):
            target[c, v, at : at + rows.shape[0]] = tile if scale is None else tile * scale

    blocks = tall // ROWS
    pad = ROWS
    origin = lat_ref[2]

    line = lax.broadcasted_iota(jnp.int32, (ROWS, LANES), 0)
    north, south = range(blocks)[0], range(blocks)[-1]

    def advance_tile(step, now, later, c):
        last = step == STEPS - 1
        shared = 0 < step < STEPS - 1
        assert HALO - REACH * 2 <= ROWS // 2

        def load(ref, m, v, r, d=0):
            at = pad + ROWS * r
            return ref[m, c, v, at : at + ROWS] if d == 0 else ref[m, c, v, pl.ds(origin + at + d, ROWS)]

        def view(get, r):
            return jnp.where(line < ROWS // 2, get(south), get(north)) if r is None else get(r)

        inner = list(range(1, blocks - 1))
        for r in inner if last else [None] + inner if shared else range(blocks):
            centre, along, across = [], [], []
            for m in range(members):
                centre.append([view(lambda r: load(now, m, v, r), r) for v in range(variables)])
                ku, kv = K * centre[m][0], K * centre[m][1]
                eu, ev = 8.0 * ku, 8.0 * kv
                along.append((16.0 * K - eu, 16.0 * K + eu, ku - K, -K - ku))
                across.append((16.0 * K - ev, 16.0 * K + ev, kv - K, -K - kv))
            for v in range(variables):
                driving = view(lambda r: source[c, v, ROWS * r : ROWS * (r + 1)], r)
                weights = [table[v * variables + w] for w in range(variables)]
                for m in range(members):
                    q = centre[m][v]
                    shifted = {d: view(lambda r: load(now, m, v, r, d), r) for d in (1, -1, 2, -2)}
                    total = driving
                    for w in range(variables):
                        total += weights[w] * centre[m][w]
                    near = along[m][0] * turn(q, -1) + along[m][1] * turn(q, 1)
                    far = along[m][2] * turn(q, -2) + along[m][3] * turn(q, 2)
                    near += across[m][0] * shifted[1] + across[m][1] * shifted[-1]
                    far += across[m][2] * shifted[2] + across[m][3] * shifted[-2]
                    total += near + far
                    if last:
                        result[m, c, v, ROWS * (r - 1) : ROWS * r] = total
                        continue
                    for to, outside in ((north, at_top), (south, at_bottom)):
                        if r is None or r == to:
                            at = pad + ROWS * to
                            later[m, c, v, at : at + ROWS] = jnp.where(outside, 0.0, total)
                    if r in inner:
                        later[m, c, v, pad + ROWS * r : pad + ROWS * (r + 1)] = total

    fetch(0)
    driven(0).start()

    @pl.loop(0, levels)
    def _(k):
        slot = k % 2
        for m in range(members):
            for v in range(variables):
                lay(*edge(above_ref, m, k, v), v, cells.at[m], pad, None)
                lay(*edge(below_ref, m, k, v), v, cells.at[m], pad + HALO + height, None)
        for v in range(variables):
            lay(*edge(above_ref, members, k, v), v, source, 0, 0.1)
            lay(*edge(below_ref, members, k, v), v, source, HALO + height, 0.1)
            for w in range(variables):
                weight = 0.25 * coupling_ref[(k * variables + v) * variables + w]
                weight = weight + (1.0 - 60.0 * K if v == w else 0.0)
                table[v * variables + w] = jnp.full((ROWS, LANES), weight, jnp.float32)
        for m in range(members):
            fetch(k, wait=(m,))
            for v in range(variables):
                lay(field[slot, m, v] + kicks[slot, m, v], side_ref[m, k], v, cells.at[m], pad + HALO, None)
        driven(k).wait()
        for v in range(variables):
            lay(drive[v], side_ref[members, k], v, source, HALO, 0.1)

        @pl.when(k + 1 < levels)
        def _():
            fetch(k + 1)
            driven(k + 1).start()

        @pl.loop(0, count)
        def _(c):
            for step in range(STEPS):
                now, later = (cells, other) if step % 2 == 0 else (other, cells)
                advance_tile(step, now, later, c)

        lane = lane_index((height, LANES))

        @pl.when(k > 0)
        def _():
            leave(k, wait=True)

        for m in range(members):
            for v in range(variables):
                for t in range(width // LANES):
                    c, offset = LANES * t // SPAN, LANES * t % SPAN
                    left = turn(result[m, c, v], -(offset + HALO))
                    if c + 1 < count:
                        right = turn(result[m, c + 1, v], SPAN - offset - HALO)
                        left = jnp.where(lane < SPAN - offset, left, right)
                    stage[m, v, :, LANES * t : LANES * (t + 1)] = left
                leave(k, m, v)

    leave(0, wait=True)


def advance(place, sources, kick, forcing, above, below, side, coupling):
    members, variables, levels, height, width = kick.shape
    assert height % ROWS == 0 and HALO == ROWS
    count = -(-width // SPAN)
    tall = height + 2 * HALO
    lat = jnp.stack([lax.axis_index("lat"), jnp.int32(lax.axis_size("lat")), jnp.int32(0)])
    here, scalars, anywhere = spec(pltpu.VMEM), spec(pltpu.SMEM), spec(pl.ANY)
    block = (variables, height, width)
    state, *others = sources
    return pl.pallas_call(
        step_kernel,
        in_specs=[anywhere] * 9 + [here] * 3 + [scalars] * 3,
        out_specs=spec(pltpu.HBM),
        out_shape=jax.ShapeDtypeStruct(kick.shape, jnp.float32),
        scratch_shapes=[
            pltpu.VMEM((members, count, variables, tall + 3 * ROWS, LANES), jnp.float32),
            pltpu.VMEM((members, count, variables, tall + 3 * ROWS, LANES), jnp.float32),
            pltpu.VMEM((count, variables, tall, LANES), jnp.float32),
            pltpu.VMEM((members, count, variables, height, LANES), jnp.float32),
            pltpu.VMEM((variables * variables, ROWS, LANES), jnp.float32),
            pltpu.VMEM((members, *block), jnp.float32),
            pltpu.VMEM((2, members, *block), jnp.float32),
            pltpu.VMEM((2, members, *block), jnp.float32),
            pltpu.VMEM(block, jnp.float32),
            pltpu.SemaphoreType.DMA((4, members)),
        ],
        compiler_params=pltpu.CompilerParams(vmem_limit_bytes=VMEM),
    )(
        far_away(state), *others, far_away(kick), far_away(forcing), above, below, side, coupling.reshape(-1), place, lat
    )


def shards(state, kick, forcing, coupling, clone_src):
    place, sources, side, top, bottom = prepared(state, kick, forcing, clone_src)
    above, below = neighbours(top, bottom)
    return advance(place, sources, kick, forcing, above, below, side, coupling)


def solution(mesh):
    in_specs = (
        P("member", None, None, "lat", "lon"),
        P("member", None, None, "lat", "lon"),
        P(None, None, "lat", "lon"),
        P(),
        P(),
    )
    out_specs = P("member", None, None, "lat", "lon")
    return jax.shard_map(shards, mesh=mesh, in_specs=in_specs, out_specs=out_specs, check_vma=False)
```
